32 devices in a mesh: dp: 16 (over z, y, core), tensor: 2 (over x).
Axes of the slice: x: 2, y: 2, z: 4, core: 2. Of those that a mesh axis runs over, the one named last changes fastest.
Arguments:
- residual: bfloat16 [16384, 1024], P(('dp', 'tensor')), may hold values from -6 to 6
- cotangent: bfloat16 [16384, 1024], P(('dp', 'tensor')), may hold values from -6 to 6
- sequence_ids: int32 [16384], P('dp'), may hold values from 0 to 4, as said below
- inner_proj: float32 [2, 1024, 2048], P(None, 'dp', 'tensor'), may hold values from -0.1875 to 0.1875
- inner_mean: float32 [2, 1024, 2048], P(None, 'dp', 'tensor'), may hold values from -40 to 40
- inner_square: float32 [2, 1024, 2048], P(None, 'dp', 'tensor'), may hold values from 204.8 to 819.2
- shared_proj: float32 [1024, 288], P(('dp', 'tensor')), may hold values from -0.1875 to 0.1875
- shared_mean: float32 [1024, 288], P(('dp', 'tensor')), may hold values from -40 to 40
- shared_square: float32 [1024, 288], P(('dp', 'tensor')), may hold values from 204.8 to 819.2
- outer_proj: float32 [2048, 1024], P('tensor', 'dp'), may hold values from -0.125 to 0.125
- outer_mean: float32 [2048, 1024], P('tensor', 'dp'), may hold values from -64 to 64
- outer_square: float32 [2048, 1024], P('tensor', 'dp'), may hold values from 655.36 to 2621.44
- conv_params: float32 [5, 2304], P(None, ('dp', 'tensor')), may hold values from -3 to 3
- conv_mean: float32 [5, 2304], P(None, ('dp', 'tensor')), may hold values from -40 to 40
- conv_square: float32 [5, 2304], P(None, ('dp', 'tensor')), may hold values from 204.8 to 819.2
- norm_gains: float32 [3072], P(('dp', 'tensor')), may hold values from 0.5 to 1.5
- gains_mean: float32 [3072], P(('dp', 'tensor')), may hold values from -40 to 40
- gains_square: float32 [3072], P(('dp', 'tensor')), may hold values from 204.8 to 819.2
- head_params: float32 [3, 32], P(None, 'tensor'), may hold values from -10 to 1, as said below
- heads_mean: float32 [3, 32], P(None, 'tensor'), may hold values from -40 to 40
- heads_square: float32 [3, 32], P(None, 'tensor'), may hold values from 204.8 to 819.2
Outputs:
- block_out: bfloat16 [16384, 1024], P(('dp', 'tensor'))
- residual_grad: bfloat16 [16384, 1024], P(('dp', 'tensor'))
- inner_next: float32 [2, 1024, 2048], P(None, 'dp', 'tensor')
- inner_mean_next: float32 [2, 1024, 2048], P(None, 'dp', 'tensor')
- inner_square_next: float32 [2, 1024, 2048], P(None, 'dp', 'tensor')
- shared_next: float32 [1024, 288], P(('dp', 'tensor'))
- shared_mean_next: float32 [1024, 288], P(('dp', 'tensor'))
- shared_square_next: float32 [1024, 288], P(('dp', 'tensor'))
- outer_next: float32 [2048, 1024], P('tensor', 'dp')
- outer_mean_next: float32 [2048, 1024], P('tensor', 'dp')
- outer_square_next: float32 [2048, 1024], P('tensor', 'dp')
- conv_next: float32 [5, 2304], P(None, ('dp', 'tensor'))
- conv_mean_next: float32 [5, 2304], P(None, ('dp', 'tensor'))
- conv_square_next: float32 [5, 2304], P(None, ('dp', 'tensor'))
- gains_next: float32 [3072], P(('dp', 'tensor'))
- gains_mean_next: float32 [3072], P(('dp', 'tensor'))
- gains_square_next: float32 [3072], P(('dp', 'tensor'))
- heads_next: float32 [3, 32], P(None, 'tensor')
- heads_mean_next: float32 [3, 32], P(None, 'tensor')
- heads_square_next: float32 [3, 32], P(None, 'tensor')
The draws below stay inside these ranges and needn't reach their ends.
Inputs may be any that keep to these rules, and one draw needn't show every extreme that they name: `sequence_ids`: within each data group (aligned block of 1024 positions) the values never fall; positions with one value below 4 form one sequence; the value 4 marks empty positions at the group's end. Every group has at least half of its positions in sequences, and in one group a single sequence fills all 1024 positions. `head_params`: row 0 is the step bias, row 1 the logarithm of the decay rate, row 2 the skip factor, which is positive.
All inputs are finite; a program needn't handle non-finite values.
Results may differ from the reference program's by a relative error of at most 0.008.
The reference program's roundings to bfloat16 on the way count: a program that leaves them out, or rounds other values in their place, can miss the bound.
Values may be sent and summed in bfloat16 or wider, within the bound.
No kernel may reach another device: no remote copies, remote signals or barrier semaphores. Data moves between devices by JAX's collectives and lax.ppermute only.
A program may use at most 192 MiB of HBM per device.

```python
import math
import jax
import jax.numpy as jnp
from jax import lax

D = 1024
H = 32
P_SIZE = 64
N = 128
DI = 2048
K = 4
Q = 256
SEQ_SLOTS = 4
STEP = 10
TOK_GRP = 1024
TOKENS = 16384


def draw_sequence_ids(key, part):
    key = jax.random.fold_in(key, 7)
    groups = TOKENS // TOK_GRP
    pad_key, full_key, cut_key = jax.random.split(key, 3)
    padding = jax.random.randint(pad_key, (groups,), 1, TOK_GRP // 2 + 1)
    full_group = jax.random.randint(full_key, (), 0, groups)
    group_index = jnp.arange(groups)
    padding = jnp.where(group_index == full_group, 0, padding)
    filled = TOK_GRP - padding
    boundaries = jax.random.randint(cut_key, (groups, SEQ_SLOTS - 1), 1, filled[:, None])
    boundaries = jnp.where((group_index == full_group)[:, None], TOK_GRP, boundaries)
    places = jnp.arange(TOK_GRP)
    numbers = jnp.sum((places[None, :, None] >= boundaries[:, None, :]).astype(jnp.int32), axis=2)
    numbers = jnp.where(places[None, :] >= filled[:, None], SEQ_SLOTS, numbers)
    return numbers.reshape(-1).astype(jnp.int32)


def draw_head_params(key, part):
    key = jax.random.fold_in(key, 11)
    keys = jax.random.split(key, 5)
    index = jnp.arange(H).astype(jnp.float32)
    fast_share = 0.5
    rise = 2.0
    quick = jax.random.uniform(keys[0], (H,)) < fast_share
    log_rate = jax.random.uniform(keys[1], (H,), minval=-0.7, maxval=0.7)
    fast_target = jax.random.uniform(keys[2], (H,), minval=jnp.log(0.02), maxval=jnp.log(0.04))
    slow_target = jax.random.uniform(keys[3], (H,), minval=jnp.log(0.0005), maxval=jnp.log(0.002))
    target = jnp.where(quick, fast_target, slow_target)
    step_bias = target - log_rate - 0.5
    skip_factor = 0.1 * (1.0 + rise * index / (H - 1)) * jax.random.uniform(keys[4], (H,), minval=0.8, maxval=1.2)
    return jnp.stack([step_bias, log_rate, skip_factor]).astype(jnp.float32)


def block_levels(rng, dims, cuts, smallest, largest):
    level = 1.0
    for dim, shards_of in cuts:
        draws = jax.random.uniform(jax.random.fold_in(jax.random.fold_in(rng, 6), dim), (shards_of,), jnp.float32, smallest / len(cuts), largest / len(cuts))
        level = level * jnp.repeat(jnp.exp(draws), dims[dim] // shards_of).reshape((-1,) + (1,) * (len(dims) - 1 - dim))
    return level


def gaussian(own_key, shape, width, bound, cuts=(), held_as=jnp.bfloat16):
    values = jax.random.normal(own_key, shape, jnp.float32) * width
    if len(cuts) > 0:
        values = block_levels(own_key, shape, cuts, -0.22, 0.18) * values
    return jnp.clip(values, min=-bound, max=bound).astype(held_as)


def setup_inputs(seed: int = 0) -> dict:
    key_list = jax.random.split(jax.random.key(seed), 22)
    return {
        "residual": gaussian(key_list[0], (TOKENS, D), 1.0, 6.0, ((0, 32),)),
        "cotangent": gaussian(key_list[1], (TOKENS, D), 1.0, 6.0, ((0, 32),)),
        "sequence_ids": draw_sequence_ids(jax.random.fold_in(key_list[21], 71), 0),
        "inner_proj": gaussian(key_list[3], (2, D, DI), D ** -0.5, 0.1875, ((1, 16), (2, 2)), jnp.float32),
        "inner_mean": gaussian(key_list[4], (2, D, DI), (0.05 * TOKENS ** 0.5), 40.0, ((1, 16), (2, 2)), jnp.float32),
        "inner_square": jnp.clip(jnp.exp(math.log(819.2) - 1.3862944 * jax.random.uniform(key_list[5], (2, D, DI), jnp.float32) ** block_levels(key_list[5], (2, D, DI), ((1, 16), (2, 2)), -0.2, 0.2)), 204.8, 819.2),
        "shared_proj": gaussian(key_list[6], (D, 2 * N + H), D ** -0.5, 0.1875, ((0, 32),), jnp.float32),
        "shared_mean": gaussian(key_list[7], (D, 2 * N + H), (0.05 * TOKENS ** 0.5), 40.0, ((0, 32),), jnp.float32),
        "shared_square": jnp.clip(jnp.exp(math.log(819.2) - 1.3862944 * jax.random.uniform(key_list[8], (D, 2 * N + H), jnp.float32) ** block_levels(key_list[8], (D, 2 * N + H), ((0, 32),), -0.2, 0.2)), 204.8, 819.2),
        "outer_proj": gaussian(key_list[9], (DI, D), DI ** -0.5, 0.125, ((0, 2), (1, 16)), jnp.float32),
        "outer_mean": gaussian(key_list[10], (DI, D), (0.09 * TOKENS ** 0.5), 64.0, ((0, 2), (1, 16)), jnp.float32),
        "outer_square": jnp.clip(jnp.exp(math.log(2621.44) - 1.3862944 * jax.random.uniform(key_list[11], (DI, D), jnp.float32) ** block_levels(key_list[11], (DI, D), ((0, 2), (1, 16)), -0.2, 0.2)), 655.36, 2621.44),
        "conv_params": gaussian(key_list[12], (K + 1, DI + 2 * N), K ** -0.5, 3.0, ((1, 32),), jnp.float32),
        "conv_mean": gaussian(key_list[13], (K + 1, DI + 2 * N), (0.05 * TOKENS ** 0.5), 40.0, ((1, 32),), jnp.float32),
        "conv_square": jnp.clip(jnp.exp(math.log(819.2) - 1.3862944 * jax.random.uniform(key_list[14], (K + 1, DI + 2 * N), jnp.float32) ** block_levels(key_list[14], (K + 1, DI + 2 * N), ((1, 32),), -0.2, 0.2)), 204.8, 819.2),
        "norm_gains": jnp.clip(1.0 + 0.1 * jax.random.normal(key_list[15], (D + DI,), jnp.float32), 0.5, 1.5),
        "gains_mean": gaussian(key_list[16], (D + DI,), (0.05 * TOKENS ** 0.5), 40.0, ((0, 32),), jnp.float32),
        "gains_square": jnp.clip(jnp.exp(math.log(819.2) - 1.3862944 * jax.random.uniform(key_list[17], (D + DI,), jnp.float32) ** block_levels(key_list[17], (D + DI,), ((0, 32),), -0.2, 0.2)), 204.8, 819.2),
        "head_params": draw_head_params(jax.random.fold_in(key_list[21], 71), 0),
        "heads_mean": gaussian(key_list[19], (3, H), (0.05 * TOKENS ** 0.5), 40.0, ((1, 2),), jnp.float32),
        "heads_square": jnp.clip(jnp.exp(math.log(819.2) - 1.3862944 * jax.random.uniform(key_list[20], (3, H), jnp.float32) ** block_levels(key_list[20], (3, H), ((1, 2),), -0.2, 0.2)), 204.8, 819.2),
    }


@jax.custom_vjp
def low(v):
    return lax.optimization_barrier(v.astype(jnp.bfloat16)).astype(jnp.float32)

@jax.custom_vjp
def low_back(v):
    return v

def low_keep(v):
    return (low(v), None)

def low_pass(kept, grad):
    return (grad,)

def back_keep(v):
    return (v, None)

def back_low(kept, grad):
    return (low(grad),)
low.defvjp(low_keep, low_pass)
low_back.defvjp(back_keep, back_low)
highest = lax.Precision.HIGHEST
norm_epsilon = 1e-05
beta_first = 0.9
beta_second = 0.95
adam_epsilon = 1e-08
weight_decay = 0.1
rate_matrix = 0.02
rate_vector = 0.3
rate_heads = 1.0

def convolve(channels, weights, segment):
    length = channels.shape[0]
    kernel_size = weights.shape[0] - 1
    summed = weights[kernel_size][None, :] + weights[kernel_size - 1][None, :] * channels
    for offset in range(1, kernel_size):
        shifted = jnp.concatenate([jnp.zeros((offset, channels.shape[1]), jnp.float32), channels[:length - offset]], axis=0)
        earlier = jnp.concatenate([jnp.full((offset,), -1, jnp.int32), segment[:length - offset]])
        matches = (earlier == segment).astype(jnp.float32)
        summed = summed + weights[kernel_size - 1 - offset][None, :] * shifted * matches[:, None]
    return jax.nn.silu(summed)

def scan_state(mixed, step_input, head_values, segment, block, head_size, state_size):
    length = mixed.shape[0]
    heads_here = step_input.shape[1]
    inner_width = heads_here * head_size
    blocks = length // block
    values = mixed[:, :inner_width].reshape(blocks, block, heads_here, head_size)
    in_state = mixed[:, inner_width:inner_width + state_size].reshape(blocks, block, state_size)
    out_state = mixed[:, inner_width + state_size:].reshape(blocks, block, state_size)
    step_size = jax.nn.softplus(step_input + head_values[0][None, :])
    step_blocks = step_size.reshape(blocks, block, heads_here).transpose(0, 2, 1)
    log_decay = -step_blocks * jnp.exp(head_values[1])[None, :, None]
    running = jnp.cumsum(log_decay, axis=2)
    segments = segment.reshape(blocks, block)
    places = jnp.arange(block)
    causal = places[:, None] >= places[None, :]
    allowed = (segments[:, :, None] == segments[:, None, :]) & causal[None]
    spread = running[:, :, :, None] - running[:, :, None, :]
    kernel = jnp.exp(jnp.where(allowed[:, None], spread, -1e+30))
    scores = jnp.einsum('bin,bjn->bij', out_state, in_state, precision=highest)
    mixing = kernel * scores[:, None] * step_blocks[:, :, None, :]
    local_part = jnp.einsum('bhij,bjhp->bihp', mixing, values, precision=highest)
    ending = running[:, :, -1:]
    tail_match = (segments == segments[:, -1:]).astype(jnp.float32)
    tail_weight = jnp.exp(ending - running) * step_blocks * tail_match[:, None, :]
    weighted = values * tail_weight.transpose(0, 2, 1)[..., None]
    fresh_state = jnp.einsum('bjhp,bjn->bhpn', weighted, in_state, precision=highest)
    linked = jnp.concatenate([jnp.zeros((1,), jnp.float32), (segments[1:, -1] == segments[:-1, -1]).astype(jnp.float32)])
    factors = jnp.exp(ending[:, :, 0]) * linked[:, None]

    def carry_state(previous, pieces):
        current = pieces[0] + pieces[1][:, None, None] * previous
        return (current, previous)
    initial = jnp.zeros((heads_here, head_size, state_size), jnp.float32)
    entering = lax.scan(carry_state, initial, (fresh_state, factors))[1]
    before_end = jnp.concatenate([jnp.full((1,), -1, jnp.int32), segments[:-1, -1]])
    inherit = (segments == before_end[:, None]).astype(jnp.float32)
    entry_scale = jnp.exp(running) * inherit[:, None, :]
    carried = jnp.einsum('bhpn,bin->bihp', entering, out_state, precision=highest) * entry_scale.transpose(0, 2, 1)[..., None]
    result = local_part + carried + head_values[2][None, None, :, None] * values
    return result.reshape(length, inner_width)

def adam_step(weight, moment, square, gradient, rate, decay):
    moment_next = beta_first * moment + (1.0 - beta_first) * gradient
    square_next = beta_second * square + (1.0 - beta_second) * gradient * gradient
    moment_hat = moment_next / (1.0 - beta_first ** STEP)
    square_hat = square_next / (1.0 - beta_second ** STEP)
    weight_next = weight - rate * (moment_hat / (jnp.sqrt(square_hat) + adam_epsilon) + decay * weight)
    return (weight_next, moment_next, square_next)

def group_forward(tokens, segment, weights):
    inner_weight, shared_weight, outer_weight, conv_weight, gain_values, head_values = weights
    live_rows = (segment < SEQ_SLOTS).astype(jnp.float32)
    inverse = lax.rsqrt(lax.optimization_barrier(jnp.mean(tokens * tokens, axis=1, keepdims=True)) + norm_epsilon)
    normed = low(tokens * inverse * gain_values[:D][None, :])
    gate_input = low_back(jnp.dot(normed, inner_weight[0], precision=highest))
    inner_values = low_back(jnp.dot(normed, inner_weight[1], precision=highest))
    common = jnp.dot(normed, shared_weight, precision=highest)
    channels = jnp.concatenate([inner_values, common[:, :2 * N]], axis=1)
    mixed_channels = low(convolve(channels, conv_weight, segment))
    ssd_out = low_back(scan_state(mixed_channels, common[:, 2 * N:], head_values, segment, Q, P_SIZE, N))
    gated_out = ssd_out * jax.nn.silu(gate_input)
    norm_scale = lax.rsqrt(lax.optimization_barrier(jnp.mean(gated_out * gated_out, axis=1, keepdims=True)) + norm_epsilon)
    scaled = low(gated_out * norm_scale * gain_values[D:][None, :])
    branch = jnp.dot(scaled, outer_weight, precision=highest) * live_rows[:, None]
    return tokens + branch

def reference(residual, cotangent, sequence_ids, inner_proj, inner_mean, inner_square, shared_proj, shared_mean, shared_square, outer_proj, outer_mean, outer_square, conv_params, conv_mean, conv_square, norm_gains, gains_mean, gains_square, head_params, heads_mean, heads_square):
    segments = sequence_ids.reshape(-1, TOK_GRP)

    def forward(tokens, inner_weight, shared_weight, outer_weight, conv_weight, gain_values, head_values):
        weights = (low(inner_weight), low(shared_weight), low(outer_weight), conv_weight, gain_values, head_values)
        grouped = tokens.reshape(-1, TOK_GRP, D)
        one_group = jax.checkpoint(lambda paired: group_forward(paired[0], paired[1], weights))
        return lax.map(one_group, (grouped, segments)).reshape(-1, D)
    output, pullback = jax.vjp(forward, residual.astype(jnp.float32), inner_proj, shared_proj, outer_proj, conv_params, norm_gains, head_params)
    gradients = pullback(cotangent.astype(jnp.float32))
    inner_new = adam_step(inner_proj, inner_mean, inner_square, gradients[1], rate_matrix, weight_decay)
    shared_new = adam_step(shared_proj, shared_mean, shared_square, gradients[2], rate_matrix, weight_decay)
    outer_new = adam_step(outer_proj, outer_mean, outer_square, gradients[3], rate_matrix, weight_decay)
    conv_new = adam_step(conv_params, conv_mean, conv_square, gradients[4], rate_vector, 0.0)
    gains_new = adam_step(norm_gains, gains_mean, gains_square, gradients[5], rate_vector, 0.0)
    heads_new = adam_step(head_params, heads_mean, heads_square, gradients[6], rate_heads, 0.0)
    return (output.astype(jnp.bfloat16), gradients[0].astype(jnp.bfloat16), inner_new[0], inner_new[1], inner_new[2], shared_new[0], shared_new[1], shared_new[2], outer_new[0], outer_new[1], outer_new[2], conv_new[0], conv_new[1], conv_new[2], gains_new[0], gains_new[1], gains_new[2], heads_new[0], heads_new[1], heads_new[2])
```

```python
import functools

import jax
import jax.numpy as jnp
from jax import lax
from jax.experimental import pallas as pl
from jax.experimental.pallas import tpu as pltpu
from jax.sharding import PartitionSpec as P

D = 1024
H = 32
N = 128
DI = 2048
SEQ_SLOTS = 4
STEP = 10
CHUNK = 128
LANES = 128
CORES = 2
HIGH_AXIS = 4

highest = lax.Precision.HIGHEST
f32 = jnp.float32
bf16 = jnp.bfloat16
norm_epsilon = 1e-05
beta_first = 0.9
beta_second = 0.95
adam_epsilon = 1e-08
weight_decay = 0.1
rate_matrix = 0.02
rate_vector = 0.3
rate_heads = 1.0

SEG, BACK, AHEAD, INHERIT, TAIL, LINKED, NEXT, LIVE = 0, 0, 3, 7, 8, 9, 10, 11


def adam_step(weight, moment, square, gradient, rate, decay):
    moment_next = beta_first * moment + (1.0 - beta_first) * gradient
    square_next = beta_second * square + (1.0 - beta_second) * gradient * gradient
    moment_hat = moment_next / (1.0 - beta_first**STEP)
    square_hat = square_next / (1.0 - beta_second**STEP)
    weight_next = weight - rate * (
        moment_hat / (jnp.sqrt(square_hat) + adam_epsilon) + decay * weight
    )
    return (weight_next, moment_next, square_next)


def swap(value, axis, size, distance):
    return lax.ppermute(value, axis, [(i, i ^ distance) for i in range(size)])


def after(value, *others):
    return lax.optimization_barrier((value,) + others)[0]


def axis_parts(dp):
    high = HIGH_AXIS
    middle = dp // (CORES * high)
    return high, middle


def gather_halves(shard, dp):
    high, middle = axis_parts(dp)
    pieces = [shard[None]]
    for step in range(1, high):
        pieces.append(swap(shard, "dp", dp, step * middle * CORES)[None])
    line = jnp.concatenate(pieces, axis=0)
    lines = [line]
    for step in range(1, middle):
        lines.append(swap(line, "dp", dp, step * CORES))
    plane = jnp.concatenate(lines, axis=0)
    return plane, swap(plane, "dp", dp, 1)


def scatter_sum(keep, send, dp):
    high, middle = axis_parts(dp)
    total = keep.astype(f32) + swap(send, "dp", dp, 1).astype(f32)
    total = total.reshape((middle, high) + total.shape[1:])
    line = total[0]
    for step in range(1, middle):
        line = line + swap(total[step].astype(bf16), "dp", dp, step * CORES).astype(f32)
    block = line[0]
    for step in range(1, high):
        block = block + swap(line[step].astype(bf16), "dp", dp, step * middle * CORES).astype(f32)
    return block


def sum_everywhere(value, dp, nt):
    distance = 1
    while distance < nt:
        value = value + swap(value, "tensor", nt, distance)
        distance *= 2
    distance = 1
    while distance < dp:
        value = value + swap(value, "dp", dp, distance)
        distance *= 2
    return value


def relative_places(dp):
    high, middle = axis_parts(dp)
    return [
        (h * middle + m) * CORES + c for c in range(CORES) for m in range(middle) for h in range(high)
    ]


def call(kernel, grid, in_specs, out_specs, out_shape, scratch, flops, scalars=0):
    params = pltpu.CompilerParams(vmem_limit_bytes=50 * 1024 * 1024)
    moved = sum(2 * s.dtype.itemsize * s.size for s in jax.tree.leaves(out_shape))
    return pl.pallas_call(
        kernel,
        grid_spec=pltpu.PrefetchScalarGridSpec(
            num_scalar_prefetch=scalars,
            grid=grid,
            in_specs=in_specs,
            out_specs=out_specs,
            scratch_shapes=scratch,
        ),
        out_shape=out_shape,
        compiler_params=params,
        cost_estimate=pl.CostEstimate(flops=int(flops), bytes_accessed=int(moved), transcendentals=0),
    )


def whole(shape):
    return pl.BlockSpec(shape, lambda *i: (0,) * len(shape))


def rows(count, width, index=lambda i: i):
    return pl.BlockSpec((count, width), lambda i, *s: (index(i), 0))


def shape(*dims, dtype=f32):
    return jax.ShapeDtypeStruct(dims, dtype)


def split(value):
    high = value.astype(bf16)
    return high, (value - high.astype(f32)).astype(bf16)


def mm(a, b, ca=1, cb=0):
    return lax.dot_general(a, b, (((ca,), (cb,)), ((), ())), preferred_element_type=f32)


def mm_left(value, exact, ca=1, cb=0):
    high, low = split(value)
    return mm(high, exact, ca, cb) + mm(low, exact, ca, cb)


def mm_right(exact, value, ca=1, cb=0):
    high, low = split(value)
    return mm(exact, high, ca, cb) + mm(exact, low, ca, cb)


def mm_both(a, b, ca=1, cb=0):
    a_high, a_low = split(a)
    b_high, b_low = split(b)
    return mm(a_high, b_high, ca, cb) + mm(a_low, b_high, ca, cb) + mm(a_high, b_low, ca, cb)


def softplus(value):
    return jnp.maximum(value, 0.0) + jnp.log1p(jnp.exp(-jnp.abs(value)))


def iota(axis):
    return lax.broadcasted_iota(jnp.int32, (CHUNK, LANES), axis)


def pair_spread(tile, pair, left):
    rows_here = tile.shape[0]
    return jnp.where(
        left[:rows_here],
        jnp.broadcast_to(tile[:, 2 * pair : 2 * pair + 1], (rows_here, LANES)),
        jnp.broadcast_to(tile[:, 2 * pair + 1 : 2 * pair + 2], (rows_here, LANES)),
    )


def assemble_kernel(dp, me, near, far, out, sems):
    half = dp // CORES
    places = relative_places(dp)
    copies = []
    for place, distance in enumerate(places):
        source = near.at[place] if place < half else far.at[place - half]
        copies.append(pltpu.make_async_copy(source, out.at[me[0] ^ distance], sems.at[place]))
    for copy in copies:
        copy.start()
    for copy in copies:
        copy.wait()


def assemble(near, far, dp, dp_rank):
    any_spec = pl.BlockSpec(memory_space=pl.ANY)
    return pl.pallas_call(
        functools.partial(assemble_kernel, dp),
        in_specs=[pl.BlockSpec(memory_space=pltpu.SMEM), any_spec, any_spec],
        out_specs=any_spec,
        out_shape=shape(dp, *near.shape[1:], dtype=near.dtype),
        scratch_shapes=[pltpu.SemaphoreType.DMA((dp,))],
        cost_estimate=pl.CostEstimate(flops=0, bytes_accessed=4 * near.size * 2, transcendentals=0),
    )(dp_rank, near, far).reshape(dp * near.shape[1], near.shape[2])


def scan_kernel(
    tok, gain, wv, shw, conv, skip, hp, aux, segr,
    normed_o, ch_o, pre_o, mix_o, ssd_o, hin_o, step_o,
    win, state,
):
    count = tok.shape[0]
    width = wv.shape[1]
    channels = width + 2 * N

    @pl.when(pl.program_id(0) == 0)
    def _():
        win[0:8, :] = jnp.zeros((8, channels), f32)
        state[...] = jnp.zeros(state.shape, f32)

    x = tok[...].astype(f32)
    inverse = lax.rsqrt(jnp.mean(x * x, axis=1, keepdims=True) + norm_epsilon)
    normed = (x * inverse * gain[...]).astype(bf16)
    normed_o[...] = normed
    win[8 : 8 + count, :width] = mm(normed, wv[...])
    common = mm(normed, shw[...])
    win[8 : 8 + count, width:] = common[:, : 2 * N]
    step_o[...] = common[:, 2 * N :] + hp[0:1, :]
    table = aux[...]
    for start in range(0, channels, 256):
        cols = slice(start, start + 256)
        here = win[8 : 8 + count, cols]
        pre = conv[4:5, cols] + conv[3:4, cols] * here
        for back in range(1, 4):
            pre = pre + conv[3 - back : 4 - back, cols] * (
                win[8 - back : 8 - back + count, cols] * table[:, BACK + back : BACK + back + 1]
            )
        ch_o[:, cols] = here
        pre_o[:, cols] = pre
        mix_o[:, cols] = (pre * jax.nn.sigmoid(pre)).astype(bf16)
    win[0:8, :] = win[count : count + 8, :]

    row, col = iota(0), iota(1)
    left = col < 64
    tri = (row >= col).astype(f32)
    for sub in range(count // CHUNK):
        at = slice(sub * CHUNK, (sub + 1) * CHUNK)
        dt = softplus(step_o[at, :])
        run = jnp.dot(tri, -(dt * hp[1:2, :]), precision=highest, preferred_element_type=f32)
        run_t, dt_t = run.T, dt.T
        allowed = (table[at, SEG : SEG + 1] == segr[:, at]) & (row >= col)
        b_in = mix_o[at, width : width + N]
        c_out = mix_o[at, width + N :]
        scores = mm(c_out, b_in, 1, 1)
        ending = run[CHUNK - 1 : CHUNK, :]
        entry = jnp.exp(run) * table[at, INHERIT : INHERIT + 1]
        tail = jnp.exp(ending - run) * dt * table[at, TAIL : TAIL + 1]
        factor = jnp.exp(ending) * table[at, LINKED : LINKED + 1][CHUNK - 1 :, :]
        entering = state[...]
        hin_o[sub] = entering
        for pair in range(width // LANES):
            lanes = slice(pair * LANES, (pair + 1) * LANES)
            x_pair = mix_o[at, lanes].astype(f32)
            mixing = []
            for head in (2 * pair, 2 * pair + 1):
                spread = run[:, head : head + 1] - run_t[head : head + 1, :]
                decays = jnp.exp(jnp.where(allowed, spread, -1e30))
                mixing.append(decays * scores * dt_t[head : head + 1, :])
            x_cross = jnp.concatenate(
                [jnp.where(left, x_pair, 0.0), jnp.where(left, 0.0, x_pair)], axis=0
            ).astype(bf16)
            local = mm_left(jnp.concatenate(mixing, axis=1), x_cross)
            before = entering[:, lanes]
            carried = mm_right(c_out, before) * pair_spread(entry, pair, left)
            ssd_o[at, lanes] = local + carried + skip[:, lanes] * x_pair
            fresh = mm_right(b_in, x_pair * pair_spread(tail, pair, left), 0, 0)
            state[:, lanes] = pair_spread(factor, pair, left) * before + fresh


def gate_kernel(normed, cot, aux, ssd, wg, out_t, gain, gate_o, sg_o, ret_o, sums_o):
    returned = (cot[...].astype(f32) * aux[:, LIVE : LIVE + 1]).astype(bf16)
    ret_o[...] = returned
    gate = mm(normed[...], wg[...])
    gate_o[...] = gate
    scaled_grad = mm(returned, out_t[...])
    sg_o[...] = scaled_grad
    gated = ssd[...] * (gate * jax.nn.sigmoid(gate))
    squares = jnp.sum(gated * gated, axis=1, keepdims=True)
    crossed = jnp.sum(scaled_grad * gain[...] * gated, axis=1, keepdims=True)
    lane = lax.broadcasted_iota(jnp.int32, sums_o.shape, 1)
    sums_o[...] = jnp.where(lane == 0, squares, jnp.where(lane == 1, crossed, 0.0))


def norm_kernel(
    rank, gate_r, sg_r, ssd_r, sums, out_t, gain, branch_o, scaled_o, dssd_o, dgate_o, gain_o
):
    @pl.when(pl.program_id(0) == 0)
    def _():
        gain_o[...] = jnp.zeros(gain_o.shape, f32)

    gate, ssd, scaled_grad = gate_r[...], ssd_r[...], sg_r[...]
    scale = lax.rsqrt(sums[:, 0:1] / DI + norm_epsilon)
    sig = jax.nn.sigmoid(gate)
    silu = gate * sig
    gated = ssd * silu
    scaled = (gated * scale * gain[...]).astype(bf16)
    scaled_o[...] = scaled
    branch_o[...] = mm(scaled, out_t[...], 1, 1).astype(bf16)
    gain_o[...] += jnp.sum(scaled_grad * gated * scale, axis=0, keepdims=True)
    grad = scale * (scaled_grad * gain[...]) - gated * (scale * scale * scale * (sums[:, 1:2] / DI))
    dssd_o[...] = (grad * silu).astype(bf16)
    dgate_o[...] = (grad * ssd * sig * (1.0 + gate * (1.0 - sig))).astype(bf16)


def scan_back_kernel(
    dssd, mix, pre, ch, ssd, hin, step, conv, skip, hp, aux, segr, heads_of,
    dval_o, dcommon_o, dconv_o, dheads_o, dskip_o,
    dmix, dwin, both, dstate, carry,
):
    width = dssd.shape[1]
    channels = width + 2 * N

    @pl.when(pl.program_id(0) == 0)
    def _():
        dwin[CHUNK:, :] = jnp.zeros((8, channels), f32)
        dstate[...] = jnp.zeros(dstate.shape, f32)
        carry[...] = jnp.zeros(carry.shape, f32)
        dconv_o[...] = jnp.zeros(dconv_o.shape, f32)
        dheads_o[...] = jnp.zeros(dheads_o.shape, f32)
        dskip_o[...] = jnp.zeros(dskip_o.shape, f32)

    row, col = iota(0), iota(1)
    left = col < 64
    table = aux[...]
    step_in = step[...]
    dt = softplus(step_in)
    rate = hp[1:2, :]
    tri = (row >= col).astype(f32)
    run = jnp.dot(tri, -(dt * rate), precision=highest, preferred_element_type=f32)
    run_t = run.T
    allowed = (table[:, SEG : SEG + 1] == segr[...]) & (col >= row)
    b_in = mix[:, width : width + N]
    c_out = mix[:, width + N :]
    scores = mm(b_in, c_out, 1, 1)
    ending = run[CHUNK - 1 : CHUNK, :]
    entry = jnp.exp(run) * table[:, INHERIT : INHERIT + 1]
    tail = jnp.exp(ending - run) * table[:, TAIL : TAIL + 1]
    factor = jnp.exp(ending) * table[:, LINKED : LINKED + 1][CHUNK - 1 :, :]
    pairs = jnp.zeros((CHUNK, CHUNK), f32)
    dc = jnp.zeros((CHUNK, N), f32)
    db = jnp.zeros((CHUNK, N), f32)
    for pair in range(width // LANES):
        lanes = slice(pair * LANES, (pair + 1) * LANES)
        x_pair = mix[:, lanes].astype(f32)
        dy_low = dssd[:, lanes]
        dy = dy_low.astype(f32)
        dt_pair = pair_spread(dt, pair, left)
        x_cross = jnp.concatenate(
            [jnp.where(left, x_pair, 0.0), jnp.where(left, 0.0, x_pair)], axis=0
        ).astype(bf16)
        dy_cross = jnp.concatenate(
            [jnp.where(left, dy, 0.0), jnp.where(left, 0.0, dy)], axis=0
        ).astype(bf16)
        inner = mm(x_cross, dy_low, 1, 1)
        mixing = []
        for place, head in enumerate((2 * pair, 2 * pair + 1)):
            spread = run_t[head : head + 1, :] - run[:, head : head + 1]
            decays = jnp.exp(jnp.where(allowed, spread, -1e30))
            mixing.append(decays * scores)
            pairs = pairs + inner[place * CHUNK : (place + 1) * CHUNK] * decays * dt[:, head : head + 1]
        d_state = dstate[:, lanes]
        tail_pair = pair_spread(tail, pair, left)
        flow = mm_left(jnp.concatenate(mixing, axis=1), dy_cross)
        flow = flow + tail_pair * mm_right(b_in, d_state)
        dmix[:, lanes] = dt_pair * flow + skip[:, lanes] * dy
        both[0:CHUNK, lanes] = flow * x_pair
        both[CHUNK:, lanes] = dy * (ssd[:, lanes] - skip[:, lanes] * x_pair)
        dskip_o[:, lanes] += jnp.sum(dy * x_pair, axis=0, keepdims=True)
        entry_dy = pair_spread(entry, pair, left) * dy
        db = db + mm_both(tail_pair * dt_pair * x_pair, d_state, 1, 1)
        dc = dc + mm_both(entry_dy, hin[0, :, lanes], 1, 1)
        dstate[:, lanes] = pair_spread(factor, pair, left) * d_state + mm_right(c_out, entry_dy, 0, 0)
    dmix[:, width : width + N] = db + mm_left(pairs, c_out)
    dmix[:, width + N :] = dc + mm_left(pairs, b_in, 0, 0)

    by_head = mm_left(both[...], heads_of[...])
    direct = by_head[0:CHUNK]
    balance = by_head[CHUNK:] - dt * direct
    later = allowed.astype(f32)
    log_grad = jnp.dot(later, balance, precision=highest, preferred_element_type=f32)
    log_grad = log_grad + table[:, NEXT : NEXT + 1] * carry[0:1, :]
    carry[0:1, :] = log_grad[0:1, :]
    step_grad = (direct - rate * log_grad) * jax.nn.sigmoid(step_in)
    dcommon_o[:, 2 * N :] = step_grad
    dheads_o[0:1, :] += jnp.sum(step_grad, axis=0, keepdims=True)
    dheads_o[1:2, :] += jnp.sum(-(log_grad * dt * rate), axis=0, keepdims=True)

    for start in range(0, channels, 256):
        cols = slice(start, start + 256)
        value = pre[:, cols]
        sig = jax.nn.sigmoid(value)
        dwin[0:CHUNK, cols] = dmix[:, cols] * (sig * (1.0 + value * (1.0 - sig)))
        here = ch[:, cols]
        own = dwin[0:CHUNK, cols]
        total = conv[3:4, cols] * own
        dconv_o[4:5, cols] += jnp.sum(own, axis=0, keepdims=True)
        dconv_o[3:4, cols] += jnp.sum(own * here, axis=0, keepdims=True)
        for ahead in range(1, 4):
            moved = dwin[ahead : ahead + CHUNK, cols] * table[:, AHEAD + ahead : AHEAD + ahead + 1]
            total = total + conv[3 - ahead : 4 - ahead, cols] * moved
            dconv_o[3 - ahead : 4 - ahead, cols] += jnp.sum(moved * here, axis=0, keepdims=True)
        if start < width:
            dval_o[:, cols] = total.astype(bf16)
        else:
            dcommon_o[:, : 2 * N] = total
    dwin[CHUNK:, :] = dwin[0:8, :]


def weight_grad_kernel(dp, me, lhs, rhs, keep_o, send_o, full):
    full[...] = mm(lhs[...], rhs[...], 0, 0)
    half = dp // CORES
    block = lhs.shape[1] // dp
    for place, distance in enumerate(relative_places(dp)):
        start = pl.multiple_of((me[0] ^ distance) * block, block)
        part = full[pl.ds(start, block), :]
        if place < half:
            keep_o[place] = part
        else:
            send_o[place - half] = part.astype(bf16)


def weight_grad(lhs, rhs, dp, dp_rank):
    length, width = rhs.shape
    depth = lhs.shape[1]
    block, half = depth // dp, dp // CORES
    piece = pl.BlockSpec((half, block, 256), lambda i, *s: (0, 0, i))
    return call(
        functools.partial(weight_grad_kernel, dp),
        (width // 256,),
        [whole((length, depth)), pl.BlockSpec((length, 256), lambda i, *s: (0, i))],
        [piece, piece],
        [shape(half, block, width), shape(half, block, width, dtype=bf16)],
        [pltpu.VMEM((depth, 256), f32)],
        2 * length * width * depth,
        scalars=1,
    )(dp_rank, lhs, rhs)


def shared_grad_kernel(lhs, rhs, out):
    out[...] = mm_right(lhs[...], rhs[...], 0, 0)


def input_grad_kernel(rank, dgate, dval, dcommon, tok, wg, wv, shw, ng_o, gain_o):
    @pl.when(pl.program_id(0) == 0)
    def _():
        gain_o[...] = jnp.zeros(gain_o.shape, f32)

    grad = mm(dgate[...], wg[...], 1, 1) + mm(dval[...], wv[...], 1, 1)
    grad = grad + mm_left(dcommon[...], shw[...], 1, 1)
    x = tok[...].astype(f32)
    inverse = lax.rsqrt(jnp.mean(x * x, axis=1, keepdims=True) + norm_epsilon)
    gain_o[...] += jnp.sum(grad * (x * inverse), axis=0, keepdims=True)
    ng_o[...] = grad.astype(ng_o.dtype)


def shards(
    dp, nt,
    residual, cotangent, sequence_ids,
    inner_proj, inner_mean, inner_square,
    shared_proj, shared_mean, shared_square,
    outer_proj, outer_mean, outer_square,
    conv_params, conv_mean, conv_square,
    norm_gains, gains_mean, gains_square,
    head_params, heads_mean, heads_square,
):
    t_rank = lax.axis_index("tensor").astype(jnp.int32)
    d_rank = lax.axis_index("dp").astype(jnp.int32)
    dp_me = d_rank[None]
    t_me = t_rank[None]
    rows_here = residual.shape[0]
    length = rows_here * nt
    width = inner_proj.shape[2]
    heads_here = head_params.shape[1]
    head_size = width // heads_here
    channels = width + 2 * N
    chunks = length // CHUNK
    wide = 2 * CHUNK
    band = min(2 * CHUNK, rows_here)
    per_piece = rows_here // band
    places = jnp.array(relative_places(dp), jnp.int32)

    def over_tensor(value):
        pieces = [value] + [swap(value, "tensor", nt, d) for d in range(1, nt)]
        if nt == 2:
            first = jnp.concatenate(pieces, axis=0)
            second = jnp.concatenate(pieces[::-1], axis=0)
            return jnp.where(t_rank == 0, first, second)
        stacked = jnp.take(jnp.stack(pieces), jnp.arange(nt) ^ t_rank, axis=0)
        return stacked.reshape((nt * value.shape[0],) + value.shape[1:])

    tokens_all = over_tensor(residual)

    def everywhere(value):
        pieces = jnp.stack([value] + [swap(value, "tensor", nt, d) for d in range(1, nt)])
        pieces = jnp.take(pieces, jnp.arange(nt) ^ t_rank, axis=0)
        both = jnp.concatenate(gather_halves(pieces, dp), axis=0)
        spots = jnp.argsort(places ^ d_rank)
        return jnp.take(both, spots, axis=0)

    small = jnp.concatenate([conv_params.reshape(1, -1), norm_gains.reshape(1, -1)], axis=1)
    small_all = everywhere(small).reshape(dp * nt, -1)
    kernel_rows, columns = conv_params.shape
    conv_full = (
        small_all[:, : kernel_rows * columns]
        .reshape(dp * nt, kernel_rows, columns)
        .transpose(1, 0, 2)
        .reshape(kernel_rows, -1)
    )
    gains_full = small_all[:, kernel_rows * columns :].reshape(-1)
    shared_full = everywhere(shared_proj.astype(bf16)).reshape(D, -1)

    value_shard = inner_proj[1].astype(bf16)
    gate_shard = inner_proj[0].astype(bf16)
    outer_shard = outer_proj.T.astype(bf16)
    value_w = assemble(*gather_halves(value_shard, dp), dp, dp_me)
    gate_w = assemble(*gather_halves(gate_shard, dp), dp, dp_me)
    outer_t = assemble(*gather_halves(outer_shard, dp), dp, dp_me)
    cot_all = over_tensor(after(cotangent, tokens_all))

    pre_gain = gains_full[:D].reshape(1, D)
    post_gain = lax.dynamic_slice_in_dim(gains_full, D + t_rank * width, width).reshape(1, width)
    conv_here = jnp.concatenate(
        [lax.dynamic_slice_in_dim(conv_full, t_rank * width, width, 1), conv_full[:, DI:]], axis=1
    )
    conv_here = jnp.pad(conv_here, ((0, 8 - kernel_rows), (0, 0)))
    shared_here = jnp.concatenate(
        [
            shared_full[:, : 2 * N],
            lax.dynamic_slice_in_dim(shared_full, 2 * N + t_rank * heads_here, heads_here, 1),
            jnp.zeros((D, LANES - heads_here), bf16),
        ],
        axis=1,
    )
    common_width = 2 * N + LANES
    head_rows = jnp.stack([head_params[0], jnp.exp(head_params[1])])
    head_rows = jnp.pad(head_rows, ((0, 6), (0, LANES - heads_here)))
    skip = jnp.repeat(head_params[2], head_size).reshape(1, width)
    heads_of = (
        jnp.arange(width)[:, None] // head_size == jnp.arange(LANES)[None, :]
    ).astype(bf16)

    ids = sequence_ids
    blocked = ids.reshape(chunks, CHUNK)
    ends, firsts = blocked[:, -1], blocked[:, 0]
    none = jnp.full((1,), -1, jnp.int32)
    before = jnp.concatenate([none, ends[:-1]])
    following = jnp.concatenate([firsts[1:], none])
    fills = [jnp.full((o,), -1, jnp.int32) for o in range(1, 4)]
    marks = [ids]
    marks += [jnp.concatenate([fills[o - 1], ids[:-o]]) == ids for o in range(1, 4)]
    marks += [jnp.concatenate([ids[o:], fills[o - 1]]) == ids for o in range(1, 4)]
    marks += [
        (blocked == before[:, None]).reshape(-1),
        (blocked == ends[:, None]).reshape(-1),
        jnp.broadcast_to((ends == before)[:, None], blocked.shape).reshape(-1),
        (blocked == following[:, None]).reshape(-1),
        ids < SEQ_SLOTS,
    ]
    aux = jnp.stack([m.astype(f32) for m in marks] + [jnp.zeros((length,), f32)] * 4, axis=1)
    segr = ids.astype(f32).reshape(1, length)
    aux_cols = aux.shape[1]

    steps = length // wide
    normed, chans, pre, mixed, ssd, entering, step_in = call(
        scan_kernel,
        (steps,),
        [
            rows(wide, D), whole((1, D)), whole((D, width)), whole((D, common_width)),
            whole((8, channels)), whole((1, width)), whole((8, LANES)), rows(wide, aux_cols),
            pl.BlockSpec((1, wide), lambda i: (0, i)),
        ],
        [
            rows(wide, D), rows(wide, channels), rows(wide, channels), rows(wide, channels),
            rows(wide, width), pl.BlockSpec((wide // CHUNK, N, width), lambda i: (i, 0, 0)),
            rows(wide, LANES),
        ],
        [
            shape(length, D, dtype=bf16), shape(length, channels), shape(length, channels),
            shape(length, channels, dtype=bf16), shape(length, width),
            shape(chunks, N, width), shape(length, LANES),
        ],
        [pltpu.VMEM((wide + 8, channels), f32), pltpu.VMEM((N, width), f32)],
        length * (2 * D * (width + common_width) + 12 * width * CHUNK),
    )(tokens_all, pre_gain, value_w, shared_here, conv_here, skip, head_rows, aux, segr)

    gate, scaled_grad, returned, sums = call(
        gate_kernel,
        (steps,),
        [
            rows(wide, D), rows(wide, D), rows(wide, aux_cols), rows(wide, width),
            whole((D, width)), whole((D, width)), whole((1, width)),
        ],
        [rows(wide, width), rows(wide, width), rows(wide, D), rows(wide, LANES)],
        [
            shape(length, width), shape(length, width), shape(length, D, dtype=bf16),
            shape(length, LANES),
        ],
        [],
        4 * length * D * width,
    )(normed, cot_all, aux, ssd, gate_w, outer_t, post_gain)
    sums = sums[:, :2].T
    distance = 1
    while distance < nt:
        sums = sums + swap(sums, "tensor", nt, distance)
        distance *= 2
    sums = sums.T

    def relative(block, rank):
        return (rank ^ (block // per_piece)) * per_piece + block % per_piece

    def rel_rows(width_here, offset=0):
        return pl.BlockSpec((band, width_here), lambda i, r: (relative(i + offset, r[0]), 0))

    plain = lambda width_here: pl.BlockSpec((band, width_here), lambda i, r: (i, 0))
    branch, scaled, dssd, dgate, post_grad = call(
        norm_kernel,
        (length // band,),
        [
            rel_rows(width), rel_rows(width), rel_rows(width), rel_rows(2),
            whole((D, width)), whole((1, width)),
        ],
        [plain(D), rel_rows(width), rel_rows(width), rel_rows(width), whole((1, width))],
        [
            shape(length, D, dtype=bf16), shape(length, width, dtype=bf16),
            shape(length, width, dtype=bf16), shape(length, width, dtype=bf16), shape(1, width),
        ],
        [],
        2 * length * D * width,
        scalars=1,
    )(t_me, gate, scaled_grad, ssd, sums, outer_t, post_gain)
    outer_part = scatter_sum(*weight_grad(returned, scaled, dp, dp_me), dp)
    gate_part = scatter_sum(*weight_grad(normed, dgate, dp, dp_me), dp)

    branch = branch.reshape(nt, rows_here, D)
    branch_sum = branch[0].astype(f32)
    for d in range(1, nt):
        branch_sum = branch_sum + swap(branch[d], "tensor", nt, d).astype(f32)
    live_here = lax.dynamic_slice_in_dim(aux[:, LIVE], t_rank * rows_here, rows_here)
    tokens = residual.astype(f32)
    block_out = (tokens + branch_sum * live_here[:, None]).astype(bf16)

    back = lambda i: chunks - 1 - i
    dval, dcommon, dconv, dheads, dskip = call(
        scan_back_kernel,
        (chunks,),
        [
            rows(CHUNK, width, back), rows(CHUNK, channels, back), rows(CHUNK, channels, back),
            rows(CHUNK, channels, back), rows(CHUNK, width, back),
            pl.BlockSpec((1, N, width), lambda i: (chunks - 1 - i, 0, 0)),
            rows(CHUNK, LANES, back), whole((8, channels)), whole((1, width)),
            whole((8, LANES)), rows(CHUNK, aux_cols, back),
            pl.BlockSpec((1, CHUNK), lambda i: (0, chunks - 1 - i)), whole((width, LANES)),
        ],
        [
            rows(CHUNK, width, back), rows(CHUNK, common_width, back), whole((8, channels)),
            whole((8, LANES)), whole((1, width)),
        ],
        [
            shape(length, width, dtype=bf16), shape(length, common_width), shape(8, channels),
            shape(8, LANES), shape(1, width),
        ],
        [
            pltpu.VMEM((CHUNK, channels), f32), pltpu.VMEM((CHUNK + 8, channels), f32),
            pltpu.VMEM((2 * CHUNK, width), f32), pltpu.VMEM((N, width), f32),
            pltpu.VMEM((8, LANES), f32),
        ],
        length * 30 * width * CHUNK,
    )(dssd, mixed, pre, chans, ssd, entering, step_in, conv_here, skip, head_rows, aux, segr, heads_of)

    def input_grad(count, offset, dtype):
        return call(
            input_grad_kernel,
            (count * per_piece,),
            [
                rel_rows(width, offset), rel_rows(width, offset), rel_rows(common_width, offset),
                rel_rows(D, offset), whole((D, width)), whole((D, width)), whole((D, common_width)),
            ],
            [plain(D), whole((1, D))],
            [shape(count * rows_here, D, dtype=dtype), shape(1, D)],
            [],
            4 * count * rows_here * D * (width + common_width),
            scalars=1,
        )(t_me, dgate, dval, dcommon, tokens_all, gate_w, value_w, shared_here)

    sent, pre_grad_sent = input_grad(nt - 1, per_piece, bf16)
    sent = sent.reshape(nt - 1, rows_here, D)
    value_part = scatter_sum(*weight_grad(normed, dval, dp, dp_me), dp)
    own, pre_grad_own = input_grad(1, 0, f32)
    normed_grad = own
    for d in range(1, nt):
        normed_grad = normed_grad + swap(sent[d - 1], "tensor", nt, d).astype(f32)

    shared_grad = pl.pallas_call(
        shared_grad_kernel,
        out_shape=shape(D, common_width),
        compiler_params=pltpu.CompilerParams(vmem_limit_bytes=50 * 1024 * 1024),
        cost_estimate=pl.CostEstimate(
            flops=4 * length * D * common_width, bytes_accessed=6 * D * common_width, transcendentals=0
        ),
    )(normed, dcommon)
    shared_rows = shared_proj.shape[0]
    shared_grad = lax.dynamic_update_slice(
        jnp.pad(shared_grad[:, : 2 * N], ((0, 0), (0, H))),
        shared_grad[:, 2 * N : 2 * N + heads_here],
        (0, 2 * N + t_rank * heads_here),
    )
    shared_grad = shared_grad.reshape(dp, nt, shared_rows, 2 * N + H)
    shared_mine = lax.dynamic_index_in_dim(shared_grad, t_rank, 1, False)
    for d in range(1, nt):
        part = lax.dynamic_index_in_dim(shared_grad, t_rank ^ d, 1, False).astype(bf16)
        shared_mine = shared_mine + swap(part, "tensor", nt, d).astype(f32)
    shared_mine = jnp.take(shared_mine, places ^ d_rank, axis=0)
    half = dp // CORES
    shared_part = scatter_sum(shared_mine[:half], shared_mine[half:].astype(bf16), dp)

    conv_grad = lax.dynamic_update_slice(
        jnp.pad(dconv[:kernel_rows, width:], ((0, 0), (DI, 0))),
        dconv[:kernel_rows, :width],
        (0, t_rank * width),
    )
    post_all = lax.dynamic_update_slice(
        jnp.zeros((1, DI), f32), post_grad, (0, t_rank * width)
    )
    head_grad = jnp.stack(
        [
            dheads[0, :heads_here],
            dheads[1, :heads_here],
            jnp.sum(dskip.reshape(heads_here, head_size), axis=1),
        ]
    )
    head_all = lax.dynamic_update_slice(
        jnp.zeros((3, H), f32), head_grad, (0, t_rank * heads_here)
    )
    vector = jnp.concatenate(
        [
            conv_grad.reshape(1, -1), pre_grad_sent + pre_grad_own, post_all, head_all.reshape(1, -1),
        ],
        axis=1,
    )
    vector = sum_everywhere(vector, dp, nt)
    conv_size = kernel_rows * (DI + 2 * N)
    place = d_rank * nt + t_rank
    conv_part = lax.dynamic_slice_in_dim(
        vector[0, :conv_size].reshape(kernel_rows, -1), place * columns, columns, 1
    )
    gain_count = norm_gains.shape[0]
    gains_part = lax.dynamic_slice_in_dim(vector[0], conv_size + place * gain_count, gain_count)
    heads_part = lax.dynamic_slice_in_dim(
        vector[0, conv_size + D + DI :].reshape(3, H), t_rank * heads_here, heads_here, 1
    )

    inverse = lax.rsqrt(jnp.mean(tokens * tokens, axis=1, keepdims=True) + norm_epsilon)
    normal_tokens = tokens * inverse
    normal_grad = normed_grad * pre_gain
    centered = normal_grad - normal_tokens * jnp.mean(
        normal_grad * normal_tokens, axis=1, keepdims=True
    )
    residual_grad = (cotangent.astype(f32) + inverse * centered).astype(bf16)

    inner_new = adam_step(
        inner_proj, inner_mean, inner_square, jnp.stack([gate_part, value_part]),
        rate_matrix, weight_decay,
    )
    shared_new = adam_step(
        shared_proj, shared_mean, shared_square, shared_part.reshape(shared_proj.shape),
        rate_matrix, weight_decay,
    )
    outer_new = adam_step(
        outer_proj, outer_mean, outer_square, outer_part.T, rate_matrix, weight_decay
    )
    conv_new = adam_step(conv_params, conv_mean, conv_square, conv_part, rate_vector, 0.0)
    gains_new = adam_step(norm_gains, gains_mean, gains_square, gains_part, rate_vector, 0.0)
    heads_new = adam_step(head_params, heads_mean, heads_square, heads_part, rate_heads, 0.0)
    return (
        (block_out, residual_grad)
        + inner_new + shared_new + outer_new + conv_new + gains_new + heads_new
    )


def solution(mesh):
    return jax.shard_map(
        functools.partial(shards, mesh.shape["dp"], mesh.shape["tensor"]),
        mesh=mesh,
        in_specs=(
            P(("dp", "tensor"), None),
            P(("dp", "tensor"), None),
            P("dp"),
            P(None, "dp", "tensor"),
            P(None, "dp", "tensor"),
            P(None, "dp", "tensor"),
            P(("dp", "tensor"), None),
            P(("dp", "tensor"), None),
            P(("dp", "tensor"), None),
            P("tensor", "dp"),
            P("tensor", "dp"),
            P("tensor", "dp"),
            P(None, ("dp", "tensor")),
            P(None, ("dp", "tensor")),
            P(None, ("dp", "tensor")),
            P(("dp", "tensor")),
            P(("dp", "tensor")),
            P(("dp", "tensor")),
            P(None, "tensor"),
            P(None, "tensor"),
            P(None, "tensor"),
        ),
        out_specs=(
            P(("dp", "tensor"), None),
            P(("dp", "tensor"), None),
            P(None, "dp", "tensor"),
            P(None, "dp", "tensor"),
            P(None, "dp", "tensor"),
            P(("dp", "tensor"), None),
            P(("dp", "tensor"), None),
            P(("dp", "tensor"), None),
            P("tensor", "dp"),
            P("tensor", "dp"),
            P("tensor", "dp"),
            P(None, ("dp", "tensor")),
            P(None, ("dp", "tensor")),
            P(None, ("dp", "tensor")),
            P(("dp", "tensor")),
            P(("dp", "tensor")),
            P(("dp", "tensor")),
            P(None, "tensor"),
            P(None, "tensor"),
            P(None, "tensor"),
        ),
        check_vma=False,
    )
```

```python
import functools

import jax
import jax.numpy as jnp
from jax import lax
from jax.experimental import pallas as pl
from jax.experimental.pallas import tpu as pltpu
from jax.sharding import PartitionSpec as P

D = 1024
H = 32
N = 128
DI = 2048
SEQ_SLOTS = 4
STEP = 10
CHUNK = 128
LANES = 128
CORES = 2
HIGH_AXIS = 4

highest = lax.Precision.HIGHEST
f32 = jnp.float32
bf16 = jnp.bfloat16
norm_epsilon = 1e-05
beta_first = 0.9
beta_second = 0.95
adam_epsilon = 1e-08
weight_decay = 0.1
rate_matrix = 0.02
rate_vector = 0.3
rate_heads = 1.0

SEG, BACK, AHEAD, INHERIT, TAIL, LINKED, NEXT, LIVE = 0, 0, 3, 7, 8, 9, 10, 11


def adam_step(weight, moment, square, gradient, rate, decay):
    moment_next = beta_first * moment + (1.0 - beta_first) * gradient
    square_next = beta_second * square + (1.0 - beta_second) * gradient * gradient
    moment_hat = moment_next / (1.0 - beta_first**STEP)
    square_hat = square_next / (1.0 - beta_second**STEP)
    weight_next = weight - rate * (
        moment_hat / (jnp.sqrt(square_hat) + adam_epsilon) + decay * weight
    )
    return (weight_next, moment_next, square_next)


def swap(value, axis, size, distance):
    return lax.ppermute(value, axis, [(i, i ^ distance) for i in range(size)])


def after(value, *others):
    return lax.optimization_barrier((value,) + others)[0]


def axis_parts(dp):
    high = HIGH_AXIS
    middle = dp // (CORES * high)
    return high, middle


def gather_halves(shard, dp):
    high, middle = axis_parts(dp)
    pieces = [shard[None]]
    for step in range(1, high):
        pieces.append(swap(shard, "dp", dp, step * middle * CORES)[None])
    line = jnp.concatenate(pieces, axis=0)
    lines = [line]
    for step in range(1, middle):
        lines.append(swap(line, "dp", dp, step * CORES))
    plane = jnp.concatenate(lines, axis=0)
    return plane, swap(plane, "dp", dp, 1)


def start_sum(keep, send, dp):
    high, middle = axis_parts(dp)
    total = keep + swap(send, "dp", dp, 1).astype(f32)
    return total.reshape((middle, high) + total.shape[1:])


def middle_sum(total, dp):
    line = total[0]
    for step in range(1, total.shape[0]):
        line = line + swap(total[step].astype(bf16), "dp", dp, step * CORES).astype(f32)
    return line


def high_sum(line, dp):
    middle = axis_parts(dp)[1]
    block = line[0]
    for step in range(1, line.shape[0]):
        block = block + swap(line[step].astype(bf16), "dp", dp, step * middle * CORES).astype(f32)
    return block


def sum_everywhere(value, dp, nt):
    distance = 1
    while distance < nt:
        value = value + swap(value, "tensor", nt, distance)
        distance *= 2
    distance = 1
    while distance < dp:
        value = value + swap(value, "dp", dp, distance)
        distance *= 2
    return value


def relative_places(dp):
    high, middle = axis_parts(dp)
    return [
        (h * middle + m) * CORES + c for c in range(CORES) for m in range(middle) for h in range(high)
    ]


def call(kernel, grid, in_specs, out_specs, out_shape, scratch, flops, scalars=0):
    params = pltpu.CompilerParams(vmem_limit_bytes=50 * 1024 * 1024)
    moved = sum(2 * s.dtype.itemsize * s.size for s in jax.tree.leaves(out_shape))
    return pl.pallas_call(
        kernel,
        grid_spec=pltpu.PrefetchScalarGridSpec(
            num_scalar_prefetch=scalars,
            grid=grid,
            in_specs=in_specs,
            out_specs=out_specs,
            scratch_shapes=scratch,
        ),
        out_shape=out_shape,
        compiler_params=params,
        cost_estimate=pl.CostEstimate(flops=int(flops), bytes_accessed=int(moved), transcendentals=0),
    )


def whole(shape):
    return pl.BlockSpec(shape, lambda *i: (0,) * len(shape))


def rows(count, width, index=lambda i: i):
    return pl.BlockSpec((count, width), lambda i, *s: (index(i), 0))


def shape(*dims, dtype=f32):
    return jax.ShapeDtypeStruct(dims, dtype)


def split(value):
    high = value.astype(bf16)
    return high, (value - high.astype(f32)).astype(bf16)


def mm(a, b, ca=1, cb=0):
    return lax.dot_general(a, b, (((ca,), (cb,)), ((), ())), preferred_element_type=f32)


def mm_left(value, exact, ca=1, cb=0):
    high, low = split(value)
    return mm(high, exact, ca, cb) + mm(low, exact, ca, cb)


def mm_right(exact, value, ca=1, cb=0):
    high, low = split(value)
    return mm(exact, high, ca, cb) + mm(exact, low, ca, cb)


def mm_both(a, b, ca=1, cb=0):
    a_high, a_low = split(a)
    b_high, b_low = split(b)
    return mm(a_high, b_high, ca, cb) + mm(a_low, b_high, ca, cb) + mm(a_high, b_low, ca, cb)


def softplus(value):
    return jnp.maximum(value, 0.0) + jnp.log1p(jnp.exp(-jnp.abs(value)))


def iota(axis):
    return lax.broadcasted_iota(jnp.int32, (CHUNK, LANES), axis)


def pair_spread(tile, pair, left):
    rows_here = tile.shape[0]
    return jnp.where(
        left[:rows_here],
        jnp.broadcast_to(tile[:, 2 * pair : 2 * pair + 1], (rows_here, LANES)),
        jnp.broadcast_to(tile[:, 2 * pair + 1 : 2 * pair + 2], (rows_here, LANES)),
    )


def assemble_kernel(dp, me, near, far, *outs):
    half = dp // CORES
    for place, distance in enumerate(relative_places(dp)):
        source, at = (near, place) if place < half else (far, place - half)
        start = 0
        for out in outs:
            out[me[0] ^ distance] = source[at, start : start + out.shape[1], :]
            start += out.shape[1]


def assemble(near, far, dp, dp_rank, counts):
    width = near.shape[2]
    vmem = pl.BlockSpec(memory_space=pltpu.VMEM)
    return pl.pallas_call(
        functools.partial(assemble_kernel, dp),
        in_specs=[pl.BlockSpec(memory_space=pltpu.SMEM), vmem, vmem],
        out_specs=[vmem] * len(counts),
        out_shape=[shape(dp, count, width, dtype=near.dtype) for count in counts],
        compiler_params=pltpu.CompilerParams(vmem_limit_bytes=24 * 1024 * 1024),
        cost_estimate=pl.CostEstimate(flops=0, bytes_accessed=4 * near.size * 2, transcendentals=0),
    )(dp_rank, near, far)


def scan_kernel(
    tok, gain, wv, shw, conv, skip, hp, aux, segr,
    normed_o, ch_o, pre_o, mix_o, ssd_o, hin_o, step_o,
    win, state,
):
    count = tok.shape[0]
    width = wv.shape[1]
    channels = width + 2 * N

    @pl.when(pl.program_id(0) == 0)
    def _():
        win[0:8, :] = jnp.zeros((8, channels), f32)
        state[...] = jnp.zeros(state.shape, f32)

    x = tok[...].astype(f32)
    inverse = lax.rsqrt(jnp.mean(x * x, axis=1, keepdims=True) + norm_epsilon)
    normed = (x * inverse * gain[...]).astype(bf16)
    normed_o[...] = normed
    win[8 : 8 + count, :width] = mm(normed, wv[...])
    common = mm(normed, shw[...])
    win[8 : 8 + count, width:] = common[:, : 2 * N]
    step_o[...] = common[:, 2 * N :] + hp[0:1, :]
    table = aux[...]
    for start in range(0, channels, 256):
        cols = slice(start, start + 256)
        here = win[8 : 8 + count, cols]
        pre = conv[4:5, cols] + conv[3:4, cols] * here
        for back in range(1, 4):
            pre = pre + conv[3 - back : 4 - back, cols] * (
                win[8 - back : 8 - back + count, cols] * table[:, BACK + back : BACK + back + 1]
            )
        ch_o[:, cols] = here
        pre_o[:, cols] = pre
        mix_o[:, cols] = (pre * jax.nn.sigmoid(pre)).astype(bf16)
    win[0:8, :] = win[count : count + 8, :]

    row, col = iota(0), iota(1)
    left = col < 64
    tri = (row >= col).astype(f32)
    for sub in range(count // CHUNK):
        at = slice(sub * CHUNK, (sub + 1) * CHUNK)
        dt = softplus(step_o[at, :])
        run = jnp.dot(tri, -(dt * hp[1:2, :]), precision=highest, preferred_element_type=f32)
        run_t, dt_t = run.T, dt.T
        allowed = (table[at, SEG : SEG + 1] == segr[:, at]) & (row >= col)
        b_in = mix_o[at, width : width + N]
        c_out = mix_o[at, width + N :]
        scores = mm(c_out, b_in, 1, 1)
        ending = run[CHUNK - 1 : CHUNK, :]
        entry = jnp.exp(run) * table[at, INHERIT : INHERIT + 1]
        tail = jnp.exp(ending - run) * dt * table[at, TAIL : TAIL + 1]
        factor = jnp.exp(ending) * table[at, LINKED : LINKED + 1][CHUNK - 1 :, :]
        entering = state[...]
        hin_o[sub] = entering
        for pair in range(width // LANES):
            lanes = slice(pair * LANES, (pair + 1) * LANES)
            x_pair = mix_o[at, lanes].astype(f32)
            mixing = []
            for head in (2 * pair, 2 * pair + 1):
                spread = run[:, head : head + 1] - run_t[head : head + 1, :]
                decays = jnp.exp(jnp.where(allowed, spread, -1e30))
                mixing.append(decays * scores * dt_t[head : head + 1, :])
            x_cross = jnp.concatenate(
                [jnp.where(left, x_pair, 0.0), jnp.where(left, 0.0, x_pair)], axis=0
            ).astype(bf16)
            local = mm_left(jnp.concatenate(mixing, axis=1), x_cross)
            before = entering[:, lanes]
            carried = mm_right(c_out, before) * pair_spread(entry, pair, left)
            ssd_o[at, lanes] = local + carried + skip[:, lanes] * x_pair
            fresh = mm_right(b_in, x_pair * pair_spread(tail, pair, left), 0, 0)
            state[:, lanes] = pair_spread(factor, pair, left) * before + fresh


def gate_kernel(normed, cot, aux, ssd, wg, out_t, gain, gate_o, sg_o, ret_o, sums_o):
    returned = (cot[...].astype(f32) * aux[:, LIVE : LIVE + 1]).astype(bf16)
    ret_o[...] = returned
    gate = mm(normed[...], wg[...])
    gate_o[...] = gate
    scaled_grad = mm(returned, out_t[...])
    sg_o[...] = scaled_grad
    gated = ssd[...] * (gate * jax.nn.sigmoid(gate))
    squares = jnp.sum(gated * gated, axis=1, keepdims=True)
    crossed = jnp.sum(scaled_grad * gain[...] * gated, axis=1, keepdims=True)
    lane = lax.broadcasted_iota(jnp.int32, sums_o.shape, 1)
    sums_o[...] = jnp.where(lane == 0, squares, jnp.where(lane == 1, crossed, 0.0))


def norm_kernel(
    rank, gate_r, sg_r, ssd_r, sums, out_t, gain, branch_o, scaled_o, dssd_o, dgate_o, gain_o
):
    @pl.when(pl.program_id(0) == 0)
    def _():
        gain_o[...] = jnp.zeros(gain_o.shape, f32)

    gate, ssd, scaled_grad = gate_r[...], ssd_r[...], sg_r[...]
    scale = lax.rsqrt(sums[:, 0:1] / DI + norm_epsilon)
    sig = jax.nn.sigmoid(gate)
    silu = gate * sig
    gated = ssd * silu
    scaled = (gated * scale * gain[...]).astype(bf16)
    scaled_o[...] = scaled
    branch_o[...] = mm(scaled, out_t[...], 1, 1).astype(bf16)
    gain_o[...] += jnp.sum(scaled_grad * gated * scale, axis=0, keepdims=True)
    grad = scale * (scaled_grad * gain[...]) - gated * (scale * scale * scale * (sums[:, 1:2] / DI))
    dssd_o[...] = (grad * silu).astype(bf16)
    dgate_o[...] = (grad * ssd * sig * (1.0 + gate * (1.0 - sig))).astype(bf16)


def scan_back_kernel(
    dssd, mix, pre, ch, ssd, hin, step, conv, skip, hp, aux, segr, heads_of,
    state_in, win_in, carry_in,
    dval_o, dcommon_o, dconv_o, dheads_o, dskip_o, dstate, dtail, carry,
    dmix, dwin, both,
):
    width = dssd.shape[1]
    channels = width + 2 * N

    @pl.when(pl.program_id(0) == 0)
    def _():
        dwin[CHUNK:, :] = win_in[...]
        dstate[...] = state_in[...]
        carry[...] = carry_in[...]
        dconv_o[...] = jnp.zeros(dconv_o.shape, f32)
        dheads_o[...] = jnp.zeros(dheads_o.shape, f32)
        dskip_o[...] = jnp.zeros(dskip_o.shape, f32)

    row, col = iota(0), iota(1)
    left = col < 64
    table = aux[...]
    step_in = step[...]
    dt = softplus(step_in)
    rate = hp[1:2, :]
    tri = (row >= col).astype(f32)
    run = jnp.dot(tri, -(dt * rate), precision=highest, preferred_element_type=f32)
    run_t = run.T
    allowed = (table[:, SEG : SEG + 1] == segr[...]) & (col >= row)
    b_in = mix[:, width : width + N]
    c_out = mix[:, width + N :]
    scores = mm(b_in, c_out, 1, 1)
    ending = run[CHUNK - 1 : CHUNK, :]
    entry = jnp.exp(run) * table[:, INHERIT : INHERIT + 1]
    tail = jnp.exp(ending - run) * table[:, TAIL : TAIL + 1]
    factor = jnp.exp(ending) * table[:, LINKED : LINKED + 1][CHUNK - 1 :, :]
    pairs = jnp.zeros((CHUNK, CHUNK), f32)
    dc = jnp.zeros((CHUNK, N), f32)
    db = jnp.zeros((CHUNK, N), f32)
    for pair in range(width // LANES):
        lanes = slice(pair * LANES, (pair + 1) * LANES)
        x_pair = mix[:, lanes].astype(f32)
        dy_low = dssd[:, lanes]
        dy = dy_low.astype(f32)
        dt_pair = pair_spread(dt, pair, left)
        x_cross = jnp.concatenate(
            [jnp.where(left, x_pair, 0.0), jnp.where(left, 0.0, x_pair)], axis=0
        ).astype(bf16)
        dy_cross = jnp.concatenate(
            [jnp.where(left, dy, 0.0), jnp.where(left, 0.0, dy)], axis=0
        ).astype(bf16)
        inner = mm(x_cross, dy_low, 1, 1)
        mixing = []
        for place, head in enumerate((2 * pair, 2 * pair + 1)):
            spread = run_t[head : head + 1, :] - run[:, head : head + 1]
            decays = jnp.exp(jnp.where(allowed, spread, -1e30))
            mixing.append(decays * scores)
            pairs = pairs + inner[place * CHUNK : (place + 1) * CHUNK] * decays * dt[:, head : head + 1]
        d_state = dstate[:, lanes]
        tail_pair = pair_spread(tail, pair, left)
        flow = mm_left(jnp.concatenate(mixing, axis=1), dy_cross)
        flow = flow + tail_pair * mm_right(b_in, d_state)
        dmix[:, lanes] = dt_pair * flow + skip[:, lanes] * dy
        both[0:CHUNK, lanes] = flow * x_pair
        both[CHUNK:, lanes] = dy * (ssd[:, lanes] - skip[:, lanes] * x_pair)
        dskip_o[:, lanes] += jnp.sum(dy * x_pair, axis=0, keepdims=True)
        entry_dy = pair_spread(entry, pair, left) * dy
        db = db + mm_both(tail_pair * dt_pair * x_pair, d_state, 1, 1)
        dc = dc + mm_both(entry_dy, hin[0, :, lanes], 1, 1)
        dstate[:, lanes] = pair_spread(factor, pair, left) * d_state + mm_right(c_out, entry_dy, 0, 0)
    dmix[:, width : width + N] = db + mm_left(pairs, c_out)
    dmix[:, width + N :] = dc + mm_left(pairs, b_in, 0, 0)

    by_head = mm_left(both[...], heads_of[...])
    direct = by_head[0:CHUNK]
    balance = by_head[CHUNK:] - dt * direct
    later = allowed.astype(f32)
    log_grad = jnp.dot(later, balance, precision=highest, preferred_element_type=f32)
    log_grad = log_grad + table[:, NEXT : NEXT + 1] * carry[0:1, :]
    carry[0:1, :] = log_grad[0:1, :]
    step_grad = (direct - rate * log_grad) * jax.nn.sigmoid(step_in)
    dcommon_o[:, 2 * N :] = step_grad
    dheads_o[0:1, :] += jnp.sum(step_grad, axis=0, keepdims=True)
    dheads_o[1:2, :] += jnp.sum(-(log_grad * dt * rate), axis=0, keepdims=True)

    for start in range(0, channels, 256):
        cols = slice(start, start + 256)
        value = pre[:, cols]
        sig = jax.nn.sigmoid(value)
        dwin[0:CHUNK, cols] = dmix[:, cols] * (sig * (1.0 + value * (1.0 - sig)))
        here = ch[:, cols]
        own = dwin[0:CHUNK, cols]
        total = conv[3:4, cols] * own
        dconv_o[4:5, cols] += jnp.sum(own, axis=0, keepdims=True)
        dconv_o[3:4, cols] += jnp.sum(own * here, axis=0, keepdims=True)
        for ahead in range(1, 4):
            moved = dwin[ahead : ahead + CHUNK, cols] * table[:, AHEAD + ahead : AHEAD + ahead + 1]
            total = total + conv[3 - ahead : 4 - ahead, cols] * moved
            dconv_o[3 - ahead : 4 - ahead, cols] += jnp.sum(moved * here, axis=0, keepdims=True)
        if start < width:
            dval_o[:, cols] = total.astype(bf16)
        else:
            dcommon_o[:, : 2 * N] = total
    dwin[CHUNK:, :] = dwin[0:8, :]
    dtail[...] = dwin[0:8, :]


def scatter_blocks(dp, me, full, keep_o, send_o, cols):
    half = dp // CORES
    block = full.shape[0] // dp
    for place, distance in enumerate(relative_places(dp)):
        start = pl.multiple_of((me[0] ^ distance) * block, block)
        part = full[pl.ds(start, block), :]
        if place < half:
            keep_o[place, :, cols] = part
        else:
            send_o[place - half, :, cols] = part.astype(bf16)


def pair_grad_kernel(dp, me, lhs0, lhs1, rhs0, rhs1, keep_o, send_o, turned, full):
    step = pl.program_id(0)
    per = pl.num_programs(0) // 2
    for first, lhs, rhs in ((0, lhs0, rhs0), (per, lhs1, rhs1)):

        @pl.when(step == first)
        def _():
            turned[...] = lhs[...].T

        @pl.when((step >= first) & (step < first + per))
        def _():
            full[...] = mm(turned[...], rhs[...])

    scatter_blocks(dp, me, full, keep_o, send_o, slice(None))


def pair_grad(lhs0, rhs0, lhs1, rhs1, dp, dp_rank):
    length, width = rhs0.shape
    depth = lhs0.shape[1]
    block, half, per = depth // dp, dp // CORES, width // 256
    piece = pl.BlockSpec((half, block, 256), lambda i, *s: (0, i // per, i % per))
    return call(
        functools.partial(pair_grad_kernel, dp),
        (2 * per,),
        [
            whole((length, depth)), whole((length, depth)),
            pl.BlockSpec((length, 256), lambda i, *s: (0, jnp.minimum(i, per - 1))),
            pl.BlockSpec((length, 256), lambda i, *s: (0, jnp.maximum(i - per, 0))),
        ],
        [piece, piece],
        [shape(half, 2 * block, width), shape(half, 2 * block, width, dtype=bf16)],
        [pltpu.VMEM((depth, length), bf16), pltpu.VMEM((depth, 256), f32)],
        4 * length * width * depth,
        scalars=1,
    )(dp_rank, lhs0, lhs1, rhs0, rhs1)


def value_grad_kernel(dp, me, lhs, dval, dcommon, keep_o, send_o, turned, full, wide):
    step = pl.program_id(0)
    last = pl.num_programs(0) - 1

    @pl.when(step == 0)
    def _():
        turned[...] = lhs[...].T

    @pl.when(step < last)
    def _():
        full[...] = mm(turned[...], dval[...])
        cols = pl.ds(pl.multiple_of(step * 256, 256), 256)
        scatter_blocks(dp, me, full, keep_o, send_o, cols)

    @pl.when(step == last)
    def _():
        wide[...] = mm_right(turned[...], dcommon[...])
        cols = slice(keep_o.shape[2] - wide.shape[1], keep_o.shape[2])
        scatter_blocks(dp, me, wide, keep_o, send_o, cols)


def value_grad(lhs, dval, dcommon, dp, dp_rank):
    length, width = dval.shape
    depth, extra = lhs.shape[1], dcommon.shape[1]
    block, half, per = depth // dp, dp // CORES, width // 256
    dims = (half, block, width + extra)
    return call(
        functools.partial(value_grad_kernel, dp),
        (per + 1,),
        [
            whole((length, depth)),
            pl.BlockSpec((length, 256), lambda i, *s: (0, jnp.minimum(i, per - 1))),
            whole((length, extra)),
        ],
        [whole(dims), whole(dims)],
        [shape(*dims), shape(*dims, dtype=bf16)],
        [
            pltpu.VMEM((depth, length), bf16), pltpu.VMEM((depth, 256), f32),
            pltpu.VMEM((depth, extra), f32),
        ],
        2 * length * (width + 2 * extra) * depth,
        scalars=1,
    )(dp_rank, lhs, dval, dcommon)


def input_grad_kernel(rank, dgate, dval, dcommon, tok, wg, wv, shw, ng_o, gain_o):
    @pl.when(pl.program_id(0) == 0)
    def _():
        gain_o[...] = jnp.zeros(gain_o.shape, f32)

    grad = mm(dgate[...], wg[...], 1, 1) + mm(dval[...], wv[...], 1, 1)
    grad = grad + mm_left(dcommon[...], shw[...], 1, 1)
    x = tok[...].astype(f32)
    inverse = lax.rsqrt(jnp.mean(x * x, axis=1, keepdims=True) + norm_epsilon)
    gain_o[...] += jnp.sum(grad * (x * inverse), axis=0, keepdims=True)
    ng_o[...] = grad.astype(ng_o.dtype)


def shards(
    dp, nt,
    residual, cotangent, sequence_ids,
    inner_proj, inner_mean, inner_square,
    shared_proj, shared_mean, shared_square,
    outer_proj, outer_mean, outer_square,
    conv_params, conv_mean, conv_square,
    norm_gains, gains_mean, gains_square,
    head_params, heads_mean, heads_square,
):
    t_rank = lax.axis_index("tensor").astype(jnp.int32)
    d_rank = lax.axis_index("dp").astype(jnp.int32)
    dp_me = d_rank[None]
    t_me = t_rank[None]
    rows_here = residual.shape[0]
    length = rows_here * nt
    width = inner_proj.shape[2]
    heads_here = head_params.shape[1]
    head_size = width // heads_here
    channels = width + 2 * N
    chunks = length // CHUNK
    wide = 2 * CHUNK
    band = min(2 * CHUNK, rows_here)
    per_piece = rows_here // band

    def over_tensor(value):
        pieces = [value] + [swap(value, "tensor", nt, d) for d in range(1, nt)]
        if nt == 2:
            first = jnp.concatenate(pieces, axis=0)
            second = jnp.concatenate(pieces[::-1], axis=0)
            return jnp.where(t_rank == 0, first, second)
        stacked = jnp.take(jnp.stack(pieces), jnp.arange(nt) ^ t_rank, axis=0)
        return stacked.reshape((nt * value.shape[0],) + value.shape[1:])

    kernel_rows, columns = conv_params.shape
    gain_count = norm_gains.shape[0]
    shared_size = shared_proj.size
    exact = jnp.concatenate([conv_params.reshape(-1), norm_gains])
    terms = []
    rest = exact
    for _ in range(3):
        term = lax.optimization_barrier(rest.astype(bf16))
        terms.append(term)
        rest = rest - term.astype(f32)
    small = jnp.concatenate([shared_proj.astype(bf16).reshape(-1)] + terms)
    small_rows = -(-small.size // width)
    while small_rows * nt % 16:
        small_rows += 1
    small = jnp.pad(small, (0, small_rows * width - small.size)).reshape(small_rows, width)
    small_pair = over_tensor(small)
    tokens_all = over_tensor(after(residual, small_pair))

    block_rows = D // dp
    value_shard = jnp.concatenate([inner_proj[1].astype(bf16), small_pair], axis=0)
    near, far = gather_halves(value_shard, dp)
    value_w, small_all = assemble(near, far, dp, dp_me, [block_rows, small_rows * nt])
    value_w = value_w.reshape(D, width)
    other_shard = jnp.concatenate(
        [inner_proj[0].astype(bf16), outer_proj.T.astype(bf16)], axis=0
    )
    other_halves = gather_halves(after(other_shard, near), dp)
    gate_w, outer_t = assemble(*other_halves, dp, dp_me, [block_rows, block_rows])
    gate_w, outer_t = gate_w.reshape(D, width), outer_t.reshape(D, width)
    cot_all = over_tensor(after(cotangent, tokens_all))

    small_all = small_all.reshape(dp * nt, small_rows * width)
    shared_full = small_all[:, :shared_size].reshape(D, -1)
    exact_all = small_all[:, shared_size : shared_size + 3 * exact.size].astype(f32)
    exact_all = exact_all.reshape(dp * nt, 3, exact.size)
    exact_all = (exact_all[:, 0] + exact_all[:, 1]) + exact_all[:, 2]
    conv_full = (
        exact_all[:, : kernel_rows * columns]
        .reshape(dp * nt, kernel_rows, columns)
        .transpose(1, 0, 2)
        .reshape(kernel_rows, -1)
    )
    gains_full = exact_all[:, kernel_rows * columns :].reshape(-1)

    pre_gain = gains_full[:D].reshape(1, D)
    post_gain = lax.dynamic_slice_in_dim(gains_full, D + t_rank * width, width).reshape(1, width)
    conv_here = jnp.concatenate(
        [lax.dynamic_slice_in_dim(conv_full, t_rank * width, width, 1), conv_full[:, DI:]], axis=1
    )
    conv_here = jnp.pad(conv_here, ((0, 8 - kernel_rows), (0, 0)))
    shared_here = jnp.concatenate(
        [
            shared_full[:, : 2 * N],
            lax.dynamic_slice_in_dim(shared_full, 2 * N + t_rank * heads_here, heads_here, 1),
            jnp.zeros((D, LANES - heads_here), bf16),
        ],
        axis=1,
    )
    common_width = 2 * N + LANES
    head_rows = jnp.stack([head_params[0], jnp.exp(head_params[1])])
    head_rows = jnp.pad(head_rows, ((0, 6), (0, LANES - heads_here)))
    skip = jnp.repeat(head_params[2], head_size).reshape(1, width)
    heads_of = (
        jnp.arange(width)[:, None] // head_size == jnp.arange(LANES)[None, :]
    ).astype(bf16)

    ids = sequence_ids
    blocked = ids.reshape(chunks, CHUNK)
    ends, firsts = blocked[:, -1], blocked[:, 0]
    none = jnp.full((1,), -1, jnp.int32)
    before = jnp.concatenate([none, ends[:-1]])
    following = jnp.concatenate([firsts[1:], none])
    fills = [jnp.full((o,), -1, jnp.int32) for o in range(1, 4)]
    marks = [ids]
    marks += [jnp.concatenate([fills[o - 1], ids[:-o]]) == ids for o in range(1, 4)]
    marks += [jnp.concatenate([ids[o:], fills[o - 1]]) == ids for o in range(1, 4)]
    marks += [
        (blocked == before[:, None]).reshape(-1),
        (blocked == ends[:, None]).reshape(-1),
        jnp.broadcast_to((ends == before)[:, None], blocked.shape).reshape(-1),
        (blocked == following[:, None]).reshape(-1),
        ids < SEQ_SLOTS,
    ]
    aux = jnp.stack([m.astype(f32) for m in marks] + [jnp.zeros((length,), f32)] * 4, axis=1)
    segr = ids.astype(f32).reshape(1, length)
    aux_cols = aux.shape[1]

    steps = length // wide
    normed, chans, pre, mixed, ssd, entering, step_in = call(
        scan_kernel,
        (steps,),
        [
            rows(wide, D), whole((1, D)), whole((D, width)), whole((D, common_width)),
            whole((8, channels)), whole((1, width)), whole((8, LANES)), rows(wide, aux_cols),
            pl.BlockSpec((1, wide), lambda i: (0, i)),
        ],
        [
            rows(wide, D), rows(wide, channels), rows(wide, channels), rows(wide, channels),
            rows(wide, width), pl.BlockSpec((wide // CHUNK, N, width), lambda i: (i, 0, 0)),
            rows(wide, LANES),
        ],
        [
            shape(length, D, dtype=bf16), shape(length, channels), shape(length, channels),
            shape(length, channels, dtype=bf16), shape(length, width),
            shape(chunks, N, width), shape(length, LANES),
        ],
        [pltpu.VMEM((wide + 8, channels), f32), pltpu.VMEM((N, width), f32)],
        length * (2 * D * (width + common_width) + 12 * width * CHUNK),
    )(tokens_all, pre_gain, value_w, shared_here, conv_here, skip, head_rows, aux, segr)

    gate, scaled_grad, returned, sums = call(
        gate_kernel,
        (steps,),
        [
            rows(wide, D), rows(wide, D), rows(wide, aux_cols), rows(wide, width),
            whole((D, width)), whole((D, width)), whole((1, width)),
        ],
        [rows(wide, width), rows(wide, width), rows(wide, D), rows(wide, LANES)],
        [
            shape(length, width), shape(length, width), shape(length, D, dtype=bf16),
            shape(length, LANES),
        ],
        [],
        4 * length * D * width,
    )(normed, cot_all, aux, ssd, gate_w, outer_t, post_gain)
    sums = sums[:, :2].T
    distance = 1
    while distance < nt:
        sums = sums + swap(sums, "tensor", nt, distance)
        distance *= 2
    sums = sums.T

    def relative(block, rank):
        return (rank ^ (block // per_piece)) * per_piece + block % per_piece

    def rel_rows(width_here, offset=0):
        return pl.BlockSpec((band, width_here), lambda i, r: (relative(i + offset, r[0]), 0))

    plain = lambda width_here: pl.BlockSpec((band, width_here), lambda i, r: (i, 0))
    branch, scaled, dssd, dgate, post_grad = call(
        norm_kernel,
        (length // band,),
        [
            rel_rows(width), rel_rows(width), rel_rows(width), rel_rows(2),
            whole((D, width)), whole((1, width)),
        ],
        [plain(D), rel_rows(width), rel_rows(width), rel_rows(width), whole((1, width))],
        [
            shape(length, D, dtype=bf16), shape(length, width, dtype=bf16),
            shape(length, width, dtype=bf16), shape(length, width, dtype=bf16), shape(1, width),
        ],
        [],
        2 * length * D * width,
        scalars=1,
    )(t_me, gate, scaled_grad, ssd, sums, outer_t, post_gain)
    sums_og = start_sum(*pair_grad(returned, scaled, normed, dgate, dp, dp_me), dp)
    dssd = after(dssd, sums_og)
    line_og = middle_sum(sums_og, dp)

    branch = branch.reshape(nt, rows_here, D)
    branch_sum = branch[0].astype(f32)
    for d in range(1, nt):
        branch_sum = branch_sum + swap(branch[d], "tensor", nt, d).astype(f32)
    live_here = lax.dynamic_slice_in_dim(aux[:, LIVE], t_rank * rows_here, rows_here)
    tokens = residual.astype(f32)
    block_out = (tokens + branch_sum * live_here[:, None]).astype(bf16)

    calls = 2
    per_call = chunks // calls
    state = jnp.zeros((N, width), f32)
    win = jnp.zeros((8, channels), f32)
    carry = jnp.zeros((8, LANES), f32)
    back_parts = []
    for part in range(calls):
        back = lambda i, top=chunks - 1 - part * per_call: top - i
        here = lambda i: per_call - 1 - i
        *results, state, win, carry = call(
            scan_back_kernel,
            (per_call,),
            [
                rows(CHUNK, width, back), rows(CHUNK, channels, back), rows(CHUNK, channels, back),
                rows(CHUNK, channels, back), rows(CHUNK, width, back),
                pl.BlockSpec((1, N, width), lambda i, back=back: (back(i), 0, 0)),
                rows(CHUNK, LANES, back), whole((8, channels)), whole((1, width)),
                whole((8, LANES)), rows(CHUNK, aux_cols, back),
                pl.BlockSpec((1, CHUNK), lambda i, back=back: (0, back(i))),
                whole((width, LANES)),
                whole((N, width)), whole((8, channels)), whole((8, LANES)),
            ],
            [
                rows(CHUNK, width, here), rows(CHUNK, common_width, here), whole((8, channels)),
                whole((8, LANES)), whole((1, width)),
                whole((N, width)), whole((8, channels)), whole((8, LANES)),
            ],
            [
                shape(length // calls, width, dtype=bf16), shape(length // calls, common_width),
                shape(8, channels), shape(8, LANES), shape(1, width),
                shape(N, width), shape(8, channels), shape(8, LANES),
            ],
            [
                pltpu.VMEM((CHUNK, channels), f32), pltpu.VMEM((CHUNK + 8, channels), f32),
                pltpu.VMEM((2 * CHUNK, width), f32),
            ],
            length // calls * 30 * width * CHUNK,
        )(
            dssd, mixed, pre, chans, ssd, entering, step_in, conv_here, skip, head_rows, aux, segr,
            heads_of, state, win, carry,
        )
        back_parts.append(results)
        if part == 0:
            state = after(state, line_og)
    dval = jnp.concatenate([back_parts[1][0], back_parts[0][0]], axis=0)
    dcommon = jnp.concatenate([back_parts[1][1], back_parts[0][1]], axis=0)
    dconv, dheads, dskip = [back_parts[0][i] + back_parts[1][i] for i in range(2, 5)]
    og_part = high_sum(line_og, dp)
    outer_part, gate_part = og_part[:block_rows], og_part[block_rows:]

    def input_grad(count, offset, dtype):
        return call(
            input_grad_kernel,
            (count * per_piece,),
            [
                rel_rows(width, offset), rel_rows(width, offset), rel_rows(common_width, offset),
                rel_rows(D, offset), whole((D, width)), whole((D, width)), whole((D, common_width)),
            ],
            [plain(D), whole((1, D))],
            [shape(count * rows_here, D, dtype=dtype), shape(1, D)],
            [],
            4 * count * rows_here * D * (width + common_width),
            scalars=1,
        )(t_me, dgate, dval, dcommon, tokens_all, gate_w, value_w, shared_here)

    value_keep, value_send = value_grad(normed, dval, dcommon, dp, dp_me)
    sent, pre_grad_sent = input_grad(nt - 1, per_piece, bf16)
    sent = sent.reshape(nt - 1, rows_here, D)
    own, pre_grad_own = input_grad(1, 0, f32)
    normed_grad = own
    for d in range(1, nt):
        normed_grad = normed_grad + swap(sent[d - 1], "tensor", nt, d).astype(f32)

    value_sum = high_sum(middle_sum(start_sum(value_keep, value_send, dp), dp), dp)
    value_part = value_sum[:, :width]
    shared_rows = shared_proj.shape[0]
    shared_sum = value_sum[:, width:].reshape(nt, shared_rows, common_width)
    shared_mine = lax.dynamic_index_in_dim(shared_sum, t_rank, 0, False)
    shared_common = shared_mine[:, : 2 * N]
    shared_part = jnp.zeros((shared_rows, 2 * N + H), f32)

    def place_heads(table, piece, rank):
        return lax.dynamic_update_slice(
            table, piece[:, 2 * N : 2 * N + heads_here], (0, 2 * N + rank * heads_here)
        )

    shared_part = place_heads(shared_part, shared_mine, t_rank)
    for d in range(1, nt):
        piece = lax.dynamic_index_in_dim(shared_sum, t_rank ^ d, 0, False)
        piece = swap(piece, "tensor", nt, d)
        shared_common = shared_common + piece[:, : 2 * N]
        shared_part = place_heads(shared_part, piece, t_rank ^ d)
    shared_part = lax.dynamic_update_slice(shared_part, shared_common, (0, 0))

    conv_grad = lax.dynamic_update_slice(
        jnp.pad(dconv[:kernel_rows, width:], ((0, 0), (DI, 0))),
        dconv[:kernel_rows, :width],
        (0, t_rank * width),
    )
    post_all = lax.dynamic_update_slice(
        jnp.zeros((1, DI), f32), post_grad, (0, t_rank * width)
    )
    head_grad = jnp.stack(
        [
            dheads[0, :heads_here],
            dheads[1, :heads_here],
            jnp.sum(dskip.reshape(heads_here, head_size), axis=1),
        ]
    )
    head_all = lax.dynamic_update_slice(
        jnp.zeros((3, H), f32), head_grad, (0, t_rank * heads_here)
    )
    vector = jnp.concatenate(
        [
            conv_grad.reshape(1, -1), pre_grad_sent + pre_grad_own, post_all, head_all.reshape(1, -1),
        ],
        axis=1,
    )
    vector = sum_everywhere(vector, dp, nt)
    conv_size = kernel_rows * (DI + 2 * N)
    place = d_rank * nt + t_rank
    conv_part = lax.dynamic_slice_in_dim(
        vector[0, :conv_size].reshape(kernel_rows, -1), place * columns, columns, 1
    )
    gains_part = lax.dynamic_slice_in_dim(vector[0], conv_size + place * gain_count, gain_count)
    heads_part = lax.dynamic_slice_in_dim(
        vector[0, conv_size + D + DI :].reshape(3, H), t_rank * heads_here, heads_here, 1
    )

    inverse = lax.rsqrt(jnp.mean(tokens * tokens, axis=1, keepdims=True) + norm_epsilon)
    normal_tokens = tokens * inverse
    normal_grad = normed_grad * pre_gain
    centered = normal_grad - normal_tokens * jnp.mean(
        normal_grad * normal_tokens, axis=1, keepdims=True
    )
    residual_grad = (cotangent.astype(f32) + inverse * centered).astype(bf16)

    inner_new = adam_step(
        inner_proj, inner_mean, inner_square, jnp.stack([gate_part, value_part]),
        rate_matrix, weight_decay,
    )
    shared_new = adam_step(
        shared_proj, shared_mean, shared_square, shared_part.reshape(shared_proj.shape),
        rate_matrix, weight_decay,
    )
    outer_new = adam_step(
        outer_proj, outer_mean, outer_square, outer_part.T, rate_matrix, weight_decay
    )
    conv_new = adam_step(conv_params, conv_mean, conv_square, conv_part, rate_vector, 0.0)
    gains_new = adam_step(norm_gains, gains_mean, gains_square, gains_part, rate_vector, 0.0)
    heads_new = adam_step(head_params, heads_mean, heads_square, heads_part, rate_heads, 0.0)
    return (
        (block_out, residual_grad)
        + inner_new + shared_new + outer_new + conv_new + gains_new + heads_new
    )


def solution(mesh):
    return jax.shard_map(
        functools.partial(shards, mesh.shape["dp"], mesh.shape["tensor"]),
        mesh=mesh,
        in_specs=(
            P(("dp", "tensor"), None),
            P(("dp", "tensor"), None),
            P("dp"),
            P(None, "dp", "tensor"),
            P(None, "dp", "tensor"),
            P(None, "dp", "tensor"),
            P(("dp", "tensor"), None),
            P(("dp", "tensor"), None),
            P(("dp", "tensor"), None),
            P("tensor", "dp"),
            P("tensor", "dp"),
            P("tensor", "dp"),
            P(None, ("dp", "tensor")),
            P(None, ("dp", "tensor")),
            P(None, ("dp", "tensor")),
            P(("dp", "tensor")),
            P(("dp", "tensor")),
            P(("dp", "tensor")),
            P(None, "tensor"),
            P(None, "tensor"),
            P(None, "tensor"),
        ),
        out_specs=(
            P(("dp", "tensor"), None),
            P(("dp", "tensor"), None),
            P(None, "dp", "tensor"),
            P(None, "dp", "tensor"),
            P(None, "dp", "tensor"),
            P(("dp", "tensor"), None),
            P(("dp", "tensor"), None),
            P(("dp", "tensor"), None),
            P("tensor", "dp"),
            P("tensor", "dp"),
            P("tensor", "dp"),
            P(None, ("dp", "tensor")),
            P(None, ("dp", "tensor")),
            P(None, ("dp", "tensor")),
            P(("dp", "tensor")),
            P(("dp", "tensor")),
            P(("dp", "tensor")),
            P(None, "tensor"),
            P(None, "tensor"),
            P(None, "tensor"),
        ),
        check_vma=False,
    )
```

```python
import functools

import jax
import jax.numpy as jnp
from jax import lax
from jax.experimental import pallas as pl
from jax.experimental.pallas import tpu as pltpu
from jax.sharding import PartitionSpec as P

D = 1024
H = 32
N = 128
DI = 2048
SEQ_SLOTS = 4
STEP = 10
CHUNK = 128
LANES = 128
CORES = 2
HIGH_AXIS = 4

highest = lax.Precision.HIGHEST
f32 = jnp.float32
bf16 = jnp.bfloat16
norm_epsilon = 1e-05
beta_first = 0.9
beta_second = 0.95
adam_epsilon = 1e-08
weight_decay = 0.1
rate_matrix = 0.02
rate_vector = 0.3
rate_heads = 1.0

SEG, BACK, AHEAD, INHERIT, TAIL, LINKED, NEXT, LIVE = 0, 0, 3, 7, 8, 9, 10, 11


def adam_step(weight, moment, square, gradient, rate, decay):
    moment_next = beta_first * moment + (1.0 - beta_first) * gradient
    square_next = beta_second * square + (1.0 - beta_second) * gradient * gradient
    moment_hat = moment_next / (1.0 - beta_first**STEP)
    square_hat = square_next / (1.0 - beta_second**STEP)
    weight_next = weight - rate * (
        moment_hat / (jnp.sqrt(square_hat) + adam_epsilon) + decay * weight
    )
    return (weight_next, moment_next, square_next)


def swap(value, axis, size, distance):
    return lax.ppermute(value, axis, [(i, i ^ distance) for i in range(size)])


def after(value, *others):
    return lax.optimization_barrier((value,) + others)[0]


def axis_parts(dp):
    high = HIGH_AXIS
    middle = dp // (CORES * high)
    return high, middle


def gather_line(shard, dp):
    high, middle = axis_parts(dp)
    pieces = [shard[None]]
    for step in range(1, high):
        pieces.append(swap(shard, "dp", dp, step * middle * CORES)[None])
    return jnp.concatenate(pieces, axis=0)


def gather_plane(line, dp, *first):
    lines = [line]
    for step in range(1, axis_parts(dp)[1]):
        lines.append(after(swap(line, "dp", dp, step * CORES), *first))
    return jnp.concatenate(lines, axis=0)


def start_sum(keep, send, dp):
    high, middle = axis_parts(dp)
    other = swap(send, "dp", dp, 1)
    parts = [slice(step * high, (step + 1) * high) for step in range(middle)]
    line = keep[parts[0]].astype(f32) + other[parts[0]].astype(f32)
    rest = [(keep[at].astype(f32) + other[at].astype(f32)).astype(bf16) for at in parts[1:]]
    return line, rest


def middle_sum(line, rest, dp):
    for step, part in enumerate(rest):
        line = line + swap(part, "dp", dp, (step + 1) * CORES).astype(f32)
    return line[0], [part.astype(bf16) for part in line[1:]]


def high_sum(block, rest, dp):
    middle = axis_parts(dp)[1]
    for step, part in enumerate(rest):
        block = block + swap(part, "dp", dp, (step + 1) * middle * CORES).astype(f32)
    return block


def sum_everywhere(value, dp, nt):
    distance = 1
    while distance < nt:
        value = value + swap(value, "tensor", nt, distance)
        distance *= 2
    distance = 1
    while distance < dp:
        value = value + swap(value, "dp", dp, distance)
        distance *= 2
    return value


def relative_places(dp):
    high, middle = axis_parts(dp)
    return [
        (h * middle + m) * CORES + c for c in range(CORES) for m in range(middle) for h in range(high)
    ]


def call(kernel, grid, in_specs, out_specs, out_shape, scratch, flops, scalars=0, aliases=None):
    params = pltpu.CompilerParams(vmem_limit_bytes=50 * 1024 * 1024)
    moved = sum(2 * s.dtype.itemsize * s.size for s in jax.tree.leaves(out_shape))
    return pl.pallas_call(
        kernel,
        grid_spec=pltpu.PrefetchScalarGridSpec(
            num_scalar_prefetch=scalars,
            grid=grid,
            in_specs=in_specs,
            out_specs=out_specs,
            scratch_shapes=scratch,
        ),
        out_shape=out_shape,
        compiler_params=params,
        input_output_aliases=aliases or {},
        cost_estimate=pl.CostEstimate(flops=int(flops), bytes_accessed=int(moved), transcendentals=0),
    )


def whole(shape):
    return pl.BlockSpec(shape, lambda *i: (0,) * len(shape))


def rows(count, width, index=lambda i: i):
    return pl.BlockSpec((count, width), lambda i, *s: (index(i), 0))


def shape(*dims, dtype=f32):
    return jax.ShapeDtypeStruct(dims, dtype)


def split(value):
    high = value.astype(bf16)
    return high, (value - high.astype(f32)).astype(bf16)


def mm(a, b, ca=1, cb=0):
    return lax.dot_general(a, b, (((ca,), (cb,)), ((), ())), preferred_element_type=f32)


def mm_left(value, exact, ca=1, cb=0):
    high, low = split(value)
    return mm(high, exact, ca, cb) + mm(low, exact, ca, cb)


def mm_right(exact, value, ca=1, cb=0):
    high, low = split(value)
    return mm(exact, high, ca, cb) + mm(exact, low, ca, cb)


def mm_both(a, b, ca=1, cb=0):
    a_high, a_low = split(a)
    b_high, b_low = split(b)
    return mm(a_high, b_high, ca, cb) + mm(a_low, b_high, ca, cb) + mm(a_high, b_low, ca, cb)


def softplus(value):
    return jnp.maximum(value, 0.0) + jnp.log1p(jnp.exp(-jnp.abs(value)))


def iota(axis):
    return lax.broadcasted_iota(jnp.int32, (CHUNK, LANES), axis)


def pair_spread(tile, pair, left):
    rows_here = tile.shape[0]
    return jnp.where(
        left[:rows_here],
        jnp.broadcast_to(tile[:, 2 * pair : 2 * pair + 1], (rows_here, LANES)),
        jnp.broadcast_to(tile[:, 2 * pair + 1 : 2 * pair + 2], (rows_here, LANES)),
    )


def assemble_kernel(dp, me, near, far, *outs):
    half = dp // CORES
    for place, distance in enumerate(relative_places(dp)):
        source, at = (near, place) if place < half else (far, place - half)
        start = 0
        for out in outs:
            out[me[0] ^ distance] = source[at, start : start + out.shape[1], :]
            start += out.shape[1]


def assemble(near, far, dp, dp_rank, counts):
    width = near.shape[2]
    vmem = pl.BlockSpec(memory_space=pltpu.VMEM)
    return pl.pallas_call(
        functools.partial(assemble_kernel, dp),
        in_specs=[pl.BlockSpec(memory_space=pltpu.SMEM), vmem, vmem],
        out_specs=[vmem] * len(counts),
        out_shape=[shape(dp, count, width, dtype=near.dtype) for count in counts],
        compiler_params=pltpu.CompilerParams(vmem_limit_bytes=24 * 1024 * 1024),
        cost_estimate=pl.CostEstimate(flops=0, bytes_accessed=4 * near.size * 2, transcendentals=0),
    )(dp_rank, near, far)


def pick_half(rank, first, second):
    half = (2 * pl.program_id(0)) // pl.num_programs(0)
    own = (half == rank[0]).astype(jnp.int32)
    return jnp.where(jnp.broadcast_to(own, first.shape) == 1, first[...], second[...])


def across(pair, left):
    return jnp.concatenate(
        [jnp.where(left, pair, 0.0), jnp.where(left, 0.0, pair)], axis=0
    ).astype(bf16)


def scan_kernel(
    rank, tok0, tok1, gain, wv, shw, conv, skip, hp, aux, segr,
    normed_o, ch_o, pre_o, mix_o, ssd_o, hin_o, step_o,
    win, state, carried, weighted,
):
    count = tok0.shape[0]
    width = wv.shape[1]
    channels = width + 2 * N

    @pl.when(pl.program_id(0) == 0)
    def _():
        win[0:8, :] = jnp.zeros((8, channels), f32)
        state[...] = jnp.zeros(state.shape, f32)

    x = pick_half(rank, tok0, tok1).astype(f32)
    inverse = lax.rsqrt(jnp.mean(x * x, axis=1, keepdims=True) + norm_epsilon)
    normed = (x * inverse * gain[...]).astype(bf16)
    normed_o[...] = normed
    win[8 : 8 + count, :width] = mm(normed, wv[...])
    common = mm(normed, shw[...])
    win[8 : 8 + count, width:] = common[:, : 2 * N]
    step_o[...] = common[:, 2 * N :] + hp[0:1, :]
    table = aux[...]
    for start in range(0, channels, 256):
        cols = slice(start, start + 256)
        here = win[8 : 8 + count, cols]
        pre = conv[4:5, cols] + conv[3:4, cols] * here
        for back in range(1, 4):
            pre = pre + conv[3 - back : 4 - back, cols] * (
                win[8 - back : 8 - back + count, cols] * table[:, BACK + back : BACK + back + 1]
            )
        ch_o[:, cols] = here
        pre_o[:, cols] = pre
        mix_o[:, cols] = (pre * jax.nn.sigmoid(pre)).astype(bf16)
    win[0:8, :] = win[count : count + 8, :]

    row, col = iota(0), iota(1)
    left = col < 64
    tri = (row >= col).astype(f32)
    for sub in range(count // CHUNK):
        at = slice(sub * CHUNK, (sub + 1) * CHUNK)
        dt = softplus(step_o[at, :])
        run = jnp.dot(tri, -(dt * hp[1:2, :]), precision=highest, preferred_element_type=f32)
        run_t = run.T
        allowed = (table[at, SEG : SEG + 1] == segr[:, at]) & (row >= col)
        b_in = mix_o[at, width : width + N]
        b_turned = b_in.astype(f32).T.astype(bf16)
        c_out = mix_o[at, width + N :]
        scores = mm(c_out, b_in, 1, 1)
        ending = run[CHUNK - 1 : CHUNK, :]
        entry = jnp.exp(run) * table[at, INHERIT : INHERIT + 1]
        tail = jnp.exp(ending - run) * table[at, TAIL : TAIL + 1]
        factor = jnp.exp(ending) * table[at, LINKED : LINKED + 1][CHUNK - 1 :, :]
        hin_o[sub] = state[...]
        carried[...] = mm_right(c_out, state[...])
        for pair in range(width // LANES):
            lanes = slice(pair * LANES, (pair + 1) * LANES)
            x_pair = mix_o[at, lanes].astype(f32)
            stepped = (x_pair * pair_spread(dt, pair, left)).astype(bf16).astype(f32)
            mixing = []
            for head in (2 * pair, 2 * pair + 1):
                spread = run[:, head : head + 1] - run_t[head : head + 1, :]
                decays = jnp.exp(jnp.where(allowed, spread, -1e30))
                mixing.append((decays * scores).astype(bf16))
            local = mm(jnp.concatenate(mixing, axis=1), across(stepped, left))
            ssd_o[at, lanes] = (
                local + carried[:, lanes] * pair_spread(entry, pair, left) + skip[:, lanes] * x_pair
            )
            high, low = split(stepped * pair_spread(tail, pair, left))
            weighted[0, :, lanes] = high
            weighted[1, :, lanes] = low
            state[:, lanes] = pair_spread(factor, pair, left) * state[:, lanes]
        state[...] += mm(b_turned, weighted[0]) + mm(b_turned, weighted[1])


def gate_kernel(rank, normed, cot0, cot1, aux, ssd, wg, out_t, gain, gate_o, sg_o, ret_o, sums_o):
    returned = (pick_half(rank, cot0, cot1).astype(f32) * aux[:, LIVE : LIVE + 1]).astype(bf16)
    ret_o[...] = returned
    gate = mm(normed[...], wg[...])
    gate_o[...] = gate
    scaled_grad = mm(returned, out_t[...])
    sg_o[...] = scaled_grad
    gated = ssd[...] * (gate * jax.nn.sigmoid(gate))
    squares = jnp.sum(gated * gated, axis=1, keepdims=True)
    crossed = jnp.sum(scaled_grad * gain[...] * gated, axis=1, keepdims=True)
    lane = lax.broadcasted_iota(jnp.int32, sums_o.shape, 1)
    sums_o[...] = jnp.where(lane == 0, squares, jnp.where(lane == 1, crossed, 0.0))


def norm_kernel(
    rank, gate_r, sg_r, ssd_r, sums, out_t, gain, branch_o, scaled_o, dssd_o, dgate_o, gain_o
):
    @pl.when(pl.program_id(0) == 0)
    def _():
        gain_o[...] = jnp.zeros(gain_o.shape, f32)

    gate, ssd, scaled_grad = gate_r[...], ssd_r[...], sg_r[...]
    scale = lax.rsqrt(sums[:, 0:1] / DI + norm_epsilon)
    sig = jax.nn.sigmoid(gate)
    silu = gate * sig
    gated = ssd * silu
    scaled = (gated * scale * gain[...]).astype(bf16)
    scaled_o[...] = scaled
    branch_o[...] = mm(scaled, out_t[...], 1, 1).astype(bf16)
    gain_o[...] += jnp.sum(scaled_grad * gated * scale, axis=0, keepdims=True)
    grad = scale * (scaled_grad * gain[...]) - gated * (scale * scale * scale * (sums[:, 1:2] / DI))
    dssd_o[...] = (grad * silu).astype(bf16)
    dgate_o[...] = (grad * ssd * sig * (1.0 + gate * (1.0 - sig))).astype(bf16)


def scan_back_kernel(
    dssd, mix, pre, ch, ssd, hin, step, conv, skip, hp, aux, segr, heads_of,
    state_in, win_in, carry_in, *rest,
):
    dval_o, dcommon_o, dconv_o, dheads_o, dskip_o, dstate, dtail, carry = rest[-14:-6]
    dmix, dwin, both, flows, entries, weighted = rest[-6:]
    width = dssd.shape[1]
    channels = width + 2 * N

    @pl.when(pl.program_id(0) == 0)
    def _():
        dwin[CHUNK:, :] = win_in[...]
        dstate[...] = state_in[...]
        carry[...] = carry_in[...]
        dconv_o[...] = jnp.zeros(dconv_o.shape, f32)
        dheads_o[...] = jnp.zeros(dheads_o.shape, f32)
        dskip_o[...] = jnp.zeros(dskip_o.shape, f32)

    row, col = iota(0), iota(1)
    left = col < 64
    table = aux[...]
    step_in = step[...]
    dt = softplus(step_in)
    rate = hp[1:2, :]
    tri = (row >= col).astype(f32)
    run = jnp.dot(tri, -(dt * rate), precision=highest, preferred_element_type=f32)
    run_t = run.T
    allowed = (table[:, SEG : SEG + 1] == segr[...]) & (col >= row)
    b_in = mix[:, width : width + N]
    c_out = mix[:, width + N :]
    scores = mm(b_in, c_out, 1, 1)
    ending = run[CHUNK - 1 : CHUNK, :]
    entry = jnp.exp(run) * table[:, INHERIT : INHERIT + 1]
    tail = jnp.exp(ending - run) * table[:, TAIL : TAIL + 1]
    factor = jnp.exp(ending) * table[:, LINKED : LINKED + 1][CHUNK - 1 :, :]
    c_turned = c_out.astype(f32).T.astype(bf16)
    pairs = jnp.zeros((CHUNK, CHUNK), f32)
    state_high, state_low = split(dstate[...])
    flows[...] = mm(b_in, state_high) + mm(b_in, state_low)
    for pair in range(width // LANES):
        lanes = slice(pair * LANES, (pair + 1) * LANES)
        x_pair = mix[:, lanes].astype(f32)
        dy_low = dssd[:, lanes]
        dy = dy_low.astype(f32)
        dt_pair = pair_spread(dt, pair, left)
        tail_pair = pair_spread(tail, pair, left)
        stepped = (x_pair * dt_pair).astype(bf16).astype(f32)
        inner = mm(across(stepped, left), dy_low, 1, 1)
        mixing = []
        for place, head in enumerate((2 * pair, 2 * pair + 1)):
            spread = run_t[head : head + 1, :] - run[:, head : head + 1]
            decays = jnp.exp(jnp.where(allowed, spread, -1e30))
            mixing.append((decays * scores).astype(bf16))
            pairs = pairs + inner[place * CHUNK : (place + 1) * CHUNK] * decays
        flow = mm(jnp.concatenate(mixing, axis=1), across(dy, left)) + tail_pair * flows[:, lanes]
        dmix[:, lanes] = dt_pair * flow + skip[:, lanes] * dy
        both[0:CHUNK, lanes] = flow * x_pair
        both[CHUNK : 2 * CHUNK, lanes] = dy * (ssd[:, lanes] - skip[:, lanes] * x_pair) - flow * stepped
        dskip_o[:, lanes] += jnp.sum(dy * x_pair, axis=0, keepdims=True)
        high, low = split(pair_spread(entry, pair, left) * dy)
        entries[0, :, lanes] = high
        entries[1, :, lanes] = low
        weighted[:, lanes] = (tail_pair * stepped).astype(bf16)
        dstate[:, lanes] = pair_spread(factor, pair, left) * dstate[:, lanes]
    dstate[...] += mm(c_turned, entries[0]) + mm(c_turned, entries[1])
    dmix[:, width : width + N] = mm(weighted[...], state_high, 1, 1) + mm_left(pairs, c_out)
    dmix[:, width + N :] = mm(entries[0], hin[0].astype(bf16), 1, 1) + mm_left(pairs, b_in, 0, 0)

    by_head = mm_left(both[...], heads_of[...])
    direct = by_head[0:CHUNK]
    balance = by_head[CHUNK:]
    later = allowed.astype(f32)
    log_grad = jnp.dot(later, balance, precision=highest, preferred_element_type=f32)
    log_grad = log_grad + table[:, NEXT : NEXT + 1] * carry[0:1, :]
    carry[0:1, :] = log_grad[0:1, :]
    step_grad = (direct - rate * log_grad) * jax.nn.sigmoid(step_in)
    dcommon_o[:, 2 * N :] = step_grad
    dheads_o[0:1, :] += jnp.sum(step_grad, axis=0, keepdims=True)
    dheads_o[1:2, :] += jnp.sum(-(log_grad * dt * rate), axis=0, keepdims=True)

    for start in range(0, channels, 256):
        cols = slice(start, start + 256)
        value = pre[:, cols]
        sig = jax.nn.sigmoid(value)
        dwin[0:CHUNK, cols] = dmix[:, cols] * (sig * (1.0 + value * (1.0 - sig)))
        here = ch[:, cols]
        own = dwin[0:CHUNK, cols]
        total = conv[3:4, cols] * own
        dconv_o[4:5, cols] += jnp.sum(own, axis=0, keepdims=True)
        dconv_o[3:4, cols] += jnp.sum(own * here, axis=0, keepdims=True)
        for ahead in range(1, 4):
            moved = dwin[ahead : ahead + CHUNK, cols] * table[:, AHEAD + ahead : AHEAD + ahead + 1]
            total = total + conv[3 - ahead : 4 - ahead, cols] * moved
            dconv_o[3 - ahead : 4 - ahead, cols] += jnp.sum(moved * here, axis=0, keepdims=True)
        if start < width:
            dval_o[:, cols] = total.astype(bf16)
        else:
            dcommon_o[:, : 2 * N] = total
    dwin[CHUNK:, :] = dwin[0:8, :]
    dtail[...] = dwin[0:8, :]


def scatter_blocks(dp, me, full, keep_o, send_o, cols):
    half = dp // CORES
    block = full.shape[0] // dp
    for place, distance in enumerate(relative_places(dp)):
        start = pl.multiple_of((me[0] ^ distance) * block, block)
        part = full[pl.ds(start, block), :].astype(bf16)
        if place < half:
            keep_o[place, :, cols] = part
        else:
            send_o[place - half, :, cols] = part


def weight_grad_kernel(dp, me, lhs, rhs, keep_o, send_o, turned, full):
    @pl.when(pl.program_id(0) == 0)
    def _():
        turned[...] = lhs[...].T

    full[...] = mm(turned[...], rhs[...])
    scatter_blocks(dp, me, full, keep_o, send_o, slice(None))


def weight_grad(lhs, rhs, dp, dp_rank):
    length, width = rhs.shape
    depth = lhs.shape[1]
    block, half = depth // dp, dp // CORES
    piece = pl.BlockSpec((half, block, 256), lambda i, *s: (0, 0, i))
    return call(
        functools.partial(weight_grad_kernel, dp),
        (width // 256,),
        [whole((length, depth)), pl.BlockSpec((length, 256), lambda i, *s: (0, i))],
        [piece, piece],
        [shape(half, block, width, dtype=bf16)] * 2,
        [pltpu.VMEM((depth, length), bf16), pltpu.VMEM((depth, 256), f32)],
        2 * length * width * depth,
        scalars=1,
    )(dp_rank, lhs, rhs)


def value_grad_kernel(dp, me, lhs, dval, dcommon, keep_o, send_o, turned, full, wide):
    step = pl.program_id(0)
    last = pl.num_programs(0) - 1

    @pl.when(step == 0)
    def _():
        turned[...] = lhs[...].T

    @pl.when(step < last)
    def _():
        full[...] = mm(turned[...], dval[...])
        cols = pl.ds(pl.multiple_of(step * 256, 256), 256)
        scatter_blocks(dp, me, full, keep_o, send_o, cols)

    @pl.when(step == last)
    def _():
        wide[...] = mm_right(turned[...], dcommon[...])
        cols = slice(keep_o.shape[2] - wide.shape[1], keep_o.shape[2])
        scatter_blocks(dp, me, wide, keep_o, send_o, cols)


def value_grad(lhs, dval, dcommon, dp, dp_rank):
    length, width = dval.shape
    depth, extra = lhs.shape[1], dcommon.shape[1]
    block, half, per = depth // dp, dp // CORES, width // 256
    dims = (half, block, width + extra)
    return call(
        functools.partial(value_grad_kernel, dp),
        (per + 1,),
        [
            whole((length, depth)),
            pl.BlockSpec((length, 256), lambda i, *s: (0, jnp.minimum(i, per - 1))),
            whole((length, extra)),
        ],
        [whole(dims), whole(dims)],
        [shape(*dims, dtype=bf16)] * 2,
        [
            pltpu.VMEM((depth, length), bf16), pltpu.VMEM((depth, 256), f32),
            pltpu.VMEM((depth, extra), f32),
        ],
        2 * length * (width + 2 * extra) * depth,
        scalars=1,
    )(dp_rank, lhs, dval, dcommon)


def input_grad_kernel(rank, dgate, dval, dcommon, tok, wg, wv, shw, ng_o, gain_o):
    @pl.when(pl.program_id(0) == 0)
    def _():
        gain_o[...] = jnp.zeros(gain_o.shape, f32)

    grad = mm(dgate[...], wg[...], 1, 1) + mm(dval[...], wv[...], 1, 1)
    grad = grad + mm_left(dcommon[...], shw[...], 1, 1)
    x = tok[...].astype(f32)
    inverse = lax.rsqrt(jnp.mean(x * x, axis=1, keepdims=True) + norm_epsilon)
    gain_o[...] += jnp.sum(grad * (x * inverse), axis=0, keepdims=True)
    ng_o[...] = grad.astype(ng_o.dtype)


def shards(
    dp, nt,
    residual, cotangent, sequence_ids,
    inner_proj, inner_mean, inner_square,
    shared_proj, shared_mean, shared_square,
    outer_proj, outer_mean, outer_square,
    conv_params, conv_mean, conv_square,
    norm_gains, gains_mean, gains_square,
    head_params, heads_mean, heads_square,
):
    t_rank = lax.axis_index("tensor").astype(jnp.int32)
    d_rank = lax.axis_index("dp").astype(jnp.int32)
    dp_me = d_rank[None]
    t_me = t_rank[None]
    rows_here = residual.shape[0]
    length = rows_here * nt
    width = inner_proj.shape[2]
    heads_here = head_params.shape[1]
    head_size = width // heads_here
    channels = width + 2 * N
    chunks = length // CHUNK
    wide = 2 * CHUNK
    band = min(2 * CHUNK, rows_here)
    per_piece = rows_here // band

    def pieces_of(value):
        return [value] + [swap(value, "tensor", nt, d) for d in range(1, nt)]

    def over_tensor(value, pieces=None):
        pieces = pieces_of(value) if pieces is None else pieces
        if nt == 2:
            first = jnp.concatenate(pieces, axis=0)
            second = jnp.concatenate(pieces[::-1], axis=0)
            return jnp.where(t_rank == 0, first, second)
        stacked = jnp.take(jnp.stack(pieces), jnp.arange(nt) ^ t_rank, axis=0)
        return stacked.reshape((nt * stacked.shape[1],) + stacked.shape[2:])

    kernel_rows, columns = conv_params.shape
    gain_count = norm_gains.shape[0]
    shared_size = shared_proj.size
    exact = jnp.concatenate([conv_params.reshape(-1), norm_gains])
    terms = []
    rest = exact
    for _ in range(3):
        term = lax.optimization_barrier(rest.astype(bf16))
        terms.append(term)
        rest = rest - term.astype(f32)
    small = jnp.concatenate([shared_proj.astype(bf16).reshape(-1)] + terms)
    small_rows = -(-small.size // width)
    while small_rows * nt % 16:
        small_rows += 1
    small = jnp.pad(small, (0, small_rows * width - small.size)).reshape(small_rows, width)
    small_pair = over_tensor(small)
    token_pieces = pieces_of(after(residual, small_pair))

    block_rows = D // dp
    value_shard = jnp.concatenate([inner_proj[1].astype(bf16), small_pair], axis=0)
    value_line = gather_line(value_shard, dp)
    near = gather_plane(value_line, dp)
    value_w, small_all = assemble(
        near, swap(near, "dp", dp, 1), dp, dp_me, [block_rows, small_rows * nt]
    )
    value_w = value_w.reshape(D, width)
    other_shard = jnp.concatenate(
        [inner_proj[0].astype(bf16), outer_proj.T.astype(bf16)], axis=0
    )
    other_line = gather_line(after(other_shard, value_line), dp)
    cot_pieces = pieces_of(after(cotangent, small_pair))

    def halves(pieces):
        if nt == 2:
            return t_me, pieces[0], pieces[1]
        all_rows = over_tensor(None, pieces)
        return jnp.zeros((1,), jnp.int32), all_rows[: length // 2], all_rows[length // 2 :]

    small_all = small_all.reshape(dp * nt, small_rows * width)
    shared_full = small_all[:, :shared_size].reshape(D, -1)
    exact_all = small_all[:, shared_size : shared_size + 3 * exact.size].astype(f32)
    exact_all = exact_all.reshape(dp * nt, 3, exact.size)
    exact_all = (exact_all[:, 0] + exact_all[:, 1]) + exact_all[:, 2]
    conv_full = (
        exact_all[:, : kernel_rows * columns]
        .reshape(dp * nt, kernel_rows, columns)
        .transpose(1, 0, 2)
        .reshape(kernel_rows, -1)
    )
    gains_full = exact_all[:, kernel_rows * columns :].reshape(-1)

    pre_gain = gains_full[:D].reshape(1, D)
    post_gain = lax.dynamic_slice_in_dim(gains_full, D + t_rank * width, width).reshape(1, width)
    conv_here = jnp.concatenate(
        [lax.dynamic_slice_in_dim(conv_full, t_rank * width, width, 1), conv_full[:, DI:]], axis=1
    )
    conv_here = jnp.pad(conv_here, ((0, 8 - kernel_rows), (0, 0)))
    shared_here = jnp.concatenate(
        [
            shared_full[:, : 2 * N],
            lax.dynamic_slice_in_dim(shared_full, 2 * N + t_rank * heads_here, heads_here, 1),
            jnp.zeros((D, LANES - heads_here), bf16),
        ],
        axis=1,
    )
    common_width = 2 * N + LANES
    head_rows = jnp.stack([head_params[0], jnp.exp(head_params[1])])
    head_rows = jnp.pad(head_rows, ((0, 6), (0, LANES - heads_here)))
    skip = jnp.repeat(head_params[2], head_size).reshape(1, width)
    heads_of = (
        jnp.arange(width)[:, None] // head_size == jnp.arange(LANES)[None, :]
    ).astype(bf16)

    ids = sequence_ids
    blocked = ids.reshape(chunks, CHUNK)
    ends, firsts = blocked[:, -1], blocked[:, 0]
    none = jnp.full((1,), -1, jnp.int32)
    before = jnp.concatenate([none, ends[:-1]])
    following = jnp.concatenate([firsts[1:], none])
    fills = [jnp.full((o,), -1, jnp.int32) for o in range(1, 4)]
    marks = [ids]
    marks += [jnp.concatenate([fills[o - 1], ids[:-o]]) == ids for o in range(1, 4)]
    marks += [jnp.concatenate([ids[o:], fills[o - 1]]) == ids for o in range(1, 4)]
    marks += [
        (blocked == before[:, None]).reshape(-1),
        (blocked == ends[:, None]).reshape(-1),
        jnp.broadcast_to((ends == before)[:, None], blocked.shape).reshape(-1),
        (blocked == following[:, None]).reshape(-1),
        ids < SEQ_SLOTS,
    ]
    aux = jnp.stack([m.astype(f32) for m in marks] + [jnp.zeros((length,), f32)] * 4, axis=1)
    segr = ids.astype(f32).reshape(1, length)
    aux_cols = aux.shape[1]

    steps = length // wide
    in_half = lambda i: i % (steps // 2)
    value_w = after(value_w, other_line, *cot_pieces[1:])
    normed, chans, pre, mixed, ssd, entering, step_in = call(
        scan_kernel,
        (steps,),
        [
            rows(wide, D, in_half), rows(wide, D, in_half), whole((1, D)), whole((D, width)),
            whole((D, common_width)), whole((8, channels)), whole((1, width)), whole((8, LANES)),
            rows(wide, aux_cols), pl.BlockSpec((1, wide), lambda i, r: (0, i)),
        ],
        [
            rows(wide, D), rows(wide, channels), rows(wide, channels), rows(wide, channels),
            rows(wide, width), pl.BlockSpec((wide // CHUNK, N, width), lambda i, r: (i, 0, 0)),
            rows(wide, LANES),
        ],
        [
            shape(length, D, dtype=bf16), shape(length, channels), shape(length, channels),
            shape(length, channels, dtype=bf16), shape(length, width),
            shape(chunks, N, width), shape(length, LANES),
        ],
        [
            pltpu.VMEM((wide + 8, channels), f32), pltpu.VMEM((N, width), f32),
            pltpu.VMEM((CHUNK, width), f32), pltpu.VMEM((2, CHUNK, width), bf16),
        ],
        length * (2 * D * (width + common_width) + 12 * width * CHUNK),
        scalars=1,
    )(*halves(token_pieces), pre_gain, value_w, shared_here, conv_here, skip, head_rows, aux, segr)

    plane = gather_plane(other_line, dp, normed)
    gate_w, outer_t = assemble(
        plane, swap(plane, "dp", dp, 1), dp, dp_me, [block_rows, block_rows]
    )
    gate_w, outer_t = gate_w.reshape(D, width), outer_t.reshape(D, width)
    cot_rank, cot0, cot1 = halves(cot_pieces)
    gate, scaled_grad, returned, sums = call(
        gate_kernel,
        (steps,),
        [
            rows(wide, D), rows(wide, D, in_half), rows(wide, D, in_half), rows(wide, aux_cols),
            rows(wide, width), whole((D, width)), whole((D, width)), whole((1, width)),
        ],
        [rows(wide, width), rows(wide, width), rows(wide, D), rows(wide, LANES)],
        [
            shape(length, width), shape(length, width), shape(length, D, dtype=bf16),
            shape(length, LANES),
        ],
        [],
        4 * length * D * width,
        scalars=1,
    )(cot_rank, normed, cot0, cot1, aux, ssd, gate_w, outer_t, post_gain)
    sums = sums[:, :2].T
    distance = 1
    while distance < nt:
        sums = sums + swap(sums, "tensor", nt, distance)
        distance *= 2
    sums = sums.T

    def relative(block, rank):
        return (rank ^ (block // per_piece)) * per_piece + block % per_piece

    def rel_rows(width_here, offset=0):
        return pl.BlockSpec((band, width_here), lambda i, r: (relative(i + offset, r[0]), 0))

    plain = lambda width_here: pl.BlockSpec((band, width_here), lambda i, r: (i, 0))
    branch, scaled, dssd, dgate, post_grad = call(
        norm_kernel,
        (length // band,),
        [
            rel_rows(width), rel_rows(width), rel_rows(width), rel_rows(2),
            whole((D, width)), whole((1, width)),
        ],
        [plain(D), rel_rows(width), rel_rows(width), rel_rows(width), whole((1, width))],
        [
            shape(length, D, dtype=bf16), shape(length, width, dtype=bf16),
            shape(length, width, dtype=bf16), shape(length, width, dtype=bf16), shape(1, width),
        ],
        [],
        2 * length * D * width,
        scalars=1,
    )(t_me, gate, scaled_grad, ssd, sums, outer_t, post_gain)
    outer_keep, outer_send = weight_grad(returned, scaled, dp, dp_me)
    gate_keep, gate_send = weight_grad(normed, after(dgate, outer_send), dp, dp_me)
    outer_line, outer_rest = start_sum(outer_keep, outer_send, dp)
    gate_line, gate_rest = start_sum(gate_keep, gate_send, dp)
    dssd = after(dssd, *outer_rest, *gate_rest)

    branch = branch.reshape(nt, rows_here, D)
    branch_sum = branch[0].astype(f32)
    for d in range(1, nt):
        branch_sum = branch_sum + swap(branch[d], "tensor", nt, d).astype(f32)
    live_here = lax.dynamic_slice_in_dim(aux[:, LIVE], t_rank * rows_here, rows_here)
    tokens = residual.astype(f32)
    block_out = (tokens + branch_sum * live_here[:, None]).astype(bf16)

    state = jnp.zeros((N, width), f32)
    win = jnp.zeros((8, channels), f32)
    carry = jnp.zeros((8, LANES), f32)
    back_parts = []
    filled = []
    top = chunks
    for part, count in enumerate((3, 3, chunks - 6)):
        back = lambda i, top=top: top - 1 - i
        top -= count
        *results, state, win, carry = call(
            scan_back_kernel,
            (count,),
            [
                rows(CHUNK, width, back), rows(CHUNK, channels, back), rows(CHUNK, channels, back),
                rows(CHUNK, channels, back), rows(CHUNK, width, back),
                pl.BlockSpec((1, N, width), lambda i, back=back: (back(i), 0, 0)),
                rows(CHUNK, LANES, back), whole((8, channels)), whole((1, width)),
                whole((8, LANES)), rows(CHUNK, aux_cols, back),
                pl.BlockSpec((1, CHUNK), lambda i, back=back: (0, back(i))),
                whole((width, LANES)),
                whole((N, width)), whole((8, channels)), whole((8, LANES)),
            ]
            + [pl.BlockSpec(memory_space=pl.ANY)] * len(filled),
            [
                rows(CHUNK, width, back), rows(CHUNK, common_width, back), whole((8, channels)),
                whole((8, LANES)), whole((1, width)),
                whole((N, width)), whole((8, channels)), whole((8, LANES)),
            ],
            [
                shape(length, width, dtype=bf16), shape(length, common_width),
                shape(8, channels), shape(8, LANES), shape(1, width),
                shape(N, width), shape(8, channels), shape(8, LANES),
            ],
            [
                pltpu.VMEM((CHUNK, channels), f32), pltpu.VMEM((CHUNK + 8, channels), f32),
                pltpu.VMEM((2 * CHUNK, width), f32), pltpu.VMEM((CHUNK, width), f32),
                pltpu.VMEM((2, CHUNK, width), bf16), pltpu.VMEM((CHUNK, width), bf16),
            ],
            count * CHUNK * 30 * width * CHUNK,
            aliases={16: 0, 17: 1} if filled else None,
        )(
            dssd, mixed, pre, chans, ssd, entering, step_in, conv_here, skip, head_rows, aux, segr,
            heads_of, state, win, carry, *filled,
        )
        filled = results[:2]
        back_parts.append(results[2:])
        if part == 0:
            outer_block, outer_far = middle_sum(after(outer_line, state), outer_rest, dp)
            state = after(state, *outer_far)
        if part == 1:
            gate_block, gate_far = middle_sum(after(gate_line, state), gate_rest, dp)
            state = after(state, *gate_far)
    dval, dcommon = filled
    dconv, dheads, dskip = [sum(parts) for parts in zip(*back_parts)]
    outer_part = high_sum(outer_block, outer_far, dp)
    gate_part = high_sum(gate_block, gate_far, dp)

    def input_grad(count, offset, dtype, positions, dgate):
        return call(
            input_grad_kernel,
            (count * per_piece,),
            [
                rel_rows(width, offset), rel_rows(width, offset), rel_rows(common_width, offset),
                plain(D), whole((D, width)), whole((D, width)), whole((D, common_width)),
            ],
            [plain(D), whole((1, D))],
            [shape(count * rows_here, D, dtype=dtype), shape(1, D)],
            [],
            4 * count * rows_here * D * (width + common_width),
            scalars=1,
        )(t_me, dgate, dval, dcommon, positions, gate_w, value_w, shared_here)

    value_keep, value_send = value_grad(normed, after(dval, outer_part, branch_sum), dcommon, dp, dp_me)
    value_line, value_rest = start_sum(value_keep, value_send, dp)
    others = token_pieces[1] if nt == 2 else jnp.concatenate(token_pieces[1:], axis=0)
    sent, pre_grad_sent = input_grad(
        nt - 1, per_piece, bf16, others, after(dgate, value_send, gate_part)
    )
    sent = sent.reshape(nt - 1, rows_here, D)
    own, pre_grad_own = input_grad(1, 0, f32, residual, after(dgate, sent, *value_rest))
    received = [swap(sent[d - 1], "tensor", nt, d) for d in range(1, nt)]

    value_block, value_far = middle_sum(after(value_line, own), value_rest, dp)
    value_sum = high_sum(value_block, value_far, dp)
    value_part = value_sum[:, :width]
    shared_rows = shared_proj.shape[0]
    shared_sum = value_sum[:, width:].reshape(nt, shared_rows, common_width)
    shared_mine = lax.dynamic_index_in_dim(shared_sum, t_rank, 0, False)
    shared_common = shared_mine[:, : 2 * N]
    shared_part = jnp.zeros((shared_rows, 2 * N + H), f32)

    def place_heads(table, piece, rank):
        return lax.dynamic_update_slice(
            table, piece[:, 2 * N : 2 * N + heads_here], (0, 2 * N + rank * heads_here)
        )

    shared_part = place_heads(shared_part, shared_mine, t_rank)
    for d in range(1, nt):
        piece = lax.dynamic_index_in_dim(shared_sum, t_rank ^ d, 0, False)
        piece = swap(piece, "tensor", nt, d)
        shared_common = shared_common + piece[:, : 2 * N]
        shared_part = place_heads(shared_part, piece, t_rank ^ d)
    shared_part = lax.dynamic_update_slice(shared_part, shared_common, (0, 0))

    conv_grad = lax.dynamic_update_slice(
        jnp.pad(dconv[:kernel_rows, width:], ((0, 0), (DI, 0))),
        dconv[:kernel_rows, :width],
        (0, t_rank * width),
    )
    post_all = lax.dynamic_update_slice(
        jnp.zeros((1, DI), f32), post_grad, (0, t_rank * width)
    )
    head_grad = jnp.stack(
        [
            dheads[0, :heads_here],
            dheads[1, :heads_here],
            jnp.sum(dskip.reshape(heads_here, head_size), axis=1),
        ]
    )
    head_all = lax.dynamic_update_slice(
        jnp.zeros((3, H), f32), head_grad, (0, t_rank * heads_here)
    )
    vector = jnp.concatenate(
        [
            conv_grad.reshape(1, -1), pre_grad_sent + pre_grad_own, post_all, head_all.reshape(1, -1),
        ],
        axis=1,
    )
    vector = sum_everywhere(after(vector, *value_far), dp, nt)
    conv_size = kernel_rows * (DI + 2 * N)
    place = d_rank * nt + t_rank
    conv_part = lax.dynamic_slice_in_dim(
        vector[0, :conv_size].reshape(kernel_rows, -1), place * columns, columns, 1
    )
    gains_part = lax.dynamic_slice_in_dim(vector[0], conv_size + place * gain_count, gain_count)
    heads_part = lax.dynamic_slice_in_dim(
        vector[0, conv_size + D + DI :].reshape(3, H), t_rank * heads_here, heads_here, 1
    )

    normed_grad = own
    for piece in received:
        normed_grad = normed_grad + after(piece, vector).astype(f32)
    inverse = lax.rsqrt(jnp.mean(tokens * tokens, axis=1, keepdims=True) + norm_epsilon)
    normal_tokens = tokens * inverse
    normal_grad = normed_grad * pre_gain
    centered = normal_grad - normal_tokens * jnp.mean(
        normal_grad * normal_tokens, axis=1, keepdims=True
    )
    residual_grad = (cotangent.astype(f32) + inverse * centered).astype(bf16)

    inner_new = adam_step(
        inner_proj, inner_mean, inner_square, jnp.stack([gate_part, value_part]),
        rate_matrix, weight_decay,
    )
    shared_new = adam_step(
        shared_proj, shared_mean, shared_square, shared_part.reshape(shared_proj.shape),
        rate_matrix, weight_decay,
    )
    outer_new = adam_step(
        outer_proj, outer_mean, outer_square, outer_part.T, rate_matrix, weight_decay
    )
    conv_new = adam_step(conv_params, conv_mean, conv_square, conv_part, rate_vector, 0.0)
    gains_new = adam_step(norm_gains, gains_mean, gains_square, gains_part, rate_vector, 0.0)
    heads_new = adam_step(head_params, heads_mean, heads_square, heads_part, rate_heads, 0.0)
    return (
        (block_out, residual_grad)
        + inner_new + shared_new + outer_new + conv_new + gains_new + heads_new
    )


def solution(mesh):
    return jax.shard_map(
        functools.partial(shards, mesh.shape["dp"], mesh.shape["tensor"]),
        mesh=mesh,
        in_specs=(
            P(("dp", "tensor"), None),
            P(("dp", "tensor"), None),
            P("dp"),
            P(None, "dp", "tensor"),
            P(None, "dp", "tensor"),
            P(None, "dp", "tensor"),
            P(("dp", "tensor"), None),
            P(("dp", "tensor"), None),
            P(("dp", "tensor"), None),
            P("tensor", "dp"),
            P("tensor", "dp"),
            P("tensor", "dp"),
            P(None, ("dp", "tensor")),
            P(None, ("dp", "tensor")),
            P(None, ("dp", "tensor")),
            P(("dp", "tensor")),
            P(("dp", "tensor")),
            P(("dp", "tensor")),
            P(None, "tensor"),
            P(None, "tensor"),
            P(None, "tensor"),
        ),
        out_specs=(
            P(("dp", "tensor"), None),
            P(("dp", "tensor"), None),
            P(None, "dp", "tensor"),
            P(None, "dp", "tensor"),
            P(None, "dp", "tensor"),
            P(("dp", "tensor"), None),
            P(("dp", "tensor"), None),
            P(("dp", "tensor"), None),
            P("tensor", "dp"),
            P("tensor", "dp"),
            P("tensor", "dp"),
            P(None, ("dp", "tensor")),
            P(None, ("dp", "tensor")),
            P(None, ("dp", "tensor")),
            P(("dp", "tensor")),
            P(("dp", "tensor")),
            P(("dp", "tensor")),
            P(None, "tensor"),
            P(None, "tensor"),
            P(None, "tensor"),
        ),
        check_vma=False,
    )
```

```python
import functools

import jax
import jax.numpy as jnp
from jax import lax
from jax.experimental import pallas as pl
from jax.experimental.pallas import tpu as pltpu
from jax.sharding import PartitionSpec as P

D = 1024
H = 32
N = 128
DI = 2048
SEQ_SLOTS = 4
STEP = 10
CHUNK = 128
LANES = 128
CORES = 2
HIGH_AXIS = 4

highest = lax.Precision.HIGHEST
f32 = jnp.float32
bf16 = jnp.bfloat16
norm_epsilon = 1e-05
beta_first = 0.9
beta_second = 0.95
adam_epsilon = 1e-08
weight_decay = 0.1
rate_matrix = 0.02
rate_vector = 0.3
rate_heads = 1.0

SEG, BACK, AHEAD, INHERIT, TAIL, LINKED, NEXT, LIVE = 0, 0, 3, 7, 8, 9, 10, 11


def adam_step(weight, moment, square, gradient, rate, decay):
    moment_next = beta_first * moment + (1.0 - beta_first) * gradient
    square_next = beta_second * square + (1.0 - beta_second) * gradient * gradient
    moment_hat = moment_next / (1.0 - beta_first**STEP)
    square_hat = square_next / (1.0 - beta_second**STEP)
    weight_next = weight - rate * (
        moment_hat / (jnp.sqrt(square_hat) + adam_epsilon) + decay * weight
    )
    return (weight_next, moment_next, square_next)


def swap(value, axis, size, distance):
    return lax.ppermute(value, axis, [(i, i ^ distance) for i in range(size)])


def tie(*values):
    return lax.optimization_barrier(values)


def axis_parts(dp):
    high = HIGH_AXIS
    middle = dp // (CORES * high)
    return high, middle


def gather_line(shard, dp):
    high, middle = axis_parts(dp)
    pieces = [shard[None]]
    for step in range(1, high):
        pieces.append(swap(shard, "dp", dp, step * middle * CORES)[None])
    return jnp.concatenate(pieces, axis=0)


def plane_parts(line, dp):
    return [swap(line, "dp", dp, step * CORES) for step in range(1, axis_parts(dp)[1])]


def start_sum(keep, send, dp):
    high, middle = axis_parts(dp)
    other = swap(send, "dp", dp, 1)
    parts = [slice(step * high, (step + 1) * high) for step in range(middle)]
    line = keep[parts[0]].astype(f32) + other[parts[0]].astype(f32)
    rest = [(keep[at].astype(f32) + other[at].astype(f32)).astype(bf16) for at in parts[1:]]
    return line, rest


def middle_swaps(rest, dp):
    return [swap(part, "dp", dp, (step + 1) * CORES) for step, part in enumerate(rest)]


def middle_sum(line, received):
    for part in received:
        line = line + part.astype(f32)
    return line[0], [part.astype(bf16) for part in line[1:]]


def high_swaps(rest, dp):
    middle = axis_parts(dp)[1]
    return [swap(part, "dp", dp, (step + 1) * middle * CORES) for step, part in enumerate(rest)]


def high_sum(block, received):
    for part in received:
        block = block + part.astype(f32)
    return block


def sum_stages(dp, nt):
    stages = [("tensor", nt, 1 << bit) for bit in range((nt - 1).bit_length())]
    return stages + [("dp", dp, 1 << bit) for bit in range((dp - 1).bit_length())]


def relative_places(dp):
    high, middle = axis_parts(dp)
    return [
        (h * middle + m) * CORES + c for c in range(CORES) for m in range(middle) for h in range(high)
    ]


def call(kernel, grid, in_specs, out_specs, out_shape, scratch, flops, mib, scalars=0, aliases=None):
    params = pltpu.CompilerParams(vmem_limit_bytes=mib * 1024 * 1024)
    moved = sum(2 * s.dtype.itemsize * s.size for s in jax.tree.leaves(out_shape))
    return pl.pallas_call(
        kernel,
        grid_spec=pltpu.PrefetchScalarGridSpec(
            num_scalar_prefetch=scalars,
            grid=grid,
            in_specs=in_specs,
            out_specs=out_specs,
            scratch_shapes=scratch,
        ),
        out_shape=out_shape,
        compiler_params=params,
        input_output_aliases=aliases or {},
        cost_estimate=pl.CostEstimate(flops=int(flops), bytes_accessed=int(moved), transcendentals=0),
    )


def whole(shape):
    return pl.BlockSpec(shape, lambda *i: (0,) * len(shape), pipeline_mode=pl.Buffered(1))


def result(shape):
    return pl.BlockSpec(shape, lambda *i: (0,) * len(shape))


def rows(count, width, index=lambda i: i):
    return pl.BlockSpec((count, width), lambda i, *s: (index(i), 0))


def shape(*dims, dtype=f32):
    return jax.ShapeDtypeStruct(dims, dtype)


def split(value):
    high = value.astype(bf16)
    return high, (value - high.astype(f32)).astype(bf16)


def mm(a, b, ca=1, cb=0):
    return lax.dot_general(a, b, (((ca,), (cb,)), ((), ())), preferred_element_type=f32)


def mm_left(value, exact, ca=1, cb=0):
    high, low = split(value)
    return mm(high, exact, ca, cb) + mm(low, exact, ca, cb)


def mm_right(exact, value, ca=1, cb=0):
    high, low = split(value)
    return mm(exact, high, ca, cb) + mm(exact, low, ca, cb)


def mm_both(a, b, ca=1, cb=0):
    a_high, a_low = split(a)
    b_high, b_low = split(b)
    return mm(a_high, b_high, ca, cb) + mm(a_low, b_high, ca, cb) + mm(a_high, b_low, ca, cb)


def softplus(value):
    return jnp.maximum(value, 0.0) + jnp.log1p(jnp.exp(-jnp.abs(value)))


def iota(axis):
    return lax.broadcasted_iota(jnp.int32, (CHUNK, LANES), axis)


def pair_spread(tile, pair, left):
    rows_here = tile.shape[0]
    return jnp.where(
        left[:rows_here],
        jnp.broadcast_to(tile[:, 2 * pair : 2 * pair + 1], (rows_here, LANES)),
        jnp.broadcast_to(tile[:, 2 * pair + 1 : 2 * pair + 2], (rows_here, LANES)),
    )


def assemble_kernel(dp, parts, me, *refs):
    half = dp // CORES
    sources, outs = refs[: 2 * parts], refs[2 * parts :]
    for place, distance in enumerate(relative_places(dp)):
        base = 0
        for part in range(parts):
            source, at = (sources[part], place) if place < half else (sources[parts + part], place - half)
            end = base + source.shape[1]
            start = 0
            for out in outs:
                low, high = max(base, start), min(end, start + out.shape[1])
                if low < high:
                    out[me[0] ^ distance, low - start : high - start, :] = source[
                        at, low - base : high - base, :
                    ]
                start += out.shape[1]
            base = end


def assemble(nears, fars, dp, dp_rank, counts):
    width, dtype = nears[0].shape[2], nears[0].dtype
    vmem = pl.BlockSpec(memory_space=pltpu.VMEM)
    moved = sum(4 * near.size * near.dtype.itemsize for near in nears)
    return pl.pallas_call(
        functools.partial(assemble_kernel, dp, len(nears)),
        in_specs=[pl.BlockSpec(memory_space=pltpu.SMEM)] + [vmem] * (2 * len(nears)),
        out_specs=[vmem] * len(counts),
        out_shape=[shape(dp, count, width, dtype=dtype) for count in counts],
        compiler_params=pltpu.CompilerParams(vmem_limit_bytes=16 * 1024 * 1024),
        cost_estimate=pl.CostEstimate(flops=0, bytes_accessed=moved, transcendentals=0),
    )(dp_rank, *nears, *fars)


def pick_half(rank, first, second):
    half = (2 * pl.program_id(0)) // pl.num_programs(0)
    own = (half == rank[0]).astype(jnp.int32)
    return jnp.where(jnp.broadcast_to(own, first.shape) == 1, first[...], second[...])


def across(pair, left):
    return jnp.concatenate(
        [jnp.where(left, pair, 0.0), jnp.where(left, 0.0, pair)], axis=0
    ).astype(bf16)


def scan_kernel(
    rank, tok0, tok1, gain, wv, shw, conv, skip, hp, aux, segr,
    normed_o, ch_o, pre_o, mix_o, ssd_o, hin_o, step_o,
    win, state, carried, weighted,
):
    count = tok0.shape[0]
    width = wv.shape[1]
    channels = width + 2 * N

    @pl.when(pl.program_id(0) == 0)
    def _():
        win[0:8, :] = jnp.zeros((8, channels), f32)
        state[...] = jnp.zeros(state.shape, f32)

    x = pick_half(rank, tok0, tok1).astype(f32)
    inverse = lax.rsqrt(jnp.mean(x * x, axis=1, keepdims=True) + norm_epsilon)
    normed = (x * inverse * gain[...]).astype(bf16)
    normed_o[...] = normed
    win[8 : 8 + count, :width] = mm(normed, wv[...])
    common = mm(normed, shw[...])
    win[8 : 8 + count, width:] = common[:, : 2 * N]
    step_o[...] = common[:, 2 * N :] + hp[0:1, :]
    table = aux[...]
    for start in range(0, channels, 256):
        cols = slice(start, start + 256)
        here = win[8 : 8 + count, cols]
        pre = conv[4:5, cols] + conv[3:4, cols] * here
        for back in range(1, 4):
            pre = pre + conv[3 - back : 4 - back, cols] * (
                win[8 - back : 8 - back + count, cols] * table[:, BACK + back : BACK + back + 1]
            )
        ch_o[:, cols] = here
        pre_o[:, cols] = pre
        mix_o[:, cols] = (pre * jax.nn.sigmoid(pre)).astype(bf16)
    win[0:8, :] = win[count : count + 8, :]

    row, col = iota(0), iota(1)
    left = col < 64
    tri = (row >= col).astype(f32)
    for sub in range(count // CHUNK):
        at = slice(sub * CHUNK, (sub + 1) * CHUNK)
        dt = softplus(step_o[at, :])
        run = jnp.dot(tri, -(dt * hp[1:2, :]), precision=highest, preferred_element_type=f32)
        run_t = run.T
        allowed = (table[at, SEG : SEG + 1] == segr[:, at]) & (row >= col)
        b_in = mix_o[at, width : width + N]
        b_turned = b_in.astype(f32).T.astype(bf16)
        c_out = mix_o[at, width + N :]
        scores = mm(c_out, b_in, 1, 1)
        ending = run[CHUNK - 1 : CHUNK, :]
        entry = jnp.exp(run) * table[at, INHERIT : INHERIT + 1]
        tail = jnp.exp(ending - run) * table[at, TAIL : TAIL + 1]
        factor = jnp.exp(ending) * table[at, LINKED : LINKED + 1][CHUNK - 1 :, :]
        hin_o[sub] = state[...]
        carried[...] = mm_right(c_out, state[...])
        for pair in range(width // LANES):
            lanes = slice(pair * LANES, (pair + 1) * LANES)
            x_pair = mix_o[at, lanes].astype(f32)
            stepped = (x_pair * pair_spread(dt, pair, left)).astype(bf16).astype(f32)
            mixing = []
            for head in (2 * pair, 2 * pair + 1):
                spread = run[:, head : head + 1] - run_t[head : head + 1, :]
                decays = jnp.exp(jnp.where(allowed, spread, -1e30))
                mixing.append((decays * scores).astype(bf16))
            local = mm(jnp.concatenate(mixing, axis=1), across(stepped, left))
            ssd_o[at, lanes] = (
                local + carried[:, lanes] * pair_spread(entry, pair, left) + skip[:, lanes] * x_pair
            )
            high, low = split(stepped * pair_spread(tail, pair, left))
            weighted[0, :, lanes] = high
            weighted[1, :, lanes] = low
            state[:, lanes] = pair_spread(factor, pair, left) * state[:, lanes]
        state[...] += mm(b_turned, weighted[0]) + mm(b_turned, weighted[1])


def gate_kernel(rank, normed, cot0, cot1, aux, ssd, wg, out_t, gain, gate_o, sg_o, ret_o, sums_o):
    returned = (pick_half(rank, cot0, cot1).astype(f32) * aux[:, LIVE : LIVE + 1]).astype(bf16)
    ret_o[...] = returned
    gate = mm(normed[...], wg[...])
    gate_o[...] = gate
    scaled_grad = mm(returned, out_t[...])
    sg_o[...] = scaled_grad
    gated = ssd[...] * (gate * jax.nn.sigmoid(gate))
    squares = jnp.sum(gated * gated, axis=1, keepdims=True)
    crossed = jnp.sum(scaled_grad * gain[...] * gated, axis=1, keepdims=True)
    lane = lax.broadcasted_iota(jnp.int32, (squares.shape[0], LANES), 1)
    table = jnp.where(lane == 0, squares, jnp.where(lane == 1, crossed, 0.0))
    sums_o[...] = table.T[:8, :]


def norm_kernel(
    rank, gate_r, sg_r, ssd_r, sums_r, out_t, gain, branch_o, scaled_o, dssd_o, dgate_o, gain_o
):
    @pl.when(pl.program_id(0) == 0)
    def _():
        gain_o[...] = jnp.zeros(gain_o.shape, f32)

    gate, ssd, scaled_grad = gate_r[...], ssd_r[...], sg_r[...]
    table = jnp.concatenate([sums_r[...], jnp.zeros((LANES - 8, sums_r.shape[1]), f32)], axis=0)
    sums = table.T
    scale = lax.rsqrt(sums[:, 0:1] / DI + norm_epsilon)
    sig = jax.nn.sigmoid(gate)
    silu = gate * sig
    gated = ssd * silu
    scaled = (gated * scale * gain[...]).astype(bf16)
    scaled_o[...] = scaled
    branch_o[...] = mm(scaled, out_t[...], 1, 1).astype(bf16)
    gain_o[...] += jnp.sum(scaled_grad * gated * scale, axis=0, keepdims=True)
    grad = scale * (scaled_grad * gain[...]) - gated * (scale * scale * scale * (sums[:, 1:2] / DI))
    dssd_o[...] = (grad * silu).astype(bf16)
    dgate_o[...] = (grad * ssd * sig * (1.0 + gate * (1.0 - sig))).astype(bf16)


def scan_back_kernel(
    dssd, mix, pre, ch, ssd, hin, step, conv, skip, hp, aux, segr, heads_of,
    state_in, win_in, carry_in, *rest,
):
    dval_o, dcommon_o, dconv_o, dheads_o, dstate, dtail, carry = rest[-14:-7]
    dmix, dwin, both, flows, entries, weighted, dskip = rest[-7:]
    width = dssd.shape[1]
    channels = width + 2 * N

    @pl.when(pl.program_id(0) == 0)
    def _():
        dwin[CHUNK:, :] = win_in[...]
        dstate[...] = state_in[...]
        carry[...] = carry_in[...]
        dconv_o[...] = jnp.zeros(dconv_o.shape, f32)
        dheads_o[...] = jnp.zeros(dheads_o.shape, f32)
        dskip[...] = jnp.zeros(dskip.shape, f32)

    row, col = iota(0), iota(1)
    left = col < 64
    table = aux[...]
    step_in = step[...]
    dt = softplus(step_in)
    rate = hp[1:2, :]
    tri = (row >= col).astype(f32)
    run = jnp.dot(tri, -(dt * rate), precision=highest, preferred_element_type=f32)
    run_t = run.T
    allowed = (table[:, SEG : SEG + 1] == segr[...]) & (col >= row)
    b_in = mix[:, width : width + N]
    c_out = mix[:, width + N :]
    scores = mm(b_in, c_out, 1, 1)
    ending = run[CHUNK - 1 : CHUNK, :]
    entry = jnp.exp(run) * table[:, INHERIT : INHERIT + 1]
    tail = jnp.exp(ending - run) * table[:, TAIL : TAIL + 1]
    factor = jnp.exp(ending) * table[:, LINKED : LINKED + 1][CHUNK - 1 :, :]
    c_turned = c_out.astype(f32).T.astype(bf16)
    pairs = jnp.zeros((CHUNK, CHUNK), f32)
    state_high, state_low = split(dstate[...])
    flows[...] = mm(b_in, state_high) + mm(b_in, state_low)
    for pair in range(width // LANES):
        lanes = slice(pair * LANES, (pair + 1) * LANES)
        x_pair = mix[:, lanes].astype(f32)
        dy_low = dssd[:, lanes]
        dy = dy_low.astype(f32)
        dt_pair = pair_spread(dt, pair, left)
        tail_pair = pair_spread(tail, pair, left)
        stepped = (x_pair * dt_pair).astype(bf16).astype(f32)
        inner = mm(across(stepped, left), dy_low, 1, 1)
        mixing = []
        for place, head in enumerate((2 * pair, 2 * pair + 1)):
            spread = run_t[head : head + 1, :] - run[:, head : head + 1]
            decays = jnp.exp(jnp.where(allowed, spread, -1e30))
            mixing.append((decays * scores).astype(bf16))
            pairs = pairs + inner[place * CHUNK : (place + 1) * CHUNK] * decays
        flow = mm(jnp.concatenate(mixing, axis=1), across(dy, left)) + tail_pair * flows[:, lanes]
        dmix[:, lanes] = dt_pair * flow + skip[:, lanes] * dy
        both[0:CHUNK, lanes] = flow * x_pair
        both[CHUNK : 2 * CHUNK, lanes] = dy * (ssd[:, lanes] - skip[:, lanes] * x_pair) - flow * stepped
        dskip[0:1, lanes] += jnp.sum(dy * x_pair, axis=0, keepdims=True)
        high, low = split(pair_spread(entry, pair, left) * dy)
        entries[0, :, lanes] = high
        entries[1, :, lanes] = low
        weighted[:, lanes] = (tail_pair * stepped).astype(bf16)
        dstate[:, lanes] = pair_spread(factor, pair, left) * dstate[:, lanes]
    dstate[...] += mm(c_turned, entries[0]) + mm(c_turned, entries[1])
    dmix[:, width : width + N] = mm(weighted[...], state_high, 1, 1) + mm_left(pairs, c_out)
    dmix[:, width + N :] = mm(entries[0], hin[0].astype(bf16), 1, 1) + mm_left(pairs, b_in, 0, 0)

    by_head = mm_left(both[...], heads_of[...])
    direct = by_head[0:CHUNK]
    balance = by_head[CHUNK:]
    later = allowed.astype(f32)
    log_grad = jnp.dot(later, balance, precision=highest, preferred_element_type=f32)
    log_grad = log_grad + table[:, NEXT : NEXT + 1] * carry[0:1, :]
    carry[0:1, :] = log_grad[0:1, :]
    step_grad = (direct - rate * log_grad) * jax.nn.sigmoid(step_in)
    dcommon_o[:, 2 * N :] = step_grad
    dheads_o[0:1, :] += jnp.sum(step_grad, axis=0, keepdims=True)
    dheads_o[1:2, :] += jnp.sum(-(log_grad * dt * rate), axis=0, keepdims=True)

    for start in range(0, channels, 256):
        cols = slice(start, start + 256)
        value = pre[:, cols]
        sig = jax.nn.sigmoid(value)
        dwin[0:CHUNK, cols] = dmix[:, cols] * (sig * (1.0 + value * (1.0 - sig)))
        here = ch[:, cols]
        own = dwin[0:CHUNK, cols]
        total = conv[3:4, cols] * own
        dconv_o[4:5, cols] += jnp.sum(own, axis=0, keepdims=True)
        dconv_o[3:4, cols] += jnp.sum(own * here, axis=0, keepdims=True)
        for ahead in range(1, 4):
            moved = dwin[ahead : ahead + CHUNK, cols] * table[:, AHEAD + ahead : AHEAD + ahead + 1]
            total = total + conv[3 - ahead : 4 - ahead, cols] * moved
            dconv_o[3 - ahead : 4 - ahead, cols] += jnp.sum(moved * here, axis=0, keepdims=True)
        if start < width:
            dval_o[:, cols] = total.astype(bf16)
        else:
            dcommon_o[:, : 2 * N] = total
    dwin[CHUNK:, :] = dwin[0:8, :]
    dtail[...] = dwin[0:8, :]

    @pl.when(pl.program_id(0) == pl.num_programs(0) - 1)
    def _():
        dheads_o[2:3, :] = mm_left(dskip[...], heads_of[...])[0:1, :]


def scatter_blocks(dp, me, full, keep_o, send_o, cols):
    half = dp // CORES
    block = full.shape[0] // dp
    for place, distance in enumerate(relative_places(dp)):
        start = pl.multiple_of((me[0] ^ distance) * block, block)
        part = full[pl.ds(start, block), :].astype(bf16)
        if place < half:
            keep_o[place, :, cols] = part
        else:
            send_o[place - half, :, cols] = part


def weight_grad_kernel(dp, me, lhs, rhs, keep_o, send_o, turned, full):
    @pl.when(pl.program_id(0) == 0)
    def _():
        turned[...] = lhs[...].T

    full[...] = mm(turned[...], rhs[...])
    scatter_blocks(dp, me, full, keep_o, send_o, slice(None))


def weight_grad(lhs, rhs, dp, dp_rank, skipped=0):
    length, width = rhs.shape[0], rhs.shape[1] - 256 * skipped
    depth = lhs.shape[1]
    block, half = depth // dp, dp // CORES
    piece = pl.BlockSpec((half, block, 256), lambda i, *s: (0, 0, i))
    return call(
        functools.partial(weight_grad_kernel, dp),
        (width // 256,),
        [whole((length, depth)), pl.BlockSpec((length, 256), lambda i, *s: (0, i + skipped))],
        [piece, piece],
        [shape(half, block, width, dtype=bf16)] * 2,
        [pltpu.VMEM((depth, length), bf16), pltpu.VMEM((depth, 256), f32)],
        2 * length * width * depth,
        16,
        scalars=1,
    )(dp_rank, lhs, rhs)


def value_grad_kernel(dp, me, lhs, dval, dcommon, keep_o, send_o, turned, full, wide):
    step = pl.program_id(0)
    last = pl.num_programs(0) - 1

    @pl.when(step == 0)
    def _():
        turned[...] = lhs[...].T

    @pl.when(step < last)
    def _():
        full[...] = mm(turned[...], dval[...])
        cols = pl.ds(pl.multiple_of(step * 256, 256), 256)
        scatter_blocks(dp, me, full, keep_o, send_o, cols)

    @pl.when(step == last)
    def _():
        wide[...] = mm_right(turned[...], dcommon[...])
        cols = slice(keep_o.shape[2] - wide.shape[1], keep_o.shape[2])
        scatter_blocks(dp, me, wide, keep_o, send_o, cols)


def value_grad(lhs, dval, dcommon, dp, dp_rank):
    length, width = dval.shape[0], 256
    depth, extra = lhs.shape[1], dcommon.shape[1]
    block, half, per = depth // dp, dp // CORES, width // 256
    dims = (half, block, width + extra)
    return call(
        functools.partial(value_grad_kernel, dp),
        (per + 1,),
        [
            whole((length, depth)),
            pl.BlockSpec((length, 256), lambda i, *s: (0, jnp.minimum(i, per - 1))),
            whole((length, extra)),
        ],
        [result(dims), result(dims)],
        [shape(*dims, dtype=bf16)] * 2,
        [
            pltpu.VMEM((depth, length), bf16), pltpu.VMEM((depth, 256), f32),
            pltpu.VMEM((depth, extra), f32),
        ],
        2 * length * (width + 2 * extra) * depth,
        24,
        scalars=1,
    )(dp_rank, lhs, dval, dcommon)


def input_grad_kernel(rank, dgate, dval, dcommon, tok, wg, wv, shw, ng_o, gain_o):
    @pl.when(pl.program_id(0) == 0)
    def _():
        gain_o[...] = jnp.zeros(gain_o.shape, f32)

    grad = mm(dgate[...], wg[...], 1, 1) + mm(dval[...], wv[...], 1, 1)
    grad = grad + mm_left(dcommon[...], shw[...], 1, 1)
    x = tok[...].astype(f32)
    inverse = lax.rsqrt(jnp.mean(x * x, axis=1, keepdims=True) + norm_epsilon)
    gain_o[...] += jnp.sum(grad * (x * inverse), axis=0, keepdims=True)
    ng_o[...] = grad.astype(ng_o.dtype)


def shards(
    dp, nt,
    residual, cotangent, sequence_ids,
    inner_proj, inner_mean, inner_square,
    shared_proj, shared_mean, shared_square,
    outer_proj, outer_mean, outer_square,
    conv_params, conv_mean, conv_square,
    norm_gains, gains_mean, gains_square,
    head_params, heads_mean, heads_square,
):
    t_rank = lax.axis_index("tensor").astype(jnp.int32)
    d_rank = lax.axis_index("dp").astype(jnp.int32)
    dp_me = d_rank[None]
    t_me = t_rank[None]
    rows_here = residual.shape[0]
    length = rows_here * nt
    width = inner_proj.shape[2]
    heads_here = head_params.shape[1]
    head_size = width // heads_here
    channels = width + 2 * N
    chunks = length // CHUNK
    wide = 2 * CHUNK
    band = min(2 * CHUNK, rows_here)
    per_piece = rows_here // band

    def pieces_of(value):
        return [value] + [swap(value, "tensor", nt, d) for d in range(1, nt)]

    def over_tensor(value, pieces=None):
        pieces = pieces_of(value) if pieces is None else pieces
        if nt == 2:
            first = jnp.concatenate(pieces, axis=0)
            second = jnp.concatenate(pieces[::-1], axis=0)
            return jnp.where(t_rank == 0, first, second)
        stacked = jnp.take(jnp.stack(pieces), jnp.arange(nt) ^ t_rank, axis=0)
        return stacked.reshape((nt * stacked.shape[1],) + stacked.shape[2:])

    kernel_rows, columns = conv_params.shape
    gain_count = norm_gains.shape[0]
    shared_size = shared_proj.size
    exact = jnp.concatenate([conv_params.reshape(-1), norm_gains])
    terms = []
    rest = exact
    for _ in range(3):
        term = lax.optimization_barrier(rest.astype(bf16))
        terms.append(term)
        rest = rest - term.astype(f32)
    small = jnp.concatenate([shared_proj.astype(bf16).reshape(-1)] + terms)
    small_rows = -(-small.size // width)
    while small_rows * nt % 16:
        small_rows += 1
    small = jnp.pad(small, (0, small_rows * width - small.size)).reshape(small_rows, width)
    small_pair = over_tensor(small)
    residual_now, small_pair = tie(residual, small_pair)
    token_pieces = pieces_of(residual_now)

    block_rows = D // dp
    value_shard = jnp.concatenate([inner_proj[1].astype(bf16), small_pair], axis=0)
    cut = -(-value_shard.shape[0] // 32) * 16
    first_line = gather_line(value_shard[:cut], dp)
    second_shard, first_line = tie(value_shard[cut:], first_line)
    second_line = gather_line(second_shard, dp)
    second_line, ids = tie(second_line, sequence_ids)
    first_near = jnp.concatenate([first_line] + plane_parts(first_line, dp), axis=0)
    other_shard = jnp.concatenate(
        [inner_proj[0].astype(bf16), outer_proj.T.astype(bf16)], axis=0
    )
    other_shard, second_line = tie(other_shard, second_line)
    other_line = gather_line(other_shard, dp)
    second_line, *parts = tie(second_line, *plane_parts(second_line, dp), *token_pieces)
    parts, token_pieces = parts[:-nt], parts[-nt:]
    second_near = jnp.concatenate([second_line] + parts, axis=0)
    cotangent_now, *token_pieces = tie(cotangent, *token_pieces)
    cot_pieces = pieces_of(cotangent_now)
    value_w, small_all = assemble(
        [first_near, second_near],
        [swap(first_near, "dp", dp, 1), swap(second_near, "dp", dp, 1)],
        dp, dp_me, [block_rows, small_rows * nt],
    )
    value_w = value_w.reshape(D, width)

    def halves(pieces):
        if nt == 2:
            return t_me, pieces[0], pieces[1]
        all_rows = over_tensor(None, pieces)
        return jnp.zeros((1,), jnp.int32), all_rows[: length // 2], all_rows[length // 2 :]

    small_all = small_all.reshape(dp * nt, small_rows * width)
    shared_full = small_all[:, :shared_size].reshape(D, -1)
    exact_all = small_all[:, shared_size : shared_size + 3 * exact.size].astype(f32)
    exact_all = exact_all.reshape(dp * nt, 3, exact.size)
    exact_all = (exact_all[:, 0] + exact_all[:, 1]) + exact_all[:, 2]
    conv_full = (
        exact_all[:, : kernel_rows * columns]
        .reshape(dp * nt, kernel_rows, columns)
        .transpose(1, 0, 2)
        .reshape(kernel_rows, -1)
    )
    gains_full = exact_all[:, kernel_rows * columns :].reshape(-1)

    pre_gain = gains_full[:D].reshape(1, D)
    post_gain = lax.dynamic_slice_in_dim(gains_full, D + t_rank * width, width).reshape(1, width)
    conv_here = jnp.concatenate(
        [lax.dynamic_slice_in_dim(conv_full, t_rank * width, width, 1), conv_full[:, DI:]], axis=1
    )
    conv_here = jnp.pad(conv_here, ((0, 8 - kernel_rows), (0, 0)))
    shared_here = jnp.concatenate(
        [
            shared_full[:, : 2 * N],
            lax.dynamic_slice_in_dim(shared_full, 2 * N + t_rank * heads_here, heads_here, 1),
            jnp.zeros((D, LANES - heads_here), bf16),
        ],
        axis=1,
    )
    common_width = 2 * N + LANES
    head_rows = jnp.stack([head_params[0], jnp.exp(head_params[1])])
    head_rows = jnp.pad(head_rows, ((0, 6), (0, LANES - heads_here)))
    skip = jnp.repeat(head_params[2], head_size).reshape(1, width)
    heads_of = (
        jnp.arange(width)[:, None] // head_size == jnp.arange(LANES)[None, :]
    ).astype(bf16)

    blocked = ids.reshape(chunks, CHUNK)
    ends, firsts = blocked[:, -1], blocked[:, 0]
    none = jnp.full((1,), -1, jnp.int32)
    before = jnp.concatenate([none, ends[:-1]])
    following = jnp.concatenate([firsts[1:], none])
    fills = [jnp.full((o,), -1, jnp.int32) for o in range(1, 4)]
    marks = [ids]
    marks += [jnp.concatenate([fills[o - 1], ids[:-o]]) == ids for o in range(1, 4)]
    marks += [jnp.concatenate([ids[o:], fills[o - 1]]) == ids for o in range(1, 4)]
    marks += [
        (blocked == before[:, None]).reshape(-1),
        (blocked == ends[:, None]).reshape(-1),
        jnp.broadcast_to((ends == before)[:, None], blocked.shape).reshape(-1),
        (blocked == following[:, None]).reshape(-1),
        ids < SEQ_SLOTS,
    ]
    aux = jnp.stack([m.astype(f32) for m in marks] + [jnp.zeros((length,), f32)] * 4, axis=1)
    segr = ids.astype(f32).reshape(1, length)
    aux_cols = aux.shape[1]

    steps = length // wide
    in_half = lambda i: i % (steps // 2)
    value_w, other_line, *cot_pieces = tie(value_w, other_line, *cot_pieces)
    plane = plane_parts(other_line, dp)
    normed, chans, pre, mixed, ssd, entering, step_in = call(
        scan_kernel,
        (steps,),
        [
            rows(wide, D, in_half), rows(wide, D, in_half), whole((1, D)), whole((D, width)),
            whole((D, common_width)), whole((8, channels)), whole((1, width)), whole((8, LANES)),
            rows(wide, aux_cols), pl.BlockSpec((1, wide), lambda i, r: (0, i)),
        ],
        [
            rows(wide, D), rows(wide, channels), rows(wide, channels), rows(wide, channels),
            rows(wide, width), pl.BlockSpec((wide // CHUNK, N, width), lambda i, r: (i, 0, 0)),
            rows(wide, LANES),
        ],
        [
            shape(length, D, dtype=bf16), shape(length, channels), shape(length, channels),
            shape(length, channels, dtype=bf16), shape(length, width),
            shape(chunks, N, width), shape(length, LANES),
        ],
        [
            pltpu.VMEM((wide + 8, channels), f32), pltpu.VMEM((N, width), f32),
            pltpu.VMEM((CHUNK, width), f32), pltpu.VMEM((2, CHUNK, width), bf16),
        ],
        length * (2 * D * (width + common_width) + 12 * width * CHUNK),
        30,
        scalars=1,
    )(*halves(token_pieces), pre_gain, value_w, shared_here, conv_here, skip, head_rows, aux, segr)

    normed, *plane = tie(normed, *plane)
    plane = jnp.concatenate([other_line] + plane, axis=0)
    gate_w, outer_t = assemble(
        [plane], [swap(plane, "dp", dp, 1)], dp, dp_me, [block_rows, block_rows]
    )
    gate_w, outer_t = gate_w.reshape(D, width), outer_t.reshape(D, width)
    cot_rank, cot0, cot1 = halves(cot_pieces)
    gate, scaled_grad, returned, sums = call(
        gate_kernel,
        (steps,),
        [
            rows(wide, D), rows(wide, D, in_half), rows(wide, D, in_half), rows(wide, aux_cols),
            rows(wide, width), whole((D, width)), whole((D, width)), whole((1, width)),
        ],
        [rows(wide, width), rows(wide, width), rows(wide, D), pl.BlockSpec((8, wide), lambda i, r: (0, i))],
        [
            shape(length, width), shape(length, width), shape(length, D, dtype=bf16),
            shape(8, length),
        ],
        [],
        4 * length * D * width,
        24,
        scalars=1,
    )(cot_rank, normed, cot0, cot1, aux, ssd, gate_w, outer_t, post_gain)
    distance = 1
    while distance < nt:
        sums = sums + swap(sums, "tensor", nt, distance)
        distance *= 2

    def relative(block, rank):
        return (rank ^ (block // per_piece)) * per_piece + block % per_piece

    def rel_rows(width_here, offset=0):
        return pl.BlockSpec((band, width_here), lambda i, r: (relative(i + offset, r[0]), 0))

    plain = lambda width_here: pl.BlockSpec((band, width_here), lambda i, r: (i, 0))
    branch, scaled, dssd, dgate, post_grad = call(
        norm_kernel,
        (length // band,),
        [
            rel_rows(width), rel_rows(width), rel_rows(width),
            pl.BlockSpec((8, band), lambda i, r: (0, relative(i, r[0]))),
            whole((D, width)), whole((1, width)),
        ],
        [plain(D), rel_rows(width), rel_rows(width), rel_rows(width), result((1, width))],
        [
            shape(length, D, dtype=bf16), shape(length, width, dtype=bf16),
            shape(length, width, dtype=bf16), shape(length, width, dtype=bf16), shape(1, width),
        ],
        [],
        2 * length * D * width,
        24,
        scalars=1,
    )(t_me, gate, scaled_grad, ssd, sums, outer_t, post_gain)
    outer_keep, outer_send = weight_grad(returned, scaled, dp, dp_me)
    dgate, outer_send = tie(dgate, outer_send)
    gate_keep, gate_send = weight_grad(normed, dgate, dp, dp_me)
    outer_line, outer_rest = start_sum(outer_keep, outer_send, dp)
    gate_line, gate_rest = start_sum(gate_keep, gate_send, dp)
    branch = branch.reshape(nt, rows_here, D)
    branch_received = [swap(branch[d], "tensor", nt, d) for d in range(1, nt)]
    dssd, *rests = tie(dssd, *outer_rest, *gate_rest)
    outer_rest, gate_rest = rests[: len(outer_rest)], rests[len(outer_rest) :]
    outer_received = middle_swaps(outer_rest, dp)
    gate_received = middle_swaps(gate_rest, dp)

    state = jnp.zeros((N, width), f32)
    win = jnp.zeros((8, channels), f32)
    carry = jnp.zeros((8, LANES), f32)
    back_parts = []
    filled = []
    top = chunks
    for part, count in enumerate((3, 3, chunks - 6)):
        back = lambda i, top=top: top - 1 - i
        top -= count
        *results, state, win, carry = call(
            scan_back_kernel,
            (count,),
            [
                rows(CHUNK, width, back), rows(CHUNK, channels, back), rows(CHUNK, channels, back),
                rows(CHUNK, channels, back), rows(CHUNK, width, back),
                pl.BlockSpec((1, N, width), lambda i, back=back: (back(i), 0, 0)),
                rows(CHUNK, LANES, back), whole((8, channels)), whole((1, width)),
                whole((8, LANES)), rows(CHUNK, aux_cols, back),
                pl.BlockSpec((1, CHUNK), lambda i, back=back: (0, back(i))),
                whole((width, LANES)),
                whole((N, width)), whole((8, channels)), whole((8, LANES)),
            ]
            + [pl.BlockSpec(memory_space=pl.ANY)] * len(filled),
            [
                rows(CHUNK, width, back), rows(CHUNK, common_width, back), result((8, channels)),
                result((8, LANES)),
                result((N, width)), result((8, channels)), result((8, LANES)),
            ],
            [
                shape(length, width, dtype=bf16), shape(length, common_width),
                shape(8, channels), shape(8, LANES),
                shape(N, width), shape(8, channels), shape(8, LANES),
            ],
            [
                pltpu.VMEM((CHUNK, channels), f32), pltpu.VMEM((CHUNK + 8, channels), f32),
                pltpu.VMEM((2 * CHUNK, width), f32), pltpu.VMEM((CHUNK, width), f32),
                pltpu.VMEM((2, CHUNK, width), bf16), pltpu.VMEM((CHUNK, width), bf16),
                pltpu.VMEM((8, width), f32),
            ],
            count * CHUNK * 30 * width * CHUNK,
            24,
            aliases={16: 0, 17: 1} if filled else None,
        )(
            dssd, mixed, pre, chans, ssd, entering, step_in, conv_here, skip, head_rows, aux, segr,
            heads_of, state, win, carry, *filled,
        )
        filled = results[:2]
        back_parts.append(results[2:])
        if part == 0:
            state, outer_line, *outer_received = tie(state, outer_line, *outer_received)
            outer_block, outer_far = middle_sum(outer_line, outer_received)
            outer_far = high_swaps(outer_far, dp)
        if part == 1:
            state, gate_line, *rests = tie(state, gate_line, *gate_received, *branch_received)
            gate_received, branch_received = rests[: len(gate_received)], rests[len(gate_received) :]
            gate_block, gate_far = middle_sum(gate_line, gate_received)
            gate_far = high_swaps(gate_far, dp)
    dval, dcommon = filled
    dval, *outer_far = tie(dval, *outer_far)
    outer_part = high_sum(outer_block, outer_far)

    branch_sum = branch[0].astype(f32)
    for piece in branch_received:
        branch_sum = branch_sum + piece.astype(f32)
    live_here = lax.dynamic_slice_in_dim(aux[:, LIVE], t_rank * rows_here, rows_here)
    tokens = residual.astype(f32)
    block_out = (tokens + branch_sum * live_here[:, None]).astype(bf16)

    def input_grad(count, offset, dtype, positions, dgate):
        return call(
            input_grad_kernel,
            (count * per_piece,),
            [
                rel_rows(width, offset), rel_rows(width, offset), rel_rows(common_width, offset),
                plain(D), whole((D, width)), whole((D, width)), whole((D, common_width)),
            ],
            [plain(D), result((1, D))],
            [shape(count * rows_here, D, dtype=dtype), shape(1, D)],
            [],
            4 * count * rows_here * D * (width + common_width),
            24,
            scalars=1,
        )(t_me, dgate, dval, dcommon, positions, gate_w, value_w, shared_here)

    sums_keep = [value_grad(normed, dval, dcommon, dp, dp_me)]
    if width > 256:
        dval_now, first_send = tie(dval, sums_keep[0][1])
        sums_keep[0] = (sums_keep[0][0], first_send)
        sums_keep.append(weight_grad(normed, dval_now, dp, dp_me, skipped=1))
    lines, parts = [], []
    for keep, send in sums_keep:
        line, part = start_sum(keep, send, dp)
        lines.append(line)
        parts.append(part)
    steps_each = len(parts[0])
    dgate, *flat = tie(dgate, *[item for part in parts for item in part])
    parts = [flat[at : at + steps_each] for at in range(0, len(flat), steps_each)]
    crossing = [middle_swaps(part, dp) for part in parts]
    others = token_pieces[1] if nt == 2 else jnp.concatenate(token_pieces[1:], axis=0)
    sent, pre_grad_sent = input_grad(nt - 1, per_piece, bf16, others, dgate)
    sent = sent.reshape(nt - 1, 2, rows_here // 2, D)
    received = [
        [swap(sent[d - 1, part], "tensor", nt, d) for d in range(1, nt)] for part in range(2)
    ]
    dgate, pre_grad_sent, *rests = tie(dgate, pre_grad_sent, *gate_far, *crossing[0])
    gate_far, crossing[0] = rests[: len(gate_far)], rests[len(gate_far) :]
    gate_part = high_sum(gate_block, gate_far)
    block, far = middle_sum(lines[0], crossing[0])
    fars = [high_swaps(far, dp)]
    blocks = [block]
    own, pre_grad_own = input_grad(1, 0, f32, residual, dgate)
    if len(parts) > 1:
        pre_grad_own, *crossing[1] = tie(pre_grad_own, *crossing[1])
        block, far = middle_sum(lines[1], crossing[1])
        fars.append(high_swaps(far, dp))
        blocks.append(block)
    pre_grad_own, *rests = tie(pre_grad_own, *received[0], *fars[0])
    received[0], fars[0] = rests[: nt - 1], rests[nt - 1 :]
    value_sums = [high_sum(blocks[0], fars[0])]
    shared_rows = shared_proj.shape[0]
    shared_sum = value_sums[0][:, 256:].reshape(nt, shared_rows, common_width)
    shared_mine = lax.dynamic_index_in_dim(shared_sum, t_rank, 0, False)
    shared_common = shared_mine[:, : 2 * N]
    shared_part = jnp.zeros((shared_rows, 2 * N + H), f32)

    def place_heads(table, piece, rank):
        return lax.dynamic_update_slice(
            table, piece[:, 2 * N : 2 * N + heads_here], (0, 2 * N + rank * heads_here)
        )

    shared_part = place_heads(shared_part, shared_mine, t_rank)
    for d in range(1, nt):
        piece = lax.dynamic_index_in_dim(shared_sum, t_rank ^ d, 0, False)
        piece = swap(piece, "tensor", nt, d)
        shared_common = shared_common + piece[:, : 2 * N]
        shared_part = place_heads(shared_part, piece, t_rank ^ d)
    shared_part = lax.dynamic_update_slice(shared_part, shared_common, (0, 0))

    pre_grad_own, *summed = tie(pre_grad_own, *[item for part in back_parts for item in part])
    dconv, dheads = [sum(summed[at::2]) for at in range(2)]
    conv_grad = lax.dynamic_update_slice(
        jnp.pad(dconv[:kernel_rows, width:], ((0, 0), (DI, 0))),
        dconv[:kernel_rows, :width],
        (0, t_rank * width),
    )
    post_all = lax.dynamic_update_slice(
        jnp.zeros((1, DI), f32), post_grad, (0, t_rank * width)
    )
    head_grad = dheads[:3, :heads_here]
    head_all = lax.dynamic_update_slice(
        jnp.zeros((3, H), f32), head_grad, (0, t_rank * heads_here)
    )
    vector = jnp.concatenate(
        [
            conv_grad.reshape(1, -1), pre_grad_sent + pre_grad_own, post_all, head_all.reshape(1, -1),
        ],
        axis=1,
    )
    for stage, (axis, size, distance) in enumerate(sum_stages(dp, nt)):
        vector = vector + swap(vector, axis, size, distance)
        if stage == 1 and len(parts) > 1:
            vector, *fars[1] = tie(vector, *fars[1])
            value_sums.append(high_sum(blocks[1], fars[1]))
        if stage == 2:
            vector, *received[1] = tie(vector, *received[1])
    value_part = jnp.concatenate([value_sums[0][:, :256]] + value_sums[1:], axis=1)
    conv_size = kernel_rows * (DI + 2 * N)
    place = d_rank * nt + t_rank
    conv_part = lax.dynamic_slice_in_dim(
        vector[0, :conv_size].reshape(kernel_rows, -1), place * columns, columns, 1
    )
    gains_part = lax.dynamic_slice_in_dim(vector[0], conv_size + place * gain_count, gain_count)
    heads_part = lax.dynamic_slice_in_dim(
        vector[0, conv_size + D + DI :].reshape(3, H), t_rank * heads_here, heads_here, 1
    )

    normed_grad = own
    for low, high in zip(*received):
        normed_grad = normed_grad + jnp.concatenate([low, high], axis=0).astype(f32)
    inverse = lax.rsqrt(jnp.mean(tokens * tokens, axis=1, keepdims=True) + norm_epsilon)
    normal_tokens = tokens * inverse
    normal_grad = normed_grad * pre_gain
    centered = normal_grad - normal_tokens * jnp.mean(
        normal_grad * normal_tokens, axis=1, keepdims=True
    )
    residual_grad = (cotangent.astype(f32) + inverse * centered).astype(bf16)

    inner_new = adam_step(
        inner_proj, inner_mean, inner_square, jnp.stack([gate_part, value_part]),
        rate_matrix, weight_decay,
    )
    shared_new = adam_step(
        shared_proj, shared_mean, shared_square, shared_part.reshape(shared_proj.shape),
        rate_matrix, weight_decay,
    )
    outer_new = adam_step(
        outer_proj, outer_mean, outer_square, outer_part.T, rate_matrix, weight_decay
    )
    conv_new = adam_step(conv_params, conv_mean, conv_square, conv_part, rate_vector, 0.0)
    gains_new = adam_step(norm_gains, gains_mean, gains_square, gains_part, rate_vector, 0.0)
    heads_new = adam_step(head_params, heads_mean, heads_square, heads_part, rate_heads, 0.0)
    return (
        (block_out, residual_grad)
        + inner_new + shared_new + outer_new + conv_new + gains_new + heads_new
    )


def solution(mesh):
    return jax.shard_map(
        functools.partial(shards, mesh.shape["dp"], mesh.shape["tensor"]),
        mesh=mesh,
        in_specs=(
            P(("dp", "tensor"), None),
            P(("dp", "tensor"), None),
            P("dp"),
            P(None, "dp", "tensor"),
            P(None, "dp", "tensor"),
            P(None, "dp", "tensor"),
            P(("dp", "tensor"), None),
            P(("dp", "tensor"), None),
            P(("dp", "tensor"), None),
            P("tensor", "dp"),
            P("tensor", "dp"),
            P("tensor", "dp"),
            P(None, ("dp", "tensor")),
            P(None, ("dp", "tensor")),
            P(None, ("dp", "tensor")),
            P(("dp", "tensor")),
            P(("dp", "tensor")),
            P(("dp", "tensor")),
            P(None, "tensor"),
            P(None, "tensor"),
            P(None, "tensor"),
        ),
        out_specs=(
            P(("dp", "tensor"), None),
            P(("dp", "tensor"), None),
            P(None, "dp", "tensor"),
            P(None, "dp", "tensor"),
            P(None, "dp", "tensor"),
            P(("dp", "tensor"), None),
            P(("dp", "tensor"), None),
            P(("dp", "tensor"), None),
            P("tensor", "dp"),
            P("tensor", "dp"),
            P("tensor", "dp"),
            P(None, ("dp", "tensor")),
            P(None, ("dp", "tensor")),
            P(None, ("dp", "tensor")),
            P(("dp", "tensor")),
            P(("dp", "tensor")),
            P(("dp", "tensor")),
            P(None, "tensor"),
            P(None, "tensor"),
            P(None, "tensor"),
        ),
        check_vma=False,
    )
```

```python
import functools

import jax
import jax.numpy as jnp
from jax import lax
from jax.experimental import pallas as pl
from jax.experimental.pallas import tpu as pltpu
from jax.sharding import PartitionSpec as P

D = 1024
H = 32
N = 128
DI = 2048
SEQ_SLOTS = 4
STEP = 10
CHUNK = 128
LANES = 128
CORES = 2
HIGH_AXIS = 4

highest = lax.Precision.HIGHEST
f32 = jnp.float32
bf16 = jnp.bfloat16
norm_epsilon = 1e-05
beta_first = 0.9
beta_second = 0.95
adam_epsilon = 1e-08
weight_decay = 0.1
rate_matrix = 0.02
rate_vector = 0.3
rate_heads = 1.0

SEG, BACK, AHEAD, INHERIT, TAIL, LINKED, NEXT, LIVE = 0, 0, 3, 7, 8, 9, 10, 11


def adam_step(weight, moment, square, gradient, rate, decay):
    moment_next = beta_first * moment + (1.0 - beta_first) * gradient
    square_next = beta_second * square + (1.0 - beta_second) * gradient * gradient
    moment_hat = moment_next / (1.0 - beta_first**STEP)
    square_hat = square_next / (1.0 - beta_second**STEP)
    weight_next = weight - rate * (
        moment_hat / (jnp.sqrt(square_hat) + adam_epsilon) + decay * weight
    )
    return (weight_next, moment_next, square_next)


def swap(value, axis, size, distance):
    return lax.ppermute(value, axis, [(i, i ^ distance) for i in range(size)])


def tie(*values):
    return lax.optimization_barrier(values)


def axis_parts(dp):
    high = HIGH_AXIS
    middle = dp // (CORES * high)
    return high, middle


def gather_line(shard, dp):
    high, middle = axis_parts(dp)
    pieces = [shard[None]]
    for step in range(1, high):
        pieces.append(swap(shard, "dp", dp, step * middle * CORES)[None])
    return jnp.concatenate(pieces, axis=0)


def plane_parts(line, dp):
    return [swap(line, "dp", dp, step * CORES) for step in range(1, axis_parts(dp)[1])]


def start_sum(keep, send, dp):
    high, middle = axis_parts(dp)
    other = swap(send, "dp", dp, 1)
    parts = [slice(step * high, (step + 1) * high) for step in range(middle)]
    line = keep[parts[0]].astype(f32) + other[parts[0]].astype(f32)
    rest = [(keep[at].astype(f32) + other[at].astype(f32)).astype(bf16) for at in parts[1:]]
    return line, rest


def middle_swaps(rest, dp):
    return [swap(part, "dp", dp, (step + 1) * CORES) for step, part in enumerate(rest)]


def middle_sum(line, received):
    for part in received:
        line = line + part.astype(f32)
    return line[0], [part.astype(bf16) for part in line[1:]]


def high_swaps(rest, dp):
    middle = axis_parts(dp)[1]
    return [swap(part, "dp", dp, (step + 1) * middle * CORES) for step, part in enumerate(rest)]


def high_sum(block, received):
    for part in received:
        block = block + part.astype(f32)
    return block


def sum_stages(dp, nt):
    stages = [("tensor", nt, 1 << bit) for bit in range((nt - 1).bit_length())]
    return stages + [("dp", dp, 1 << bit) for bit in range((dp - 1).bit_length())]


def relative_places(dp):
    high, middle = axis_parts(dp)
    return [
        (h * middle + m) * CORES + c for c in range(CORES) for m in range(middle) for h in range(high)
    ]


def call(kernel, grid, in_specs, out_specs, out_shape, scratch, flops, mib, scalars=0, aliases=None):
    params = pltpu.CompilerParams(vmem_limit_bytes=mib * 1024 * 1024)
    moved = sum(2 * s.dtype.itemsize * s.size for s in jax.tree.leaves(out_shape))
    return pl.pallas_call(
        kernel,
        grid_spec=pltpu.PrefetchScalarGridSpec(
            num_scalar_prefetch=scalars,
            grid=grid,
            in_specs=in_specs,
            out_specs=out_specs,
            scratch_shapes=scratch,
        ),
        out_shape=out_shape,
        compiler_params=params,
        input_output_aliases=aliases or {},
        cost_estimate=pl.CostEstimate(
            flops=int(flops) // 16, bytes_accessed=int(moved) // 16, transcendentals=0
        ),
    )


def whole(shape):
    return pl.BlockSpec(shape, lambda *i: (0,) * len(shape), pipeline_mode=pl.Buffered(1))


def result(shape):
    return pl.BlockSpec(shape, lambda *i: (0,) * len(shape))


def rows(count, width, index=lambda i: i):
    return pl.BlockSpec((count, width), lambda i, *s: (index(i), 0))


def shape(*dims, dtype=f32):
    return jax.ShapeDtypeStruct(dims, dtype)


def split(value):
    high = value.astype(bf16)
    return high, (value - high.astype(f32)).astype(bf16)


def mm(a, b, ca=1, cb=0):
    return lax.dot_general(a, b, (((ca,), (cb,)), ((), ())), preferred_element_type=f32)


def mm_left(value, exact, ca=1, cb=0):
    high, low = split(value)
    return mm(high, exact, ca, cb) + mm(low, exact, ca, cb)


def mm_right(exact, value, ca=1, cb=0):
    high, low = split(value)
    return mm(exact, high, ca, cb) + mm(exact, low, ca, cb)


def mm_both(a, b, ca=1, cb=0):
    a_high, a_low = split(a)
    b_high, b_low = split(b)
    return mm(a_high, b_high, ca, cb) + mm(a_low, b_high, ca, cb) + mm(a_high, b_low, ca, cb)


def sigmoid(value):
    return 0.5 * jnp.tanh(0.5 * value) + 0.5


def softplus(value):
    return jnp.maximum(value, 0.0) + jnp.log1p(jnp.exp(-jnp.abs(value)))


def iota(axis):
    return lax.broadcasted_iota(jnp.int32, (CHUNK, LANES), axis)


def pair_spread(tile, pair, left):
    rows_here = tile.shape[0]
    return jnp.where(
        left[:rows_here],
        jnp.broadcast_to(tile[:, 2 * pair : 2 * pair + 1], (rows_here, LANES)),
        jnp.broadcast_to(tile[:, 2 * pair + 1 : 2 * pair + 2], (rows_here, LANES)),
    )


def assemble_kernel(dp, parts, moves, me, *refs):
    half = dp // CORES
    sources, outs = refs[: 2 * parts], refs[2 * parts :]
    for place, distance in enumerate(relative_places(dp)):
        block = me[0] ^ distance
        base = 0
        for part in range(parts):
            source, at = (sources[part], place) if place < half else (sources[parts + part], place - half)
            end = base + source.shape[1]
            for first, last, lanes, out, each, extra, row in moves:
                low, high = max(base, first), min(end, last)
                if low < high:
                    outs[out][
                        block * each + extra, row + low - first : row + high - first, :
                    ] = source[at, low - base : high - base, lanes]
            base = end


def assemble(nears, fars, dp, dp_rank, moves, shapes):
    vmem = pl.BlockSpec(memory_space=pltpu.VMEM)
    moved = sum(4 * near.size * near.dtype.itemsize for near in nears)
    return pl.pallas_call(
        functools.partial(assemble_kernel, dp, len(nears), moves),
        in_specs=[pl.BlockSpec(memory_space=pltpu.SMEM)] + [vmem] * (2 * len(nears)),
        out_specs=[vmem] * len(shapes),
        out_shape=[shape(*dims, dtype=bf16) for dims in shapes],
        compiler_params=pltpu.CompilerParams(vmem_limit_bytes=16 * 1024 * 1024),
        cost_estimate=pl.CostEstimate(flops=0, bytes_accessed=moved, transcendentals=0),
    )(dp_rank, *nears, *fars)


def pick_half(rank, first, second):
    half = (2 * pl.program_id(0)) // pl.num_programs(0)
    own = (half == rank[0]).astype(jnp.int32)
    return jnp.where(jnp.broadcast_to(own, first.shape) == 1, first[...], second[...])


def across(pair, left):
    return jnp.concatenate(
        [jnp.where(left, pair, 0.0), jnp.where(left, 0.0, pair)], axis=0
    ).astype(bf16)


def scan_kernel(
    heads, rank, tok0, tok1, gain, wv, shw, conv, skip, hp, aux, segr,
    normed_o, ch_o, pre_o, mix_o, ssd_o, hin_o, step_o,
    win, state, carried, weighted,
):
    count = tok0.shape[0]
    width = wv.shape[1]
    channels = width + 2 * N

    @pl.when(pl.program_id(0) == 0)
    def _():
        win[0:8, :] = jnp.zeros((8, channels), f32)
        state[...] = jnp.zeros(state.shape, f32)

    x = pick_half(rank, tok0, tok1).astype(f32)
    inverse = lax.rsqrt(jnp.mean(x * x, axis=1, keepdims=True) + norm_epsilon)
    normed = (x * inverse * gain[...]).astype(bf16)
    normed_o[...] = normed
    win[8 : 8 + count, :width] = mm(normed, wv[...])
    common = mm(normed, shw[...])
    win[8 : 8 + count, width:] = common[:, : 2 * N]
    turn = lax.rem(LANES - heads * rank[1], LANES)
    step_o[...] = pltpu.roll(common[:, 2 * N :], turn, 1) + hp[0:1, :]
    table = aux[...]
    for start in range(0, channels, 256):
        cols = slice(start, start + 256)
        here = win[8 : 8 + count, cols]
        pre = conv[4:5, cols] + conv[3:4, cols] * here
        for back in range(1, 4):
            pre = pre + conv[3 - back : 4 - back, cols] * (
                win[8 - back : 8 - back + count, cols] * table[:, BACK + back : BACK + back + 1]
            )
        ch_o[:, cols] = here
        pre_o[:, cols] = pre
        mix_o[:, cols] = (pre * sigmoid(pre)).astype(bf16)
    win[0:8, :] = win[count : count + 8, :]

    row, col = iota(0), iota(1)
    left = col < 64
    tri = (row >= col).astype(f32)
    for sub in range(count // CHUNK):
        at = slice(sub * CHUNK, (sub + 1) * CHUNK)
        dt = softplus(step_o[at, :])
        run = jnp.dot(tri, -(dt * hp[1:2, :]), precision=highest, preferred_element_type=f32)
        run_t = run.T
        allowed = (table[at, SEG : SEG + 1] == segr[:, at]) & (row >= col)
        b_in = mix_o[at, width : width + N]
        b_turned = b_in.astype(f32).T.astype(bf16)
        c_out = mix_o[at, width + N :]
        scores = jnp.where(allowed, mm(c_out, b_in, 1, 1), 0.0)
        ending = run[CHUNK - 1 : CHUNK, :]
        entry = jnp.exp(run) * table[at, INHERIT : INHERIT + 1]
        tail = jnp.exp(ending - run) * table[at, TAIL : TAIL + 1]
        factor = jnp.exp(ending) * table[at, LINKED : LINKED + 1][CHUNK - 1 :, :]
        hin_o[sub] = state[...]
        carried[...] = mm_right(c_out, state[...])
        for pair in range(width // LANES):
            lanes = slice(pair * LANES, (pair + 1) * LANES)
            x_pair = mix_o[at, lanes].astype(f32)
            stepped = (x_pair * pair_spread(dt, pair, left)).astype(bf16).astype(f32)
            mixing = []
            for head in (2 * pair, 2 * pair + 1):
                spread = run[:, head : head + 1] - run_t[head : head + 1, :]
                mixing.append((jnp.exp(jnp.minimum(spread, 0.0)) * scores).astype(bf16))
            local = mm(jnp.concatenate(mixing, axis=1), across(stepped, left))
            ssd_o[at, lanes] = (
                local + carried[:, lanes] * pair_spread(entry, pair, left) + skip[:, lanes] * x_pair
            )
            high, low = split(stepped * pair_spread(tail, pair, left))
            weighted[0, :, lanes] = high
            weighted[1, :, lanes] = low
            state[:, lanes] = pair_spread(factor, pair, left) * state[:, lanes]
        state[...] += mm(b_turned, weighted[0]) + mm(b_turned, weighted[1])


def gate_kernel(rank, normed, cot0, cot1, aux, ssd, wg, out_t, gain, gate_o, sg_o, ret_o, sums_o):
    returned = (pick_half(rank, cot0, cot1).astype(f32) * aux[:, LIVE : LIVE + 1]).astype(bf16)
    ret_o[...] = returned
    gate = mm(normed[...], wg[...])
    gate_o[...] = gate
    scaled_grad = mm(returned, out_t[...])
    sg_o[...] = scaled_grad
    gated = ssd[...] * (gate * sigmoid(gate))
    squares = jnp.sum(gated * gated, axis=1, keepdims=True)
    crossed = jnp.sum(scaled_grad * gain[...] * gated, axis=1, keepdims=True)
    lane = lax.broadcasted_iota(jnp.int32, (squares.shape[0], LANES), 1)
    table = jnp.where(lane == 0, squares, jnp.where(lane == 1, crossed, 0.0))
    sums_o[...] = table.T[:8, :]


def norm_kernel(
    rank, gate_r, sg_r, ssd_r, sums_r, out_t, gain, branch_o, scaled_o, dssd_o, dgate_o, gain_o
):
    @pl.when(pl.program_id(0) == 0)
    def _():
        gain_o[...] = jnp.zeros(gain_o.shape, f32)

    gate, ssd, scaled_grad = gate_r[...], ssd_r[...], sg_r[...]
    table = jnp.concatenate([sums_r[...], jnp.zeros((LANES - 8, sums_r.shape[1]), f32)], axis=0)
    sums = table.T
    scale = lax.rsqrt(sums[:, 0:1] / DI + norm_epsilon)
    sig = sigmoid(gate)
    silu = gate * sig
    gated = ssd * silu
    scaled = (gated * scale * gain[...]).astype(bf16)
    scaled_o[...] = scaled
    branch_o[...] = mm(scaled, out_t[...], 1, 1).astype(bf16)
    gain_o[...] += jnp.sum(scaled_grad * gated * scale, axis=0, keepdims=True)
    grad = scale * (scaled_grad * gain[...]) - gated * (scale * scale * scale * (sums[:, 1:2] / DI))
    dssd_o[...] = (grad * silu).astype(bf16)
    dgate_o[...] = (grad * ssd * sig * (1.0 + gate * (1.0 - sig))).astype(bf16)


def scan_back_kernel(
    heads, rank, dssd, mix, pre, ch, ssd, hin, step, conv, skip, hp, aux, segr, heads_of,
    state_in, win_in, carry_in, *rest,
):
    dval_o, dcommon_o, dconv_o, dheads_o, dstate, dtail, carry = rest[-14:-7]
    dmix, dwin, both, flows, entries, weighted, dskip = rest[-7:]
    width = dssd.shape[1]
    channels = width + 2 * N

    @pl.when(pl.program_id(0) == 0)
    def _():
        dwin[CHUNK:, :] = win_in[...]
        dstate[...] = state_in[...]
        carry[...] = carry_in[...]
        dconv_o[...] = jnp.zeros(dconv_o.shape, f32)
        dheads_o[...] = jnp.zeros(dheads_o.shape, f32)
        dskip[...] = jnp.zeros(dskip.shape, f32)

    row, col = iota(0), iota(1)
    left = col < 64
    table = aux[...]
    step_in = step[...]
    dt = softplus(step_in)
    rate = hp[1:2, :]
    tri = (row >= col).astype(f32)
    run = jnp.dot(tri, -(dt * rate), precision=highest, preferred_element_type=f32)
    run_t = run.T
    allowed = (table[:, SEG : SEG + 1] == segr[...]) & (col >= row)
    b_in = mix[:, width : width + N]
    c_out = mix[:, width + N :]
    scores = jnp.where(allowed, mm(b_in, c_out, 1, 1), 0.0)
    ending = run[CHUNK - 1 : CHUNK, :]
    entry = jnp.exp(run) * table[:, INHERIT : INHERIT + 1]
    tail = jnp.exp(ending - run) * table[:, TAIL : TAIL + 1]
    factor = jnp.exp(ending) * table[:, LINKED : LINKED + 1][CHUNK - 1 :, :]
    c_turned = c_out.astype(f32).T.astype(bf16)
    pairs = jnp.zeros((CHUNK, CHUNK), f32)
    state_high, state_low = split(dstate[...])
    flows[...] = mm(b_in, state_high) + mm(b_in, state_low)
    for pair in range(width // LANES):
        lanes = slice(pair * LANES, (pair + 1) * LANES)
        x_pair = mix[:, lanes].astype(f32)
        dy_low = dssd[:, lanes]
        dy = dy_low.astype(f32)
        dt_pair = pair_spread(dt, pair, left)
        tail_pair = pair_spread(tail, pair, left)
        stepped = (x_pair * dt_pair).astype(bf16).astype(f32)
        inner = mm(across(stepped, left), dy_low, 1, 1)
        mixing = []
        for place, head in enumerate((2 * pair, 2 * pair + 1)):
            spread = run_t[head : head + 1, :] - run[:, head : head + 1]
            decays = jnp.exp(jnp.minimum(spread, 0.0))
            mixing.append((decays * scores).astype(bf16))
            pairs = pairs + inner[place * CHUNK : (place + 1) * CHUNK] * decays
        flow = mm(jnp.concatenate(mixing, axis=1), across(dy, left)) + tail_pair * flows[:, lanes]
        dmix[:, lanes] = dt_pair * flow + skip[:, lanes] * dy
        both[0:CHUNK, lanes] = flow * x_pair
        both[CHUNK : 2 * CHUNK, lanes] = dy * (ssd[:, lanes] - skip[:, lanes] * x_pair) - flow * stepped
        dskip[0:1, lanes] += jnp.sum(dy * x_pair, axis=0, keepdims=True)
        high, low = split(pair_spread(entry, pair, left) * dy)
        entries[0, :, lanes] = high
        entries[1, :, lanes] = low
        weighted[:, lanes] = (tail_pair * stepped).astype(bf16)
        dstate[:, lanes] = pair_spread(factor, pair, left) * dstate[:, lanes]
    pairs = jnp.where(allowed, pairs, 0.0)
    dstate[...] += mm(c_turned, entries[0]) + mm(c_turned, entries[1])
    dmix[:, width : width + N] = mm(weighted[...], state_high, 1, 1) + mm_left(pairs, c_out)
    dmix[:, width + N :] = mm(entries[0], hin[0].astype(bf16), 1, 1) + mm_left(pairs, b_in, 0, 0)

    by_head = mm_left(both[...], heads_of[...])
    direct = by_head[0:CHUNK]
    balance = by_head[CHUNK:]
    later = allowed.astype(f32)
    log_grad = jnp.dot(later, balance, precision=highest, preferred_element_type=f32)
    log_grad = log_grad + table[:, NEXT : NEXT + 1] * carry[0:1, :]
    carry[0:1, :] = log_grad[0:1, :]
    step_grad = (direct - rate * log_grad) * sigmoid(step_in)
    dcommon_o[:, 2 * N :] = pltpu.roll(step_grad, heads * rank[0], 1)
    dheads_o[0:1, :] += jnp.sum(step_grad, axis=0, keepdims=True)
    dheads_o[1:2, :] += jnp.sum(-(log_grad * dt * rate), axis=0, keepdims=True)

    for start in range(0, channels, 256):
        cols = slice(start, start + 256)
        value = pre[:, cols]
        sig = sigmoid(value)
        dwin[0:CHUNK, cols] = dmix[:, cols] * (sig * (1.0 + value * (1.0 - sig)))
        here = ch[:, cols]
        own = dwin[0:CHUNK, cols]
        total = conv[3:4, cols] * own
        dconv_o[4:5, cols] += jnp.sum(own, axis=0, keepdims=True)
        dconv_o[3:4, cols] += jnp.sum(own * here, axis=0, keepdims=True)
        for ahead in range(1, 4):
            moved = dwin[ahead : ahead + CHUNK, cols] * table[:, AHEAD + ahead : AHEAD + ahead + 1]
            total = total + conv[3 - ahead : 4 - ahead, cols] * moved
            dconv_o[3 - ahead : 4 - ahead, cols] += jnp.sum(moved * here, axis=0, keepdims=True)
        if start < width:
            dval_o[:, cols] = total.astype(bf16)
        else:
            dcommon_o[:, : 2 * N] = total
    dwin[CHUNK:, :] = dwin[0:8, :]
    dtail[...] = dwin[0:8, :]

    @pl.when(pl.program_id(0) == pl.num_programs(0) - 1)
    def _():
        dheads_o[2:3, :] = mm_left(dskip[...], heads_of[...])[0:1, :]


def scatter_blocks(dp, me, full, keep_o, send_o, cols):
    half = dp // CORES
    block = full.shape[0] // dp
    for place, distance in enumerate(relative_places(dp)):
        start = pl.multiple_of((me[0] ^ distance) * block, block)
        part = full[pl.ds(start, block), :].astype(bf16)
        if place < half:
            keep_o[place, :, cols] = part
        else:
            send_o[place - half, :, cols] = part


def weight_grad_kernel(dp, me, lhs, rhs, keep_o, send_o, turned, full):
    @pl.when(pl.program_id(0) == 0)
    def _():
        turned[...] = lhs[...].T

    full[...] = mm(turned[...], rhs[...])
    scatter_blocks(dp, me, full, keep_o, send_o, slice(None))


def weight_grad(lhs, rhs, dp, dp_rank, skipped=0):
    length, width = rhs.shape[0], rhs.shape[1] - 256 * skipped
    depth = lhs.shape[1]
    block, half = depth // dp, dp // CORES
    piece = pl.BlockSpec((half, block, 256), lambda i, *s: (0, 0, i))
    return call(
        functools.partial(weight_grad_kernel, dp),
        (width // 256,),
        [whole((length, depth)), pl.BlockSpec((length, 256), lambda i, *s: (0, i + skipped))],
        [piece, piece],
        [shape(half, block, width, dtype=bf16)] * 2,
        [pltpu.VMEM((depth, length), bf16), pltpu.VMEM((depth, 256), f32)],
        2 * length * width * depth,
        16,
        scalars=1,
    )(dp_rank, lhs, rhs)


def value_grad_kernel(dp, me, lhs, dval, dcommon, keep_o, send_o, turned, full, wide):
    step = pl.program_id(0)
    last = pl.num_programs(0) - 1

    @pl.when(step == 0)
    def _():
        turned[...] = lhs[...].T

    @pl.when(step < last)
    def _():
        full[...] = mm(turned[...], dval[...])
        cols = pl.ds(pl.multiple_of(step * 256, 256), 256)
        scatter_blocks(dp, me, full, keep_o, send_o, cols)

    @pl.when(step == last)
    def _():
        wide[...] = mm_right(turned[...], dcommon[...])
        cols = slice(keep_o.shape[2] - wide.shape[1], keep_o.shape[2])
        scatter_blocks(dp, me, wide, keep_o, send_o, cols)


def value_grad(lhs, dval, dcommon, dp, dp_rank):
    length, width = dval.shape[0], 256
    depth, extra = lhs.shape[1], dcommon.shape[1]
    block, half, per = depth // dp, dp // CORES, width // 256
    dims = (half, block, width + extra)
    return call(
        functools.partial(value_grad_kernel, dp),
        (per + 1,),
        [
            whole((length, depth)),
            pl.BlockSpec((length, 256), lambda i, *s: (0, jnp.minimum(i, per - 1))),
            whole((length, extra)),
        ],
        [result(dims), result(dims)],
        [shape(*dims, dtype=bf16)] * 2,
        [
            pltpu.VMEM((depth, length), bf16), pltpu.VMEM((depth, 256), f32),
            pltpu.VMEM((depth, extra), f32),
        ],
        2 * length * (width + 2 * extra) * depth,
        24,
        scalars=1,
    )(dp_rank, lhs, dval, dcommon)


def input_grad_kernel(rank, dgate, dval, dcommon, tok, wg, wv, shw, ng_o, gain_o):
    @pl.when(pl.program_id(0) == 0)
    def _():
        gain_o[...] = jnp.zeros(gain_o.shape, f32)

    grad = mm(dgate[...], wg[...], 1, 1) + mm(dval[...], wv[...], 1, 1)
    grad = grad + mm_left(dcommon[...], shw[...], 1, 1)
    x = tok[...].astype(f32)
    inverse = lax.rsqrt(jnp.mean(x * x, axis=1, keepdims=True) + norm_epsilon)
    gain_o[...] += jnp.sum(grad * (x * inverse), axis=0, keepdims=True)
    ng_o[...] = grad.astype(ng_o.dtype)


def shards(
    dp, nt,
    residual, cotangent, sequence_ids,
    inner_proj, inner_mean, inner_square,
    shared_proj, shared_mean, shared_square,
    outer_proj, outer_mean, outer_square,
    conv_params, conv_mean, conv_square,
    norm_gains, gains_mean, gains_square,
    head_params, heads_mean, heads_square,
):
    t_rank = lax.axis_index("tensor").astype(jnp.int32)
    d_rank = lax.axis_index("dp").astype(jnp.int32)
    dp_me = d_rank[None]
    t_me = t_rank[None]
    rows_here = residual.shape[0]
    length = rows_here * nt
    width = inner_proj.shape[2]
    heads_here = head_params.shape[1]
    head_size = width // heads_here
    channels = width + 2 * N
    chunks = length // CHUNK
    wide = 2 * CHUNK
    band = min(2 * CHUNK, rows_here)
    per_piece = rows_here // band

    def pieces_of(value):
        return [value] + [swap(value, "tensor", nt, d) for d in range(1, nt)]

    def over_tensor(value, pieces=None):
        pieces = pieces_of(value) if pieces is None else pieces
        if nt == 2:
            first = jnp.concatenate(pieces, axis=0)
            second = jnp.concatenate(pieces[::-1], axis=0)
            return jnp.where(t_rank == 0, first, second)
        stacked = jnp.take(jnp.stack(pieces), jnp.arange(nt) ^ t_rank, axis=0)
        return stacked.reshape((nt * stacked.shape[1],) + stacked.shape[2:])

    kernel_rows, columns = conv_params.shape
    gain_count = norm_gains.shape[0]
    shared_size = shared_proj.size
    exact = jnp.concatenate([conv_params.reshape(-1), norm_gains])
    terms = []
    rest = exact
    for _ in range(3):
        term = lax.optimization_barrier(rest.astype(bf16))
        terms.append(term)
        rest = rest - term.astype(f32)
    common_width = 2 * N + LANES
    shared_rows = shared_proj.shape[0]
    packed = width == 1024 and shared_rows == 32
    if packed:
        wide_shared = jnp.pad(shared_proj.astype(bf16), ((0, 0), (0, common_width - 2 * N - H)))
        flat = jnp.concatenate(terms)
        flat = jnp.pad(flat, (0, 16 * 256 - flat.size)).reshape(16, 256)
        small = jnp.concatenate([wide_shared[:16], wide_shared[16:], flat], axis=1)
        small_rows = 16
    else:
        small = jnp.concatenate([shared_proj.astype(bf16).reshape(-1)] + terms)
        small_rows = -(-small.size // width)
        while small_rows * nt % 16:
            small_rows += 1
        small = jnp.pad(small, (0, small_rows * width - small.size)).reshape(small_rows, width)
    small_pair = over_tensor(small)
    residual_now, small_pair = tie(residual, small_pair)
    token_pieces = pieces_of(residual_now)

    block_rows = D // dp
    value_shard = jnp.concatenate([inner_proj[1].astype(bf16), small_pair], axis=0)
    cut = -(-value_shard.shape[0] // 32) * 16
    first_line = gather_line(value_shard[:cut], dp)
    second_shard, first_line = tie(value_shard[cut:], first_line)
    second_line = gather_line(second_shard, dp)
    second_line, ids = tie(second_line, sequence_ids)
    first_near = jnp.concatenate([first_line] + plane_parts(first_line, dp), axis=0)
    other_shard = jnp.concatenate(
        [inner_proj[0].astype(bf16), outer_proj.T.astype(bf16)], axis=0
    )
    other_shard, second_line = tie(other_shard, second_line)
    other_line = gather_line(other_shard, dp)
    second_line, *parts = tie(second_line, *plane_parts(second_line, dp), *token_pieces)
    parts, token_pieces = parts[:-nt], parts[-nt:]
    second_near = jnp.concatenate([second_line] + parts, axis=0)
    cotangent_now, *token_pieces = tie(cotangent, *token_pieces)
    cot_cut = rows_here // 2
    cot_early = [swap(cotangent_now[:cot_cut], "tensor", nt, d) for d in range(1, nt)]
    cot_late = [swap(cotangent_now[cot_cut:], "tensor", nt, d) for d in range(1, nt)]
    fars = [swap(first_near, "dp", dp, 1), swap(second_near, "dp", dp, 1)]
    first_far, second_far, *cot_early = tie(*fars, *cot_early)
    full = slice(None)
    moves = [(0, block_rows, full, 0, 1, 0, 0)]
    dims = [(dp, block_rows, width)]
    if packed:
        for t in range(nt):
            at = (block_rows + 16 * t, block_rows + 16 * t + 16)
            moves.append(at + (slice(0, common_width), 1, nt, t, 0))
            moves.append(at + (slice(common_width, 2 * common_width), 1, nt, t, 16))
            moves.append(at + (slice(2 * common_width, width), 2, nt, t, 0))
        dims += [(dp * nt, 32, common_width), (dp * nt, 16, 256)]
    else:
        moves.append((block_rows, block_rows + small_rows * nt, full, 1, 1, 0, 0))
        dims += [(dp, small_rows * nt, width)]
    value_w, *small_all = assemble(
        [first_near, second_near], [first_far, second_far], dp, dp_me, moves, dims
    )
    value_w = value_w.reshape(D, width)

    def halves(pieces):
        if nt == 2:
            return t_me, pieces[0], pieces[1]
        all_rows = over_tensor(None, pieces)
        return jnp.zeros((1,), jnp.int32), all_rows[: length // 2], all_rows[length // 2 :]

    if packed:
        shared_here = small_all[0].reshape(D, common_width)
        exact_all = small_all[1].reshape(dp * nt, -1)[:, : 3 * exact.size].astype(f32)
    else:
        small_all = small_all[0].reshape(dp * nt, small_rows * width)
        shared_here = small_all[:, :shared_size].reshape(D, -1)
        shared_here = jnp.pad(shared_here, ((0, 0), (0, common_width - 2 * N - H)))
        exact_all = small_all[:, shared_size : shared_size + 3 * exact.size].astype(f32)
    exact_all = exact_all.reshape(dp * nt, 3, exact.size)
    exact_all = (exact_all[:, 0] + exact_all[:, 1]) + exact_all[:, 2]
    conv_full = (
        exact_all[:, : kernel_rows * columns]
        .reshape(dp * nt, kernel_rows, columns)
        .transpose(1, 0, 2)
        .reshape(kernel_rows, -1)
    )
    gains_full = exact_all[:, kernel_rows * columns :].reshape(-1)

    pre_gain = gains_full[:D].reshape(1, D)
    post_gain = lax.dynamic_slice_in_dim(gains_full, D + t_rank * width, width).reshape(1, width)
    conv_here = jnp.concatenate(
        [lax.dynamic_slice_in_dim(conv_full, t_rank * width, width, 1), conv_full[:, DI:]], axis=1
    )
    conv_here = jnp.pad(conv_here, ((0, 8 - kernel_rows), (0, 0)))
    head_rows = jnp.stack([head_params[0], jnp.exp(head_params[1])])
    head_rows = jnp.pad(head_rows, ((0, 6), (0, LANES - heads_here)))
    skip = jnp.repeat(head_params[2], head_size).reshape(1, width)
    heads_of = (
        jnp.arange(width)[:, None] // head_size == jnp.arange(LANES)[None, :]
    ).astype(bf16)

    blocked = ids.reshape(chunks, CHUNK)
    ends, firsts = blocked[:, -1], blocked[:, 0]
    none = jnp.full((1,), -1, jnp.int32)
    before = jnp.concatenate([none, ends[:-1]])
    following = jnp.concatenate([firsts[1:], none])
    fills = [jnp.full((o,), -1, jnp.int32) for o in range(1, 4)]
    marks = [ids]
    marks += [jnp.concatenate([fills[o - 1], ids[:-o]]) == ids for o in range(1, 4)]
    marks += [jnp.concatenate([ids[o:], fills[o - 1]]) == ids for o in range(1, 4)]
    marks += [
        (blocked == before[:, None]).reshape(-1),
        (blocked == ends[:, None]).reshape(-1),
        jnp.broadcast_to((ends == before)[:, None], blocked.shape).reshape(-1),
        (blocked == following[:, None]).reshape(-1),
        ids < SEQ_SLOTS,
    ]
    aux = jnp.stack([m.astype(f32) for m in marks] + [jnp.zeros((length,), f32)] * 4, axis=1)
    segr = ids.astype(f32).reshape(1, length)
    aux_cols = aux.shape[1]

    steps = length // wide
    in_half = lambda i: i % (steps // 2)
    value_w, other_line, *cot_late = tie(value_w, other_line, *cot_late)
    cot_pieces = [cotangent] + [
        jnp.concatenate([early, late], axis=0) for early, late in zip(cot_early, cot_late)
    ]
    plane = plane_parts(other_line, dp)
    tok_rank, tok0, tok1 = halves(token_pieces)
    normed, chans, pre, mixed, ssd, entering, step_in = call(
        functools.partial(scan_kernel, heads_here),
        (steps,),
        [
            rows(wide, D, in_half), rows(wide, D, in_half), whole((1, D)), whole((D, width)),
            whole((D, common_width)), whole((8, channels)), whole((1, width)), whole((8, LANES)),
            rows(wide, aux_cols), pl.BlockSpec((1, wide), lambda i, r: (0, i)),
        ],
        [
            rows(wide, D), rows(wide, channels), rows(wide, channels), rows(wide, channels),
            rows(wide, width), pl.BlockSpec((wide // CHUNK, N, width), lambda i, r: (i, 0, 0)),
            rows(wide, LANES),
        ],
        [
            shape(length, D, dtype=bf16), shape(length, channels), shape(length, channels),
            shape(length, channels, dtype=bf16), shape(length, width),
            shape(chunks, N, width), shape(length, LANES),
        ],
        [
            pltpu.VMEM((wide + 8, channels), f32), pltpu.VMEM((N, width), f32),
            pltpu.VMEM((CHUNK, width), f32), pltpu.VMEM((2, CHUNK, width), bf16),
        ],
        length * (2 * D * (width + common_width) + 12 * width * CHUNK),
        48,
        scalars=1,
    )(jnp.concatenate([tok_rank, t_me]), tok0, tok1, pre_gain, value_w, shared_here, conv_here, skip, head_rows, aux, segr)

    normed, *plane = tie(normed, *plane)
    plane = jnp.concatenate([other_line] + plane, axis=0)
    moves = [
        (0, block_rows, full, 0, 1, 0, 0), (block_rows, 2 * block_rows, full, 1, 1, 0, 0)
    ]
    gate_w, outer_t = assemble(
        [plane], [swap(plane, "dp", dp, 1)], dp, dp_me, moves, [(dp, block_rows, width)] * 2
    )
    gate_w, outer_t = gate_w.reshape(D, width), outer_t.reshape(D, width)
    cot_rank, cot0, cot1 = halves(cot_pieces)
    gate, scaled_grad, returned, sums = call(
        gate_kernel,
        (steps,),
        [
            rows(wide, D), rows(wide, D, in_half), rows(wide, D, in_half), rows(wide, aux_cols),
            rows(wide, width), whole((D, width)), whole((D, width)), whole((1, width)),
        ],
        [rows(wide, width), rows(wide, width), rows(wide, D), pl.BlockSpec((8, wide), lambda i, r: (0, i))],
        [
            shape(length, width), shape(length, width), shape(length, D, dtype=bf16),
            shape(8, length),
        ],
        [],
        4 * length * D * width,
        24,
        scalars=1,
    )(cot_rank, normed, cot0, cot1, aux, ssd, gate_w, outer_t, post_gain)
    distance = 1
    while distance < nt:
        sums = sums + swap(sums, "tensor", nt, distance)
        distance *= 2

    def relative(block, rank):
        return (rank ^ (block // per_piece)) * per_piece + block % per_piece

    def rel_rows(width_here, offset=0):
        return pl.BlockSpec((band, width_here), lambda i, r: (relative(i + offset, r[0]), 0))

    plain = lambda width_here: pl.BlockSpec((band, width_here), lambda i, r: (i, 0))
    branch, scaled, dssd, dgate, post_grad = call(
        norm_kernel,
        (length // band,),
        [
            rel_rows(width), rel_rows(width), rel_rows(width),
            pl.BlockSpec((8, band), lambda i, r: (0, relative(i, r[0]))),
            whole((D, width)), whole((1, width)),
        ],
        [plain(D), rel_rows(width), rel_rows(width), rel_rows(width), result((1, width))],
        [
            shape(length, D, dtype=bf16), shape(length, width, dtype=bf16),
            shape(length, width, dtype=bf16), shape(length, width, dtype=bf16), shape(1, width),
        ],
        [],
        2 * length * D * width,
        24,
        scalars=1,
    )(t_me, gate, scaled_grad, ssd, sums, outer_t, post_gain)
    outer_keep, outer_send = weight_grad(returned, scaled, dp, dp_me)
    dgate, outer_send = tie(dgate, outer_send)
    gate_keep, gate_send = weight_grad(normed, dgate, dp, dp_me)
    outer_line, outer_rest = start_sum(outer_keep, outer_send, dp)
    gate_line, gate_rest = start_sum(gate_keep, gate_send, dp)
    branch = branch.reshape(nt, rows_here, D)
    branch_received = [swap(branch[d], "tensor", nt, d) for d in range(1, nt)]
    dssd, *rests = tie(dssd, *outer_rest, *gate_rest)
    outer_rest, gate_rest = rests[: len(outer_rest)], rests[len(outer_rest) :]
    outer_received = middle_swaps(outer_rest, dp)
    gate_received = middle_swaps(gate_rest, dp)

    state = jnp.zeros((N, width), f32)
    win = jnp.zeros((8, channels), f32)
    carry = jnp.zeros((8, LANES), f32)
    back_parts = []
    filled = []
    top = chunks
    for part, count in enumerate((3, 3, chunks - 6)):
        back = lambda i, top=top: top - 1 - i
        top -= count
        *results, state, win, carry = call(
            functools.partial(scan_back_kernel, heads_here),
            (count,),
            [
                rows(CHUNK, width, back), rows(CHUNK, channels, back), rows(CHUNK, channels, back),
                rows(CHUNK, channels, back), rows(CHUNK, width, back),
                pl.BlockSpec((1, N, width), lambda i, r, back=back: (back(i), 0, 0)),
                rows(CHUNK, LANES, back), whole((8, channels)), whole((1, width)),
                whole((8, LANES)), rows(CHUNK, aux_cols, back),
                pl.BlockSpec((1, CHUNK), lambda i, r, back=back: (0, back(i))),
                whole((width, LANES)),
                whole((N, width)), whole((8, channels)), whole((8, LANES)),
            ]
            + [pl.BlockSpec(memory_space=pl.ANY)] * len(filled),
            [
                rows(CHUNK, width, back), rows(CHUNK, common_width, back), result((8, channels)),
                result((8, LANES)),
                result((N, width)), result((8, channels)), result((8, LANES)),
            ],
            [
                shape(length, width, dtype=bf16), shape(length, common_width),
                shape(8, channels), shape(8, LANES),
                shape(N, width), shape(8, channels), shape(8, LANES),
            ],
            [
                pltpu.VMEM((CHUNK, channels), f32), pltpu.VMEM((CHUNK + 8, channels), f32),
                pltpu.VMEM((2 * CHUNK, width), f32), pltpu.VMEM((CHUNK, width), f32),
                pltpu.VMEM((2, CHUNK, width), bf16), pltpu.VMEM((CHUNK, width), bf16),
                pltpu.VMEM((8, width), f32),
            ],
            count * CHUNK * 30 * width * CHUNK,
            48,
            scalars=1,
            aliases={17: 0, 18: 1} if filled else None,
        )(
            t_me, dssd, mixed, pre, chans, ssd, entering, step_in, conv_here, skip, head_rows, aux, segr,
            heads_of, state, win, carry, *filled,
        )
        filled = results[:2]
        back_parts.append(results[2:])
        if part == 0:
            state, outer_line, *outer_received = tie(state, outer_line, *outer_received)
            outer_block, outer_far = middle_sum(outer_line, outer_received)
            outer_far = high_swaps(outer_far, dp)
        if part == 1:
            state, gate_line, *rests = tie(
                state, gate_line, *branch_received, *gate_received, *outer_far
            )
            branch_received = rests[: nt - 1]
            gate_received, outer_far = rests[nt - 1 : -len(outer_far)], rests[-len(outer_far) :]
            gate_block, gate_far = middle_sum(gate_line, gate_received)
            gate_far = high_swaps(gate_far, dp)
    dval, dcommon = filled
    dval, *gate_far = tie(dval, *gate_far)
    outer_part = high_sum(outer_block, outer_far)
    gate_part = high_sum(gate_block, gate_far)

    branch_sum = branch[0].astype(f32)
    for piece in branch_received:
        branch_sum = branch_sum + piece.astype(f32)
    live_here = lax.dynamic_slice_in_dim(aux[:, LIVE], t_rank * rows_here, rows_here)
    tokens = residual.astype(f32)
    block_out = (tokens + branch_sum * live_here[:, None]).astype(bf16)

    def input_grad(count, offset, dtype, positions, dgate):
        return call(
            input_grad_kernel,
            (count * per_piece,),
            [
                rel_rows(width, offset), rel_rows(width, offset), rel_rows(common_width, offset),
                plain(D), whole((D, width)), whole((D, width)), whole((D, common_width)),
            ],
            [plain(D), result((1, D))],
            [shape(count * rows_here, D, dtype=dtype), shape(1, D)],
            [],
            4 * count * rows_here * D * (width + common_width),
            24,
            scalars=1,
        )(t_me, dgate, dval, dcommon, positions, gate_w, value_w, shared_here)

    keep, send = value_grad(normed, dval, dcommon, dp, dp_me)
    line, part = start_sum(keep, send, dp)
    dgate, *part = tie(dgate, *part)
    crossing = middle_swaps(part, dp)
    others = token_pieces[1] if nt == 2 else jnp.concatenate(token_pieces[1:], axis=0)
    sent, pre_grad_sent = input_grad(nt - 1, per_piece, bf16, others, dgate)
    sent = sent.reshape(nt - 1, 2, rows_here // 2, D)
    received = [
        [swap(sent[d - 1, at], "tensor", nt, d) for d in range(1, nt)] for at in range(2)
    ]
    dgate, pre_grad_sent = tie(dgate, pre_grad_sent)
    own, pre_grad_own = input_grad(1, 0, f32, residual, dgate)
    dval, pre_grad_own, *crossing = tie(dval, pre_grad_own, *crossing)
    block, far = middle_sum(line, crossing)
    fars = [high_swaps(far, dp)]
    blocks = [block]
    small_grads = [item for each in back_parts for item in each]
    two = width > 256
    if two:
        keep, send = weight_grad(normed, dval, dp, dp_me, skipped=1)
        line, part = start_sum(keep, send, dp)
        pre_grad_own, *rests = tie(pre_grad_own, *received[0], *part)
        received[0], part = rests[: nt - 1], rests[nt - 1 :]
        crossing = middle_swaps(part, dp)
    dconv, dheads = [sum(small_grads[at::2]) for at in range(2)]
    conv_grad = lax.dynamic_update_slice(
        jnp.pad(dconv[:kernel_rows, width:], ((0, 0), (DI, 0))),
        dconv[:kernel_rows, :width],
        (0, t_rank * width),
    )
    post_all = lax.dynamic_update_slice(
        jnp.zeros((1, DI), f32), post_grad, (0, t_rank * width)
    )
    head_grad = dheads[:3, :heads_here]
    head_all = lax.dynamic_update_slice(
        jnp.zeros((3, H), f32), head_grad, (0, t_rank * heads_here)
    )
    vector = jnp.concatenate(
        [
            conv_grad.reshape(1, -1), pre_grad_sent + pre_grad_own, post_all, head_all.reshape(1, -1),
        ],
        axis=1,
    )
    for stage, (axis, size, distance) in enumerate(sum_stages(dp, nt)):
        vector = vector + swap(vector, axis, size, distance)
        if stage == 0:
            vector, *fars[0] = tie(vector, *fars[0])
            value_sums = [high_sum(blocks[0], fars[0])]
        if stage == 1 and two:
            vector, *rests = tie(vector, *received[1], *crossing)
            received[1], crossing = rests[: nt - 1], rests[nt - 1 :]
            block, far = middle_sum(line, crossing)
            value_sums.append(high_sum(block, high_swaps(far, dp)))
    shared_sum = value_sums[0][:, 256:].reshape(nt, shared_rows, common_width)
    shared_mine = lax.dynamic_index_in_dim(shared_sum, t_rank, 0, False)
    for d in range(1, nt):
        piece = lax.dynamic_index_in_dim(shared_sum, t_rank ^ d, 0, False)
        shared_mine = shared_mine + swap(piece, "tensor", nt, d)
    shared_part = shared_mine[:, : 2 * N + H]
    value_part = jnp.concatenate([value_sums[0][:, :256]] + value_sums[1:], axis=1)
    conv_size = kernel_rows * (DI + 2 * N)
    place = d_rank * nt + t_rank
    conv_part = lax.dynamic_slice_in_dim(
        vector[0, :conv_size].reshape(kernel_rows, -1), place * columns, columns, 1
    )
    gains_part = lax.dynamic_slice_in_dim(vector[0], conv_size + place * gain_count, gain_count)
    heads_part = lax.dynamic_slice_in_dim(
        vector[0, conv_size + D + DI :].reshape(3, H), t_rank * heads_here, heads_here, 1
    )

    normed_grad = own
    for low, high in zip(*received):
        normed_grad = normed_grad + jnp.concatenate([low, high], axis=0).astype(f32)
    inverse = lax.rsqrt(jnp.mean(tokens * tokens, axis=1, keepdims=True) + norm_epsilon)
    normal_tokens = tokens * inverse
    normal_grad = normed_grad * pre_gain
    centered = normal_grad - normal_tokens * jnp.mean(
        normal_grad * normal_tokens, axis=1, keepdims=True
    )
    residual_grad = (cotangent.astype(f32) + inverse * centered).astype(bf16)

    inner_new = adam_step(
        inner_proj, inner_mean, inner_square, jnp.stack([gate_part, value_part]),
        rate_matrix, weight_decay,
    )
    shared_new = adam_step(
        shared_proj, shared_mean, shared_square, shared_part.reshape(shared_proj.shape),
        rate_matrix, weight_decay,
    )
    outer_new = adam_step(
        outer_proj, outer_mean, outer_square, outer_part.T, rate_matrix, weight_decay
    )
    conv_new = adam_step(conv_params, conv_mean, conv_square, conv_part, rate_vector, 0.0)
    gains_new = adam_step(norm_gains, gains_mean, gains_square, gains_part, rate_vector, 0.0)
    heads_new = adam_step(head_params, heads_mean, heads_square, heads_part, rate_heads, 0.0)
    return (
        (block_out, residual_grad)
        + inner_new + shared_new + outer_new + conv_new + gains_new + heads_new
    )


def solution(mesh):
    return jax.shard_map(
        functools.partial(shards, mesh.shape["dp"], mesh.shape["tensor"]),
        mesh=mesh,
        in_specs=(
            P(("dp", "tensor"), None),
            P(("dp", "tensor"), None),
            P("dp"),
            P(None, "dp", "tensor"),
            P(None, "dp", "tensor"),
            P(None, "dp", "tensor"),
            P(("dp", "tensor"), None),
            P(("dp", "tensor"), None),
            P(("dp", "tensor"), None),
            P("tensor", "dp"),
            P("tensor", "dp"),
            P("tensor", "dp"),
            P(None, ("dp", "tensor")),
            P(None, ("dp", "tensor")),
            P(None, ("dp", "tensor")),
            P(("dp", "tensor")),
            P(("dp", "tensor")),
            P(("dp", "tensor")),
            P(None, "tensor"),
            P(None, "tensor"),
            P(None, "tensor"),
        ),
        out_specs=(
            P(("dp", "tensor"), None),
            P(("dp", "tensor"), None),
            P(None, "dp", "tensor"),
            P(None, "dp", "tensor"),
            P(None, "dp", "tensor"),
            P(("dp", "tensor"), None),
            P(("dp", "tensor"), None),
            P(("dp", "tensor"), None),
            P("tensor", "dp"),
            P("tensor", "dp"),
            P("tensor", "dp"),
            P(None, ("dp", "tensor")),
            P(None, ("dp", "tensor")),
            P(None, ("dp", "tensor")),
            P(("dp", "tensor")),
            P(("dp", "tensor")),
            P(("dp", "tensor")),
            P(None, "tensor"),
            P(None, "tensor"),
            P(None, "tensor"),
        ),
        check_vma=False,
    )
```

```python
import functools

import jax
import jax.numpy as jnp
from jax import lax
from jax.experimental import pallas as pl
from jax.experimental.pallas import tpu as pltpu
from jax.sharding import PartitionSpec as P

D = 1024
H = 32
N = 128
DI = 2048
SEQ_SLOTS = 4
STEP = 10
CHUNK = 128
LANES = 128
CORES = 2
HIGH_AXIS = 4

highest = lax.Precision.HIGHEST
f32 = jnp.float32
bf16 = jnp.bfloat16
norm_epsilon = 1e-05
beta_first = 0.9
beta_second = 0.95
adam_epsilon = 1e-08
weight_decay = 0.1
rate_matrix = 0.02
rate_vector = 0.3
rate_heads = 1.0

SEG, BACK, AHEAD, INHERIT, TAIL, LINKED, NEXT, LIVE = 0, 0, 3, 7, 8, 9, 10, 11


def adam_step(weight, moment, square, gradient, rate, decay):
    moment_next = beta_first * moment + (1.0 - beta_first) * gradient
    square_next = beta_second * square + (1.0 - beta_second) * gradient * gradient
    moment_hat = moment_next / (1.0 - beta_first**STEP)
    square_hat = square_next / (1.0 - beta_second**STEP)
    weight_next = weight - rate * (
        moment_hat / (jnp.sqrt(square_hat) + adam_epsilon) + decay * weight
    )
    return (weight_next, moment_next, square_next)


def swap(value, axis, size, distance):
    return lax.ppermute(value, axis, [(i, i ^ distance) for i in range(size)])


def tie(*values):
    return lax.optimization_barrier(values)


def axis_parts(dp):
    high = HIGH_AXIS
    middle = dp // (CORES * high)
    return high, middle


def gather_line(shard, dp):
    high, middle = axis_parts(dp)
    pieces = [shard[None]]
    for step in range(1, high):
        pieces.append(swap(shard, "dp", dp, step * middle * CORES)[None])
    return jnp.concatenate(pieces, axis=0)


def plane_parts(line, dp):
    return [swap(line, "dp", dp, step * CORES) for step in range(1, axis_parts(dp)[1])]


def start_sum(keep, send, dp):
    high, middle = axis_parts(dp)
    other = swap(send, "dp", dp, 1)
    parts = [slice(step * high, (step + 1) * high) for step in range(middle)]
    line = keep[parts[0]].astype(f32) + other[parts[0]].astype(f32)
    rest = [(keep[at].astype(f32) + other[at].astype(f32)).astype(bf16) for at in parts[1:]]
    return line, rest


def middle_swaps(rest, dp):
    return [swap(part, "dp", dp, (step + 1) * CORES) for step, part in enumerate(rest)]


def middle_sum(line, received):
    for part in received:
        line = line + part.astype(f32)
    return line[0], [part.astype(bf16) for part in line[1:]]


def high_swaps(rest, dp):
    middle = axis_parts(dp)[1]
    return [swap(part, "dp", dp, (step + 1) * middle * CORES) for step, part in enumerate(rest)]


def high_sum(block, received):
    for part in received:
        block = block + part.astype(f32)
    return block


def sum_stages(dp, nt):
    stages = [("tensor", nt, 1 << bit) for bit in range((nt - 1).bit_length())]
    return stages + [("dp", dp, 1 << bit) for bit in range((dp - 1).bit_length())]


def relative_places(dp):
    high, middle = axis_parts(dp)
    return [
        (h * middle + m) * CORES + c for c in range(CORES) for m in range(middle) for h in range(high)
    ]


def call(kernel, grid, in_specs, out_specs, out_shape, scratch, flops, mib, scalars=0, aliases=None):
    params = pltpu.CompilerParams(vmem_limit_bytes=mib * 1024 * 1024)
    moved = sum(2 * s.dtype.itemsize * s.size for s in jax.tree.leaves(out_shape))
    return pl.pallas_call(
        kernel,
        grid_spec=pltpu.PrefetchScalarGridSpec(
            num_scalar_prefetch=scalars,
            grid=grid,
            in_specs=in_specs,
            out_specs=out_specs,
            scratch_shapes=scratch,
        ),
        out_shape=out_shape,
        compiler_params=params,
        input_output_aliases=aliases or {},
        cost_estimate=pl.CostEstimate(
            flops=int(flops) // 16, bytes_accessed=int(moved) // 16, transcendentals=0
        ),
    )


def whole(shape):
    return pl.BlockSpec(shape, lambda *i: (0,) * len(shape), pipeline_mode=pl.Buffered(1))


def result(shape):
    return pl.BlockSpec(shape, lambda *i: (0,) * len(shape))


def rows(count, width, index=lambda i: i):
    return pl.BlockSpec((count, width), lambda i, *s: (index(i), 0))


def shape(*dims, dtype=f32):
    return jax.ShapeDtypeStruct(dims, dtype)


def split(value):
    high = value.astype(bf16)
    return high, (value - high.astype(f32)).astype(bf16)


def mm(a, b, ca=1, cb=0):
    return lax.dot_general(a, b, (((ca,), (cb,)), ((), ())), preferred_element_type=f32)


def mm_left(value, exact, ca=1, cb=0):
    high, low = split(value)
    return mm(high, exact, ca, cb) + mm(low, exact, ca, cb)


def mm_right(exact, value, ca=1, cb=0):
    high, low = split(value)
    return mm(exact, high, ca, cb) + mm(exact, low, ca, cb)


def mm_both(a, b, ca=1, cb=0):
    a_high, a_low = split(a)
    b_high, b_low = split(b)
    return mm(a_high, b_high, ca, cb) + mm(a_low, b_high, ca, cb) + mm(a_high, b_low, ca, cb)


def sigmoid(value):
    return 0.5 * jnp.tanh(0.5 * value) + 0.5


def softplus(value):
    return jnp.maximum(value, 0.0) + jnp.log1p(jnp.exp(-jnp.abs(value)))


def iota(axis):
    return lax.broadcasted_iota(jnp.int32, (CHUNK, LANES), axis)


def pair_spread(tile, pair, left):
    rows_here = tile.shape[0]
    return jnp.where(
        left[:rows_here],
        jnp.broadcast_to(tile[:, 2 * pair : 2 * pair + 1], (rows_here, LANES)),
        jnp.broadcast_to(tile[:, 2 * pair + 1 : 2 * pair + 2], (rows_here, LANES)),
    )


def assemble_kernel(dp, parts, moves, me, *refs):
    half = dp // CORES
    sources, outs = refs[: 2 * parts], refs[2 * parts :]
    for place, distance in enumerate(relative_places(dp)):
        block = me[0] ^ distance
        base = 0
        for part in range(parts):
            source, at = (sources[part], place) if place < half else (sources[parts + part], place - half)
            end = base + source.shape[1]
            for first, last, lanes, out, each, extra, row in moves:
                low, high = max(base, first), min(end, last)
                if low < high:
                    outs[out][
                        block * each + extra, row + low - first : row + high - first, :
                    ] = source[at, low - base : high - base, lanes]
            base = end


def assemble(nears, fars, dp, dp_rank, moves, shapes):
    vmem = pl.BlockSpec(memory_space=pltpu.VMEM)
    moved = sum(4 * near.size * near.dtype.itemsize for near in nears)
    return pl.pallas_call(
        functools.partial(assemble_kernel, dp, len(nears), moves),
        in_specs=[pl.BlockSpec(memory_space=pltpu.SMEM)] + [vmem] * (2 * len(nears)),
        out_specs=[vmem] * len(shapes),
        out_shape=[shape(*dims, dtype=bf16) for dims in shapes],
        compiler_params=pltpu.CompilerParams(vmem_limit_bytes=16 * 1024 * 1024),
        cost_estimate=pl.CostEstimate(flops=0, bytes_accessed=moved, transcendentals=0),
    )(dp_rank, *nears, *fars)


def pick_half(rank, first, second):
    half = (2 * pl.program_id(0)) // pl.num_programs(0)
    own = (half == rank[0]).astype(jnp.int32)
    return jnp.where(jnp.broadcast_to(own, first.shape) == 1, first[...], second[...])


def across(pair, left):
    return jnp.concatenate(
        [jnp.where(left, pair, 0.0), jnp.where(left, 0.0, pair)], axis=0
    ).astype(bf16)


def scan_kernel(
    heads, rank, tok0, tok1, gain, wv, shw, conv, skip, hp, aux, segr,
    normed_o, ch_o, pre_o, mix_o, ssd_o, hin_o, step_o,
    win, state, carried, weighted,
):
    count = tok0.shape[0]
    width = wv.shape[1]
    channels = width + 2 * N

    @pl.when(pl.program_id(0) == 0)
    def _():
        win[0:8, :] = jnp.zeros((8, channels), f32)
        state[...] = jnp.zeros(state.shape, f32)

    x = pick_half(rank, tok0, tok1).astype(f32)
    inverse = lax.rsqrt(jnp.mean(x * x, axis=1, keepdims=True) + norm_epsilon)
    normed = (x * inverse * gain[...]).astype(bf16)
    normed_o[...] = normed
    win[8 : 8 + count, :width] = mm(normed, wv[...])
    common = mm(normed, shw[...])
    win[8 : 8 + count, width:] = common[:, : 2 * N]
    turn = lax.rem(LANES - heads * rank[1], LANES)
    step_o[...] = pltpu.roll(common[:, 2 * N :], turn, 1) + hp[0:1, :]
    table = aux[...]
    for start in range(0, channels, 256):
        cols = slice(start, start + 256)
        here = win[8 : 8 + count, cols]
        pre = conv[4:5, cols] + conv[3:4, cols] * here
        for back in range(1, 4):
            pre = pre + conv[3 - back : 4 - back, cols] * (
                win[8 - back : 8 - back + count, cols] * table[:, BACK + back : BACK + back + 1]
            )
        ch_o[:, cols] = here
        pre_o[:, cols] = pre
        mix_o[:, cols] = (pre * sigmoid(pre)).astype(bf16)
    win[0:8, :] = win[count : count + 8, :]

    row, col = iota(0), iota(1)
    left = col < 64
    tri = (row >= col).astype(f32)
    for sub in range(count // CHUNK):
        at = slice(sub * CHUNK, (sub + 1) * CHUNK)
        dt = softplus(step_o[at, :])
        run = jnp.dot(tri, -(dt * hp[1:2, :]), precision=highest, preferred_element_type=f32)
        run_t = run.T
        allowed = (table[at, SEG : SEG + 1] == segr[:, at]) & (row >= col)
        b_in = mix_o[at, width : width + N]
        b_turned = b_in.astype(f32).T.astype(bf16)
        c_out = mix_o[at, width + N :]
        scores = jnp.where(allowed, mm(c_out, b_in, 1, 1), 0.0)
        ending = run[CHUNK - 1 : CHUNK, :]
        entry = jnp.exp(run) * table[at, INHERIT : INHERIT + 1]
        tail = jnp.exp(ending - run) * table[at, TAIL : TAIL + 1]
        factor = jnp.exp(ending) * table[at, LINKED : LINKED + 1][CHUNK - 1 :, :]
        hin_o[sub] = state[...]
        carried[...] = mm_right(c_out, state[...])
        for pair in range(width // LANES):
            lanes = slice(pair * LANES, (pair + 1) * LANES)
            x_pair = mix_o[at, lanes].astype(f32)
            stepped = (x_pair * pair_spread(dt, pair, left)).astype(bf16).astype(f32)
            mixing = []
            for head in (2 * pair, 2 * pair + 1):
                spread = run[:, head : head + 1] - run_t[head : head + 1, :]
                mixing.append((jnp.exp(jnp.minimum(spread, 0.0)) * scores).astype(bf16))
            local = mm(jnp.concatenate(mixing, axis=1), across(stepped, left))
            ssd_o[at, lanes] = (
                local + carried[:, lanes] * pair_spread(entry, pair, left) + skip[:, lanes] * x_pair
            )
            high, low = split(stepped * pair_spread(tail, pair, left))
            weighted[0, :, lanes] = high
            weighted[1, :, lanes] = low
            state[:, lanes] = pair_spread(factor, pair, left) * state[:, lanes]
        state[...] += mm(b_turned, weighted[0]) + mm(b_turned, weighted[1])


def gate_kernel(rank, normed, cot0, cot1, aux, ssd, wg, out_t, gain, gate_o, sg_o, ret_o, sums_o):
    returned = (pick_half(rank, cot0, cot1).astype(f32) * aux[:, LIVE : LIVE + 1]).astype(bf16)
    ret_o[...] = returned
    gate = mm(normed[...], wg[...])
    gate_o[...] = gate
    scaled_grad = mm(returned, out_t[...])
    sg_o[...] = scaled_grad
    gated = ssd[...] * (gate * sigmoid(gate))
    squares = jnp.sum(gated * gated, axis=1, keepdims=True)
    crossed = jnp.sum(scaled_grad * gain[...] * gated, axis=1, keepdims=True)
    lane = lax.broadcasted_iota(jnp.int32, (squares.shape[0], LANES), 1)
    table = jnp.where(lane == 0, squares, jnp.where(lane == 1, crossed, 0.0))
    sums_o[...] = table.T[:8, :]


def norm_kernel(
    rank, gate_r, sg_r, ssd_r, sums_r, out_t, gain, branch_o, scaled_o, dssd_o, dgate_o, gain_o
):
    @pl.when(pl.program_id(0) == 0)
    def _():
        gain_o[...] = jnp.zeros(gain_o.shape, f32)

    gate, ssd, scaled_grad = gate_r[...], ssd_r[...], sg_r[...]
    table = jnp.concatenate([sums_r[...], jnp.zeros((LANES - 8, sums_r.shape[1]), f32)], axis=0)
    sums = table.T
    scale = lax.rsqrt(sums[:, 0:1] / DI + norm_epsilon)
    sig = sigmoid(gate)
    silu = gate * sig
    gated = ssd * silu
    scaled = (gated * scale * gain[...]).astype(bf16)
    scaled_o[...] = scaled
    branch_o[...] = mm(scaled, out_t[...], 1, 1).astype(bf16)
    gain_o[...] += jnp.sum(scaled_grad * gated * scale, axis=0, keepdims=True)
    grad = scale * (scaled_grad * gain[...]) - gated * (scale * scale * scale * (sums[:, 1:2] / DI))
    dssd_o[...] = (grad * silu).astype(bf16)
    dgate_o[...] = (grad * ssd * sig * (1.0 + gate * (1.0 - sig))).astype(bf16)


def scan_back_kernel(
    heads, rank, dssd, mix, pre, ch, ssd, hin, step, conv, skip, hp, aux, segr, heads_of,
    state_in, win_in, carry_in, *rest,
):
    dval_o, dcommon_o, dconv_o, dheads_o, dstate, dtail, carry = rest[-14:-7]
    dmix, dwin, both, flows, entries, weighted, dskip = rest[-7:]
    width = dssd.shape[1]
    channels = width + 2 * N

    @pl.when(pl.program_id(0) == 0)
    def _():
        dwin[CHUNK:, :] = win_in[...]
        dstate[...] = state_in[...]
        carry[...] = carry_in[...]
        dconv_o[...] = jnp.zeros(dconv_o.shape, f32)
        dheads_o[...] = jnp.zeros(dheads_o.shape, f32)
        dskip[...] = jnp.zeros(dskip.shape, f32)

    row, col = iota(0), iota(1)
    left = col < 64
    table = aux[...]
    step_in = step[...]
    dt = softplus(step_in)
    rate = hp[1:2, :]
    tri = (row >= col).astype(f32)
    run = jnp.dot(tri, -(dt * rate), precision=highest, preferred_element_type=f32)
    run_t = run.T
    allowed = (table[:, SEG : SEG + 1] == segr[...]) & (col >= row)
    b_in = mix[:, width : width + N]
    c_out = mix[:, width + N :]
    scores = jnp.where(allowed, mm(b_in, c_out, 1, 1), 0.0)
    ending = run[CHUNK - 1 : CHUNK, :]
    entry = jnp.exp(run) * table[:, INHERIT : INHERIT + 1]
    tail = jnp.exp(ending - run) * table[:, TAIL : TAIL + 1]
    factor = jnp.exp(ending) * table[:, LINKED : LINKED + 1][CHUNK - 1 :, :]
    c_turned = c_out.astype(f32).T.astype(bf16)
    pairs = jnp.zeros((CHUNK, CHUNK), f32)
    state_high, state_low = split(dstate[...])
    flows[...] = mm(b_in, state_high) + mm(b_in, state_low)
    for pair in range(width // LANES):
        lanes = slice(pair * LANES, (pair + 1) * LANES)
        x_pair = mix[:, lanes].astype(f32)
        dy_low = dssd[:, lanes]
        dy = dy_low.astype(f32)
        dt_pair = pair_spread(dt, pair, left)
        tail_pair = pair_spread(tail, pair, left)
        stepped = (x_pair * dt_pair).astype(bf16).astype(f32)
        inner = mm(across(stepped, left), dy_low, 1, 1)
        mixing = []
        for place, head in enumerate((2 * pair, 2 * pair + 1)):
            spread = run_t[head : head + 1, :] - run[:, head : head + 1]
            decays = jnp.exp(jnp.minimum(spread, 0.0))
            mixing.append((decays * scores).astype(bf16))
            pairs = pairs + inner[place * CHUNK : (place + 1) * CHUNK] * decays
        flow = mm(jnp.concatenate(mixing, axis=1), across(dy, left)) + tail_pair * flows[:, lanes]
        dmix[:, lanes] = dt_pair * flow + skip[:, lanes] * dy
        both[0:CHUNK, lanes] = flow * x_pair
        both[CHUNK : 2 * CHUNK, lanes] = dy * (ssd[:, lanes] - skip[:, lanes] * x_pair) - flow * stepped
        dskip[0:1, lanes] += jnp.sum(dy * x_pair, axis=0, keepdims=True)
        high, low = split(pair_spread(entry, pair, left) * dy)
        entries[0, :, lanes] = high
        entries[1, :, lanes] = low
        weighted[:, lanes] = (tail_pair * stepped).astype(bf16)
        dstate[:, lanes] = pair_spread(factor, pair, left) * dstate[:, lanes]
    pairs = jnp.where(allowed, pairs, 0.0)
    dstate[...] += mm(c_turned, entries[0]) + mm(c_turned, entries[1])
    dmix[:, width : width + N] = mm(weighted[...], state_high, 1, 1) + mm_left(pairs, c_out)
    dmix[:, width + N :] = mm(entries[0], hin[0].astype(bf16), 1, 1) + mm_left(pairs, b_in, 0, 0)

    by_head = mm_left(both[...], heads_of[...])
    direct = by_head[0:CHUNK]
    balance = by_head[CHUNK:]
    later = allowed.astype(f32)
    log_grad = jnp.dot(later, balance, precision=highest, preferred_element_type=f32)
    log_grad = log_grad + table[:, NEXT : NEXT + 1] * carry[0:1, :]
    carry[0:1, :] = log_grad[0:1, :]
    step_grad = (direct - rate * log_grad) * sigmoid(step_in)
    dcommon_o[:, 2 * N :] = pltpu.roll(step_grad, heads * rank[0], 1)
    dheads_o[0:1, :] += jnp.sum(step_grad, axis=0, keepdims=True)
    dheads_o[1:2, :] += jnp.sum(-(log_grad * dt * rate), axis=0, keepdims=True)

    for start in range(0, channels, 256):
        cols = slice(start, start + 256)
        value = pre[:, cols]
        sig = sigmoid(value)
        dwin[0:CHUNK, cols] = dmix[:, cols] * (sig * (1.0 + value * (1.0 - sig)))
        here = ch[:, cols]
        own = dwin[0:CHUNK, cols]
        total = conv[3:4, cols] * own
        dconv_o[4:5, cols] += jnp.sum(own, axis=0, keepdims=True)
        dconv_o[3:4, cols] += jnp.sum(own * here, axis=0, keepdims=True)
        for ahead in range(1, 4):
            moved = dwin[ahead : ahead + CHUNK, cols] * table[:, AHEAD + ahead : AHEAD + ahead + 1]
            total = total + conv[3 - ahead : 4 - ahead, cols] * moved
            dconv_o[3 - ahead : 4 - ahead, cols] += jnp.sum(moved * here, axis=0, keepdims=True)
        if start < width:
            dval_o[:, cols] = total.astype(bf16)
        else:
            dcommon_o[:, : 2 * N] = total
    dwin[CHUNK:, :] = dwin[0:8, :]
    dtail[...] = dwin[0:8, :]

    @pl.when(pl.program_id(0) == pl.num_programs(0) - 1)
    def _():
        dheads_o[2:3, :] = mm_left(dskip[...], heads_of[...])[0:1, :]


def scatter_blocks(dp, me, full, keep_o, send_o, cols):
    half = dp // CORES
    block = full.shape[0] // dp
    for place, distance in enumerate(relative_places(dp)):
        start = pl.multiple_of((me[0] ^ distance) * block, block)
        part = full[pl.ds(start, block), :].astype(bf16)
        if place < half:
            keep_o[place, :, cols] = part
        else:
            send_o[place - half, :, cols] = part


def weight_grad_kernel(dp, me, lhs, rhs, keep_o, send_o, turned, full):
    @pl.when(pl.program_id(0) == 0)
    def _():
        turned[...] = lhs[...].T

    full[...] = mm(turned[...], rhs[...])
    scatter_blocks(dp, me, full, keep_o, send_o, slice(None))


def weight_grad(lhs, rhs, dp, dp_rank, skipped=0):
    length, width = rhs.shape[0], rhs.shape[1] - 256 * skipped
    depth = lhs.shape[1]
    block, half = depth // dp, dp // CORES
    piece = pl.BlockSpec((half, block, 256), lambda i, *s: (0, 0, i))
    return call(
        functools.partial(weight_grad_kernel, dp),
        (width // 256,),
        [whole((length, depth)), pl.BlockSpec((length, 256), lambda i, *s: (0, i + skipped))],
        [piece, piece],
        [shape(half, block, width, dtype=bf16)] * 2,
        [pltpu.VMEM((depth, length), bf16), pltpu.VMEM((depth, 256), f32)],
        2 * length * width * depth,
        10,
        scalars=1,
    )(dp_rank, lhs, rhs)


def value_grad_kernel(dp, me, lhs, dval, dcommon, keep_o, send_o, turned, full, wide):
    step = pl.program_id(0)
    last = pl.num_programs(0) - 1

    @pl.when(step == 0)
    def _():
        turned[...] = lhs[...].T

    @pl.when(step < last)
    def _():
        full[...] = mm(turned[...], dval[...])
        cols = pl.ds(pl.multiple_of(step * 256, 256), 256)
        scatter_blocks(dp, me, full, keep_o, send_o, cols)

    @pl.when(step == last)
    def _():
        wide[...] = mm_right(turned[...], dcommon[...])
        cols = slice(keep_o.shape[2] - wide.shape[1], keep_o.shape[2])
        scatter_blocks(dp, me, wide, keep_o, send_o, cols)


def value_grad(lhs, dval, dcommon, dp, dp_rank):
    length, width = dval.shape[0], 256
    depth, extra = lhs.shape[1], dcommon.shape[1]
    block, half, per = depth // dp, dp // CORES, width // 256
    dims = (half, block, width + extra)
    return call(
        functools.partial(value_grad_kernel, dp),
        (per + 1,),
        [
            whole((length, depth)),
            pl.BlockSpec((length, 256), lambda i, *s: (0, jnp.minimum(i, per - 1))),
            whole((length, extra)),
        ],
        [result(dims), result(dims)],
        [shape(*dims, dtype=bf16)] * 2,
        [
            pltpu.VMEM((depth, length), bf16), pltpu.VMEM((depth, 256), f32),
            pltpu.VMEM((depth, extra), f32),
        ],
        2 * length * (width + 2 * extra) * depth,
        15,
        scalars=1,
    )(dp_rank, lhs, dval, dcommon)


def input_grad_kernel(rank, dgate, dval, dcommon, tok, wg, wv, shw, ng_o, gain_o):
    @pl.when(pl.program_id(0) == 0)
    def _():
        gain_o[...] = jnp.zeros(gain_o.shape, f32)

    grad = mm(dgate[...], wg[...], 1, 1) + mm(dval[...], wv[...], 1, 1)
    grad = grad + mm_left(dcommon[...], shw[...], 1, 1)
    x = tok[...].astype(f32)
    inverse = lax.rsqrt(jnp.mean(x * x, axis=1, keepdims=True) + norm_epsilon)
    gain_o[...] += jnp.sum(grad * (x * inverse), axis=0, keepdims=True)
    ng_o[...] = grad.astype(ng_o.dtype)


def shards(
    dp, nt,
    residual, cotangent, sequence_ids,
    inner_proj, inner_mean, inner_square,
    shared_proj, shared_mean, shared_square,
    outer_proj, outer_mean, outer_square,
    conv_params, conv_mean, conv_square,
    norm_gains, gains_mean, gains_square,
    head_params, heads_mean, heads_square,
):
    t_rank = lax.axis_index("tensor").astype(jnp.int32)
    d_rank = lax.axis_index("dp").astype(jnp.int32)
    dp_me = d_rank[None]
    t_me = t_rank[None]
    rows_here = residual.shape[0]
    length = rows_here * nt
    width = inner_proj.shape[2]
    heads_here = head_params.shape[1]
    head_size = width // heads_here
    channels = width + 2 * N
    chunks = length // CHUNK
    wide = 2 * CHUNK
    band = min(2 * CHUNK, rows_here)
    per_piece = rows_here // band

    def pieces_of(value):
        return [value] + [swap(value, "tensor", nt, d) for d in range(1, nt)]

    def over_tensor(value, pieces=None):
        pieces = pieces_of(value) if pieces is None else pieces
        if nt == 2:
            first = jnp.concatenate(pieces, axis=0)
            second = jnp.concatenate(pieces[::-1], axis=0)
            return jnp.where(t_rank == 0, first, second)
        stacked = jnp.take(jnp.stack(pieces), jnp.arange(nt) ^ t_rank, axis=0)
        return stacked.reshape((nt * stacked.shape[1],) + stacked.shape[2:])

    kernel_rows, columns = conv_params.shape
    gain_count = norm_gains.shape[0]
    shared_size = shared_proj.size
    exact = jnp.concatenate([conv_params.reshape(-1), norm_gains])
    terms = []
    rest = exact
    for _ in range(3):
        term = lax.optimization_barrier(rest.astype(bf16))
        terms.append(term)
        rest = rest - term.astype(f32)
    common_width = 2 * N + LANES
    shared_rows = shared_proj.shape[0]
    packed = width == 1024 and shared_rows == 32
    if packed:
        wide_shared = jnp.pad(shared_proj.astype(bf16), ((0, 0), (0, common_width - 2 * N - H)))
        flat = jnp.concatenate(terms)
        flat = jnp.pad(flat, (0, 16 * 256 - flat.size)).reshape(16, 256)
        small = jnp.concatenate([wide_shared[:16], wide_shared[16:], flat], axis=1)
        small_rows = 16
    else:
        small = jnp.concatenate([shared_proj.astype(bf16).reshape(-1)] + terms)
        small_rows = -(-small.size // width)
        while small_rows * nt % 16:
            small_rows += 1
        small = jnp.pad(small, (0, small_rows * width - small.size)).reshape(small_rows, width)
    small_pair = over_tensor(small)
    token_pieces = pieces_of(residual)

    block_rows = D // dp
    value_shard = jnp.concatenate([inner_proj[1].astype(bf16), small_pair], axis=0)
    cut = -(-value_shard.shape[0] // 32) * 16
    first_line = gather_line(value_shard[:cut], dp)
    second_shard, first_line = tie(value_shard[cut:], first_line)
    second_line = gather_line(second_shard, dp)
    second_line, ids = tie(second_line, sequence_ids)
    first_near = jnp.concatenate([first_line] + plane_parts(first_line, dp), axis=0)
    other_shard = jnp.concatenate(
        [inner_proj[0].astype(bf16), outer_proj.T.astype(bf16)], axis=0
    )
    other_shard, second_line = tie(other_shard, second_line)
    other_line = gather_line(other_shard, dp)
    second_line, *parts = tie(second_line, *plane_parts(second_line, dp), *token_pieces)
    parts, token_pieces = parts[:-nt], parts[-nt:]
    second_near = jnp.concatenate([second_line] + parts, axis=0)
    cotangent_now, *token_pieces = tie(cotangent, *token_pieces)
    cot_pieces = pieces_of(cotangent_now)
    first_far, second_far = swap(first_near, "dp", dp, 1), swap(second_near, "dp", dp, 1)
    full = slice(None)
    moves = [(0, block_rows, full, 0, 1, 0, 0)]
    dims = [(dp, block_rows, width)]
    if packed:
        for t in range(nt):
            at = (block_rows + 16 * t, block_rows + 16 * t + 16)
            moves.append(at + (slice(0, common_width), 1, nt, t, 0))
            moves.append(at + (slice(common_width, 2 * common_width), 1, nt, t, 16))
            moves.append(at + (slice(2 * common_width, width), 2, nt, t, 0))
        dims += [(dp * nt, 32, common_width), (dp * nt, 16, 256)]
    else:
        moves.append((block_rows, block_rows + small_rows * nt, full, 1, 1, 0, 0))
        dims += [(dp, small_rows * nt, width)]
    value_w, *small_all = assemble(
        [first_near, second_near], [first_far, second_far], dp, dp_me, moves, dims
    )
    value_w = value_w.reshape(D, width)

    def halves(pieces):
        if nt == 2:
            return t_me, pieces[0], pieces[1]
        all_rows = over_tensor(None, pieces)
        return jnp.zeros((1,), jnp.int32), all_rows[: length // 2], all_rows[length // 2 :]

    if packed:
        shared_here = small_all[0].reshape(D, common_width)
        exact_all = small_all[1].reshape(dp * nt, -1)[:, : 3 * exact.size].astype(f32)
    else:
        small_all = small_all[0].reshape(dp * nt, small_rows * width)
        shared_here = small_all[:, :shared_size].reshape(D, -1)
        shared_here = jnp.pad(shared_here, ((0, 0), (0, common_width - 2 * N - H)))
        exact_all = small_all[:, shared_size : shared_size + 3 * exact.size].astype(f32)
    exact_all = exact_all.reshape(dp * nt, 3, exact.size)
    exact_all = (exact_all[:, 0] + exact_all[:, 1]) + exact_all[:, 2]
    conv_full = (
        exact_all[:, : kernel_rows * columns]
        .reshape(dp * nt, kernel_rows, columns)
        .transpose(1, 0, 2)
        .reshape(kernel_rows, -1)
    )
    gains_full = exact_all[:, kernel_rows * columns :].reshape(-1)

    pre_gain = gains_full[:D].reshape(1, D)
    post_gain = lax.dynamic_slice_in_dim(gains_full, D + t_rank * width, width).reshape(1, width)
    conv_here = jnp.concatenate(
        [lax.dynamic_slice_in_dim(conv_full, t_rank * width, width, 1), conv_full[:, DI:]], axis=1
    )
    conv_here = jnp.pad(conv_here, ((0, 8 - kernel_rows), (0, 0)))
    head_rows = jnp.stack([head_params[0], jnp.exp(head_params[1])])
    head_rows = jnp.pad(head_rows, ((0, 6), (0, LANES - heads_here)))
    skip = jnp.repeat(head_params[2], head_size).reshape(1, width)
    heads_of = (
        jnp.arange(width)[:, None] // head_size == jnp.arange(LANES)[None, :]
    ).astype(bf16)

    blocked = ids.reshape(chunks, CHUNK)
    ends, firsts = blocked[:, -1], blocked[:, 0]
    none = jnp.full((1,), -1, jnp.int32)
    before = jnp.concatenate([none, ends[:-1]])
    following = jnp.concatenate([firsts[1:], none])
    fills = [jnp.full((o,), -1, jnp.int32) for o in range(1, 4)]
    marks = [ids]
    marks += [jnp.concatenate([fills[o - 1], ids[:-o]]) == ids for o in range(1, 4)]
    marks += [jnp.concatenate([ids[o:], fills[o - 1]]) == ids for o in range(1, 4)]
    marks += [
        (blocked == before[:, None]).reshape(-1),
        (blocked == ends[:, None]).reshape(-1),
        jnp.broadcast_to((ends == before)[:, None], blocked.shape).reshape(-1),
        (blocked == following[:, None]).reshape(-1),
        ids < SEQ_SLOTS,
    ]
    aux = jnp.stack([m.astype(f32) for m in marks] + [jnp.zeros((length,), f32)] * 4, axis=1)
    segr = ids.astype(f32).reshape(1, length)
    aux_cols = aux.shape[1]

    steps = length // wide
    in_half = lambda i: i % (steps // 2)
    value_w, other_line, *cot_pieces = tie(value_w, other_line, *cot_pieces)
    plane = plane_parts(other_line, dp)
    tok_rank, tok0, tok1 = halves(token_pieces)
    normed, chans, pre, mixed, ssd, entering, step_in = call(
        functools.partial(scan_kernel, heads_here),
        (steps,),
        [
            rows(wide, D, in_half), rows(wide, D, in_half), whole((1, D)), whole((D, width)),
            whole((D, common_width)), whole((8, channels)), whole((1, width)), whole((8, LANES)),
            rows(wide, aux_cols), pl.BlockSpec((1, wide), lambda i, r: (0, i)),
        ],
        [
            rows(wide, D), rows(wide, channels), rows(wide, channels), rows(wide, channels),
            rows(wide, width), pl.BlockSpec((wide // CHUNK, N, width), lambda i, r: (i, 0, 0)),
            rows(wide, LANES),
        ],
        [
            shape(length, D, dtype=bf16), shape(length, channels), shape(length, channels),
            shape(length, channels, dtype=bf16), shape(length, width),
            shape(chunks, N, width), shape(length, LANES),
        ],
        [
            pltpu.VMEM((wide + 8, channels), f32), pltpu.VMEM((N, width), f32),
            pltpu.VMEM((CHUNK, width), f32), pltpu.VMEM((2, CHUNK, width), bf16),
        ],
        length * (2 * D * (width + common_width) + 12 * width * CHUNK),
        22,
        scalars=1,
    )(jnp.concatenate([tok_rank, t_me]), tok0, tok1, pre_gain, value_w, shared_here, conv_here, skip, head_rows, aux, segr)

    normed, *plane = tie(normed, *plane)
    plane = jnp.concatenate([other_line] + plane, axis=0)
    moves = [
        (0, block_rows, full, 0, 1, 0, 0), (block_rows, 2 * block_rows, full, 1, 1, 0, 0)
    ]
    gate_w, outer_t = assemble(
        [plane], [swap(plane, "dp", dp, 1)], dp, dp_me, moves, [(dp, block_rows, width)] * 2
    )
    gate_w, outer_t = gate_w.reshape(D, width), outer_t.reshape(D, width)
    cot_rank, cot0, cot1 = halves(cot_pieces)
    gate, scaled_grad, returned, sums = call(
        gate_kernel,
        (steps,),
        [
            rows(wide, D), rows(wide, D, in_half), rows(wide, D, in_half), rows(wide, aux_cols),
            rows(wide, width), whole((D, width)), whole((D, width)), whole((1, width)),
        ],
        [rows(wide, width), rows(wide, width), rows(wide, D), pl.BlockSpec((8, wide), lambda i, r: (0, i))],
        [
            shape(length, width), shape(length, width), shape(length, D, dtype=bf16),
            shape(8, length),
        ],
        [],
        4 * length * D * width,
        15,
        scalars=1,
    )(cot_rank, normed, cot0, cot1, aux, ssd, gate_w, outer_t, post_gain)
    distance = 1
    while distance < nt:
        sums = sums + swap(sums, "tensor", nt, distance)
        distance *= 2

    def relative(block, rank):
        return (rank ^ (block // per_piece)) * per_piece + block % per_piece

    def rel_rows(width_here, offset=0):
        return pl.BlockSpec((band, width_here), lambda i, r: (relative(i + offset, r[0]), 0))

    plain = lambda width_here: pl.BlockSpec((band, width_here), lambda i, r: (i, 0))
    branch, scaled, dssd, dgate, post_grad = call(
        norm_kernel,
        (length // band,),
        [
            rel_rows(width), rel_rows(width), rel_rows(width),
            pl.BlockSpec((8, band), lambda i, r: (0, relative(i, r[0]))),
            whole((D, width)), whole((1, width)),
        ],
        [plain(D), rel_rows(width), rel_rows(width), rel_rows(width), result((1, width))],
        [
            shape(length, D, dtype=bf16), shape(length, width, dtype=bf16),
            shape(length, width, dtype=bf16), shape(length, width, dtype=bf16), shape(1, width),
        ],
        [],
        2 * length * D * width,
        15,
        scalars=1,
    )(t_me, gate, scaled_grad, ssd, sums, outer_t, post_gain)
    outer_keep, outer_send = weight_grad(returned, scaled, dp, dp_me)
    dgate, outer_send = tie(dgate, outer_send)
    gate_keep, gate_send = weight_grad(normed, dgate, dp, dp_me)
    outer_line, outer_rest = start_sum(outer_keep, outer_send, dp)
    gate_line, gate_rest = start_sum(gate_keep, gate_send, dp)
    branch = branch.reshape(nt, rows_here, D)
    branch_received = [swap(branch[d], "tensor", nt, d) for d in range(1, nt)]
    dssd, *rests = tie(dssd, *outer_rest, *gate_rest)
    outer_rest, gate_rest = rests[: len(outer_rest)], rests[len(outer_rest) :]
    outer_received = middle_swaps(outer_rest, dp)
    gate_received = middle_swaps(gate_rest, dp)

    state = jnp.zeros((N, width), f32)
    win = jnp.zeros((8, channels), f32)
    carry = jnp.zeros((8, LANES), f32)
    back_parts = []
    filled = []
    top = chunks
    for part, count in enumerate((3, 3, chunks - 6)):
        back = lambda i, top=top: top - 1 - i
        top -= count
        *results, state, win, carry = call(
            functools.partial(scan_back_kernel, heads_here),
            (count,),
            [
                rows(CHUNK, width, back), rows(CHUNK, channels, back), rows(CHUNK, channels, back),
                rows(CHUNK, channels, back), rows(CHUNK, width, back),
                pl.BlockSpec((1, N, width), lambda i, r, back=back: (back(i), 0, 0)),
                rows(CHUNK, LANES, back), whole((8, channels)), whole((1, width)),
                whole((8, LANES)), rows(CHUNK, aux_cols, back),
                pl.BlockSpec((1, CHUNK), lambda i, r, back=back: (0, back(i))),
                whole((width, LANES)),
                whole((N, width)), whole((8, channels)), whole((8, LANES)),
            ]
            + [pl.BlockSpec(memory_space=pl.ANY)] * len(filled),
            [
                rows(CHUNK, width, back), rows(CHUNK, common_width, back), result((8, channels)),
                result((8, LANES)),
                result((N, width)), result((8, channels)), result((8, LANES)),
            ],
            [
                shape(length, width, dtype=bf16), shape(length, common_width),
                shape(8, channels), shape(8, LANES),
                shape(N, width), shape(8, channels), shape(8, LANES),
            ],
            [
                pltpu.VMEM((CHUNK, channels), f32), pltpu.VMEM((CHUNK + 8, channels), f32),
                pltpu.VMEM((2 * CHUNK, width), f32), pltpu.VMEM((CHUNK, width), f32),
                pltpu.VMEM((2, CHUNK, width), bf16), pltpu.VMEM((CHUNK, width), bf16),
                pltpu.VMEM((8, width), f32),
            ],
            count * CHUNK * 30 * width * CHUNK,
            14,
            scalars=1,
            aliases={17: 0, 18: 1} if filled else None,
        )(
            t_me, dssd, mixed, pre, chans, ssd, entering, step_in, conv_here, skip, head_rows, aux, segr,
            heads_of, state, win, carry, *filled,
        )
        filled = results[:2]
        back_parts.append(results[2:])
        if part == 0:
            state, outer_line, *outer_received = tie(state, outer_line, *outer_received)
            outer_block, outer_far = middle_sum(outer_line, outer_received)
            outer_far = high_swaps(outer_far, dp)
        if part == 1:
            state, gate_line, *rests = tie(
                state, gate_line, *branch_received, *gate_received, *outer_far
            )
            branch_received = rests[: nt - 1]
            gate_received, outer_far = rests[nt - 1 : -len(outer_far)], rests[-len(outer_far) :]
            gate_block, gate_far = middle_sum(gate_line, gate_received)
            gate_far = high_swaps(gate_far, dp)
    dval, dcommon = filled
    dval, *gate_far = tie(dval, *gate_far)
    outer_part = high_sum(outer_block, outer_far)
    gate_part = high_sum(gate_block, gate_far)

    branch_sum = branch[0].astype(f32)
    for piece in branch_received:
        branch_sum = branch_sum + piece.astype(f32)
    live_here = lax.dynamic_slice_in_dim(aux[:, LIVE], t_rank * rows_here, rows_here)
    tokens = residual.astype(f32)
    block_out = (tokens + branch_sum * live_here[:, None]).astype(bf16)

    def input_grad(count, offset, dtype, positions, dgate):
        return call(
            input_grad_kernel,
            (count * per_piece,),
            [
                rel_rows(width, offset), rel_rows(width, offset), rel_rows(common_width, offset),
                plain(D), whole((D, width)), whole((D, width)), whole((D, common_width)),
            ],
            [plain(D), result((1, D))],
            [shape(count * rows_here, D, dtype=dtype), shape(1, D)],
            [],
            4 * count * rows_here * D * (width + common_width),
            13,
            scalars=1,
        )(t_me, dgate, dval, dcommon, positions, gate_w, value_w, shared_here)

    keep, send = value_grad(normed, dval, dcommon, dp, dp_me)
    line, part = start_sum(keep, send, dp)
    two = width > 256
    lines, parts = [line], [part]
    if two:
        dval, *parts[0] = tie(dval, *parts[0])
        keep, send = weight_grad(normed, dval, dp, dp_me, skipped=1)
        line, part = start_sum(keep, send, dp)
        lines.append(line)
        parts.append(part)
    each = len(part)
    dgate, *flat = tie(dgate, *[item for part in parts for item in part])
    crossing = [middle_swaps(flat[at : at + each], dp) for at in range(0, len(flat), each)]
    others = token_pieces[1] if nt == 2 else jnp.concatenate(token_pieces[1:], axis=0)
    sent, pre_grad_sent = input_grad(nt - 1, per_piece, bf16, others, dgate)
    sent = sent.reshape(nt - 1, rows_here, D)
    received = [swap(sent[d - 1], "tensor", nt, d) for d in range(1, nt)]
    small_grads = [item for each_part in back_parts for item in each_part]
    dgate, pre_grad_sent, *rests = tie(dgate, pre_grad_sent, *crossing[0], *small_grads)
    crossing[0], small_grads = rests[:each], rests[each:]
    block, far = middle_sum(lines[0], crossing[0])
    blocks, fars = [block], [high_swaps(far, dp)]
    own, pre_grad_own = input_grad(1, 0, f32, residual, dgate)
    if two:
        pre_grad_own, *rests = tie(pre_grad_own, *crossing[1], *fars[0])
        crossing[1], fars[0] = rests[:each], rests[each:]
        block, far = middle_sum(lines[1], crossing[1])
        pre_grad_own, *far = tie(pre_grad_own, *far)
        blocks.append(block)
        fars.append(high_swaps(far, dp))
    dconv, dheads = [sum(small_grads[at::2]) for at in range(2)]
    conv_grad = lax.dynamic_update_slice(
        jnp.pad(dconv[:kernel_rows, width:], ((0, 0), (DI, 0))),
        dconv[:kernel_rows, :width],
        (0, t_rank * width),
    )
    post_all = lax.dynamic_update_slice(
        jnp.zeros((1, DI), f32), post_grad, (0, t_rank * width)
    )
    head_grad = dheads[:3, :heads_here]
    head_all = lax.dynamic_update_slice(
        jnp.zeros((3, H), f32), head_grad, (0, t_rank * heads_here)
    )
    vector = jnp.concatenate(
        [
            conv_grad.reshape(1, -1), pre_grad_sent + pre_grad_own, post_all, head_all.reshape(1, -1),
        ],
        axis=1,
    )
    for stage, (axis, size, distance) in enumerate(sum_stages(dp, nt)):
        vector = vector + swap(vector, axis, size, distance)
        if stage == 0:
            value_sums = [high_sum(blocks[0], fars[0])]
        if stage == 1:
            vector, *received = tie(vector, *received)
        if stage == 1 and two:
            vector, *fars[1] = tie(vector, *fars[1])
            value_sums.append(high_sum(blocks[1], fars[1]))
    shared_sum = value_sums[0][:, 256:].reshape(nt, shared_rows, common_width)
    shared_mine = lax.dynamic_index_in_dim(shared_sum, t_rank, 0, False)
    for d in range(1, nt):
        piece = lax.dynamic_index_in_dim(shared_sum, t_rank ^ d, 0, False)
        shared_mine = shared_mine + swap(piece, "tensor", nt, d)
    shared_part = shared_mine[:, : 2 * N + H]
    value_part = jnp.concatenate([value_sums[0][:, :256]] + value_sums[1:], axis=1)
    conv_size = kernel_rows * (DI + 2 * N)
    place = d_rank * nt + t_rank
    conv_part = lax.dynamic_slice_in_dim(
        vector[0, :conv_size].reshape(kernel_rows, -1), place * columns, columns, 1
    )
    gains_part = lax.dynamic_slice_in_dim(vector[0], conv_size + place * gain_count, gain_count)
    heads_part = lax.dynamic_slice_in_dim(
        vector[0, conv_size + D + DI :].reshape(3, H), t_rank * heads_here, heads_here, 1
    )

    normed_grad = own
    for piece in received:
        normed_grad = normed_grad + piece.astype(f32)
    inverse = lax.rsqrt(jnp.mean(tokens * tokens, axis=1, keepdims=True) + norm_epsilon)
    normal_tokens = tokens * inverse
    normal_grad = normed_grad * pre_gain
    centered = normal_grad - normal_tokens * jnp.mean(
        normal_grad * normal_tokens, axis=1, keepdims=True
    )
    residual_grad = (cotangent.astype(f32) + inverse * centered).astype(bf16)

    inner_new = adam_step(
        inner_proj, inner_mean, inner_square, jnp.stack([gate_part, value_part]),
        rate_matrix, weight_decay,
    )
    shared_new = adam_step(
        shared_proj, shared_mean, shared_square, shared_part.reshape(shared_proj.shape),
        rate_matrix, weight_decay,
    )
    outer_new = adam_step(
        outer_proj, outer_mean, outer_square, outer_part.T, rate_matrix, weight_decay
    )
    conv_new = adam_step(conv_params, conv_mean, conv_square, conv_part, rate_vector, 0.0)
    gains_new = adam_step(norm_gains, gains_mean, gains_square, gains_part, rate_vector, 0.0)
    heads_new = adam_step(head_params, heads_mean, heads_square, heads_part, rate_heads, 0.0)
    return (
        (block_out, residual_grad)
        + inner_new + shared_new + outer_new + conv_new + gains_new + heads_new
    )


def solution(mesh):
    return jax.shard_map(
        functools.partial(shards, mesh.shape["dp"], mesh.shape["tensor"]),
        mesh=mesh,
        in_specs=(
            P(("dp", "tensor"), None),
            P(("dp", "tensor"), None),
            P("dp"),
            P(None, "dp", "tensor"),
            P(None, "dp", "tensor"),
            P(None, "dp", "tensor"),
            P(("dp", "tensor"), None),
            P(("dp", "tensor"), None),
            P(("dp", "tensor"), None),
            P("tensor", "dp"),
            P("tensor", "dp"),
            P("tensor", "dp"),
            P(None, ("dp", "tensor")),
            P(None, ("dp", "tensor")),
            P(None, ("dp", "tensor")),
            P(("dp", "tensor")),
            P(("dp", "tensor")),
            P(("dp", "tensor")),
            P(None, "tensor"),
            P(None, "tensor"),
            P(None, "tensor"),
        ),
        out_specs=(
            P(("dp", "tensor"), None),
            P(("dp", "tensor"), None),
            P(None, "dp", "tensor"),
            P(None, "dp", "tensor"),
            P(None, "dp", "tensor"),
            P(("dp", "tensor"), None),
            P(("dp", "tensor"), None),
            P(("dp", "tensor"), None),
            P("tensor", "dp"),
            P("tensor", "dp"),
            P("tensor", "dp"),
            P(None, ("dp", "tensor")),
            P(None, ("dp", "tensor")),
            P(None, ("dp", "tensor")),
            P(("dp", "tensor")),
            P(("dp", "tensor")),
            P(("dp", "tensor")),
            P(None, "tensor"),
            P(None, "tensor"),
            P(None, "tensor"),
        ),
        check_vma=False,
    )
```

```python
import functools

import jax
import jax.numpy as jnp
from jax import lax
from jax.experimental import pallas as pl
from jax.experimental.pallas import tpu as pltpu
from jax.sharding import PartitionSpec as P

D = 1024
H = 32
N = 128
DI = 2048
SEQ_SLOTS = 4
STEP = 10
CHUNK = 128
LANES = 128
CORES = 2
HIGH_AXIS = 4

highest = lax.Precision.HIGHEST
f32 = jnp.float32
bf16 = jnp.bfloat16
norm_epsilon = 1e-05
beta_first = 0.9
beta_second = 0.95
adam_epsilon = 1e-08
weight_decay = 0.1
rate_matrix = 0.02
rate_vector = 0.3
rate_heads = 1.0

SEG, BACK, AHEAD, INHERIT, TAIL, LINKED, NEXT, LIVE = 0, 0, 3, 7, 8, 9, 10, 11


def adam_step(weight, moment, square, gradient, rate, decay):
    moment_next = beta_first * moment + (1.0 - beta_first) * gradient
    square_next = beta_second * square + (1.0 - beta_second) * gradient * gradient
    moment_hat = moment_next / (1.0 - beta_first**STEP)
    square_hat = square_next / (1.0 - beta_second**STEP)
    weight_next = weight - rate * (
        moment_hat / (jnp.sqrt(square_hat) + adam_epsilon) + decay * weight
    )
    return (weight_next, moment_next, square_next)


def swap(value, axis, size, distance):
    return lax.ppermute(value, axis, [(i, i ^ distance) for i in range(size)])


def tie(*values):
    return lax.optimization_barrier(values)


def axis_parts(dp):
    high = HIGH_AXIS
    middle = dp // (CORES * high)
    return high, middle


def gather_line(shard, dp):
    high, middle = axis_parts(dp)
    pieces = [shard[None]]
    for step in range(1, high):
        pieces.append(swap(shard, "dp", dp, step * middle * CORES)[None])
    return jnp.concatenate(pieces, axis=0)


def plane_parts(line, dp):
    return [swap(line, "dp", dp, step * CORES) for step in range(1, axis_parts(dp)[1])]


def start_sum(keep, send, dp):
    high, middle = axis_parts(dp)
    other = swap(send, "dp", dp, 1)
    parts = [slice(step * high, (step + 1) * high) for step in range(middle)]
    line = keep[parts[0]].astype(f32) + other[parts[0]].astype(f32)
    rest = [(keep[at].astype(f32) + other[at].astype(f32)).astype(bf16) for at in parts[1:]]
    return line, rest


def middle_swaps(rest, dp):
    return [swap(part, "dp", dp, (step + 1) * CORES) for step, part in enumerate(rest)]


def middle_sum(line, received):
    for part in received:
        line = line + part.astype(f32)
    return line[0], [part.astype(bf16) for part in line[1:]]


def high_swaps(rest, dp):
    middle = axis_parts(dp)[1]
    return [swap(part, "dp", dp, (step + 1) * middle * CORES) for step, part in enumerate(rest)]


def high_sum(block, received):
    for part in received:
        block = block + part.astype(f32)
    return block


def sum_stages(dp, nt):
    stages = [("tensor", nt, 1 << bit) for bit in range((nt - 1).bit_length())]
    return stages + [("dp", dp, 1 << bit) for bit in range((dp - 1).bit_length())]


def relative_places(dp):
    high, middle = axis_parts(dp)
    return [
        (h * middle + m) * CORES + c for c in range(CORES) for m in range(middle) for h in range(high)
    ]


def call(kernel, grid, in_specs, out_specs, out_shape, scratch, flops, mib, scalars=0, aliases=None):
    params = pltpu.CompilerParams(vmem_limit_bytes=mib * 1024 * 1024)
    moved = sum(2 * s.dtype.itemsize * s.size for s in jax.tree.leaves(out_shape))
    return pl.pallas_call(
        kernel,
        grid_spec=pltpu.PrefetchScalarGridSpec(
            num_scalar_prefetch=scalars,
            grid=grid,
            in_specs=in_specs,
            out_specs=out_specs,
            scratch_shapes=scratch,
        ),
        out_shape=out_shape,
        compiler_params=params,
        input_output_aliases=aliases or {},
        cost_estimate=pl.CostEstimate(
            flops=int(flops) // 16, bytes_accessed=int(moved) // 16, transcendentals=0
        ),
    )


def whole(shape):
    return pl.BlockSpec(shape, lambda *i: (0,) * len(shape), pipeline_mode=pl.Buffered(1))


def result(shape):
    return pl.BlockSpec(shape, lambda *i: (0,) * len(shape))


def rows(count, width, index=lambda i: i):
    return pl.BlockSpec((count, width), lambda i, *s: (index(i), 0))


def shape(*dims, dtype=f32):
    return jax.ShapeDtypeStruct(dims, dtype)


def split(value):
    high = value.astype(bf16)
    return high, (value - high.astype(f32)).astype(bf16)


def mm(a, b, ca=1, cb=0):
    return lax.dot_general(a, b, (((ca,), (cb,)), ((), ())), preferred_element_type=f32)


def mm_left(value, exact, ca=1, cb=0):
    high, low = split(value)
    return mm(high, exact, ca, cb) + mm(low, exact, ca, cb)


def mm_right(exact, value, ca=1, cb=0):
    high, low = split(value)
    return mm(exact, high, ca, cb) + mm(exact, low, ca, cb)


def mm_both(a, b, ca=1, cb=0):
    a_high, a_low = split(a)
    b_high, b_low = split(b)
    return mm(a_high, b_high, ca, cb) + mm(a_low, b_high, ca, cb) + mm(a_high, b_low, ca, cb)


def sigmoid(value):
    return 0.5 * jnp.tanh(0.5 * value) + 0.5


def softplus(value):
    return jnp.maximum(value, 0.0) + jnp.log1p(jnp.exp(-jnp.abs(value)))


def iota(axis):
    return lax.broadcasted_iota(jnp.int32, (CHUNK, LANES), axis)


def pair_spread(tile, pair, left):
    rows_here = tile.shape[0]
    return jnp.where(
        left[:rows_here],
        jnp.broadcast_to(tile[:, 2 * pair : 2 * pair + 1], (rows_here, LANES)),
        jnp.broadcast_to(tile[:, 2 * pair + 1 : 2 * pair + 2], (rows_here, LANES)),
    )


def assemble_kernel(dp, parts, moves, me, *refs):
    high, middle = axis_parts(dp)
    each = CORES * middle
    sources, outs = refs[: parts * each], refs[parts * each :]
    for place, distance in enumerate(relative_places(dp)):
        block = me[0] ^ distance
        base = 0
        for part in range(parts):
            source, at = sources[part * each + place // high], place % high
            end = base + source.shape[1]
            for first, last, lanes, out, count, extra, row in moves:
                low, top = max(base, first), min(end, last)
                if low < top:
                    outs[out][
                        block * count + extra, row + low - first : row + top - first, :
                    ] = source[at, low - base : top - base, lanes]
            base = end


def assemble(parts, dp, dp_rank, moves, shapes):
    vmem = pl.BlockSpec(memory_space=pltpu.VMEM)
    lines = [line for part in parts for line in part]
    moved = sum(2 * line.size * line.dtype.itemsize for line in lines)
    return pl.pallas_call(
        functools.partial(assemble_kernel, dp, len(parts), moves),
        in_specs=[pl.BlockSpec(memory_space=pltpu.SMEM)] + [vmem] * len(lines),
        out_specs=[vmem] * len(shapes),
        out_shape=[shape(*dims, dtype=bf16) for dims in shapes],
        compiler_params=pltpu.CompilerParams(vmem_limit_bytes=16 * 1024 * 1024),
        cost_estimate=pl.CostEstimate(flops=0, bytes_accessed=moved, transcendentals=0),
    )(dp_rank, *lines)


def pick_half(rank, first, second):
    half = (2 * pl.program_id(0)) // pl.num_programs(0)
    own = (half == rank[0]).astype(jnp.int32)
    return jnp.where(jnp.broadcast_to(own, first.shape) == 1, first[...], second[...])


def across(pair, left):
    return jnp.concatenate(
        [jnp.where(left, pair, 0.0), jnp.where(left, 0.0, pair)], axis=0
    ).astype(bf16)


def scan_kernel(
    heads, rank, tok0, tok1, gain, wv, shw, conv, skip, hp, aux, segr,
    normed_o, ch_o, pre_o, mix_o, ssd_o, hin_o, step_o,
    win, state, carried, weighted,
):
    count = tok0.shape[0]
    width = wv.shape[1]
    channels = width + 2 * N

    @pl.when(pl.program_id(0) == 0)
    def _():
        win[0:8, :] = jnp.zeros((8, channels), f32)
        state[...] = jnp.zeros(state.shape, f32)

    x = pick_half(rank, tok0, tok1).astype(f32)
    inverse = lax.rsqrt(jnp.mean(x * x, axis=1, keepdims=True) + norm_epsilon)
    normed = (x * inverse * gain[...]).astype(bf16)
    normed_o[...] = normed
    win[8 : 8 + count, :width] = mm(normed, wv[...])
    common = mm(normed, shw[...])
    win[8 : 8 + count, width:] = common[:, : 2 * N]
    turn = lax.rem(LANES - heads * rank[1], LANES)
    step_o[...] = pltpu.roll(common[:, 2 * N :], turn, 1) + hp[0:1, :]
    table = aux[...]
    for start in range(0, channels, 256):
        cols = slice(start, start + 256)
        here = win[8 : 8 + count, cols]
        pre = conv[4:5, cols] + conv[3:4, cols] * here
        for back in range(1, 4):
            pre = pre + conv[3 - back : 4 - back, cols] * (
                win[8 - back : 8 - back + count, cols] * table[:, BACK + back : BACK + back + 1]
            )
        ch_o[:, cols] = here
        pre_o[:, cols] = pre
        mix_o[:, cols] = (pre * sigmoid(pre)).astype(bf16)
    win[0:8, :] = win[count : count + 8, :]

    row, col = iota(0), iota(1)
    left = col < 64
    tri = (row >= col).astype(f32)
    for sub in range(count // CHUNK):
        at = slice(sub * CHUNK, (sub + 1) * CHUNK)
        dt = softplus(step_o[at, :])
        run = jnp.dot(tri, -(dt * hp[1:2, :]), precision=highest, preferred_element_type=f32)
        run_t = run.T
        allowed = (table[at, SEG : SEG + 1] == segr[:, at]) & (row >= col)
        b_in = mix_o[at, width : width + N]
        b_turned = b_in.astype(f32).T.astype(bf16)
        c_out = mix_o[at, width + N :]
        scores = jnp.where(allowed, mm(c_out, b_in, 1, 1), 0.0)
        ending = run[CHUNK - 1 : CHUNK, :]
        entry = jnp.exp(run) * table[at, INHERIT : INHERIT + 1]
        tail = jnp.exp(ending - run) * table[at, TAIL : TAIL + 1]
        factor = jnp.exp(ending) * table[at, LINKED : LINKED + 1][CHUNK - 1 :, :]
        hin_o[sub] = state[...]
        carried[...] = mm_right(c_out, state[...])
        for pair in range(width // LANES):
            lanes = slice(pair * LANES, (pair + 1) * LANES)
            x_pair = mix_o[at, lanes].astype(f32)
            stepped = (x_pair * pair_spread(dt, pair, left)).astype(bf16).astype(f32)
            mixing = []
            for head in (2 * pair, 2 * pair + 1):
                spread = run[:, head : head + 1] - run_t[head : head + 1, :]
                mixing.append((jnp.exp(jnp.minimum(spread, 0.0)) * scores).astype(bf16))
            local = mm(jnp.concatenate(mixing, axis=1), across(stepped, left))
            ssd_o[at, lanes] = (
                local + carried[:, lanes] * pair_spread(entry, pair, left) + skip[:, lanes] * x_pair
            )
            high, low = split(stepped * pair_spread(tail, pair, left))
            weighted[0, :, lanes] = high
            weighted[1, :, lanes] = low
            state[:, lanes] = pair_spread(factor, pair, left) * state[:, lanes]
        state[...] += mm(b_turned, weighted[0]) + mm(b_turned, weighted[1])


def gate_kernel(rank, normed, cot0, cot1, aux, ssd, wg, out_t, gain, gate_o, sg_o, ret_o, sums_o):
    returned = (pick_half(rank, cot0, cot1).astype(f32) * aux[:, LIVE : LIVE + 1]).astype(bf16)
    ret_o[...] = returned
    gate = mm(normed[...], wg[...])
    gate_o[...] = gate
    scaled_grad = mm(returned, out_t[...])
    sg_o[...] = scaled_grad
    gated = ssd[...] * (gate * sigmoid(gate))
    squares = jnp.sum(gated * gated, axis=1, keepdims=True)
    crossed = jnp.sum(scaled_grad * gain[...] * gated, axis=1, keepdims=True)
    lane = lax.broadcasted_iota(jnp.int32, (squares.shape[0], LANES), 1)
    table = jnp.where(lane == 0, squares, jnp.where(lane == 1, crossed, 0.0))
    sums_o[...] = table.T[:8, :]


def norm_kernel(
    rank, gate_r, sg_r, ssd_r, sums_r, out_t, gain, branch_o, scaled_o, dssd_o, dgate_o, gain_o
):
    @pl.when(pl.program_id(0) == 0)
    def _():
        gain_o[...] = jnp.zeros(gain_o.shape, f32)

    gate, ssd, scaled_grad = gate_r[...], ssd_r[...], sg_r[...]
    table = jnp.concatenate([sums_r[...], jnp.zeros((LANES - 8, sums_r.shape[1]), f32)], axis=0)
    sums = table.T
    scale = lax.rsqrt(sums[:, 0:1] / DI + norm_epsilon)
    sig = sigmoid(gate)
    silu = gate * sig
    gated = ssd * silu
    scaled = (gated * scale * gain[...]).astype(bf16)
    scaled_o[...] = scaled
    branch_o[...] = mm(scaled, out_t[...], 1, 1).astype(bf16)
    gain_o[...] += jnp.sum(scaled_grad * gated * scale, axis=0, keepdims=True)
    grad = scale * (scaled_grad * gain[...]) - gated * (scale * scale * scale * (sums[:, 1:2] / DI))
    dssd_o[...] = (grad * silu).astype(bf16)
    dgate_o[...] = (grad * ssd * sig * (1.0 + gate * (1.0 - sig))).astype(bf16)


def scan_back_kernel(
    heads, rank, dssd, mix, pre, ch, ssd, hin, step, conv, skip, hp, aux, segr, heads_of,
    state_in, win_in, carry_in, *rest,
):
    dval_o, dcommon_o, dconv_o, dheads_o, dstate, dtail, carry = rest[-14:-7]
    dmix, dwin, both, flows, entries, weighted, dskip = rest[-7:]
    width = dssd.shape[1]
    channels = width + 2 * N

    @pl.when(pl.program_id(0) == 0)
    def _():
        dwin[CHUNK:, :] = win_in[...]
        dstate[...] = state_in[...]
        carry[...] = carry_in[...]
        dconv_o[...] = jnp.zeros(dconv_o.shape, f32)
        dheads_o[...] = jnp.zeros(dheads_o.shape, f32)
        dskip[...] = jnp.zeros(dskip.shape, f32)

    row, col = iota(0), iota(1)
    left = col < 64
    table = aux[...]
    step_in = step[...]
    dt = softplus(step_in)
    rate = hp[1:2, :]
    tri = (row >= col).astype(f32)
    run = jnp.dot(tri, -(dt * rate), precision=highest, preferred_element_type=f32)
    run_t = run.T
    allowed = (table[:, SEG : SEG + 1] == segr[...]) & (col >= row)
    b_in = mix[:, width : width + N]
    c_out = mix[:, width + N :]
    scores = jnp.where(allowed, mm(b_in, c_out, 1, 1), 0.0)
    ending = run[CHUNK - 1 : CHUNK, :]
    entry = jnp.exp(run) * table[:, INHERIT : INHERIT + 1]
    tail = jnp.exp(ending - run) * table[:, TAIL : TAIL + 1]
    factor = jnp.exp(ending) * table[:, LINKED : LINKED + 1][CHUNK - 1 :, :]
    c_turned = c_out.astype(f32).T.astype(bf16)
    pairs = jnp.zeros((CHUNK, CHUNK), f32)
    state_high, state_low = split(dstate[...])
    flows[...] = mm(b_in, state_high) + mm(b_in, state_low)
    for pair in range(width // LANES):
        lanes = slice(pair * LANES, (pair + 1) * LANES)
        x_pair = mix[:, lanes].astype(f32)
        dy_low = dssd[:, lanes]
        dy = dy_low.astype(f32)
        dt_pair = pair_spread(dt, pair, left)
        tail_pair = pair_spread(tail, pair, left)
        stepped = (x_pair * dt_pair).astype(bf16).astype(f32)
        inner = mm(across(stepped, left), dy_low, 1, 1)
        mixing = []
        for place, head in enumerate((2 * pair, 2 * pair + 1)):
            spread = run_t[head : head + 1, :] - run[:, head : head + 1]
            decays = jnp.exp(jnp.minimum(spread, 0.0))
            mixing.append((decays * scores).astype(bf16))
            pairs = pairs + inner[place * CHUNK : (place + 1) * CHUNK] * decays
        flow = mm(jnp.concatenate(mixing, axis=1), across(dy, left)) + tail_pair * flows[:, lanes]
        dmix[:, lanes] = dt_pair * flow + skip[:, lanes] * dy
        both[0:CHUNK, lanes] = flow * x_pair
        both[CHUNK : 2 * CHUNK, lanes] = dy * (ssd[:, lanes] - skip[:, lanes] * x_pair) - flow * stepped
        dskip[0:1, lanes] += jnp.sum(dy * x_pair, axis=0, keepdims=True)
        high, low = split(pair_spread(entry, pair, left) * dy)
        entries[0, :, lanes] = high
        entries[1, :, lanes] = low
        weighted[:, lanes] = (tail_pair * stepped).astype(bf16)
        dstate[:, lanes] = pair_spread(factor, pair, left) * dstate[:, lanes]
    pairs = jnp.where(allowed, pairs, 0.0)
    dstate[...] += mm(c_turned, entries[0]) + mm(c_turned, entries[1])
    dmix[:, width : width + N] = mm(weighted[...], state_high, 1, 1) + mm_left(pairs, c_out)
    dmix[:, width + N :] = mm(entries[0], hin[0].astype(bf16), 1, 1) + mm_left(pairs, b_in, 0, 0)

    by_head = mm_left(both[...], heads_of[...])
    direct = by_head[0:CHUNK]
    balance = by_head[CHUNK:]
    later = allowed.astype(f32)
    log_grad = jnp.dot(later, balance, precision=highest, preferred_element_type=f32)
    log_grad = log_grad + table[:, NEXT : NEXT + 1] * carry[0:1, :]
    carry[0:1, :] = log_grad[0:1, :]
    step_grad = (direct - rate * log_grad) * sigmoid(step_in)
    dcommon_o[:, 2 * N :] = pltpu.roll(step_grad, heads * rank[0], 1)
    dheads_o[0:1, :] += jnp.sum(step_grad, axis=0, keepdims=True)
    dheads_o[1:2, :] += jnp.sum(-(log_grad * dt * rate), axis=0, keepdims=True)

    for start in range(0, channels, 256):
        cols = slice(start, start + 256)
        value = pre[:, cols]
        sig = sigmoid(value)
        dwin[0:CHUNK, cols] = dmix[:, cols] * (sig * (1.0 + value * (1.0 - sig)))
        here = ch[:, cols]
        own = dwin[0:CHUNK, cols]
        total = conv[3:4, cols] * own
        dconv_o[4:5, cols] += jnp.sum(own, axis=0, keepdims=True)
        dconv_o[3:4, cols] += jnp.sum(own * here, axis=0, keepdims=True)
        for ahead in range(1, 4):
            moved = dwin[ahead : ahead + CHUNK, cols] * table[:, AHEAD + ahead : AHEAD + ahead + 1]
            total = total + conv[3 - ahead : 4 - ahead, cols] * moved
            dconv_o[3 - ahead : 4 - ahead, cols] += jnp.sum(moved * here, axis=0, keepdims=True)
        if start < width:
            dval_o[:, cols] = total.astype(bf16)
        else:
            dcommon_o[:, : 2 * N] = total
    dwin[CHUNK:, :] = dwin[0:8, :]
    dtail[...] = dwin[0:8, :]

    @pl.when(pl.program_id(0) == pl.num_programs(0) - 1)
    def _():
        dheads_o[2:3, :] = mm_left(dskip[...], heads_of[...])[0:1, :]


def scatter_blocks(dp, me, full, keep_o, send_o, cols):
    half = dp // CORES
    block = full.shape[0] // dp
    for place, distance in enumerate(relative_places(dp)):
        start = pl.multiple_of((me[0] ^ distance) * block, block)
        part = full[pl.ds(start, block), :].astype(bf16)
        if place < half:
            keep_o[place, :, cols] = part
        else:
            send_o[place - half, :, cols] = part


def weight_grad_kernel(dp, me, lhs, rhs, keep_o, send_o, turned, full):
    @pl.when(pl.program_id(0) == 0)
    def _():
        turned[...] = lhs[...].T

    full[...] = mm(turned[...], rhs[...])
    scatter_blocks(dp, me, full, keep_o, send_o, slice(None))


def weight_grad(lhs, rhs, dp, dp_rank, skipped=0):
    length, width = rhs.shape[0], rhs.shape[1] - 256 * skipped
    depth = lhs.shape[1]
    block, half = depth // dp, dp // CORES
    piece = pl.BlockSpec((half, block, 256), lambda i, *s: (0, 0, i))
    return call(
        functools.partial(weight_grad_kernel, dp),
        (width // 256,),
        [whole((length, depth)), pl.BlockSpec((length, 256), lambda i, *s: (0, i + skipped))],
        [piece, piece],
        [shape(half, block, width, dtype=bf16)] * 2,
        [pltpu.VMEM((depth, length), bf16), pltpu.VMEM((depth, 256), f32)],
        2 * length * width * depth,
        10,
        scalars=1,
    )(dp_rank, lhs, rhs)


def value_grad_kernel(dp, me, lhs, dval, dcommon, keep_o, send_o, turned, full, wide):
    step = pl.program_id(0)
    last = pl.num_programs(0) - 1

    @pl.when(step == 0)
    def _():
        turned[...] = lhs[...].T

    @pl.when(step < last)
    def _():
        full[...] = mm(turned[...], dval[...])
        cols = pl.ds(pl.multiple_of(step * 256, 256), 256)
        scatter_blocks(dp, me, full, keep_o, send_o, cols)

    @pl.when(step == last)
    def _():
        wide[...] = mm_right(turned[...], dcommon[...])
        cols = slice(keep_o.shape[2] - wide.shape[1], keep_o.shape[2])
        scatter_blocks(dp, me, wide, keep_o, send_o, cols)


def value_grad(lhs, dval, dcommon, dp, dp_rank):
    length, width = dval.shape[0], 256
    depth, extra = lhs.shape[1], dcommon.shape[1]
    block, half, per = depth // dp, dp // CORES, width // 256
    dims = (half, block, width + extra)
    return call(
        functools.partial(value_grad_kernel, dp),
        (per + 1,),
        [
            whole((length, depth)),
            pl.BlockSpec((length, 256), lambda i, *s: (0, jnp.minimum(i, per - 1))),
            whole((length, extra)),
        ],
        [result(dims), result(dims)],
        [shape(*dims, dtype=bf16)] * 2,
        [
            pltpu.VMEM((depth, length), bf16), pltpu.VMEM((depth, 256), f32),
            pltpu.VMEM((depth, extra), f32),
        ],
        2 * length * (width + 2 * extra) * depth,
        15,
        scalars=1,
    )(dp_rank, lhs, dval, dcommon)


def input_grad_kernel(
    away, rank, dgate, dval, dcommon, tok0, tok1, wg, wv, shw, sent_o, own_o, gain_o
):
    step = pl.program_id(0)

    @pl.when(step == 0)
    def _():
        gain_o[...] = jnp.zeros(gain_o.shape, f32)

    grad = mm(dgate[...], wg[...], 1, 1) + mm(dval[...], wv[...], 1, 1)
    grad = grad + mm_left(dcommon[...], shw[...], 1, 1)
    first = jnp.broadcast_to((step < away).astype(jnp.int32), tok0.shape) == 1
    x = jnp.where(first, tok0[...], tok1[...]).astype(f32)
    inverse = lax.rsqrt(jnp.mean(x * x, axis=1, keepdims=True) + norm_epsilon)
    gain_o[...] += jnp.sum(grad * (x * inverse), axis=0, keepdims=True)

    @pl.when(step < away)
    def _():
        sent_o[...] = grad.astype(bf16)

    @pl.when(step >= away)
    def _():
        own_o[...] = grad


def shards(
    dp, nt,
    residual, cotangent, sequence_ids,
    inner_proj, inner_mean, inner_square,
    shared_proj, shared_mean, shared_square,
    outer_proj, outer_mean, outer_square,
    conv_params, conv_mean, conv_square,
    norm_gains, gains_mean, gains_square,
    head_params, heads_mean, heads_square,
):
    t_rank = lax.axis_index("tensor").astype(jnp.int32)
    d_rank = lax.axis_index("dp").astype(jnp.int32)
    dp_me = d_rank[None]
    t_me = t_rank[None]
    rows_here = residual.shape[0]
    length = rows_here * nt
    width = inner_proj.shape[2]
    heads_here = head_params.shape[1]
    head_size = width // heads_here
    channels = width + 2 * N
    chunks = length // CHUNK
    wide = 2 * CHUNK
    band = min(2 * CHUNK, rows_here)
    per_piece = rows_here // band

    def pieces_of(value):
        return [value] + [swap(value, "tensor", nt, d) for d in range(1, nt)]

    def over_tensor(value, pieces=None):
        pieces = pieces_of(value) if pieces is None else pieces
        if nt == 2:
            first = jnp.concatenate(pieces, axis=0)
            second = jnp.concatenate(pieces[::-1], axis=0)
            return jnp.where(t_rank == 0, first, second)
        stacked = jnp.take(jnp.stack(pieces), jnp.arange(nt) ^ t_rank, axis=0)
        return stacked.reshape((nt * stacked.shape[1],) + stacked.shape[2:])

    kernel_rows, columns = conv_params.shape
    gain_count = norm_gains.shape[0]
    shared_size = shared_proj.size
    exact = jnp.concatenate([conv_params.reshape(-1), norm_gains])
    terms = []
    rest = exact
    for _ in range(3):
        term = lax.optimization_barrier(rest.astype(bf16))
        terms.append(term)
        rest = rest - term.astype(f32)
    common_width = 2 * N + LANES
    shared_rows = shared_proj.shape[0]
    packed = width == 1024 and shared_rows == 32
    if packed:
        wide_shared = jnp.pad(shared_proj.astype(bf16), ((0, 0), (0, common_width - 2 * N - H)))
        flat = jnp.concatenate(terms)
        flat = jnp.pad(flat, (0, 16 * 256 - flat.size)).reshape(16, 256)
        small = jnp.concatenate([wide_shared[:16], wide_shared[16:], flat], axis=1)
        small_rows = 16
    else:
        small = jnp.concatenate([shared_proj.astype(bf16).reshape(-1)] + terms)
        small_rows = -(-small.size // width)
        while small_rows * nt % 16:
            small_rows += 1
        small = jnp.pad(small, (0, small_rows * width - small.size)).reshape(small_rows, width)
    small_pair = over_tensor(small)
    token_pieces = pieces_of(residual)

    block_rows = D // dp
    value_shard = jnp.concatenate([inner_proj[1].astype(bf16), small_pair], axis=0)
    cut = -(-value_shard.shape[0] // 32) * 16
    first_line = gather_line(value_shard[:cut], dp)
    second_shard, first_line = tie(value_shard[cut:], first_line)
    second_line = gather_line(second_shard, dp)
    second_line, ids = tie(second_line, sequence_ids)
    first_near = [first_line] + plane_parts(first_line, dp)
    other_shard = jnp.concatenate(
        [inner_proj[0].astype(bf16), outer_proj.T.astype(bf16)], axis=0
    )
    other_shard, second_line = tie(other_shard, second_line)
    other_line = gather_line(other_shard, dp)
    cot_cut = rows_here // 2
    cot_early = [swap(cotangent[:cot_cut], "tensor", nt, d) for d in range(1, nt)]
    second_line, *rests = tie(
        second_line, *plane_parts(second_line, dp), *token_pieces, *cot_early
    )
    count = len(rests) - 2 * nt + 1
    second_near = [second_line] + rests[:count]
    token_pieces, cot_early = rests[count : count + nt], rests[count + nt :]
    cotangent_now, *token_pieces = tie(cotangent[cot_cut:], *token_pieces)
    cot_late = [swap(cotangent_now, "tensor", nt, d) for d in range(1, nt)]
    first_all = first_near + [swap(line, "dp", dp, 1) for line in first_near]
    second_all = second_near + [swap(line, "dp", dp, 1) for line in second_near]
    full = slice(None)
    moves = [(0, block_rows, full, 0, 1, 0, 0)]
    dims = [(dp, block_rows, width)]
    if packed:
        for t in range(nt):
            at = (block_rows + 16 * t, block_rows + 16 * t + 16)
            moves.append(at + (slice(0, common_width), 1, nt, t, 0))
            moves.append(at + (slice(common_width, 2 * common_width), 1, nt, t, 16))
            moves.append(at + (slice(2 * common_width, width), 2, nt, t, 0))
        dims += [(dp * nt, 32, common_width), (dp * nt, 16, 256)]
    else:
        moves.append((block_rows, block_rows + small_rows * nt, full, 1, 1, 0, 0))
        dims += [(dp, small_rows * nt, width)]
    value_w, *small_all = assemble([first_all, second_all], dp, dp_me, moves, dims)
    value_w = value_w.reshape(D, width)

    def halves(pieces):
        if nt == 2:
            return t_me, pieces[0], pieces[1]
        all_rows = over_tensor(None, pieces)
        return jnp.zeros((1,), jnp.int32), all_rows[: length // 2], all_rows[length // 2 :]

    if packed:
        shared_here = small_all[0].reshape(D, common_width)
        exact_all = small_all[1].reshape(dp * nt, -1)[:, : 3 * exact.size].astype(f32)
    else:
        small_all = small_all[0].reshape(dp * nt, small_rows * width)
        shared_here = small_all[:, :shared_size].reshape(D, -1)
        shared_here = jnp.pad(shared_here, ((0, 0), (0, common_width - 2 * N - H)))
        exact_all = small_all[:, shared_size : shared_size + 3 * exact.size].astype(f32)
    exact_all = exact_all.reshape(dp * nt, 3, exact.size)
    exact_all = (exact_all[:, 0] + exact_all[:, 1]) + exact_all[:, 2]
    conv_full = (
        exact_all[:, : kernel_rows * columns]
        .reshape(dp * nt, kernel_rows, columns)
        .transpose(1, 0, 2)
        .reshape(kernel_rows, -1)
    )
    gains_full = exact_all[:, kernel_rows * columns :].reshape(-1)

    pre_gain = gains_full[:D].reshape(1, D)
    post_gain = lax.dynamic_slice_in_dim(gains_full, D + t_rank * width, width).reshape(1, width)
    conv_here = jnp.concatenate(
        [lax.dynamic_slice_in_dim(conv_full, t_rank * width, width, 1), conv_full[:, DI:]], axis=1
    )
    conv_here = jnp.pad(conv_here, ((0, 8 - kernel_rows), (0, 0)))
    head_rows = jnp.stack([head_params[0], jnp.exp(head_params[1])])
    head_rows = jnp.pad(head_rows, ((0, 6), (0, LANES - heads_here)))
    skip = jnp.repeat(head_params[2], head_size).reshape(1, width)
    heads_of = (
        jnp.arange(width)[:, None] // head_size == jnp.arange(LANES)[None, :]
    ).astype(bf16)

    blocked = ids.reshape(chunks, CHUNK)
    ends, firsts = blocked[:, -1], blocked[:, 0]
    none = jnp.full((1,), -1, jnp.int32)
    before = jnp.concatenate([none, ends[:-1]])
    following = jnp.concatenate([firsts[1:], none])
    fills = [jnp.full((o,), -1, jnp.int32) for o in range(1, 4)]
    marks = [ids]
    marks += [jnp.concatenate([fills[o - 1], ids[:-o]]) == ids for o in range(1, 4)]
    marks += [jnp.concatenate([ids[o:], fills[o - 1]]) == ids for o in range(1, 4)]
    marks += [
        (blocked == before[:, None]).reshape(-1),
        (blocked == ends[:, None]).reshape(-1),
        jnp.broadcast_to((ends == before)[:, None], blocked.shape).reshape(-1),
        (blocked == following[:, None]).reshape(-1),
        ids < SEQ_SLOTS,
    ]
    aux = jnp.stack([m.astype(f32) for m in marks] + [jnp.zeros((length,), f32)] * 4, axis=1)
    segr = ids.astype(f32).reshape(1, length)
    aux_cols = aux.shape[1]

    steps = length // wide
    in_half = lambda i: i % (steps // 2)
    value_w, other_line, *cot_late = tie(value_w, other_line, *cot_late)
    cot_pieces = [cotangent] + [
        jnp.concatenate([early, late], axis=0) for early, late in zip(cot_early, cot_late)
    ]
    other_far = swap(other_line, "dp", dp, 1)
    plane = plane_parts(other_line, dp)
    tok_rank, tok0, tok1 = halves(token_pieces)
    normed, chans, pre, mixed, ssd, entering, step_in = call(
        functools.partial(scan_kernel, heads_here),
        (steps,),
        [
            rows(wide, D, in_half), rows(wide, D, in_half), whole((1, D)), whole((D, width)),
            whole((D, common_width)), whole((8, channels)), whole((1, width)), whole((8, LANES)),
            rows(wide, aux_cols), pl.BlockSpec((1, wide), lambda i, r: (0, i)),
        ],
        [
            rows(wide, D), rows(wide, channels), rows(wide, channels), rows(wide, channels),
            rows(wide, width), pl.BlockSpec((wide // CHUNK, N, width), lambda i, r: (i, 0, 0)),
            rows(wide, LANES),
        ],
        [
            shape(length, D, dtype=bf16), shape(length, channels), shape(length, channels),
            shape(length, channels, dtype=bf16), shape(length, width),
            shape(chunks, N, width), shape(length, LANES),
        ],
        [
            pltpu.VMEM((wide + 8, channels), f32), pltpu.VMEM((N, width), f32),
            pltpu.VMEM((CHUNK, width), f32), pltpu.VMEM((2, CHUNK, width), bf16),
        ],
        length * (2 * D * (width + common_width) + 12 * width * CHUNK),
        22,
        scalars=1,
    )(jnp.concatenate([tok_rank, t_me]), tok0, tok1, pre_gain, value_w, shared_here, conv_here, skip, head_rows, aux, segr)

    normed, other_far, *plane = tie(normed, other_far, *plane)
    moves = [
        (0, block_rows, full, 0, 1, 0, 0), (block_rows, 2 * block_rows, full, 1, 1, 0, 0)
    ]
    other_all = [other_line] + plane + [other_far] + [swap(line, "dp", dp, 1) for line in plane]
    gate_w, outer_t = assemble([other_all], dp, dp_me, moves, [(dp, block_rows, width)] * 2)
    gate_w, outer_t = gate_w.reshape(D, width), outer_t.reshape(D, width)
    cot_rank, cot0, cot1 = halves(cot_pieces)
    gate, scaled_grad, returned, sums = call(
        gate_kernel,
        (steps,),
        [
            rows(wide, D), rows(wide, D, in_half), rows(wide, D, in_half), rows(wide, aux_cols),
            rows(wide, width), whole((D, width)), whole((D, width)), whole((1, width)),
        ],
        [rows(wide, width), rows(wide, width), rows(wide, D), pl.BlockSpec((8, wide), lambda i, r: (0, i))],
        [
            shape(length, width), shape(length, width), shape(length, D, dtype=bf16),
            shape(8, length),
        ],
        [],
        4 * length * D * width,
        15,
        scalars=1,
    )(cot_rank, normed, cot0, cot1, aux, ssd, gate_w, outer_t, post_gain)
    distance = 1
    while distance < nt:
        sums = sums + swap(sums, "tensor", nt, distance)
        distance *= 2

    def relative(block, rank):
        return (rank ^ (block // per_piece)) * per_piece + block % per_piece

    def rel_rows(width_here, offset=0):
        return pl.BlockSpec((band, width_here), lambda i, r: (relative(i + offset, r[0]), 0))

    plain = lambda width_here: pl.BlockSpec((band, width_here), lambda i, r: (i, 0))
    branch, scaled, dssd, dgate, post_grad = call(
        norm_kernel,
        (length // band,),
        [
            rel_rows(width), rel_rows(width), rel_rows(width),
            pl.BlockSpec((8, band), lambda i, r: (0, relative(i, r[0]))),
            whole((D, width)), whole((1, width)),
        ],
        [plain(D), rel_rows(width), rel_rows(width), rel_rows(width), result((1, width))],
        [
            shape(length, D, dtype=bf16), shape(length, width, dtype=bf16),
            shape(length, width, dtype=bf16), shape(length, width, dtype=bf16), shape(1, width),
        ],
        [],
        2 * length * D * width,
        15,
        scalars=1,
    )(t_me, gate, scaled_grad, ssd, sums, outer_t, post_gain)
    outer_keep, outer_send = weight_grad(returned, scaled, dp, dp_me)
    dgate, outer_send = tie(dgate, outer_send)
    gate_keep, gate_send = weight_grad(normed, dgate, dp, dp_me)
    outer_line, outer_rest = start_sum(outer_keep, outer_send, dp)
    gate_line, gate_rest = start_sum(gate_keep, gate_send, dp)
    branch = branch.reshape(nt, rows_here, D)
    branch_received = [swap(branch[d], "tensor", nt, d) for d in range(1, nt)]
    dssd, *rests = tie(dssd, *outer_rest, *gate_rest)
    outer_rest, gate_rest = rests[: len(outer_rest)], rests[len(outer_rest) :]
    outer_received = middle_swaps(outer_rest, dp)
    gate_received = middle_swaps(gate_rest, dp)

    state = jnp.zeros((N, width), f32)
    win = jnp.zeros((8, channels), f32)
    carry = jnp.zeros((8, LANES), f32)
    back_parts = []
    filled = []
    top = chunks
    for part, count in enumerate((3, 3, chunks - 6)):
        back = lambda i, top=top: top - 1 - i
        top -= count
        *results, state, win, carry = call(
            functools.partial(scan_back_kernel, heads_here),
            (count,),
            [
                rows(CHUNK, width, back), rows(CHUNK, channels, back), rows(CHUNK, channels, back),
                rows(CHUNK, channels, back), rows(CHUNK, width, back),
                pl.BlockSpec((1, N, width), lambda i, r, back=back: (back(i), 0, 0)),
                rows(CHUNK, LANES, back), whole((8, channels)), whole((1, width)),
                whole((8, LANES)), rows(CHUNK, aux_cols, back),
                pl.BlockSpec((1, CHUNK), lambda i, r, back=back: (0, back(i))),
                whole((width, LANES)),
                whole((N, width)), whole((8, channels)), whole((8, LANES)),
            ]
            + [pl.BlockSpec(memory_space=pl.ANY)] * len(filled),
            [
                rows(CHUNK, width, back), rows(CHUNK, common_width, back), result((8, channels)),
                result((8, LANES)),
                result((N, width)), result((8, channels)), result((8, LANES)),
            ],
            [
                shape(length, width, dtype=bf16), shape(length, common_width),
                shape(8, channels), shape(8, LANES),
                shape(N, width), shape(8, channels), shape(8, LANES),
            ],
            [
                pltpu.VMEM((CHUNK, channels), f32), pltpu.VMEM((CHUNK + 8, channels), f32),
                pltpu.VMEM((2 * CHUNK, width), f32), pltpu.VMEM((CHUNK, width), f32),
                pltpu.VMEM((2, CHUNK, width), bf16), pltpu.VMEM((CHUNK, width), bf16),
                pltpu.VMEM((8, width), f32),
            ],
            count * CHUNK * 30 * width * CHUNK,
            14,
            scalars=1,
            aliases={17: 0, 18: 1} if filled else None,
        )(
            t_me, dssd, mixed, pre, chans, ssd, entering, step_in, conv_here, skip, head_rows, aux, segr,
            heads_of, state, win, carry, *filled,
        )
        filled = results[:2]
        back_parts.append(results[2:])
        if part == 0:
            state, outer_line, *outer_received = tie(state, outer_line, *outer_received)
            outer_block, outer_far = middle_sum(outer_line, outer_received)
            outer_far = high_swaps(outer_far, dp)
        if part == 1:
            state, gate_line, *rests = tie(
                state, gate_line, *branch_received, *gate_received, *outer_far
            )
            branch_received = rests[: nt - 1]
            gate_received, outer_far = rests[nt - 1 : -len(outer_far)], rests[-len(outer_far) :]
            gate_block, gate_far = middle_sum(gate_line, gate_received)
            gate_far = high_swaps(gate_far, dp)
    dval, dcommon = filled
    dval, *gate_far = tie(dval, *gate_far)

    branch_sum = branch[0].astype(f32)
    for piece in branch_received:
        branch_sum = branch_sum + piece.astype(f32)
    live_here = lax.dynamic_slice_in_dim(aux[:, LIVE], t_rank * rows_here, rows_here)
    tokens = residual.astype(f32)
    block_out = (tokens + branch_sum * live_here[:, None]).astype(bf16)

    away = (nt - 1) * per_piece

    def input_grad(others, dgate):
        away_rows = lambda width_here: pl.BlockSpec(
            (band, width_here), lambda i, r: (jnp.minimum(i, away - 1), 0)
        )
        own_rows = lambda width_here: pl.BlockSpec(
            (band, width_here), lambda i, r: (jnp.maximum(i - away, 0), 0)
        )
        turned = lambda i: lax.rem(i + per_piece, nt * per_piece)
        here = lambda width_here: pl.BlockSpec(
            (band, width_here), lambda i, r: (relative(turned(i), r[0]), 0)
        )
        return call(
            functools.partial(input_grad_kernel, away),
            (nt * per_piece,),
            [
                here(width), here(width), here(common_width), away_rows(D), own_rows(D),
                whole((D, width)), whole((D, width)), whole((D, common_width)),
            ],
            [away_rows(D), own_rows(D), result((1, D))],
            [shape((nt - 1) * rows_here, D, dtype=bf16), shape(rows_here, D), shape(1, D)],
            [],
            4 * length * D * (width + common_width),
            24,
            scalars=1,
        )(t_me, dgate, dval, dcommon, others, residual, gate_w, value_w, shared_here)

    keep, send = value_grad(normed, dval, dcommon, dp, dp_me)
    line, part = start_sum(keep, send, dp)
    two = width > 256
    lines, parts = [line], [part]
    if two:
        dval, *parts[0] = tie(dval, *parts[0])
        keep, send = weight_grad(normed, dval, dp, dp_me, skipped=1)
        line, part = start_sum(keep, send, dp)
        lines.append(line)
        parts.append(part)
    crossing = [middle_swaps(parts[0], dp)]
    dgate, *part = tie(dgate, *part)
    if two:
        crossing.append(middle_swaps(part, dp))
    others = token_pieces[1] if nt == 2 else jnp.concatenate(token_pieces[1:], axis=0)
    sent, own, pre_grad = input_grad(others, dgate)
    sent = sent.reshape(nt - 1, rows_here, D)
    received = [swap(sent[d - 1], "tensor", nt, d) for d in range(1, nt)]
    small_grads = [item for each_part in back_parts for item in each_part]
    pre_grad, *rests = tie(pre_grad, *crossing[0], *small_grads)
    crossing[0], small_grads = rests[: len(crossing[0])], rests[len(crossing[0]) :]
    block, far = middle_sum(lines[0], crossing[0])
    pre_grad, *far = tie(pre_grad, *far)
    blocks, fars = [block], [high_swaps(far, dp)]
    if two:
        pre_grad, *crossing[1] = tie(pre_grad, *crossing[1])
        block, far = middle_sum(lines[1], crossing[1])
        pre_grad, *far = tie(pre_grad, *far)
        blocks.append(block)
        fars.append(high_swaps(far, dp))
    dconv, dheads = [sum(small_grads[at::2]) for at in range(2)]
    conv_grad = lax.dynamic_update_slice(
        jnp.pad(dconv[:kernel_rows, width:], ((0, 0), (DI, 0))),
        dconv[:kernel_rows, :width],
        (0, t_rank * width),
    )
    post_all = lax.dynamic_update_slice(
        jnp.zeros((1, DI), f32), post_grad, (0, t_rank * width)
    )
    head_grad = dheads[:3, :heads_here]
    head_all = lax.dynamic_update_slice(
        jnp.zeros((3, H), f32), head_grad, (0, t_rank * heads_here)
    )
    vector = jnp.concatenate(
        [
            conv_grad.reshape(1, -1), pre_grad, post_all, head_all.reshape(1, -1),
        ],
        axis=1,
    )
    for stage, (axis, size, distance) in enumerate(sum_stages(dp, nt)):
        vector = vector + swap(vector, axis, size, distance)
        if stage == 0:
            vector, *fars[0] = tie(vector, *fars[0])
            value_sums = [high_sum(blocks[0], fars[0])]
            vector, outer_block, gate_block = tie(vector, outer_block, gate_block)
            outer_part = high_sum(outer_block, outer_far)
            gate_part = high_sum(gate_block, gate_far)
        if stage == 1:
            vector, *received = tie(vector, *received)
        if stage == 1 and two:
            vector, *fars[1] = tie(vector, *fars[1])
            value_sums.append(high_sum(blocks[1], fars[1]))
    shared_sum = value_sums[0][:, 256:].reshape(nt, shared_rows, common_width)
    shared_mine = lax.dynamic_index_in_dim(shared_sum, t_rank, 0, False)
    for d in range(1, nt):
        piece = lax.dynamic_index_in_dim(shared_sum, t_rank ^ d, 0, False)
        shared_mine = shared_mine + swap(piece, "tensor", nt, d)
    shared_part = shared_mine[:, : 2 * N + H]
    value_part = jnp.concatenate([value_sums[0][:, :256]] + value_sums[1:], axis=1)
    conv_size = kernel_rows * (DI + 2 * N)
    place = d_rank * nt + t_rank
    conv_part = lax.dynamic_slice_in_dim(
        vector[0, :conv_size].reshape(kernel_rows, -1), place * columns, columns, 1
    )
    gains_part = lax.dynamic_slice_in_dim(vector[0], conv_size + place * gain_count, gain_count)
    heads_part = lax.dynamic_slice_in_dim(
        vector[0, conv_size + D + DI :].reshape(3, H), t_rank * heads_here, heads_here, 1
    )

    normed_grad = own
    for piece in received:
        normed_grad = normed_grad + piece.astype(f32)
    inverse = lax.rsqrt(jnp.mean(tokens * tokens, axis=1, keepdims=True) + norm_epsilon)
    normal_tokens = tokens * inverse
    normal_grad = normed_grad * pre_gain
    centered = normal_grad - normal_tokens * jnp.mean(
        normal_grad * normal_tokens, axis=1, keepdims=True
    )
    residual_grad = (cotangent.astype(f32) + inverse * centered).astype(bf16)

    inner_new = adam_step(
        inner_proj, inner_mean, inner_square, jnp.stack([gate_part, value_part]),
        rate_matrix, weight_decay,
    )
    shared_new = adam_step(
        shared_proj, shared_mean, shared_square, shared_part.reshape(shared_proj.shape),
        rate_matrix, weight_decay,
    )
    outer_new = adam_step(
        outer_proj, outer_mean, outer_square, outer_part.T, rate_matrix, weight_decay
    )
    conv_new = adam_step(conv_params, conv_mean, conv_square, conv_part, rate_vector, 0.0)
    gains_new = adam_step(norm_gains, gains_mean, gains_square, gains_part, rate_vector, 0.0)
    heads_new = adam_step(head_params, heads_mean, heads_square, heads_part, rate_heads, 0.0)
    return (
        (block_out, residual_grad)
        + inner_new + shared_new + outer_new + conv_new + gains_new + heads_new
    )


def solution(mesh):
    return jax.shard_map(
        functools.partial(shards, mesh.shape["dp"], mesh.shape["tensor"]),
        mesh=mesh,
        in_specs=(
            P(("dp", "tensor"), None),
            P(("dp", "tensor"), None),
            P("dp"),
            P(None, "dp", "tensor"),
            P(None, "dp", "tensor"),
            P(None, "dp", "tensor"),
            P(("dp", "tensor"), None),
            P(("dp", "tensor"), None),
            P(("dp", "tensor"), None),
            P("tensor", "dp"),
            P("tensor", "dp"),
            P("tensor", "dp"),
            P(None, ("dp", "tensor")),
            P(None, ("dp", "tensor")),
            P(None, ("dp", "tensor")),
            P(("dp", "tensor")),
            P(("dp", "tensor")),
            P(("dp", "tensor")),
            P(None, "tensor"),
            P(None, "tensor"),
            P(None, "tensor"),
        ),
        out_specs=(
            P(("dp", "tensor"), None),
            P(("dp", "tensor"), None),
            P(None, "dp", "tensor"),
            P(None, "dp", "tensor"),
            P(None, "dp", "tensor"),
            P(("dp", "tensor"), None),
            P(("dp", "tensor"), None),
            P(("dp", "tensor"), None),
            P("tensor", "dp"),
            P("tensor", "dp"),
            P("tensor", "dp"),
            P(None, ("dp", "tensor")),
            P(None, ("dp", "tensor")),
            P(None, ("dp", "tensor")),
            P(("dp", "tensor")),
            P(("dp", "tensor")),
            P(("dp", "tensor")),
            P(None, "tensor"),
            P(None, "tensor"),
            P(None, "tensor"),
        ),
        check_vma=False,
    )
```

```python
import functools

import jax
import jax.numpy as jnp
from jax import lax
from jax.experimental import pallas as pl
from jax.experimental.pallas import tpu as pltpu
from jax.sharding import PartitionSpec as P

D = 1024
H = 32
N = 128
DI = 2048
SEQ_SLOTS = 4
STEP = 10
CHUNK = 128
LANES = 128
CORES = 2
HIGH_AXIS = 4

highest = lax.Precision.HIGHEST
f32 = jnp.float32
bf16 = jnp.bfloat16
norm_epsilon = 1e-05
beta_first = 0.9
beta_second = 0.95
adam_epsilon = 1e-08
weight_decay = 0.1
rate_matrix = 0.02
rate_vector = 0.3
rate_heads = 1.0

SEG, BACK, AHEAD, INHERIT, TAIL, LINKED, NEXT, LIVE = 0, 0, 3, 7, 8, 9, 10, 11


def adam_step(weight, moment, square, gradient, rate, decay):
    moment_next = beta_first * moment + (1.0 - beta_first) * gradient
    square_next = beta_second * square + (1.0 - beta_second) * gradient * gradient
    moment_hat = moment_next / (1.0 - beta_first**STEP)
    square_hat = square_next / (1.0 - beta_second**STEP)
    weight_next = weight - rate * (
        moment_hat / (jnp.sqrt(square_hat) + adam_epsilon) + decay * weight
    )
    return (weight_next, moment_next, square_next)


def swap(value, axis, size, distance):
    return lax.ppermute(value, axis, [(i, i ^ distance) for i in range(size)])


def tie(*values):
    return lax.optimization_barrier(values)


def axis_parts(dp):
    high = HIGH_AXIS
    middle = dp // (CORES * high)
    return high, middle


def gather_line(shard, dp):
    high, middle = axis_parts(dp)
    pieces = [shard[None]]
    for step in range(1, high):
        pieces.append(swap(shard, "dp", dp, step * middle * CORES)[None])
    return jnp.concatenate(pieces, axis=0)


def plane_parts(line, dp):
    return [swap(line, "dp", dp, step * CORES) for step in range(1, axis_parts(dp)[1])]


def start_sum(keep, send, dp):
    high, middle = axis_parts(dp)
    other = swap(send, "dp", dp, 1)
    parts = [slice(step * high, (step + 1) * high) for step in range(middle)]
    line = keep[parts[0]].astype(f32) + other[parts[0]].astype(f32)
    rest = [(keep[at].astype(f32) + other[at].astype(f32)).astype(bf16) for at in parts[1:]]
    return line, rest


def middle_swaps(rest, dp):
    return [swap(part, "dp", dp, (step + 1) * CORES) for step, part in enumerate(rest)]


def middle_sum(line, received):
    for part in received:
        line = line + part.astype(f32)
    return line[0], [part.astype(bf16) for part in line[1:]]


def high_swaps(rest, dp):
    middle = axis_parts(dp)[1]
    return [swap(part, "dp", dp, (step + 1) * middle * CORES) for step, part in enumerate(rest)]


def high_sum(block, received):
    for part in received:
        block = block + part.astype(f32)
    return block


def sum_stages(dp, nt):
    stages = [("tensor", nt, 1 << bit) for bit in range((nt - 1).bit_length())]
    return stages + [("dp", dp, 1 << bit) for bit in range((dp - 1).bit_length())]


def relative_places(dp):
    high, middle = axis_parts(dp)
    return [
        (h * middle + m) * CORES + c for c in range(CORES) for m in range(middle) for h in range(high)
    ]


def call(kernel, grid, in_specs, out_specs, out_shape, scratch, flops, mib, scalars=0, aliases=None):
    params = pltpu.CompilerParams(vmem_limit_bytes=mib * 1024 * 1024)
    moved = sum(2 * s.dtype.itemsize * s.size for s in jax.tree.leaves(out_shape))
    return pl.pallas_call(
        kernel,
        grid_spec=pltpu.PrefetchScalarGridSpec(
            num_scalar_prefetch=scalars,
            grid=grid,
            in_specs=in_specs,
            out_specs=out_specs,
            scratch_shapes=scratch,
        ),
        out_shape=out_shape,
        compiler_params=params,
        input_output_aliases=aliases or {},
        cost_estimate=pl.CostEstimate(
            flops=int(flops) // 16, bytes_accessed=int(moved) // 16, transcendentals=0
        ),
    )


def whole(shape):
    return pl.BlockSpec(shape, lambda *i: (0,) * len(shape), pipeline_mode=pl.Buffered(1))


def result(shape):
    return pl.BlockSpec(shape, lambda *i: (0,) * len(shape))


def rows(count, width, index=lambda i: i):
    return pl.BlockSpec((count, width), lambda i, *s: (index(i), 0))


def shape(*dims, dtype=f32):
    return jax.ShapeDtypeStruct(dims, dtype)


def split(value):
    high = value.astype(bf16)
    return high, (value - high.astype(f32)).astype(bf16)


def mm(a, b, ca=1, cb=0):
    return lax.dot_general(a, b, (((ca,), (cb,)), ((), ())), preferred_element_type=f32)


def mm_left(value, exact, ca=1, cb=0):
    high, low = split(value)
    return mm(high, exact, ca, cb) + mm(low, exact, ca, cb)


def mm_right(exact, value, ca=1, cb=0):
    high, low = split(value)
    return mm(exact, high, ca, cb) + mm(exact, low, ca, cb)


def mm_both(a, b, ca=1, cb=0):
    a_high, a_low = split(a)
    b_high, b_low = split(b)
    return mm(a_high, b_high, ca, cb) + mm(a_low, b_high, ca, cb) + mm(a_high, b_low, ca, cb)


def sigmoid(value):
    return 0.5 * jnp.tanh(0.5 * value) + 0.5


def softplus(value):
    return jnp.maximum(value, 0.0) + jnp.log1p(jnp.exp(-jnp.abs(value)))


def iota(axis):
    return lax.broadcasted_iota(jnp.int32, (CHUNK, LANES), axis)


def pair_spread(tile, pair, left):
    rows_here = tile.shape[0]
    return jnp.where(
        left[:rows_here],
        jnp.broadcast_to(tile[:, 2 * pair : 2 * pair + 1], (rows_here, LANES)),
        jnp.broadcast_to(tile[:, 2 * pair + 1 : 2 * pair + 2], (rows_here, LANES)),
    )


def assemble_kernel(dp, parts, moves, me, *refs):
    high, middle = axis_parts(dp)
    each = CORES * middle
    sources, outs = refs[: parts * each], refs[parts * each :]
    for place, distance in enumerate(relative_places(dp)):
        block = me[0] ^ distance
        base = 0
        for part in range(parts):
            source, at = sources[part * each + place // high], place % high
            end = base + source.shape[1]
            for first, last, lanes, out, count, extra, row in moves:
                low, top = max(base, first), min(end, last)
                if low < top:
                    outs[out][
                        block * count + extra, row + low - first : row + top - first, :
                    ] = source[at, low - base : top - base, lanes]
            base = end


def assemble(parts, dp, dp_rank, moves, shapes):
    vmem = pl.BlockSpec(memory_space=pltpu.VMEM)
    lines = [line for part in parts for line in part]
    moved = sum(2 * line.size * line.dtype.itemsize for line in lines)
    return pl.pallas_call(
        functools.partial(assemble_kernel, dp, len(parts), moves),
        in_specs=[pl.BlockSpec(memory_space=pltpu.SMEM)] + [vmem] * len(lines),
        out_specs=[vmem] * len(shapes),
        out_shape=[shape(*dims, dtype=bf16) for dims in shapes],
        compiler_params=pltpu.CompilerParams(vmem_limit_bytes=16 * 1024 * 1024),
        cost_estimate=pl.CostEstimate(flops=0, bytes_accessed=moved, transcendentals=0),
    )(dp_rank, *lines)


def pick_half(rank, first, second):
    half = (2 * pl.program_id(0)) // pl.num_programs(0)
    own = (half == rank[0]).astype(jnp.int32)
    return jnp.where(jnp.broadcast_to(own, first.shape) == 1, first[...], second[...])


def across(pair, left):
    return jnp.concatenate(
        [jnp.where(left, pair, 0.0), jnp.where(left, 0.0, pair)], axis=0
    ).astype(bf16)


def scan_kernel(
    heads, rank, tok0, tok1, gain, wv, shw, conv, skip, hp, aux, segr,
    normed_o, ch_o, pre_o, mix_o, ssd_o, hin_o, step_o,
    win, state, carried, weighted,
):
    count = tok0.shape[0]
    width = wv.shape[1]
    channels = width + 2 * N

    @pl.when(pl.program_id(0) == 0)
    def _():
        win[0:8, :] = jnp.zeros((8, channels), f32)
        state[...] = jnp.zeros(state.shape, f32)

    x = pick_half(rank, tok0, tok1).astype(f32)
    inverse = lax.rsqrt(jnp.mean(x * x, axis=1, keepdims=True) + norm_epsilon)
    normed = (x * inverse * gain[...]).astype(bf16)
    normed_o[...] = normed
    win[8 : 8 + count, :width] = mm(normed, wv[...])
    common = mm(normed, shw[...])
    win[8 : 8 + count, width:] = common[:, : 2 * N]
    turn = lax.rem(LANES - heads * rank[1], LANES)
    step_o[...] = pltpu.roll(common[:, 2 * N :], turn, 1) + hp[0:1, :]
    table = aux[...]
    for start in range(0, channels, 256):
        cols = slice(start, start + 256)
        here = win[8 : 8 + count, cols]
        pre = conv[4:5, cols] + conv[3:4, cols] * here
        for back in range(1, 4):
            pre = pre + conv[3 - back : 4 - back, cols] * (
                win[8 - back : 8 - back + count, cols] * table[:, BACK + back : BACK + back + 1]
            )
        ch_o[:, cols] = here
        pre_o[:, cols] = pre
        mix_o[:, cols] = (pre * sigmoid(pre)).astype(bf16)
    win[0:8, :] = win[count : count + 8, :]

    row, col = iota(0), iota(1)
    left = col < 64
    tri = (row >= col).astype(f32)
    for sub in range(count // CHUNK):
        at = slice(sub * CHUNK, (sub + 1) * CHUNK)
        dt = softplus(step_o[at, :])
        run = jnp.dot(tri, -(dt * hp[1:2, :]), precision=highest, preferred_element_type=f32)
        run_t = run.T
        allowed = (table[at, SEG : SEG + 1] == segr[:, at]) & (row >= col)
        b_in = mix_o[at, width : width + N]
        b_turned = b_in.astype(f32).T.astype(bf16)
        c_out = mix_o[at, width + N :]
        scores = jnp.where(allowed, mm(c_out, b_in, 1, 1), 0.0)
        ending = run[CHUNK - 1 : CHUNK, :]
        entry = jnp.exp(run) * table[at, INHERIT : INHERIT + 1]
        tail = jnp.exp(ending - run) * table[at, TAIL : TAIL + 1]
        factor = jnp.exp(ending) * table[at, LINKED : LINKED + 1][CHUNK - 1 :, :]
        hin_o[sub] = state[...]
        carried[...] = mm_right(c_out, state[...])
        for pair in range(width // LANES):
            lanes = slice(pair * LANES, (pair + 1) * LANES)
            x_pair = mix_o[at, lanes].astype(f32)
            stepped = (x_pair * pair_spread(dt, pair, left)).astype(bf16).astype(f32)
            mixing = []
            for head in (2 * pair, 2 * pair + 1):
                spread = run[:, head : head + 1] - run_t[head : head + 1, :]
                mixing.append((jnp.exp(jnp.minimum(spread, 0.0)) * scores).astype(bf16))
            local = mm(jnp.concatenate(mixing, axis=1), across(stepped, left))
            ssd_o[at, lanes] = (
                local + carried[:, lanes] * pair_spread(entry, pair, left) + skip[:, lanes] * x_pair
            )
            high, low = split(stepped * pair_spread(tail, pair, left))
            weighted[0, :, lanes] = high
            weighted[1, :, lanes] = low
            state[:, lanes] = pair_spread(factor, pair, left) * state[:, lanes]
        state[...] += mm(b_turned, weighted[0]) + mm(b_turned, weighted[1])


def gate_kernel(rank, normed, cot0, cot1, aux, ssd, wg, out_t, gain, gate_o, sg_o, ret_o, sums_o):
    returned = (pick_half(rank, cot0, cot1).astype(f32) * aux[:, LIVE : LIVE + 1]).astype(bf16)
    ret_o[...] = returned
    gate = mm(normed[...], wg[...])
    gate_o[...] = gate
    scaled_grad = mm(returned, out_t[...])
    sg_o[...] = scaled_grad
    gated = ssd[...] * (gate * sigmoid(gate))
    squares = jnp.sum(gated * gated, axis=1, keepdims=True)
    crossed = jnp.sum(scaled_grad * gain[...] * gated, axis=1, keepdims=True)
    lane = lax.broadcasted_iota(jnp.int32, (squares.shape[0], LANES), 1)
    table = jnp.where(lane == 0, squares, jnp.where(lane == 1, crossed, 0.0))
    sums_o[...] = table.T[:8, :]


def norm_kernel(
    rank, gate_r, sg_r, ssd_r, sums_r, out_t, gain, branch_o, scaled_o, dssd_o, dgate_o, gain_o
):
    @pl.when(pl.program_id(0) == 0)
    def _():
        gain_o[...] = jnp.zeros(gain_o.shape, f32)

    gate, ssd, scaled_grad = gate_r[...], ssd_r[...], sg_r[...]
    table = jnp.concatenate([sums_r[...], jnp.zeros((LANES - 8, sums_r.shape[1]), f32)], axis=0)
    sums = table.T
    scale = lax.rsqrt(sums[:, 0:1] / DI + norm_epsilon)
    sig = sigmoid(gate)
    silu = gate * sig
    gated = ssd * silu
    scaled = (gated * scale * gain[...]).astype(bf16)
    scaled_o[...] = scaled
    branch_o[...] = mm(scaled, out_t[...], 1, 1).astype(bf16)
    gain_o[...] += jnp.sum(scaled_grad * gated * scale, axis=0, keepdims=True)
    grad = scale * (scaled_grad * gain[...]) - gated * (scale * scale * scale * (sums[:, 1:2] / DI))
    dssd_o[...] = (grad * silu).astype(bf16)
    dgate_o[...] = (grad * ssd * sig * (1.0 + gate * (1.0 - sig))).astype(bf16)


def scan_back_kernel(
    heads, rank, dssd, mix, pre, ch, ssd, hin, step, conv, skip, hp, aux, segr, heads_of,
    state_in, win_in, carry_in, *rest,
):
    dval_o, dcommon_o, dconv_o, dheads_o, dstate, dtail, carry = rest[-14:-7]
    dmix, dwin, both, flows, entries, weighted, dskip = rest[-7:]
    width = dssd.shape[1]
    channels = width + 2 * N

    @pl.when(pl.program_id(0) == 0)
    def _():
        dwin[CHUNK:, :] = win_in[...]
        dstate[...] = state_in[...]
        carry[...] = carry_in[...]
        dconv_o[...] = jnp.zeros(dconv_o.shape, f32)
        dheads_o[...] = jnp.zeros(dheads_o.shape, f32)
        dskip[...] = jnp.zeros(dskip.shape, f32)

    row, col = iota(0), iota(1)
    left = col < 64
    table = aux[...]
    step_in = step[...]
    dt = softplus(step_in)
    rate = hp[1:2, :]
    tri = (row >= col).astype(f32)
    run = jnp.dot(tri, -(dt * rate), precision=highest, preferred_element_type=f32)
    run_t = run.T
    allowed = (table[:, SEG : SEG + 1] == segr[...]) & (col >= row)
    b_in = mix[:, width : width + N]
    c_out = mix[:, width + N :]
    scores = jnp.where(allowed, mm(b_in, c_out, 1, 1), 0.0)
    ending = run[CHUNK - 1 : CHUNK, :]
    entry = jnp.exp(run) * table[:, INHERIT : INHERIT + 1]
    tail = jnp.exp(ending - run) * table[:, TAIL : TAIL + 1]
    factor = jnp.exp(ending) * table[:, LINKED : LINKED + 1][CHUNK - 1 :, :]
    c_turned = c_out.astype(f32).T.astype(bf16)
    pairs = jnp.zeros((CHUNK, CHUNK), f32)
    state_high, state_low = split(dstate[...])
    flows[...] = mm(b_in, state_high) + mm(b_in, state_low)
    for pair in range(width // LANES):
        lanes = slice(pair * LANES, (pair + 1) * LANES)
        x_pair = mix[:, lanes].astype(f32)
        dy_low = dssd[:, lanes]
        dy = dy_low.astype(f32)
        dt_pair = pair_spread(dt, pair, left)
        tail_pair = pair_spread(tail, pair, left)
        stepped = (x_pair * dt_pair).astype(bf16).astype(f32)
        inner = mm(across(stepped, left), dy_low, 1, 1)
        mixing = []
        for place, head in enumerate((2 * pair, 2 * pair + 1)):
            spread = run_t[head : head + 1, :] - run[:, head : head + 1]
            decays = jnp.exp(jnp.minimum(spread, 0.0))
            mixing.append((decays * scores).astype(bf16))
            pairs = pairs + inner[place * CHUNK : (place + 1) * CHUNK] * decays
        flow = mm(jnp.concatenate(mixing, axis=1), across(dy, left)) + tail_pair * flows[:, lanes]
        dmix[:, lanes] = dt_pair * flow + skip[:, lanes] * dy
        both[0:CHUNK, lanes] = flow * x_pair
        both[CHUNK : 2 * CHUNK, lanes] = dy * (ssd[:, lanes] - skip[:, lanes] * x_pair) - flow * stepped
        dskip[0:1, lanes] += jnp.sum(dy * x_pair, axis=0, keepdims=True)
        high, low = split(pair_spread(entry, pair, left) * dy)
        entries[0, :, lanes] = high
        entries[1, :, lanes] = low
        weighted[:, lanes] = (tail_pair * stepped).astype(bf16)
        dstate[:, lanes] = pair_spread(factor, pair, left) * dstate[:, lanes]
    pairs = jnp.where(allowed, pairs, 0.0)
    dstate[...] += mm(c_turned, entries[0]) + mm(c_turned, entries[1])
    dmix[:, width : width + N] = mm(weighted[...], state_high, 1, 1) + mm_left(pairs, c_out)
    dmix[:, width + N :] = mm(entries[0], hin[0].astype(bf16), 1, 1) + mm_left(pairs, b_in, 0, 0)

    by_head = mm_left(both[...], heads_of[...])
    direct = by_head[0:CHUNK]
    balance = by_head[CHUNK:]
    later = allowed.astype(f32)
    log_grad = jnp.dot(later, balance, precision=highest, preferred_element_type=f32)
    log_grad = log_grad + table[:, NEXT : NEXT + 1] * carry[0:1, :]
    carry[0:1, :] = log_grad[0:1, :]
    step_grad = (direct - rate * log_grad) * sigmoid(step_in)
    dcommon_o[:, 2 * N :] = pltpu.roll(step_grad, heads * rank[0], 1)
    dheads_o[0:1, :] += jnp.sum(step_grad, axis=0, keepdims=True)
    dheads_o[1:2, :] += jnp.sum(-(log_grad * dt * rate), axis=0, keepdims=True)

    for start in range(0, channels, 256):
        cols = slice(start, start + 256)
        value = pre[:, cols]
        sig = sigmoid(value)
        dwin[0:CHUNK, cols] = dmix[:, cols] * (sig * (1.0 + value * (1.0 - sig)))
        here = ch[:, cols]
        own = dwin[0:CHUNK, cols]
        total = conv[3:4, cols] * own
        dconv_o[4:5, cols] += jnp.sum(own, axis=0, keepdims=True)
        dconv_o[3:4, cols] += jnp.sum(own * here, axis=0, keepdims=True)
        for ahead in range(1, 4):
            moved = dwin[ahead : ahead + CHUNK, cols] * table[:, AHEAD + ahead : AHEAD + ahead + 1]
            total = total + conv[3 - ahead : 4 - ahead, cols] * moved
            dconv_o[3 - ahead : 4 - ahead, cols] += jnp.sum(moved * here, axis=0, keepdims=True)
        if start < width:
            dval_o[:, cols] = total.astype(bf16)
        else:
            dcommon_o[:, : 2 * N] = total
    dwin[CHUNK:, :] = dwin[0:8, :]
    dtail[...] = dwin[0:8, :]

    @pl.when(pl.program_id(0) == pl.num_programs(0) - 1)
    def _():
        dheads_o[2:3, :] = mm_left(dskip[...], heads_of[...])[0:1, :]


def scatter_blocks(dp, me, full, keep_o, send_o, cols):
    half = dp // CORES
    block = full.shape[0] // dp
    for place, distance in enumerate(relative_places(dp)):
        start = pl.multiple_of((me[0] ^ distance) * block, block)
        part = full[pl.ds(start, block), :].astype(bf16)
        if place < half:
            keep_o[place, :, cols] = part
        else:
            send_o[place - half, :, cols] = part


def weight_grad_kernel(dp, me, lhs, rhs, keep_o, send_o, turned, full):
    @pl.when(pl.program_id(0) == 0)
    def _():
        turned[...] = lhs[...].T

    full[...] = mm(turned[...], rhs[...])
    scatter_blocks(dp, me, full, keep_o, send_o, slice(None))


def weight_grad(lhs, rhs, dp, dp_rank, skipped=0):
    length, width = rhs.shape[0], rhs.shape[1] - 256 * skipped
    depth = lhs.shape[1]
    block, half = depth // dp, dp // CORES
    piece = pl.BlockSpec((half, block, 256), lambda i, *s: (0, 0, i))
    return call(
        functools.partial(weight_grad_kernel, dp),
        (width // 256,),
        [whole((length, depth)), pl.BlockSpec((length, 256), lambda i, *s: (0, i + skipped))],
        [piece, piece],
        [shape(half, block, width, dtype=bf16)] * 2,
        [pltpu.VMEM((depth, length), bf16), pltpu.VMEM((depth, 256), f32)],
        2 * length * width * depth,
        10,
        scalars=1,
    )(dp_rank, lhs, rhs)


def value_grad_kernel(dp, me, lhs, dval, dcommon, keep_o, send_o, turned, full, wide):
    step = pl.program_id(0)
    last = pl.num_programs(0) - 1

    @pl.when(step == 0)
    def _():
        turned[...] = lhs[...].T

    @pl.when(step < last)
    def _():
        full[...] = mm(turned[...], dval[...])
        cols = pl.ds(pl.multiple_of(step * 256, 256), 256)
        scatter_blocks(dp, me, full, keep_o, send_o, cols)

    @pl.when(step == last)
    def _():
        wide[...] = mm_right(turned[...], dcommon[...])
        cols = slice(keep_o.shape[2] - wide.shape[1], keep_o.shape[2])
        scatter_blocks(dp, me, wide, keep_o, send_o, cols)


def value_grad(lhs, dval, dcommon, dp, dp_rank):
    length, width = dval.shape
    depth, extra = lhs.shape[1], dcommon.shape[1]
    block, half, per = depth // dp, dp // CORES, width // 256
    dims = (half, block, width + extra)
    return call(
        functools.partial(value_grad_kernel, dp),
        (per + 1,),
        [
            whole((length, depth)),
            pl.BlockSpec((length, 256), lambda i, *s: (0, jnp.minimum(i, per - 1))),
            whole((length, extra)),
        ],
        [result(dims), result(dims)],
        [shape(*dims, dtype=bf16)] * 2,
        [
            pltpu.VMEM((depth, length), bf16), pltpu.VMEM((depth, 256), f32),
            pltpu.VMEM((depth, extra), f32),
        ],
        2 * length * (width + 2 * extra) * depth,
        15,
        scalars=1,
    )(dp_rank, lhs, dval, dcommon)


def input_grad_kernel(
    away, rank, dgate, dval, dcommon, tok0, tok1, wg, wv, shw, sent_o, own_o, gain_o
):
    step = pl.program_id(0)

    @pl.when(step == 0)
    def _():
        gain_o[...] = jnp.zeros(gain_o.shape, f32)

    grad = mm(dgate[...], wg[...], 1, 1) + mm(dval[...], wv[...], 1, 1)
    grad = grad + mm_left(dcommon[...], shw[...], 1, 1)
    first = jnp.broadcast_to((step < away).astype(jnp.int32), tok0.shape) == 1
    x = jnp.where(first, tok0[...], tok1[...]).astype(f32)
    inverse = lax.rsqrt(jnp.mean(x * x, axis=1, keepdims=True) + norm_epsilon)
    gain_o[...] += jnp.sum(grad * (x * inverse), axis=0, keepdims=True)

    @pl.when(step < away)
    def _():
        sent_o[...] = grad.astype(bf16)

    @pl.when(step >= away)
    def _():
        own_o[...] = grad


def shards(
    dp, nt,
    residual, cotangent, sequence_ids,
    inner_proj, inner_mean, inner_square,
    shared_proj, shared_mean, shared_square,
    outer_proj, outer_mean, outer_square,
    conv_params, conv_mean, conv_square,
    norm_gains, gains_mean, gains_square,
    head_params, heads_mean, heads_square,
):
    t_rank = lax.axis_index("tensor").astype(jnp.int32)
    d_rank = lax.axis_index("dp").astype(jnp.int32)
    dp_me = d_rank[None]
    t_me = t_rank[None]
    rows_here = residual.shape[0]
    length = rows_here * nt
    width = inner_proj.shape[2]
    heads_here = head_params.shape[1]
    head_size = width // heads_here
    channels = width + 2 * N
    chunks = length // CHUNK
    wide = 2 * CHUNK
    band = min(2 * CHUNK, rows_here)
    per_piece = rows_here // band

    def pieces_of(value):
        return [value] + [swap(value, "tensor", nt, d) for d in range(1, nt)]

    def over_tensor(value, pieces=None):
        pieces = pieces_of(value) if pieces is None else pieces
        if nt == 2:
            first = jnp.concatenate(pieces, axis=0)
            second = jnp.concatenate(pieces[::-1], axis=0)
            return jnp.where(t_rank == 0, first, second)
        stacked = jnp.take(jnp.stack(pieces), jnp.arange(nt) ^ t_rank, axis=0)
        return stacked.reshape((nt * stacked.shape[1],) + stacked.shape[2:])

    kernel_rows, columns = conv_params.shape
    gain_count = norm_gains.shape[0]
    shared_size = shared_proj.size
    exact = jnp.concatenate([conv_params.reshape(-1), norm_gains])
    terms = []
    rest = exact
    for _ in range(3):
        term = lax.optimization_barrier(rest.astype(bf16))
        terms.append(term)
        rest = rest - term.astype(f32)
    common_width = 2 * N + LANES
    shared_rows = shared_proj.shape[0]
    packed = width == 1024 and shared_rows == 32
    if packed:
        wide_shared = jnp.pad(shared_proj.astype(bf16), ((0, 0), (0, common_width - 2 * N - H)))
        flat = jnp.concatenate(terms)
        flat = jnp.pad(flat, (0, 16 * 256 - flat.size)).reshape(16, 256)
        small = jnp.concatenate([wide_shared[:16], wide_shared[16:], flat], axis=1)
        small_rows = 16
    else:
        small = jnp.concatenate([shared_proj.astype(bf16).reshape(-1)] + terms)
        small_rows = -(-small.size // width)
        while small_rows * nt % 16:
            small_rows += 1
        small = jnp.pad(small, (0, small_rows * width - small.size)).reshape(small_rows, width)
    small_pair = over_tensor(small)
    cut_rows = rows_here // 2

    def exchange(value):
        return [swap(value, "tensor", nt, d) for d in range(1, nt)]

    tok_early, tok_late = exchange(residual[:cut_rows]), exchange(residual[cut_rows:])

    block_rows = D // dp
    value_shard = jnp.concatenate([inner_proj[1].astype(bf16), small_pair], axis=0)
    cut = -(-value_shard.shape[0] // 32) * 16
    first_line, *tok_early = tie(gather_line(value_shard[:cut], dp), *tok_early)
    second_shard, first_line = tie(value_shard[cut:], first_line)
    second_line = gather_line(second_shard, dp)
    second_line, ids, *tok_late = tie(second_line, sequence_ids, *tok_late)
    token_pieces = [residual] + [
        jnp.concatenate([early, late], axis=0) for early, late in zip(tok_early, tok_late)
    ]
    first_near = [first_line] + plane_parts(first_line, dp)
    other_shard = jnp.concatenate(
        [inner_proj[0].astype(bf16), outer_proj.T.astype(bf16)], axis=0
    )
    other_shard, second_line = tie(other_shard, second_line)
    other_line = gather_line(other_shard, dp)
    cot_early, cot_late = exchange(cotangent[:cut_rows]), exchange(cotangent[cut_rows:])
    second_line, *rests = tie(second_line, *plane_parts(second_line, dp), *cot_early)
    second_near, cot_early = [second_line] + rests[: 1 - nt], rests[1 - nt :]
    first_all = first_near + [swap(line, "dp", dp, 1) for line in first_near]
    second_all = second_near + [swap(line, "dp", dp, 1) for line in second_near]
    second_all[-1], *cot_late = tie(second_all[-1], *cot_late)
    full = slice(None)
    moves = [(0, block_rows, full, 0, 1, 0, 0)]
    dims = [(dp, block_rows, width)]
    if packed:
        for t in range(nt):
            at = (block_rows + 16 * t, block_rows + 16 * t + 16)
            moves.append(at + (slice(0, common_width), 1, nt, t, 0))
            moves.append(at + (slice(common_width, 2 * common_width), 1, nt, t, 16))
            moves.append(at + (slice(2 * common_width, width), 2, nt, t, 0))
        dims += [(dp * nt, 32, common_width), (dp * nt, 16, 256)]
    else:
        moves.append((block_rows, block_rows + small_rows * nt, full, 1, 1, 0, 0))
        dims += [(dp, small_rows * nt, width)]
    value_w, *small_all = assemble([first_all, second_all], dp, dp_me, moves, dims)
    value_w = value_w.reshape(D, width)

    def halves(pieces):
        if nt == 2:
            return t_me, pieces[0], pieces[1]
        all_rows = over_tensor(None, pieces)
        return jnp.zeros((1,), jnp.int32), all_rows[: length // 2], all_rows[length // 2 :]

    if packed:
        shared_here = small_all[0].reshape(D, common_width)
        exact_all = small_all[1].reshape(dp * nt, -1)[:, : 3 * exact.size].astype(f32)
    else:
        small_all = small_all[0].reshape(dp * nt, small_rows * width)
        shared_here = small_all[:, :shared_size].reshape(D, -1)
        shared_here = jnp.pad(shared_here, ((0, 0), (0, common_width - 2 * N - H)))
        exact_all = small_all[:, shared_size : shared_size + 3 * exact.size].astype(f32)
    exact_all = exact_all.reshape(dp * nt, 3, exact.size)
    exact_all = (exact_all[:, 0] + exact_all[:, 1]) + exact_all[:, 2]
    conv_full = (
        exact_all[:, : kernel_rows * columns]
        .reshape(dp * nt, kernel_rows, columns)
        .transpose(1, 0, 2)
        .reshape(kernel_rows, -1)
    )
    gains_full = exact_all[:, kernel_rows * columns :].reshape(-1)

    pre_gain = gains_full[:D].reshape(1, D)
    post_gain = lax.dynamic_slice_in_dim(gains_full, D + t_rank * width, width).reshape(1, width)
    conv_here = jnp.concatenate(
        [lax.dynamic_slice_in_dim(conv_full, t_rank * width, width, 1), conv_full[:, DI:]], axis=1
    )
    conv_here = jnp.pad(conv_here, ((0, 8 - kernel_rows), (0, 0)))
    head_rows = jnp.stack([head_params[0], jnp.exp(head_params[1])])
    head_rows = jnp.pad(head_rows, ((0, 6), (0, LANES - heads_here)))
    skip = jnp.repeat(head_params[2], head_size).reshape(1, width)
    heads_of = (
        jnp.arange(width)[:, None] // head_size == jnp.arange(LANES)[None, :]
    ).astype(bf16)

    blocked = ids.reshape(chunks, CHUNK)
    ends, firsts = blocked[:, -1], blocked[:, 0]
    none = jnp.full((1,), -1, jnp.int32)
    before = jnp.concatenate([none, ends[:-1]])
    following = jnp.concatenate([firsts[1:], none])
    fills = [jnp.full((o,), -1, jnp.int32) for o in range(1, 4)]
    marks = [ids]
    marks += [jnp.concatenate([fills[o - 1], ids[:-o]]) == ids for o in range(1, 4)]
    marks += [jnp.concatenate([ids[o:], fills[o - 1]]) == ids for o in range(1, 4)]
    marks += [
        (blocked == before[:, None]).reshape(-1),
        (blocked == ends[:, None]).reshape(-1),
        jnp.broadcast_to((ends == before)[:, None], blocked.shape).reshape(-1),
        (blocked == following[:, None]).reshape(-1),
        ids < SEQ_SLOTS,
    ]
    aux = jnp.stack([m.astype(f32) for m in marks] + [jnp.zeros((length,), f32)] * 4, axis=1)
    segr = ids.astype(f32).reshape(1, length)
    aux_cols = aux.shape[1]

    steps = length // wide
    in_half = lambda i: i % (steps // 2)
    value_w, other_line = tie(value_w, other_line)
    cot_pieces = [cotangent] + [
        jnp.concatenate([early, late], axis=0) for early, late in zip(cot_early, cot_late)
    ]
    other_far = swap(other_line, "dp", dp, 1)
    plane = plane_parts(other_line, dp)
    tok_rank, tok0, tok1 = halves(token_pieces)
    normed, chans, pre, mixed, ssd, entering, step_in = call(
        functools.partial(scan_kernel, heads_here),
        (steps,),
        [
            rows(wide, D, in_half), rows(wide, D, in_half), whole((1, D)), whole((D, width)),
            whole((D, common_width)), whole((8, channels)), whole((1, width)), whole((8, LANES)),
            rows(wide, aux_cols), pl.BlockSpec((1, wide), lambda i, r: (0, i)),
        ],
        [
            rows(wide, D), rows(wide, channels), rows(wide, channels), rows(wide, channels),
            rows(wide, width), pl.BlockSpec((wide // CHUNK, N, width), lambda i, r: (i, 0, 0)),
            rows(wide, LANES),
        ],
        [
            shape(length, D, dtype=bf16), shape(length, channels), shape(length, channels),
            shape(length, channels, dtype=bf16), shape(length, width),
            shape(chunks, N, width), shape(length, LANES),
        ],
        [
            pltpu.VMEM((wide + 8, channels), f32), pltpu.VMEM((N, width), f32),
            pltpu.VMEM((CHUNK, width), f32), pltpu.VMEM((2, CHUNK, width), bf16),
        ],
        length * (2 * D * (width + common_width) + 12 * width * CHUNK),
        22,
        scalars=1,
    )(jnp.concatenate([tok_rank, t_me]), tok0, tok1, pre_gain, value_w, shared_here, conv_here, skip, head_rows, aux, segr)

    normed, other_far, *plane = tie(normed, other_far, *plane)
    moves = [
        (0, block_rows, full, 0, 1, 0, 0), (block_rows, 2 * block_rows, full, 1, 1, 0, 0)
    ]
    other_all = [other_line] + plane + [other_far] + [swap(line, "dp", dp, 1) for line in plane]
    gate_w, outer_t = assemble([other_all], dp, dp_me, moves, [(dp, block_rows, width)] * 2)
    gate_w, outer_t = gate_w.reshape(D, width), outer_t.reshape(D, width)
    cot_rank, cot0, cot1 = halves(cot_pieces)
    gate, scaled_grad, returned, sums = call(
        gate_kernel,
        (steps,),
        [
            rows(wide, D), rows(wide, D, in_half), rows(wide, D, in_half), rows(wide, aux_cols),
            rows(wide, width), whole((D, width)), whole((D, width)), whole((1, width)),
        ],
        [rows(wide, width), rows(wide, width), rows(wide, D), pl.BlockSpec((8, wide), lambda i, r: (0, i))],
        [
            shape(length, width), shape(length, width), shape(length, D, dtype=bf16),
            shape(8, length),
        ],
        [],
        4 * length * D * width,
        15,
        scalars=1,
    )(cot_rank, normed, cot0, cot1, aux, ssd, gate_w, outer_t, post_gain)
    distance = 1
    while distance < nt:
        sums = sums + swap(sums, "tensor", nt, distance)
        distance *= 2

    def relative(block, rank):
        return (rank ^ (block // per_piece)) * per_piece + block % per_piece

    def rel_rows(width_here, offset=0):
        return pl.BlockSpec((band, width_here), lambda i, r: (relative(i + offset, r[0]), 0))

    plain = lambda width_here: pl.BlockSpec((band, width_here), lambda i, r: (i, 0))
    branch, scaled, dssd, dgate, post_grad = call(
        norm_kernel,
        (length // band,),
        [
            rel_rows(width), rel_rows(width), rel_rows(width),
            pl.BlockSpec((8, band), lambda i, r: (0, relative(i, r[0]))),
            whole((D, width)), whole((1, width)),
        ],
        [plain(D), rel_rows(width), rel_rows(width), rel_rows(width), result((1, width))],
        [
            shape(length, D, dtype=bf16), shape(length, width, dtype=bf16),
            shape(length, width, dtype=bf16), shape(length, width, dtype=bf16), shape(1, width),
        ],
        [],
        2 * length * D * width,
        15,
        scalars=1,
    )(t_me, gate, scaled_grad, ssd, sums, outer_t, post_gain)
    outer_keep, outer_send = weight_grad(returned, scaled, dp, dp_me)
    dgate, outer_send = tie(dgate, outer_send)
    gate_keep, gate_send = weight_grad(normed, dgate, dp, dp_me)
    outer_line, outer_rest = start_sum(outer_keep, outer_send, dp)
    gate_line, gate_rest = start_sum(gate_keep, gate_send, dp)
    branch = branch.reshape(nt, rows_here, D)
    branch_received = [swap(branch[d], "tensor", nt, d) for d in range(1, nt)]
    dssd, *rests = tie(dssd, *outer_rest, *gate_rest)
    outer_rest, gate_rest = rests[: len(outer_rest)], rests[len(outer_rest) :]
    outer_received = middle_swaps(outer_rest, dp)
    gate_received = middle_swaps(gate_rest, dp)

    state = jnp.zeros((N, width), f32)
    win = jnp.zeros((8, channels), f32)
    carry = jnp.zeros((8, LANES), f32)
    back_parts = []
    filled = []
    top = chunks
    for part, count in enumerate((3, 3, chunks - 6)):
        back = lambda i, top=top: top - 1 - i
        top -= count
        *results, state, win, carry = call(
            functools.partial(scan_back_kernel, heads_here),
            (count,),
            [
                rows(CHUNK, width, back), rows(CHUNK, channels, back), rows(CHUNK, channels, back),
                rows(CHUNK, channels, back), rows(CHUNK, width, back),
                pl.BlockSpec((1, N, width), lambda i, r, back=back: (back(i), 0, 0)),
                rows(CHUNK, LANES, back), whole((8, channels)), whole((1, width)),
                whole((8, LANES)), rows(CHUNK, aux_cols, back),
                pl.BlockSpec((1, CHUNK), lambda i, r, back=back: (0, back(i))),
                whole((width, LANES)),
                whole((N, width)), whole((8, channels)), whole((8, LANES)),
            ]
            + [pl.BlockSpec(memory_space=pl.ANY)] * len(filled),
            [
                rows(CHUNK, width, back), rows(CHUNK, common_width, back), result((8, channels)),
                result((8, LANES)),
                result((N, width)), result((8, channels)), result((8, LANES)),
            ],
            [
                shape(length, width, dtype=bf16), shape(length, common_width),
                shape(8, channels), shape(8, LANES),
                shape(N, width), shape(8, channels), shape(8, LANES),
            ],
            [
                pltpu.VMEM((CHUNK, channels), f32), pltpu.VMEM((CHUNK + 8, channels), f32),
                pltpu.VMEM((2 * CHUNK, width), f32), pltpu.VMEM((CHUNK, width), f32),
                pltpu.VMEM((2, CHUNK, width), bf16), pltpu.VMEM((CHUNK, width), bf16),
                pltpu.VMEM((8, width), f32),
            ],
            count * CHUNK * 30 * width * CHUNK,
            14,
            scalars=1,
            aliases={17: 0, 18: 1} if filled else None,
        )(
            t_me, dssd, mixed, pre, chans, ssd, entering, step_in, conv_here, skip, head_rows, aux, segr,
            heads_of, state, win, carry, *filled,
        )
        filled = results[:2]
        back_parts.append(results[2:])
        if part == 0:
            state, outer_line, *outer_received = tie(state, outer_line, *outer_received)
            outer_block, outer_far = middle_sum(outer_line, outer_received)
            outer_far = high_swaps(outer_far, dp)
        if part == 1:
            state, gate_line, *rests = tie(
                state, gate_line, *branch_received, *gate_received, *outer_far
            )
            branch_received = rests[: nt - 1]
            gate_received, outer_far = rests[nt - 1 : -len(outer_far)], rests[-len(outer_far) :]
            gate_block, gate_far = middle_sum(gate_line, gate_received)
            gate_far = high_swaps(gate_far, dp)
    dval, dcommon = filled
    dval, *gate_far = tie(dval, *gate_far)

    branch_sum = branch[0].astype(f32)
    for piece in branch_received:
        branch_sum = branch_sum + piece.astype(f32)
    live_here = lax.dynamic_slice_in_dim(aux[:, LIVE], t_rank * rows_here, rows_here)
    tokens = residual.astype(f32)
    block_out = (tokens + branch_sum * live_here[:, None]).astype(bf16)

    away = (nt - 1) * per_piece

    def input_grad(others, dgate):
        away_rows = lambda width_here: pl.BlockSpec(
            (band, width_here), lambda i, r: (jnp.minimum(i, away - 1), 0)
        )
        own_rows = lambda width_here: pl.BlockSpec(
            (band, width_here), lambda i, r: (jnp.maximum(i - away, 0), 0)
        )
        turned = lambda i: lax.rem(i + per_piece, nt * per_piece)
        here = lambda width_here: pl.BlockSpec(
            (band, width_here), lambda i, r: (relative(turned(i), r[0]), 0)
        )
        return call(
            functools.partial(input_grad_kernel, away),
            (nt * per_piece,),
            [
                here(width), here(width), here(common_width), away_rows(D), own_rows(D),
                whole((D, width)), whole((D, width)), whole((D, common_width)),
            ],
            [away_rows(D), own_rows(D), result((1, D))],
            [shape((nt - 1) * rows_here, D, dtype=bf16), shape(rows_here, D), shape(1, D)],
            [],
            4 * length * D * (width + common_width),
            24,
            scalars=1,
        )(t_me, dgate, dval, dcommon, others, residual, gate_w, value_w, shared_here)

    others = token_pieces[1] if nt == 2 else jnp.concatenate(token_pieces[1:], axis=0)
    sent, own, pre_grad = input_grad(others, dgate)
    sent, dval = tie(sent, dval)
    sent = sent.reshape(nt - 1, rows_here, D)
    received = [swap(sent[d - 1], "tensor", nt, d) for d in range(1, nt)]
    keep, send = value_grad(normed, dval, dcommon, dp, dp_me)
    line, part = start_sum(keep, send, dp)
    line, *part = tie(line, *part)
    crossing = middle_swaps(part, dp)
    small_grads = [item for each_part in back_parts for item in each_part]

    dconv, dheads = [sum(small_grads[at::2]) for at in range(2)]
    conv_grad = lax.dynamic_update_slice(
        jnp.pad(dconv[:kernel_rows, width:], ((0, 0), (DI, 0))),
        dconv[:kernel_rows, :width],
        (0, t_rank * width),
    )
    post_all = lax.dynamic_update_slice(
        jnp.zeros((1, DI), f32), post_grad, (0, t_rank * width)
    )
    head_grad = dheads[:3, :heads_here]
    head_all = lax.dynamic_update_slice(
        jnp.zeros((3, H), f32), head_grad, (0, t_rank * heads_here)
    )
    vector = jnp.concatenate(
        [
            conv_grad.reshape(1, -1), pre_grad, post_all, head_all.reshape(1, -1),
        ],
        axis=1,
    )
    for stage, (axis, size, distance) in enumerate(sum_stages(dp, nt)):
        vector = vector + swap(vector, axis, size, distance)
        if stage == 0:
            vector, line, *crossing = tie(vector, line, *crossing)
            block, far = middle_sum(line, crossing)
            far = high_swaps(far, dp)
        if stage == 2:
            vector, outer_block, gate_block, *received = tie(
                vector, outer_block, gate_block, *received
            )
            outer_part = high_sum(outer_block, outer_far)
            gate_part = high_sum(gate_block, gate_far)
        if stage == 3:
            vector, *far = tie(vector, *far)
            value_sum = high_sum(block, far)
    shared_sum = value_sum[:, width:].reshape(nt, shared_rows, common_width)
    shared_mine = lax.dynamic_index_in_dim(shared_sum, t_rank, 0, False)
    for d in range(1, nt):
        piece = lax.dynamic_index_in_dim(shared_sum, t_rank ^ d, 0, False)
        shared_mine = shared_mine + swap(piece, "tensor", nt, d)
    shared_part = shared_mine[:, : 2 * N + H]
    value_part = value_sum[:, :width]
    conv_size = kernel_rows * (DI + 2 * N)
    place = d_rank * nt + t_rank
    conv_part = lax.dynamic_slice_in_dim(
        vector[0, :conv_size].reshape(kernel_rows, -1), place * columns, columns, 1
    )
    gains_part = lax.dynamic_slice_in_dim(vector[0], conv_size + place * gain_count, gain_count)
    heads_part = lax.dynamic_slice_in_dim(
        vector[0, conv_size + D + DI :].reshape(3, H), t_rank * heads_here, heads_here, 1
    )

    normed_grad = own
    for piece in received:
        normed_grad = normed_grad + piece.astype(f32)
    inverse = lax.rsqrt(jnp.mean(tokens * tokens, axis=1, keepdims=True) + norm_epsilon)
    normal_tokens = tokens * inverse
    normal_grad = normed_grad * pre_gain
    centered = normal_grad - normal_tokens * jnp.mean(
        normal_grad * normal_tokens, axis=1, keepdims=True
    )
    residual_grad = (cotangent.astype(f32) + inverse * centered).astype(bf16)

    inner_new = adam_step(
        inner_proj, inner_mean, inner_square, jnp.stack([gate_part, value_part]),
        rate_matrix, weight_decay,
    )
    shared_new = adam_step(
        shared_proj, shared_mean, shared_square, shared_part.reshape(shared_proj.shape),
        rate_matrix, weight_decay,
    )
    outer_new = adam_step(
        outer_proj, outer_mean, outer_square, outer_part.T, rate_matrix, weight_decay
    )
    conv_new = adam_step(conv_params, conv_mean, conv_square, conv_part, rate_vector, 0.0)
    gains_new = adam_step(norm_gains, gains_mean, gains_square, gains_part, rate_vector, 0.0)
    heads_new = adam_step(head_params, heads_mean, heads_square, heads_part, rate_heads, 0.0)
    return (
        (block_out, residual_grad)
        + inner_new + shared_new + outer_new + conv_new + gains_new + heads_new
    )


def solution(mesh):
    return jax.shard_map(
        functools.partial(shards, mesh.shape["dp"], mesh.shape["tensor"]),
        mesh=mesh,
        in_specs=(
            P(("dp", "tensor"), None),
            P(("dp", "tensor"), None),
            P("dp"),
            P(None, "dp", "tensor"),
            P(None, "dp", "tensor"),
            P(None, "dp", "tensor"),
            P(("dp", "tensor"), None),
            P(("dp", "tensor"), None),
            P(("dp", "tensor"), None),
            P("tensor", "dp"),
            P("tensor", "dp"),
            P("tensor", "dp"),
            P(None, ("dp", "tensor")),
            P(None, ("dp", "tensor")),
            P(None, ("dp", "tensor")),
            P(("dp", "tensor")),
            P(("dp", "tensor")),
            P(("dp", "tensor")),
            P(None, "tensor"),
            P(None, "tensor"),
            P(None, "tensor"),
        ),
        out_specs=(
            P(("dp", "tensor"), None),
            P(("dp", "tensor"), None),
            P(None, "dp", "tensor"),
            P(None, "dp", "tensor"),
            P(None, "dp", "tensor"),
            P(("dp", "tensor"), None),
            P(("dp", "tensor"), None),
            P(("dp", "tensor"), None),
            P("tensor", "dp"),
            P("tensor", "dp"),
            P("tensor", "dp"),
            P(None, ("dp", "tensor")),
            P(None, ("dp", "tensor")),
            P(None, ("dp", "tensor")),
            P(("dp", "tensor")),
            P(("dp", "tensor")),
            P(("dp", "tensor")),
            P(None, "tensor"),
            P(None, "tensor"),
            P(None, "tensor"),
        ),
        check_vma=False,
    )
```

```python
import functools

import jax
import jax.numpy as jnp
from jax import lax
from jax.experimental import pallas as pl
from jax.experimental.pallas import tpu as pltpu
from jax.sharding import PartitionSpec as P

D = 1024
H = 32
N = 128
DI = 2048
SEQ_SLOTS = 4
STEP = 10
CHUNK = 128
LANES = 128
CORES = 2
HIGH_AXIS = 4

highest = lax.Precision.HIGHEST
f32 = jnp.float32
bf16 = jnp.bfloat16
norm_epsilon = 1e-05
beta_first = 0.9
beta_second = 0.95
adam_epsilon = 1e-08
weight_decay = 0.1
rate_matrix = 0.02
rate_vector = 0.3
rate_heads = 1.0

SEG, BACK, AHEAD, INHERIT, TAIL, LINKED, NEXT, LIVE = 0, 0, 3, 7, 8, 9, 10, 11


def adam_step(weight, moment, square, gradient, rate, decay):
    moment_next = beta_first * moment + (1.0 - beta_first) * gradient
    square_next = beta_second * square + (1.0 - beta_second) * gradient * gradient
    moment_hat = moment_next / (1.0 - beta_first**STEP)
    square_hat = square_next / (1.0 - beta_second**STEP)
    weight_next = weight - rate * (
        moment_hat / (jnp.sqrt(square_hat) + adam_epsilon) + decay * weight
    )
    return (weight_next, moment_next, square_next)


def swap(value, axis, size, distance):
    return lax.ppermute(value, axis, [(i, i ^ distance) for i in range(size)])


def tie(*values):
    return lax.optimization_barrier(values)


def axis_parts(dp):
    high = HIGH_AXIS
    middle = dp // (CORES * high)
    return high, middle


def gather_line(shard, dp):
    high, middle = axis_parts(dp)
    pieces = [shard[None]]
    for step in range(1, high):
        pieces.append(swap(shard, "dp", dp, step * middle * CORES)[None])
    return jnp.concatenate(pieces, axis=0)


def plane_parts(line, dp):
    return [swap(line, "dp", dp, step * CORES) for step in range(1, axis_parts(dp)[1])]


def start_sum(keep, send, dp):
    high, middle = axis_parts(dp)
    other = swap(send, "dp", dp, 1)
    parts = [slice(step * high, (step + 1) * high) for step in range(middle)]
    line = keep[parts[0]].astype(f32) + other[parts[0]].astype(f32)
    rest = [(keep[at].astype(f32) + other[at].astype(f32)).astype(bf16) for at in parts[1:]]
    return line, rest


def middle_swaps(rest, dp):
    return [swap(part, "dp", dp, (step + 1) * CORES) for step, part in enumerate(rest)]


def middle_sum(line, received):
    for part in received:
        line = line + part.astype(f32)
    return line[0], [part.astype(bf16) for part in line[1:]]


def high_swaps(rest, dp):
    middle = axis_parts(dp)[1]
    return [swap(part, "dp", dp, (step + 1) * middle * CORES) for step, part in enumerate(rest)]


def high_sum(block, received):
    for part in received:
        block = block + part.astype(f32)
    return block


def sum_stages(dp, nt):
    stages = [("tensor", nt, 1 << bit) for bit in range((nt - 1).bit_length())]
    return stages + [("dp", dp, 1 << bit) for bit in range((dp - 1).bit_length())]


def relative_places(dp):
    high, middle = axis_parts(dp)
    return [
        (h * middle + m) * CORES + c for c in range(CORES) for m in range(middle) for h in range(high)
    ]


def call(kernel, grid, in_specs, out_specs, out_shape, scratch, flops, mib, scalars=0, aliases=None):
    params = pltpu.CompilerParams(vmem_limit_bytes=mib * 1024 * 1024)
    moved = sum(2 * s.dtype.itemsize * s.size for s in jax.tree.leaves(out_shape))
    return pl.pallas_call(
        kernel,
        grid_spec=pltpu.PrefetchScalarGridSpec(
            num_scalar_prefetch=scalars,
            grid=grid,
            in_specs=in_specs,
            out_specs=out_specs,
            scratch_shapes=scratch,
        ),
        out_shape=out_shape,
        compiler_params=params,
        input_output_aliases=aliases or {},
        cost_estimate=pl.CostEstimate(
            flops=int(flops) // 16, bytes_accessed=int(moved) // 16, transcendentals=0
        ),
    )


def whole(shape):
    return pl.BlockSpec(shape, lambda *i: (0,) * len(shape), pipeline_mode=pl.Buffered(1))


def result(shape):
    return pl.BlockSpec(shape, lambda *i: (0,) * len(shape))


def rows(count, width, index=lambda i: i):
    return pl.BlockSpec((count, width), lambda i, *s: (index(i), 0))


def shape(*dims, dtype=f32):
    return jax.ShapeDtypeStruct(dims, dtype)


def split(value):
    high = value.astype(bf16)
    return high, (value - high.astype(f32)).astype(bf16)


def mm(a, b, ca=1, cb=0):
    return lax.dot_general(a, b, (((ca,), (cb,)), ((), ())), preferred_element_type=f32)


def mm_left(value, exact, ca=1, cb=0):
    high, low = split(value)
    return mm(high, exact, ca, cb) + mm(low, exact, ca, cb)


def mm_right(exact, value, ca=1, cb=0):
    high, low = split(value)
    return mm(exact, high, ca, cb) + mm(exact, low, ca, cb)


def mm_both(a, b, ca=1, cb=0):
    a_high, a_low = split(a)
    b_high, b_low = split(b)
    return mm(a_high, b_high, ca, cb) + mm(a_low, b_high, ca, cb) + mm(a_high, b_low, ca, cb)


def sigmoid(value):
    return 0.5 * jnp.tanh(0.5 * value) + 0.5


def softplus(value):
    return jnp.maximum(value, 0.0) + jnp.log1p(jnp.exp(-jnp.abs(value)))


def iota(axis):
    return lax.broadcasted_iota(jnp.int32, (CHUNK, LANES), axis)


def pair_spread(tile, pair, left):
    rows_here = tile.shape[0]
    return jnp.where(
        left[:rows_here],
        jnp.broadcast_to(tile[:, 2 * pair : 2 * pair + 1], (rows_here, LANES)),
        jnp.broadcast_to(tile[:, 2 * pair + 1 : 2 * pair + 2], (rows_here, LANES)),
    )


def assemble_kernel(dp, parts, moves, me, *refs):
    high, middle = axis_parts(dp)
    each = CORES * middle
    sources, outs = refs[: parts * each], refs[parts * each :]
    for place, distance in enumerate(relative_places(dp)):
        block = me[0] ^ distance
        base = 0
        for part in range(parts):
            source, at = sources[part * each + place // high], place % high
            end = base + source.shape[1]
            for first, last, lanes, out, count, extra, row in moves:
                low, top = max(base, first), min(end, last)
                if low < top:
                    outs[out][
                        block * count + extra, row + low - first : row + top - first, :
                    ] = source[at, low - base : top - base, lanes]
            base = end


def assemble(parts, dp, dp_rank, moves, shapes):
    vmem = pl.BlockSpec(memory_space=pltpu.VMEM)
    lines = [line for part in parts for line in part]
    moved = sum(2 * line.size * line.dtype.itemsize for line in lines)
    return pl.pallas_call(
        functools.partial(assemble_kernel, dp, len(parts), moves),
        in_specs=[pl.BlockSpec(memory_space=pltpu.SMEM)] + [vmem] * len(lines),
        out_specs=[vmem] * len(shapes),
        out_shape=[shape(*dims, dtype=bf16) for dims in shapes],
        compiler_params=pltpu.CompilerParams(vmem_limit_bytes=16 * 1024 * 1024),
        cost_estimate=pl.CostEstimate(flops=0, bytes_accessed=moved, transcendentals=0),
    )(dp_rank, *lines)


def pick_half(rank, first, second):
    half = (2 * pl.program_id(0)) // pl.num_programs(0)
    own = (half == rank[0]).astype(jnp.int32)
    return jnp.where(jnp.broadcast_to(own, first.shape) == 1, first[...], second[...])


def across(pair, left):
    return jnp.concatenate(
        [jnp.where(left, pair, 0.0), jnp.where(left, 0.0, pair)], axis=0
    ).astype(bf16)


def scan_kernel(
    heads, rank, tok0, tok1, gain, wv, shw, conv, skip, hp, aux, segr,
    normed_o, ch_o, pre_o, mix_o, ssd_o, hin_o, step_o,
    win, state, carried, weighted,
):
    count = tok0.shape[0]
    width = wv.shape[1]
    channels = width + 2 * N

    @pl.when(pl.program_id(0) == 0)
    def _():
        win[0:8, :] = jnp.zeros((8, channels), f32)
        state[...] = jnp.zeros(state.shape, f32)

    x = pick_half(rank, tok0, tok1).astype(f32)
    inverse = lax.rsqrt(jnp.mean(x * x, axis=1, keepdims=True) + norm_epsilon)
    normed = (x * inverse * gain[...]).astype(bf16)
    normed_o[...] = normed
    win[8 : 8 + count, :width] = mm(normed, wv[...])
    common = mm(normed, shw[...])
    win[8 : 8 + count, width:] = common[:, : 2 * N]
    turn = lax.rem(LANES - heads * rank[1], LANES)
    step_o[...] = pltpu.roll(common[:, 2 * N :], turn, 1) + hp[0:1, :]
    table = aux[...]
    for start in range(0, channels, 256):
        cols = slice(start, start + 256)
        here = win[8 : 8 + count, cols]
        pre = conv[4:5, cols] + conv[3:4, cols] * here
        for back in range(1, 4):
            pre = pre + conv[3 - back : 4 - back, cols] * (
                win[8 - back : 8 - back + count, cols] * table[:, BACK + back : BACK + back + 1]
            )
        ch_o[:, cols] = here
        pre_o[:, cols] = pre
        mix_o[:, cols] = (pre * sigmoid(pre)).astype(bf16)
    win[0:8, :] = win[count : count + 8, :]

    row, col = iota(0), iota(1)
    left = col < 64
    tri = (row >= col).astype(f32)
    for sub in range(count // CHUNK):
        at = slice(sub * CHUNK, (sub + 1) * CHUNK)
        dt = softplus(step_o[at, :])
        run = jnp.dot(tri, -(dt * hp[1:2, :]), precision=highest, preferred_element_type=f32)
        run_t = run.T
        allowed = (table[at, SEG : SEG + 1] == segr[:, at]) & (row >= col)
        b_in = mix_o[at, width : width + N]
        b_turned = b_in.astype(f32).T.astype(bf16)
        c_out = mix_o[at, width + N :]
        scores = jnp.where(allowed, mm(c_out, b_in, 1, 1), 0.0)
        ending = run[CHUNK - 1 : CHUNK, :]
        entry = jnp.exp(run) * table[at, INHERIT : INHERIT + 1]
        tail = jnp.exp(ending - run) * table[at, TAIL : TAIL + 1]
        factor = jnp.exp(ending) * table[at, LINKED : LINKED + 1][CHUNK - 1 :, :]
        hin_o[sub] = state[...]
        carried[...] = mm_right(c_out, state[...])
        for pair in range(width // LANES):
            lanes = slice(pair * LANES, (pair + 1) * LANES)
            x_pair = mix_o[at, lanes].astype(f32)
            stepped = (x_pair * pair_spread(dt, pair, left)).astype(bf16).astype(f32)
            mixing = []
            for head in (2 * pair, 2 * pair + 1):
                spread = run[:, head : head + 1] - run_t[head : head + 1, :]
                mixing.append((jnp.exp(jnp.minimum(spread, 0.0)) * scores).astype(bf16))
            local = mm(jnp.concatenate(mixing, axis=1), across(stepped, left))
            ssd_o[at, lanes] = (
                local + carried[:, lanes] * pair_spread(entry, pair, left) + skip[:, lanes] * x_pair
            )
            high, low = split(stepped * pair_spread(tail, pair, left))
            weighted[0, :, lanes] = high
            weighted[1, :, lanes] = low
            state[:, lanes] = pair_spread(factor, pair, left) * state[:, lanes]
        state[...] += mm(b_turned, weighted[0]) + mm(b_turned, weighted[1])


def gate_kernel(rank, normed, cot0, cot1, aux, ssd, wg, out_t, gain, gate_o, sg_o, ret_o, sums_o):
    returned = (pick_half(rank, cot0, cot1).astype(f32) * aux[:, LIVE : LIVE + 1]).astype(bf16)
    ret_o[...] = returned
    gate = mm(normed[...], wg[...])
    gate_o[...] = gate
    scaled_grad = mm(returned, out_t[...])
    sg_o[...] = scaled_grad
    gated = ssd[...] * (gate * sigmoid(gate))
    squares = jnp.sum(gated * gated, axis=1, keepdims=True)
    crossed = jnp.sum(scaled_grad * gain[...] * gated, axis=1, keepdims=True)
    lane = lax.broadcasted_iota(jnp.int32, (squares.shape[0], LANES), 1)
    table = jnp.where(lane == 0, squares, jnp.where(lane == 1, crossed, 0.0))
    sums_o[...] = table.T[:8, :]


def norm_kernel(
    rank, gate_r, sg_r, ssd_r, sums_r, out_t, gain, branch_o, scaled_o, dssd_o, dgate_o, gain_o
):
    @pl.when(pl.program_id(0) == 0)
    def _():
        gain_o[...] = jnp.zeros(gain_o.shape, f32)

    gate, ssd, scaled_grad = gate_r[...], ssd_r[...], sg_r[...]
    table = jnp.concatenate([sums_r[...], jnp.zeros((LANES - 8, sums_r.shape[1]), f32)], axis=0)
    sums = table.T
    scale = lax.rsqrt(sums[:, 0:1] / DI + norm_epsilon)
    sig = sigmoid(gate)
    silu = gate * sig
    gated = ssd * silu
    scaled = (gated * scale * gain[...]).astype(bf16)
    scaled_o[...] = scaled
    branch_o[...] = mm(scaled, out_t[...], 1, 1).astype(bf16)
    gain_o[...] += jnp.sum(scaled_grad * gated * scale, axis=0, keepdims=True)
    grad = scale * (scaled_grad * gain[...]) - gated * (scale * scale * scale * (sums[:, 1:2] / DI))
    dssd_o[...] = (grad * silu).astype(bf16)
    dgate_o[...] = (grad * ssd * sig * (1.0 + gate * (1.0 - sig))).astype(bf16)


def scan_back_kernel(
    heads, rank, dssd, mix, pre, ch, ssd, hin, step, conv, skip, hp, aux, segr, heads_of,
    state_in, win_in, carry_in, *rest,
):
    dval_o, dcommon_o, dconv_o, dheads_o, dstate, dtail, carry = rest[-14:-7]
    dmix, dwin, both, flows, entries, weighted, dskip = rest[-7:]
    width = dssd.shape[1]
    channels = width + 2 * N

    @pl.when(pl.program_id(0) == 0)
    def _():
        dwin[CHUNK:, :] = win_in[...]
        dstate[...] = state_in[...]
        carry[...] = carry_in[...]
        dconv_o[...] = jnp.zeros(dconv_o.shape, f32)
        dheads_o[...] = jnp.zeros(dheads_o.shape, f32)
        dskip[...] = jnp.zeros(dskip.shape, f32)

    row, col = iota(0), iota(1)
    left = col < 64
    table = aux[...]
    step_in = step[...]
    dt = softplus(step_in)
    rate = hp[1:2, :]
    tri = (row >= col).astype(f32)
    run = jnp.dot(tri, -(dt * rate), precision=highest, preferred_element_type=f32)
    run_t = run.T
    allowed = (table[:, SEG : SEG + 1] == segr[...]) & (col >= row)
    b_in = mix[:, width : width + N]
    c_out = mix[:, width + N :]
    scores = jnp.where(allowed, mm(b_in, c_out, 1, 1), 0.0)
    ending = run[CHUNK - 1 : CHUNK, :]
    entry = jnp.exp(run) * table[:, INHERIT : INHERIT + 1]
    tail = jnp.exp(ending - run) * table[:, TAIL : TAIL + 1]
    factor = jnp.exp(ending) * table[:, LINKED : LINKED + 1][CHUNK - 1 :, :]
    c_turned = c_out.astype(f32).T.astype(bf16)
    pairs = jnp.zeros((CHUNK, CHUNK), f32)
    state_high, state_low = split(dstate[...])
    flows[...] = mm(b_in, state_high) + mm(b_in, state_low)
    for pair in range(width // LANES):
        lanes = slice(pair * LANES, (pair + 1) * LANES)
        x_pair = mix[:, lanes].astype(f32)
        dy_low = dssd[:, lanes]
        dy = dy_low.astype(f32)
        dt_pair = pair_spread(dt, pair, left)
        tail_pair = pair_spread(tail, pair, left)
        stepped = (x_pair * dt_pair).astype(bf16).astype(f32)
        inner = mm(across(stepped, left), dy_low, 1, 1)
        mixing = []
        for place, head in enumerate((2 * pair, 2 * pair + 1)):
            spread = run_t[head : head + 1, :] - run[:, head : head + 1]
            decays = jnp.exp(jnp.minimum(spread, 0.0))
            mixing.append((decays * scores).astype(bf16))
            pairs = pairs + inner[place * CHUNK : (place + 1) * CHUNK] * decays
        flow = mm(jnp.concatenate(mixing, axis=1), across(dy, left)) + tail_pair * flows[:, lanes]
        dmix[:, lanes] = dt_pair * flow + skip[:, lanes] * dy
        both[0:CHUNK, lanes] = flow * x_pair
        both[CHUNK : 2 * CHUNK, lanes] = dy * (ssd[:, lanes] - skip[:, lanes] * x_pair) - flow * stepped
        dskip[0:1, lanes] += jnp.sum(dy * x_pair, axis=0, keepdims=True)
        high, low = split(pair_spread(entry, pair, left) * dy)
        entries[0, :, lanes] = high
        entries[1, :, lanes] = low
        weighted[:, lanes] = (tail_pair * stepped).astype(bf16)
        dstate[:, lanes] = pair_spread(factor, pair, left) * dstate[:, lanes]
    pairs = jnp.where(allowed, pairs, 0.0)
    dstate[...] += mm(c_turned, entries[0]) + mm(c_turned, entries[1])
    dmix[:, width : width + N] = mm(weighted[...], state_high, 1, 1) + mm_left(pairs, c_out)
    dmix[:, width + N :] = mm(entries[0], hin[0].astype(bf16), 1, 1) + mm_left(pairs, b_in, 0, 0)

    by_head = mm_left(both[...], heads_of[...])
    direct = by_head[0:CHUNK]
    balance = by_head[CHUNK:]
    later = allowed.astype(f32)
    log_grad = jnp.dot(later, balance, precision=highest, preferred_element_type=f32)
    log_grad = log_grad + table[:, NEXT : NEXT + 1] * carry[0:1, :]
    carry[0:1, :] = log_grad[0:1, :]
    step_grad = (direct - rate * log_grad) * sigmoid(step_in)
    dcommon_o[:, 2 * N :] = pltpu.roll(step_grad, heads * rank[0], 1)
    dheads_o[0:1, :] += jnp.sum(step_grad, axis=0, keepdims=True)
    dheads_o[1:2, :] += jnp.sum(-(log_grad * dt * rate), axis=0, keepdims=True)

    for start in range(0, channels, 256):
        cols = slice(start, start + 256)
        value = pre[:, cols]
        sig = sigmoid(value)
        dwin[0:CHUNK, cols] = dmix[:, cols] * (sig * (1.0 + value * (1.0 - sig)))
        here = ch[:, cols]
        own = dwin[0:CHUNK, cols]
        total = conv[3:4, cols] * own
        dconv_o[4:5, cols] += jnp.sum(own, axis=0, keepdims=True)
        dconv_o[3:4, cols] += jnp.sum(own * here, axis=0, keepdims=True)
        for ahead in range(1, 4):
            moved = dwin[ahead : ahead + CHUNK, cols] * table[:, AHEAD + ahead : AHEAD + ahead + 1]
            total = total + conv[3 - ahead : 4 - ahead, cols] * moved
            dconv_o[3 - ahead : 4 - ahead, cols] += jnp.sum(moved * here, axis=0, keepdims=True)
        if start < width:
            dval_o[:, cols] = total.astype(bf16)
        else:
            dcommon_o[:, : 2 * N] = total
    dwin[CHUNK:, :] = dwin[0:8, :]
    dtail[...] = dwin[0:8, :]

    @pl.when(pl.program_id(0) == pl.num_programs(0) - 1)
    def _():
        dheads_o[2:3, :] = mm_left(dskip[...], heads_of[...])[0:1, :]


def scatter_blocks(dp, me, full, keep_o, send_o, cols):
    half = dp // CORES
    block = full.shape[0] // dp
    for place, distance in enumerate(relative_places(dp)):
        start = pl.multiple_of((me[0] ^ distance) * block, block)
        part = full[pl.ds(start, block), :].astype(bf16)
        if place < half:
            keep_o[place, :, cols] = part
        else:
            send_o[place - half, :, cols] = part


def weight_grad_kernel(dp, me, lhs, rhs, keep_o, send_o, turned, full):
    @pl.when(pl.program_id(0) == 0)
    def _():
        turned[...] = lhs[...].T

    full[...] = mm(turned[...], rhs[...])
    scatter_blocks(dp, me, full, keep_o, send_o, slice(None))


def weight_grad(lhs, rhs, dp, dp_rank, skipped=0):
    length, width = rhs.shape[0], rhs.shape[1] - 256 * skipped
    depth = lhs.shape[1]
    block, half = depth // dp, dp // CORES
    piece = pl.BlockSpec((half, block, 256), lambda i, *s: (0, 0, i))
    return call(
        functools.partial(weight_grad_kernel, dp),
        (width // 256,),
        [whole((length, depth)), pl.BlockSpec((length, 256), lambda i, *s: (0, i + skipped))],
        [piece, piece],
        [shape(half, block, width, dtype=bf16)] * 2,
        [pltpu.VMEM((depth, length), bf16), pltpu.VMEM((depth, 256), f32)],
        2 * length * width * depth,
        10,
        scalars=1,
    )(dp_rank, lhs, rhs)


def value_grad_kernel(dp, me, lhs, dval, dcommon, keep_o, send_o, turned, full, wide):
    step = pl.program_id(0)
    last = pl.num_programs(0) - 1

    @pl.when(step == 0)
    def _():
        turned[...] = lhs[...].T

    @pl.when(step < last)
    def _():
        full[...] = mm(turned[...], dval[...])
        cols = pl.ds(pl.multiple_of(step * 256, 256), 256)
        scatter_blocks(dp, me, full, keep_o, send_o, cols)

    @pl.when(step == last)
    def _():
        wide[...] = mm_right(turned[...], dcommon[...])
        cols = slice(keep_o.shape[2] - wide.shape[1], keep_o.shape[2])
        scatter_blocks(dp, me, wide, keep_o, send_o, cols)


def value_grad(lhs, dval, dcommon, dp, dp_rank):
    length, width = dval.shape
    depth, extra = lhs.shape[1], dcommon.shape[1]
    block, half, per = depth // dp, dp // CORES, width // 256
    dims = (half, block, width + extra)
    return call(
        functools.partial(value_grad_kernel, dp),
        (per + 1,),
        [
            whole((length, depth)),
            pl.BlockSpec((length, 256), lambda i, *s: (0, jnp.minimum(i, per - 1))),
            whole((length, extra)),
        ],
        [result(dims), result(dims)],
        [shape(*dims, dtype=bf16)] * 2,
        [
            pltpu.VMEM((depth, length), bf16), pltpu.VMEM((depth, 256), f32),
            pltpu.VMEM((depth, extra), f32),
        ],
        2 * length * (width + 2 * extra) * depth,
        15,
        scalars=1,
    )(dp_rank, lhs, dval, dcommon)


def input_grad_kernel(
    away, rank, dgate, dval, dcommon, tok0, tok1, wg, wv, shw, sent_o, own_o, gain_o
):
    step = pl.program_id(0)

    @pl.when(step == 0)
    def _():
        gain_o[...] = jnp.zeros(gain_o.shape, f32)

    grad = mm(dgate[...], wg[...], 1, 1) + mm(dval[...], wv[...], 1, 1)
    grad = grad + mm_left(dcommon[...], shw[...], 1, 1)
    first = jnp.broadcast_to((step < away).astype(jnp.int32), tok0.shape) == 1
    x = jnp.where(first, tok0[...], tok1[...]).astype(f32)
    inverse = lax.rsqrt(jnp.mean(x * x, axis=1, keepdims=True) + norm_epsilon)
    gain_o[...] += jnp.sum(grad * (x * inverse), axis=0, keepdims=True)

    @pl.when(step < away)
    def _():
        sent_o[...] = grad.astype(bf16)

    @pl.when(step >= away)
    def _():
        own_o[...] = grad


def shards(
    dp, nt,
    residual, cotangent, sequence_ids,
    inner_proj, inner_mean, inner_square,
    shared_proj, shared_mean, shared_square,
    outer_proj, outer_mean, outer_square,
    conv_params, conv_mean, conv_square,
    norm_gains, gains_mean, gains_square,
    head_params, heads_mean, heads_square,
):
    t_rank = lax.axis_index("tensor").astype(jnp.int32)
    d_rank = lax.axis_index("dp").astype(jnp.int32)
    dp_me = d_rank[None]
    t_me = t_rank[None]
    rows_here = residual.shape[0]
    length = rows_here * nt
    width = inner_proj.shape[2]
    heads_here = head_params.shape[1]
    head_size = width // heads_here
    channels = width + 2 * N
    chunks = length // CHUNK
    wide = 2 * CHUNK
    band = min(2 * CHUNK, rows_here)
    per_piece = rows_here // band

    def pieces_of(value):
        return [value] + [swap(value, "tensor", nt, d) for d in range(1, nt)]

    def over_tensor(value, pieces=None):
        pieces = pieces_of(value) if pieces is None else pieces
        if nt == 2:
            first = jnp.concatenate(pieces, axis=0)
            second = jnp.concatenate(pieces[::-1], axis=0)
            return jnp.where(t_rank == 0, first, second)
        stacked = jnp.take(jnp.stack(pieces), jnp.arange(nt) ^ t_rank, axis=0)
        return stacked.reshape((nt * stacked.shape[1],) + stacked.shape[2:])

    kernel_rows, columns = conv_params.shape
    gain_count = norm_gains.shape[0]
    shared_size = shared_proj.size
    exact = jnp.concatenate([conv_params.reshape(-1), norm_gains])
    terms = []
    rest = exact
    for _ in range(3):
        term = lax.optimization_barrier(rest.astype(bf16))
        terms.append(term)
        rest = rest - term.astype(f32)
    common_width = 2 * N + LANES
    shared_rows = shared_proj.shape[0]
    packed = width == 1024 and shared_rows == 32
    if packed:
        wide_shared = jnp.pad(shared_proj.astype(bf16), ((0, 0), (0, common_width - 2 * N - H)))
        flat = jnp.concatenate(terms)
        flat = jnp.pad(flat, (0, 16 * 256 - flat.size)).reshape(16, 256)
        small = jnp.concatenate([wide_shared[:16], wide_shared[16:], flat], axis=1)
        small_rows = 16
    else:
        small = jnp.concatenate([shared_proj.astype(bf16).reshape(-1)] + terms)
        small_rows = -(-small.size // width)
        while small_rows * nt % 16:
            small_rows += 1
        small = jnp.pad(small, (0, small_rows * width - small.size)).reshape(small_rows, width)
    small_pair = over_tensor(small)
    token_pieces = pieces_of(residual)

    block_rows = D // dp
    value_shard = jnp.concatenate([inner_proj[1].astype(bf16), small_pair], axis=0)
    cut = -(-value_shard.shape[0] // 32) * 16
    first_line = gather_line(value_shard[:cut], dp)
    second_shard, first_line = tie(value_shard[cut:], first_line)
    second_line = gather_line(second_shard, dp)
    second_line, ids = tie(second_line, sequence_ids)
    first_near = [first_line] + plane_parts(first_line, dp)
    other_shard = jnp.concatenate(
        [inner_proj[0].astype(bf16), outer_proj.T.astype(bf16)], axis=0
    )
    other_shard, second_line = tie(other_shard, second_line)
    other_line = gather_line(other_shard, dp)
    cot_cut = rows_here // 2
    cot_early = [swap(cotangent[:cot_cut], "tensor", nt, d) for d in range(1, nt)]
    second_line, *rests = tie(
        second_line, *plane_parts(second_line, dp), *token_pieces, *cot_early
    )
    count = len(rests) - 2 * nt + 1
    second_near = [second_line] + rests[:count]
    token_pieces, cot_early = rests[count : count + nt], rests[count + nt :]
    cotangent_now, *token_pieces = tie(cotangent[cot_cut:], *token_pieces)
    cot_late = [swap(cotangent_now, "tensor", nt, d) for d in range(1, nt)]
    first_all = first_near + [swap(line, "dp", dp, 1) for line in first_near]
    second_all = second_near + [swap(line, "dp", dp, 1) for line in second_near]
    full = slice(None)
    moves = [(0, block_rows, full, 0, 1, 0, 0)]
    dims = [(dp, block_rows, width)]
    if packed:
        for t in range(nt):
            at = (block_rows + 16 * t, block_rows + 16 * t + 16)
            moves.append(at + (slice(0, common_width), 1, nt, t, 0))
            moves.append(at + (slice(common_width, 2 * common_width), 1, nt, t, 16))
            moves.append(at + (slice(2 * common_width, width), 2, nt, t, 0))
        dims += [(dp * nt, 32, common_width), (dp * nt, 16, 256)]
    else:
        moves.append((block_rows, block_rows + small_rows * nt, full, 1, 1, 0, 0))
        dims += [(dp, small_rows * nt, width)]
    value_w, *small_all = assemble([first_all, second_all], dp, dp_me, moves, dims)
    value_w = value_w.reshape(D, width)

    def halves(pieces):
        if nt == 2:
            return t_me, pieces[0], pieces[1]
        all_rows = over_tensor(None, pieces)
        return jnp.zeros((1,), jnp.int32), all_rows[: length // 2], all_rows[length // 2 :]

    if packed:
        shared_here = small_all[0].reshape(D, common_width)
        exact_all = small_all[1].reshape(dp * nt, -1)[:, : 3 * exact.size].astype(f32)
    else:
        small_all = small_all[0].reshape(dp * nt, small_rows * width)
        shared_here = small_all[:, :shared_size].reshape(D, -1)
        shared_here = jnp.pad(shared_here, ((0, 0), (0, common_width - 2 * N - H)))
        exact_all = small_all[:, shared_size : shared_size + 3 * exact.size].astype(f32)
    exact_all = exact_all.reshape(dp * nt, 3, exact.size)
    exact_all = (exact_all[:, 0] + exact_all[:, 1]) + exact_all[:, 2]
    conv_full = (
        exact_all[:, : kernel_rows * columns]
        .reshape(dp * nt, kernel_rows, columns)
        .transpose(1, 0, 2)
        .reshape(kernel_rows, -1)
    )
    gains_full = exact_all[:, kernel_rows * columns :].reshape(-1)

    pre_gain = gains_full[:D].reshape(1, D)
    post_gain = lax.dynamic_slice_in_dim(gains_full, D + t_rank * width, width).reshape(1, width)
    conv_here = jnp.concatenate(
        [lax.dynamic_slice_in_dim(conv_full, t_rank * width, width, 1), conv_full[:, DI:]], axis=1
    )
    conv_here = jnp.pad(conv_here, ((0, 8 - kernel_rows), (0, 0)))
    head_rows = jnp.stack([head_params[0], jnp.exp(head_params[1])])
    head_rows = jnp.pad(head_rows, ((0, 6), (0, LANES - heads_here)))
    skip = jnp.repeat(head_params[2], head_size).reshape(1, width)
    heads_of = (
        jnp.arange(width)[:, None] // head_size == jnp.arange(LANES)[None, :]
    ).astype(bf16)

    blocked = ids.reshape(chunks, CHUNK)
    ends, firsts = blocked[:, -1], blocked[:, 0]
    none = jnp.full((1,), -1, jnp.int32)
    before = jnp.concatenate([none, ends[:-1]])
    following = jnp.concatenate([firsts[1:], none])
    fills = [jnp.full((o,), -1, jnp.int32) for o in range(1, 4)]
    marks = [ids]
    marks += [jnp.concatenate([fills[o - 1], ids[:-o]]) == ids for o in range(1, 4)]
    marks += [jnp.concatenate([ids[o:], fills[o - 1]]) == ids for o in range(1, 4)]
    marks += [
        (blocked == before[:, None]).reshape(-1),
        (blocked == ends[:, None]).reshape(-1),
        jnp.broadcast_to((ends == before)[:, None], blocked.shape).reshape(-1),
        (blocked == following[:, None]).reshape(-1),
        ids < SEQ_SLOTS,
    ]
    aux = jnp.stack([m.astype(f32) for m in marks] + [jnp.zeros((length,), f32)] * 4, axis=1)
    segr = ids.astype(f32).reshape(1, length)
    aux_cols = aux.shape[1]

    steps = length // wide
    in_half = lambda i: i % (steps // 2)
    value_w, other_line, *cot_late = tie(value_w, other_line, *cot_late)
    cot_pieces = [cotangent] + [
        jnp.concatenate([early, late], axis=0) for early, late in zip(cot_early, cot_late)
    ]
    other_far = swap(other_line, "dp", dp, 1)
    plane = plane_parts(other_line, dp)
    tok_rank, tok0, tok1 = halves(token_pieces)
    normed, chans, pre, mixed, ssd, entering, step_in = call(
        functools.partial(scan_kernel, heads_here),
        (steps,),
        [
            rows(wide, D, in_half), rows(wide, D, in_half), whole((1, D)), whole((D, width)),
            whole((D, common_width)), whole((8, channels)), whole((1, width)), whole((8, LANES)),
            rows(wide, aux_cols), pl.BlockSpec((1, wide), lambda i, r: (0, i)),
        ],
        [
            rows(wide, D), rows(wide, channels), rows(wide, channels), rows(wide, channels),
            rows(wide, width), pl.BlockSpec((wide // CHUNK, N, width), lambda i, r: (i, 0, 0)),
            rows(wide, LANES),
        ],
        [
            shape(length, D, dtype=bf16), shape(length, channels), shape(length, channels),
            shape(length, channels, dtype=bf16), shape(length, width),
            shape(chunks, N, width), shape(length, LANES),
        ],
        [
            pltpu.VMEM((wide + 8, channels), f32), pltpu.VMEM((N, width), f32),
            pltpu.VMEM((CHUNK, width), f32), pltpu.VMEM((2, CHUNK, width), bf16),
        ],
        length * (2 * D * (width + common_width) + 12 * width * CHUNK),
        22,
        scalars=1,
    )(jnp.concatenate([tok_rank, t_me]), tok0, tok1, pre_gain, value_w, shared_here, conv_here, skip, head_rows, aux, segr)

    normed, other_far, *plane = tie(normed, other_far, *plane)
    moves = [
        (0, block_rows, full, 0, 1, 0, 0), (block_rows, 2 * block_rows, full, 1, 1, 0, 0)
    ]
    other_all = [other_line] + plane + [other_far] + [swap(line, "dp", dp, 1) for line in plane]
    gate_w, outer_t = assemble([other_all], dp, dp_me, moves, [(dp, block_rows, width)] * 2)
    gate_w, outer_t = gate_w.reshape(D, width), outer_t.reshape(D, width)
    cot_rank, cot0, cot1 = halves(cot_pieces)
    gate, scaled_grad, returned, sums = call(
        gate_kernel,
        (steps,),
        [
            rows(wide, D), rows(wide, D, in_half), rows(wide, D, in_half), rows(wide, aux_cols),
            rows(wide, width), whole((D, width)), whole((D, width)), whole((1, width)),
        ],
        [rows(wide, width), rows(wide, width), rows(wide, D), pl.BlockSpec((8, wide), lambda i, r: (0, i))],
        [
            shape(length, width), shape(length, width), shape(length, D, dtype=bf16),
            shape(8, length),
        ],
        [],
        4 * length * D * width,
        15,
        scalars=1,
    )(cot_rank, normed, cot0, cot1, aux, ssd, gate_w, outer_t, post_gain)
    distance = 1
    while distance < nt:
        sums = sums + swap(sums, "tensor", nt, distance)
        distance *= 2

    def relative(block, rank):
        return (rank ^ (block // per_piece)) * per_piece + block % per_piece

    def rel_rows(width_here, offset=0):
        return pl.BlockSpec((band, width_here), lambda i, r: (relative(i + offset, r[0]), 0))

    plain = lambda width_here: pl.BlockSpec((band, width_here), lambda i, r: (i, 0))
    branch, scaled, dssd, dgate, post_grad = call(
        norm_kernel,
        (length // band,),
        [
            rel_rows(width), rel_rows(width), rel_rows(width),
            pl.BlockSpec((8, band), lambda i, r: (0, relative(i, r[0]))),
            whole((D, width)), whole((1, width)),
        ],
        [plain(D), rel_rows(width), rel_rows(width), rel_rows(width), result((1, width))],
        [
            shape(length, D, dtype=bf16), shape(length, width, dtype=bf16),
            shape(length, width, dtype=bf16), shape(length, width, dtype=bf16), shape(1, width),
        ],
        [],
        2 * length * D * width,
        15,
        scalars=1,
    )(t_me, gate, scaled_grad, ssd, sums, outer_t, post_gain)
    outer_keep, outer_send = weight_grad(returned, scaled, dp, dp_me)
    dgate, outer_send = tie(dgate, outer_send)
    gate_keep, gate_send = weight_grad(normed, dgate, dp, dp_me)
    outer_line, outer_rest = start_sum(outer_keep, outer_send, dp)
    gate_line, gate_rest = start_sum(gate_keep, gate_send, dp)
    branch = branch.reshape(nt, rows_here, D)
    branch_received = [swap(branch[d], "tensor", nt, d) for d in range(1, nt)]
    dssd, *rests = tie(dssd, *outer_rest, *gate_rest)
    outer_rest, gate_rest = rests[: len(outer_rest)], rests[len(outer_rest) :]
    outer_received = middle_swaps(outer_rest, dp)
    gate_received = middle_swaps(gate_rest, dp)

    state = jnp.zeros((N, width), f32)
    win = jnp.zeros((8, channels), f32)
    carry = jnp.zeros((8, LANES), f32)
    back_parts = []
    filled = []
    top = chunks
    for part, count in enumerate((3, 3, chunks - 6)):
        back = lambda i, top=top: top - 1 - i
        top -= count
        *results, state, win, carry = call(
            functools.partial(scan_back_kernel, heads_here),
            (count,),
            [
                rows(CHUNK, width, back), rows(CHUNK, channels, back), rows(CHUNK, channels, back),
                rows(CHUNK, channels, back), rows(CHUNK, width, back),
                pl.BlockSpec((1, N, width), lambda i, r, back=back: (back(i), 0, 0)),
                rows(CHUNK, LANES, back), whole((8, channels)), whole((1, width)),
                whole((8, LANES)), rows(CHUNK, aux_cols, back),
                pl.BlockSpec((1, CHUNK), lambda i, r, back=back: (0, back(i))),
                whole((width, LANES)),
                whole((N, width)), whole((8, channels)), whole((8, LANES)),
            ]
            + [pl.BlockSpec(memory_space=pl.ANY)] * len(filled),
            [
                rows(CHUNK, width, back), rows(CHUNK, common_width, back), result((8, channels)),
                result((8, LANES)),
                result((N, width)), result((8, channels)), result((8, LANES)),
            ],
            [
                shape(length, width, dtype=bf16), shape(length, common_width),
                shape(8, channels), shape(8, LANES),
                shape(N, width), shape(8, channels), shape(8, LANES),
            ],
            [
                pltpu.VMEM((CHUNK, channels), f32), pltpu.VMEM((CHUNK + 8, channels), f32),
                pltpu.VMEM((2 * CHUNK, width), f32), pltpu.VMEM((CHUNK, width), f32),
                pltpu.VMEM((2, CHUNK, width), bf16), pltpu.VMEM((CHUNK, width), bf16),
                pltpu.VMEM((8, width), f32),
            ],
            count * CHUNK * 30 * width * CHUNK,
            14,
            scalars=1,
            aliases={17: 0, 18: 1} if filled else None,
        )(
            t_me, dssd, mixed, pre, chans, ssd, entering, step_in, conv_here, skip, head_rows, aux, segr,
            heads_of, state, win, carry, *filled,
        )
        filled = results[:2]
        back_parts.append(results[2:])
        if part == 0:
            state, outer_line, *outer_received = tie(state, outer_line, *outer_received)
            outer_block, outer_far = middle_sum(outer_line, outer_received)
            outer_far = high_swaps(outer_far, dp)
        if part == 1:
            state, gate_line, *rests = tie(
                state, gate_line, *branch_received, *gate_received, *outer_far
            )
            branch_received = rests[: nt - 1]
            gate_received, outer_far = rests[nt - 1 : -len(outer_far)], rests[-len(outer_far) :]
            gate_block, gate_far = middle_sum(gate_line, gate_received)
            gate_far = high_swaps(gate_far, dp)
    dval, dcommon = filled
    dval, *gate_far = tie(dval, *gate_far)

    branch_sum = branch[0].astype(f32)
    for piece in branch_received:
        branch_sum = branch_sum + piece.astype(f32)
    live_here = lax.dynamic_slice_in_dim(aux[:, LIVE], t_rank * rows_here, rows_here)
    tokens = residual.astype(f32)
    block_out = (tokens + branch_sum * live_here[:, None]).astype(bf16)

    away = (nt - 1) * per_piece

    def input_grad(others, dgate):
        away_rows = lambda width_here: pl.BlockSpec(
            (band, width_here), lambda i, r: (jnp.minimum(i, away - 1), 0)
        )
        own_rows = lambda width_here: pl.BlockSpec(
            (band, width_here), lambda i, r: (jnp.maximum(i - away, 0), 0)
        )
        turned = lambda i: lax.rem(i + per_piece, nt * per_piece)
        here = lambda width_here: pl.BlockSpec(
            (band, width_here), lambda i, r: (relative(turned(i), r[0]), 0)
        )
        return call(
            functools.partial(input_grad_kernel, away),
            (nt * per_piece,),
            [
                here(width), here(width), here(common_width), away_rows(D), own_rows(D),
                whole((D, width)), whole((D, width)), whole((D, common_width)),
            ],
            [away_rows(D), own_rows(D), result((1, D))],
            [shape((nt - 1) * rows_here, D, dtype=bf16), shape(rows_here, D), shape(1, D)],
            [],
            4 * length * D * (width + common_width),
            50,
            scalars=1,
        )(t_me, dgate, dval, dcommon, others, residual, gate_w, value_w, shared_here)

    others = token_pieces[1] if nt == 2 else jnp.concatenate(token_pieces[1:], axis=0)
    sent, own, pre_grad = input_grad(others, dgate)
    sent, dval = tie(sent, dval)
    sent = sent.reshape(nt - 1, rows_here, D)
    received = [swap(sent[d - 1], "tensor", nt, d) for d in range(1, nt)]
    keep, send = value_grad(normed, dval, dcommon, dp, dp_me)
    line, part = start_sum(keep, send, dp)
    line, *part = tie(line, *part)
    crossing = middle_swaps(part, dp)
    small_grads = [item for each_part in back_parts for item in each_part]

    dconv, dheads = [sum(small_grads[at::2]) for at in range(2)]
    conv_grad = lax.dynamic_update_slice(
        jnp.pad(dconv[:kernel_rows, width:], ((0, 0), (DI, 0))),
        dconv[:kernel_rows, :width],
        (0, t_rank * width),
    )
    post_all = lax.dynamic_update_slice(
        jnp.zeros((1, DI), f32), post_grad, (0, t_rank * width)
    )
    head_grad = dheads[:3, :heads_here]
    head_all = lax.dynamic_update_slice(
        jnp.zeros((3, H), f32), head_grad, (0, t_rank * heads_here)
    )
    vector = jnp.concatenate(
        [
            conv_grad.reshape(1, -1), pre_grad, post_all, head_all.reshape(1, -1),
        ],
        axis=1,
    )
    for stage, (axis, size, distance) in enumerate(sum_stages(dp, nt)):
        vector = vector + swap(vector, axis, size, distance)
        if stage == 0:
            vector, line, *crossing = tie(vector, line, *crossing)
            block, far = middle_sum(line, crossing)
            far = high_swaps(far, dp)
        if stage == 2:
            vector, outer_block, gate_block, *received = tie(
                vector, outer_block, gate_block, *received
            )
            outer_part = high_sum(outer_block, outer_far)
            gate_part = high_sum(gate_block, gate_far)
        if stage == 3:
            vector, *far = tie(vector, *far)
            value_sum = high_sum(block, far)
    shared_sum = value_sum[:, width:].reshape(nt, shared_rows, common_width)
    shared_mine = lax.dynamic_index_in_dim(shared_sum, t_rank, 0, False)
    for d in range(1, nt):
        piece = lax.dynamic_index_in_dim(shared_sum, t_rank ^ d, 0, False)
        shared_mine = shared_mine + swap(piece, "tensor", nt, d)
    shared_part = shared_mine[:, : 2 * N + H]
    value_part = value_sum[:, :width]
    conv_size = kernel_rows * (DI + 2 * N)
    place = d_rank * nt + t_rank
    conv_part = lax.dynamic_slice_in_dim(
        vector[0, :conv_size].reshape(kernel_rows, -1), place * columns, columns, 1
    )
    gains_part = lax.dynamic_slice_in_dim(vector[0], conv_size + place * gain_count, gain_count)
    heads_part = lax.dynamic_slice_in_dim(
        vector[0, conv_size + D + DI :].reshape(3, H), t_rank * heads_here, heads_here, 1
    )

    normed_grad = own
    for piece in received:
        normed_grad = normed_grad + piece.astype(f32)
    inverse = lax.rsqrt(jnp.mean(tokens * tokens, axis=1, keepdims=True) + norm_epsilon)
    normal_tokens = tokens * inverse
    normal_grad = normed_grad * pre_gain
    centered = normal_grad - normal_tokens * jnp.mean(
        normal_grad * normal_tokens, axis=1, keepdims=True
    )
    residual_grad = (cotangent.astype(f32) + inverse * centered).astype(bf16)

    inner_new = adam_step(
        inner_proj, inner_mean, inner_square, jnp.stack([gate_part, value_part]),
        rate_matrix, weight_decay,
    )
    shared_new = adam_step(
        shared_proj, shared_mean, shared_square, shared_part.reshape(shared_proj.shape),
        rate_matrix, weight_decay,
    )
    outer_new = adam_step(
        outer_proj, outer_mean, outer_square, outer_part.T, rate_matrix, weight_decay
    )
    conv_new = adam_step(conv_params, conv_mean, conv_square, conv_part, rate_vector, 0.0)
    gains_new = adam_step(norm_gains, gains_mean, gains_square, gains_part, rate_vector, 0.0)
    heads_new = adam_step(head_params, heads_mean, heads_square, heads_part, rate_heads, 0.0)
    return (
        (block_out, residual_grad)
        + inner_new + shared_new + outer_new + conv_new + gains_new + heads_new
    )


def solution(mesh):
    return jax.shard_map(
        functools.partial(shards, mesh.shape["dp"], mesh.shape["tensor"]),
        mesh=mesh,
        in_specs=(
            P(("dp", "tensor"), None),
            P(("dp", "tensor"), None),
            P("dp"),
            P(None, "dp", "tensor"),
            P(None, "dp", "tensor"),
            P(None, "dp", "tensor"),
            P(("dp", "tensor"), None),
            P(("dp", "tensor"), None),
            P(("dp", "tensor"), None),
            P("tensor", "dp"),
            P("tensor", "dp"),
            P("tensor", "dp"),
            P(None, ("dp", "tensor")),
            P(None, ("dp", "tensor")),
            P(None, ("dp", "tensor")),
            P(("dp", "tensor")),
            P(("dp", "tensor")),
            P(("dp", "tensor")),
            P(None, "tensor"),
            P(None, "tensor"),
            P(None, "tensor"),
        ),
        out_specs=(
            P(("dp", "tensor"), None),
            P(("dp", "tensor"), None),
            P(None, "dp", "tensor"),
            P(None, "dp", "tensor"),
            P(None, "dp", "tensor"),
            P(("dp", "tensor"), None),
            P(("dp", "tensor"), None),
            P(("dp", "tensor"), None),
            P("tensor", "dp"),
            P("tensor", "dp"),
            P("tensor", "dp"),
            P(None, ("dp", "tensor")),
            P(None, ("dp", "tensor")),
            P(None, ("dp", "tensor")),
            P(("dp", "tensor")),
            P(("dp", "tensor")),
            P(("dp", "tensor")),
            P(None, "tensor"),
            P(None, "tensor"),
            P(None, "tensor"),
        ),
        check_vma=False,
    )
```

```python
import functools

import jax
import jax.numpy as jnp
from jax import lax
from jax.experimental import pallas as pl
from jax.experimental.pallas import tpu as pltpu
from jax.sharding import PartitionSpec as P

D = 1024
H = 32
N = 128
DI = 2048
SEQ_SLOTS = 4
STEP = 10
CHUNK = 128
LANES = 128
CORES = 2
HIGH_AXIS = 4

highest = lax.Precision.HIGHEST
f32 = jnp.float32
bf16 = jnp.bfloat16
norm_epsilon = 1e-05
beta_first = 0.9
beta_second = 0.95
adam_epsilon = 1e-08
weight_decay = 0.1
rate_matrix = 0.02
rate_vector = 0.3
rate_heads = 1.0

SEG, BACK, AHEAD, INHERIT, TAIL, LINKED, NEXT, LIVE = 0, 0, 3, 7, 8, 9, 10, 11


def adam_step(weight, moment, square, gradient, rate, decay):
    moment_next = beta_first * moment + (1.0 - beta_first) * gradient
    square_next = beta_second * square + (1.0 - beta_second) * gradient * gradient
    moment_hat = moment_next / (1.0 - beta_first**STEP)
    square_hat = square_next / (1.0 - beta_second**STEP)
    weight_next = weight - rate * (
        moment_hat / (jnp.sqrt(square_hat) + adam_epsilon) + decay * weight
    )
    return (weight_next, moment_next, square_next)


def swap(value, axis, size, distance):
    return lax.ppermute(value, axis, [(i, i ^ distance) for i in range(size)])


def tie(*values):
    return lax.optimization_barrier(values)


def axis_parts(dp):
    high = HIGH_AXIS
    middle = dp // (CORES * high)
    return high, middle


def gather_line(shard, dp):
    high, middle = axis_parts(dp)
    pieces = [shard[None]]
    for step in range(1, high):
        pieces.append(swap(shard, "dp", dp, step * middle * CORES)[None])
    return jnp.concatenate(pieces, axis=0)


def plane_parts(line, dp):
    return [swap(line, "dp", dp, step * CORES) for step in range(1, axis_parts(dp)[1])]


def start_sum(keep, send, dp):
    high, middle = axis_parts(dp)
    other = swap(send, "dp", dp, 1)
    parts = [slice(step * high, (step + 1) * high) for step in range(middle)]
    line = keep[parts[0]].astype(f32) + other[parts[0]].astype(f32)
    rest = [(keep[at].astype(f32) + other[at].astype(f32)).astype(bf16) for at in parts[1:]]
    return line, rest


def middle_swaps(rest, dp):
    return [swap(part, "dp", dp, (step + 1) * CORES) for step, part in enumerate(rest)]


def middle_sum(line, received):
    for part in received:
        line = line + part.astype(f32)
    return line[0], [part.astype(bf16) for part in line[1:]]


def high_swaps(rest, dp):
    middle = axis_parts(dp)[1]
    return [swap(part, "dp", dp, (step + 1) * middle * CORES) for step, part in enumerate(rest)]


def high_sum(block, received):
    for part in received:
        block = block + part.astype(f32)
    return block


def sum_stages(dp, nt):
    stages = [("tensor", nt, 1 << bit) for bit in range((nt - 1).bit_length())]
    return stages + [("dp", dp, 1 << bit) for bit in range((dp - 1).bit_length())]


def relative_places(dp):
    high, middle = axis_parts(dp)
    return [
        (h * middle + m) * CORES + c for c in range(CORES) for m in range(middle) for h in range(high)
    ]


def call(kernel, grid, in_specs, out_specs, out_shape, scratch, flops, mib, scalars=0, aliases=None):
    params = pltpu.CompilerParams(vmem_limit_bytes=mib * 1024 * 1024)
    moved = sum(2 * s.dtype.itemsize * s.size for s in jax.tree.leaves(out_shape))
    return pl.pallas_call(
        kernel,
        grid_spec=pltpu.PrefetchScalarGridSpec(
            num_scalar_prefetch=scalars,
            grid=grid,
            in_specs=in_specs,
            out_specs=out_specs,
            scratch_shapes=scratch,
        ),
        out_shape=out_shape,
        compiler_params=params,
        input_output_aliases=aliases or {},
        cost_estimate=pl.CostEstimate(
            flops=int(flops) // 16, bytes_accessed=int(moved) // 16, transcendentals=0
        ),
    )


def whole(shape):
    return pl.BlockSpec(shape, lambda *i: (0,) * len(shape), pipeline_mode=pl.Buffered(1))


def result(shape):
    return pl.BlockSpec(shape, lambda *i: (0,) * len(shape))


def rows(count, width, index=lambda i: i):
    return pl.BlockSpec((count, width), lambda i, *s: (index(i), 0))


def shape(*dims, dtype=f32):
    return jax.ShapeDtypeStruct(dims, dtype)


def split(value):
    high = value.astype(bf16)
    return high, (value - high.astype(f32)).astype(bf16)


def mm(a, b, ca=1, cb=0):
    return lax.dot_general(a, b, (((ca,), (cb,)), ((), ())), preferred_element_type=f32)


def mm_left(value, exact, ca=1, cb=0):
    high, low = split(value)
    return mm(high, exact, ca, cb) + mm(low, exact, ca, cb)


def mm_right(exact, value, ca=1, cb=0):
    high, low = split(value)
    return mm(exact, high, ca, cb) + mm(exact, low, ca, cb)


def mm_both(a, b, ca=1, cb=0):
    a_high, a_low = split(a)
    b_high, b_low = split(b)
    return mm(a_high, b_high, ca, cb) + mm(a_low, b_high, ca, cb) + mm(a_high, b_low, ca, cb)


def sigmoid(value):
    return 0.5 * jnp.tanh(0.5 * value) + 0.5


def softplus(value):
    return jnp.maximum(value, 0.0) + jnp.log1p(jnp.exp(-jnp.abs(value)))


def iota(axis):
    return lax.broadcasted_iota(jnp.int32, (CHUNK, LANES), axis)


def pair_spread(tile, pair, left):
    rows_here = tile.shape[0]
    return jnp.where(
        left[:rows_here],
        jnp.broadcast_to(tile[:, 2 * pair : 2 * pair + 1], (rows_here, LANES)),
        jnp.broadcast_to(tile[:, 2 * pair + 1 : 2 * pair + 2], (rows_here, LANES)),
    )


def assemble_kernel(dp, parts, moves, me, *refs):
    half = dp // CORES
    sources, outs = refs[: 2 * parts], refs[2 * parts :]
    for place, distance in enumerate(relative_places(dp)):
        block = me[0] ^ distance
        base = 0
        for part in range(parts):
            source, at = (sources[part], place) if place < half else (sources[parts + part], place - half)
            end = base + source.shape[1]
            for first, last, lanes, out, each, extra, row in moves:
                low, high = max(base, first), min(end, last)
                if low < high:
                    outs[out][
                        block * each + extra, row + low - first : row + high - first, :
                    ] = source[at, low - base : high - base, lanes]
            base = end


def assemble(nears, fars, dp, dp_rank, moves, shapes):
    vmem = pl.BlockSpec(memory_space=pltpu.VMEM)
    moved = sum(4 * near.size * near.dtype.itemsize for near in nears)
    return pl.pallas_call(
        functools.partial(assemble_kernel, dp, len(nears), moves),
        in_specs=[pl.BlockSpec(memory_space=pltpu.SMEM)] + [vmem] * (2 * len(nears)),
        out_specs=[vmem] * len(shapes),
        out_shape=[shape(*dims, dtype=bf16) for dims in shapes],
        compiler_params=pltpu.CompilerParams(vmem_limit_bytes=16 * 1024 * 1024),
        cost_estimate=pl.CostEstimate(flops=0, bytes_accessed=moved, transcendentals=0),
    )(dp_rank, *nears, *fars)


def pick_half(rank, first, second):
    half = (2 * pl.program_id(0)) // pl.num_programs(0)
    own = (half == rank[0]).astype(jnp.int32)
    return jnp.where(jnp.broadcast_to(own, first.shape) == 1, first[...], second[...])


def across(pair, left):
    return jnp.concatenate(
        [jnp.where(left, pair, 0.0), jnp.where(left, 0.0, pair)], axis=0
    ).astype(bf16)


def scan_kernel(
    heads, rank, tok0, tok1, gain, wv, shw, conv, skip, hp, aux, segr,
    normed_o, ch_o, pre_o, mix_o, ssd_o, hin_o, step_o,
    win, state, carried, weighted,
):
    count = tok0.shape[0]
    width = wv.shape[1]
    channels = width + 2 * N

    @pl.when(pl.program_id(0) == 0)
    def _():
        win[0:8, :] = jnp.zeros((8, channels), f32)
        state[...] = jnp.zeros(state.shape, f32)

    x = pick_half(rank, tok0, tok1).astype(f32)
    inverse = lax.rsqrt(jnp.mean(x * x, axis=1, keepdims=True) + norm_epsilon)
    normed = (x * inverse * gain[...]).astype(bf16)
    normed_o[...] = normed
    win[8 : 8 + count, :width] = mm(normed, wv[...])
    common = mm(normed, shw[...])
    win[8 : 8 + count, width:] = common[:, : 2 * N]
    turn = lax.rem(LANES - heads * rank[1], LANES)
    step_o[...] = pltpu.roll(common[:, 2 * N :], turn, 1) + hp[0:1, :]
    table = aux[...]
    for start in range(0, channels, 256):
        cols = slice(start, start + 256)
        here = win[8 : 8 + count, cols]
        pre = conv[4:5, cols] + conv[3:4, cols] * here
        for back in range(1, 4):
            pre = pre + conv[3 - back : 4 - back, cols] * (
                win[8 - back : 8 - back + count, cols] * table[:, BACK + back : BACK + back + 1]
            )
        ch_o[:, cols] = here
        pre_o[:, cols] = pre
        mix_o[:, cols] = (pre * sigmoid(pre)).astype(bf16)
    win[0:8, :] = win[count : count + 8, :]

    row, col = iota(0), iota(1)
    left = col < 64
    tri = (row >= col).astype(f32)
    for sub in range(count // CHUNK):
        at = slice(sub * CHUNK, (sub + 1) * CHUNK)
        dt = softplus(step_o[at, :])
        run = jnp.dot(tri, -(dt * hp[1:2, :]), precision=highest, preferred_element_type=f32)
        run_t = run.T
        allowed = (table[at, SEG : SEG + 1] == segr[:, at]) & (row >= col)
        b_in = mix_o[at, width : width + N]
        b_turned = b_in.astype(f32).T.astype(bf16)
        c_out = mix_o[at, width + N :]
        scores = jnp.where(allowed, mm(c_out, b_in, 1, 1), 0.0)
        ending = run[CHUNK - 1 : CHUNK, :]
        entry = jnp.exp(run) * table[at, INHERIT : INHERIT + 1]
        tail = jnp.exp(ending - run) * table[at, TAIL : TAIL + 1]
        factor = jnp.exp(ending) * table[at, LINKED : LINKED + 1][CHUNK - 1 :, :]
        hin_o[sub] = state[...]
        carried[...] = mm_right(c_out, state[...])
        for pair in range(width // LANES):
            lanes = slice(pair * LANES, (pair + 1) * LANES)
            x_pair = mix_o[at, lanes].astype(f32)
            stepped = (x_pair * pair_spread(dt, pair, left)).astype(bf16).astype(f32)
            mixing = []
            for head in (2 * pair, 2 * pair + 1):
                spread = run[:, head : head + 1] - run_t[head : head + 1, :]
                mixing.append((jnp.exp(jnp.minimum(spread, 0.0)) * scores).astype(bf16))
            local = mm(jnp.concatenate(mixing, axis=1), across(stepped, left))
            ssd_o[at, lanes] = (
                local + carried[:, lanes] * pair_spread(entry, pair, left) + skip[:, lanes] * x_pair
            )
            high, low = split(stepped * pair_spread(tail, pair, left))
            weighted[0, :, lanes] = high
            weighted[1, :, lanes] = low
            state[:, lanes] = pair_spread(factor, pair, left) * state[:, lanes]
        state[...] += mm(b_turned, weighted[0]) + mm(b_turned, weighted[1])


def gate_kernel(rank, normed, cot0, cot1, aux, ssd, wg, out_t, gain, gate_o, sg_o, ret_o, sums_o):
    returned = (pick_half(rank, cot0, cot1).astype(f32) * aux[:, LIVE : LIVE + 1]).astype(bf16)
    ret_o[...] = returned
    gate = mm(normed[...], wg[...])
    gate_o[...] = gate
    scaled_grad = mm(returned, out_t[...])
    sg_o[...] = scaled_grad
    gated = ssd[...] * (gate * sigmoid(gate))
    squares = jnp.sum(gated * gated, axis=1, keepdims=True)
    crossed = jnp.sum(scaled_grad * gain[...] * gated, axis=1, keepdims=True)
    lane = lax.broadcasted_iota(jnp.int32, (squares.shape[0], LANES), 1)
    table = jnp.where(lane == 0, squares, jnp.where(lane == 1, crossed, 0.0))
    sums_o[...] = table.T[:8, :]


def norm_kernel(
    rank, gate_r, sg_r, ssd_r, sums_r, out_t, gain, branch_o, scaled_o, dssd_o, dgate_o, gain_o
):
    @pl.when(pl.program_id(0) == 0)
    def _():
        gain_o[...] = jnp.zeros(gain_o.shape, f32)

    gate, ssd, scaled_grad = gate_r[...], ssd_r[...], sg_r[...]
    table = jnp.concatenate([sums_r[...], jnp.zeros((LANES - 8, sums_r.shape[1]), f32)], axis=0)
    sums = table.T
    scale = lax.rsqrt(sums[:, 0:1] / DI + norm_epsilon)
    sig = sigmoid(gate)
    silu = gate * sig
    gated = ssd * silu
    scaled = (gated * scale * gain[...]).astype(bf16)
    scaled_o[...] = scaled
    branch_o[...] = mm(scaled, out_t[...], 1, 1).astype(bf16)
    gain_o[...] += jnp.sum(scaled_grad * gated * scale, axis=0, keepdims=True)
    grad = scale * (scaled_grad * gain[...]) - gated * (scale * scale * scale * (sums[:, 1:2] / DI))
    dssd_o[...] = (grad * silu).astype(bf16)
    dgate_o[...] = (grad * ssd * sig * (1.0 + gate * (1.0 - sig))).astype(bf16)


def scan_back_kernel(
    heads, rank, dssd, mix, pre, ch, ssd, hin, step, conv, skip, hp, aux, segr, heads_of,
    state_in, win_in, carry_in, *rest,
):
    dval_o, dcommon_o, dconv_o, dheads_o, dstate, dtail, carry = rest[-14:-7]
    dmix, dwin, both, flows, entries, weighted, dskip = rest[-7:]
    width = dssd.shape[1]
    channels = width + 2 * N

    @pl.when(pl.program_id(0) == 0)
    def _():
        dwin[CHUNK:, :] = win_in[...]
        dstate[...] = state_in[...]
        carry[...] = carry_in[...]
        dconv_o[...] = jnp.zeros(dconv_o.shape, f32)
        dheads_o[...] = jnp.zeros(dheads_o.shape, f32)
        dskip[...] = jnp.zeros(dskip.shape, f32)

    row, col = iota(0), iota(1)
    left = col < 64
    table = aux[...]
    step_in = step[...]
    dt = softplus(step_in)
    rate = hp[1:2, :]
    tri = (row >= col).astype(f32)
    run = jnp.dot(tri, -(dt * rate), precision=highest, preferred_element_type=f32)
    run_t = run.T
    allowed = (table[:, SEG : SEG + 1] == segr[...]) & (col >= row)
    b_in = mix[:, width : width + N]
    c_out = mix[:, width + N :]
    scores = jnp.where(allowed, mm(b_in, c_out, 1, 1), 0.0)
    ending = run[CHUNK - 1 : CHUNK, :]
    entry = jnp.exp(run) * table[:, INHERIT : INHERIT + 1]
    tail = jnp.exp(ending - run) * table[:, TAIL : TAIL + 1]
    factor = jnp.exp(ending) * table[:, LINKED : LINKED + 1][CHUNK - 1 :, :]
    c_turned = c_out.astype(f32).T.astype(bf16)
    pairs = jnp.zeros((CHUNK, CHUNK), f32)
    state_high, state_low = split(dstate[...])
    flows[...] = mm(b_in, state_high) + mm(b_in, state_low)
    for pair in range(width // LANES):
        lanes = slice(pair * LANES, (pair + 1) * LANES)
        x_pair = mix[:, lanes].astype(f32)
        dy_low = dssd[:, lanes]
        dy = dy_low.astype(f32)
        dt_pair = pair_spread(dt, pair, left)
        tail_pair = pair_spread(tail, pair, left)
        stepped = (x_pair * dt_pair).astype(bf16).astype(f32)
        inner = mm(across(stepped, left), dy_low, 1, 1)
        mixing = []
        for place, head in enumerate((2 * pair, 2 * pair + 1)):
            spread = run_t[head : head + 1, :] - run[:, head : head + 1]
            decays = jnp.exp(jnp.minimum(spread, 0.0))
            mixing.append((decays * scores).astype(bf16))
            pairs = pairs + inner[place * CHUNK : (place + 1) * CHUNK] * decays
        flow = mm(jnp.concatenate(mixing, axis=1), across(dy, left)) + tail_pair * flows[:, lanes]
        dmix[:, lanes] = dt_pair * flow + skip[:, lanes] * dy
        both[0:CHUNK, lanes] = flow * x_pair
        both[CHUNK : 2 * CHUNK, lanes] = dy * (ssd[:, lanes] - skip[:, lanes] * x_pair) - flow * stepped
        dskip[0:1, lanes] += jnp.sum(dy * x_pair, axis=0, keepdims=True)
        high, low = split(pair_spread(entry, pair, left) * dy)
        entries[0, :, lanes] = high
        entries[1, :, lanes] = low
        weighted[:, lanes] = (tail_pair * stepped).astype(bf16)
        dstate[:, lanes] = pair_spread(factor, pair, left) * dstate[:, lanes]
    pairs = jnp.where(allowed, pairs, 0.0)
    dstate[...] += mm(c_turned, entries[0]) + mm(c_turned, entries[1])
    dmix[:, width : width + N] = mm(weighted[...], state_high, 1, 1) + mm_left(pairs, c_out)
    dmix[:, width + N :] = mm(entries[0], hin[0].astype(bf16), 1, 1) + mm_left(pairs, b_in, 0, 0)

    by_head = mm_left(both[...], heads_of[...])
    direct = by_head[0:CHUNK]
    balance = by_head[CHUNK:]
    later = allowed.astype(f32)
    log_grad = jnp.dot(later, balance, precision=highest, preferred_element_type=f32)
    log_grad = log_grad + table[:, NEXT : NEXT + 1] * carry[0:1, :]
    carry[0:1, :] = log_grad[0:1, :]
    step_grad = (direct - rate * log_grad) * sigmoid(step_in)
    dcommon_o[:, 2 * N :] = pltpu.roll(step_grad, heads * rank[0], 1)
    dheads_o[0:1, :] += jnp.sum(step_grad, axis=0, keepdims=True)
    dheads_o[1:2, :] += jnp.sum(-(log_grad * dt * rate), axis=0, keepdims=True)

    for start in range(0, channels, 256):
        cols = slice(start, start + 256)
        value = pre[:, cols]
        sig = sigmoid(value)
        dwin[0:CHUNK, cols] = dmix[:, cols] * (sig * (1.0 + value * (1.0 - sig)))
        here = ch[:, cols]
        own = dwin[0:CHUNK, cols]
        total = conv[3:4, cols] * own
        dconv_o[4:5, cols] += jnp.sum(own, axis=0, keepdims=True)
        dconv_o[3:4, cols] += jnp.sum(own * here, axis=0, keepdims=True)
        for ahead in range(1, 4):
            moved = dwin[ahead : ahead + CHUNK, cols] * table[:, AHEAD + ahead : AHEAD + ahead + 1]
            total = total + conv[3 - ahead : 4 - ahead, cols] * moved
            dconv_o[3 - ahead : 4 - ahead, cols] += jnp.sum(moved * here, axis=0, keepdims=True)
        if start < width:
            dval_o[:, cols] = total.astype(bf16)
        else:
            dcommon_o[:, : 2 * N] = total
    dwin[CHUNK:, :] = dwin[0:8, :]
    dtail[...] = dwin[0:8, :]

    @pl.when(pl.program_id(0) == pl.num_programs(0) - 1)
    def _():
        dheads_o[2:3, :] = mm_left(dskip[...], heads_of[...])[0:1, :]


def scatter_blocks(dp, me, full, keep_o, send_o, cols):
    half = dp // CORES
    block = full.shape[0] // dp
    for place, distance in enumerate(relative_places(dp)):
        start = pl.multiple_of((me[0] ^ distance) * block, block)
        part = full[pl.ds(start, block), :].astype(bf16)
        if place < half:
            keep_o[place, :, cols] = part
        else:
            send_o[place - half, :, cols] = part


def weight_grad_kernel(dp, me, lhs, rhs, keep_o, send_o, turned, full):
    @pl.when(pl.program_id(0) == 0)
    def _():
        turned[...] = lhs[...].T

    full[...] = mm(turned[...], rhs[...])
    scatter_blocks(dp, me, full, keep_o, send_o, slice(None))


def weight_grad(lhs, rhs, dp, dp_rank, skipped=0):
    length, width = rhs.shape[0], rhs.shape[1] - 256 * skipped
    depth = lhs.shape[1]
    block, half = depth // dp, dp // CORES
    piece = pl.BlockSpec((half, block, 256), lambda i, *s: (0, 0, i))
    return call(
        functools.partial(weight_grad_kernel, dp),
        (width // 256,),
        [whole((length, depth)), pl.BlockSpec((length, 256), lambda i, *s: (0, i + skipped))],
        [piece, piece],
        [shape(half, block, width, dtype=bf16)] * 2,
        [pltpu.VMEM((depth, length), bf16), pltpu.VMEM((depth, 256), f32)],
        2 * length * width * depth,
        10,
        scalars=1,
    )(dp_rank, lhs, rhs)


def value_grad_kernel(dp, me, lhs, dval, dcommon, keep_o, send_o, turned, full, wide):
    step = pl.program_id(0)
    last = pl.num_programs(0) - 1

    @pl.when(step == 0)
    def _():
        turned[...] = lhs[...].T

    @pl.when(step < last)
    def _():
        full[...] = mm(turned[...], dval[...])
        cols = pl.ds(pl.multiple_of(step * 256, 256), 256)
        scatter_blocks(dp, me, full, keep_o, send_o, cols)

    @pl.when(step == last)
    def _():
        wide[...] = mm_right(turned[...], dcommon[...])
        cols = slice(keep_o.shape[2] - wide.shape[1], keep_o.shape[2])
        scatter_blocks(dp, me, wide, keep_o, send_o, cols)


def value_grad(lhs, dval, dcommon, dp, dp_rank):
    length, width = dval.shape[0], 256
    depth, extra = lhs.shape[1], dcommon.shape[1]
    block, half, per = depth // dp, dp // CORES, width // 256
    dims = (half, block, width + extra)
    return call(
        functools.partial(value_grad_kernel, dp),
        (per + 1,),
        [
            whole((length, depth)),
            pl.BlockSpec((length, 256), lambda i, *s: (0, jnp.minimum(i, per - 1))),
            whole((length, extra)),
        ],
        [result(dims), result(dims)],
        [shape(*dims, dtype=bf16)] * 2,
        [
            pltpu.VMEM((depth, length), bf16), pltpu.VMEM((depth, 256), f32),
            pltpu.VMEM((depth, extra), f32),
        ],
        2 * length * (width + 2 * extra) * depth,
        15,
        scalars=1,
    )(dp_rank, lhs, dval, dcommon)


def input_grad_kernel(rank, dgate, dval, dcommon, tok, wg, wv, shw, ng_o, gain_o):
    @pl.when(pl.program_id(0) == 0)
    def _():
        gain_o[...] = jnp.zeros(gain_o.shape, f32)

    grad = mm(dgate[...], wg[...], 1, 1) + mm(dval[...], wv[...], 1, 1)
    grad = grad + mm_left(dcommon[...], shw[...], 1, 1)
    x = tok[...].astype(f32)
    inverse = lax.rsqrt(jnp.mean(x * x, axis=1, keepdims=True) + norm_epsilon)
    gain_o[...] += jnp.sum(grad * (x * inverse), axis=0, keepdims=True)
    ng_o[...] = grad.astype(ng_o.dtype)


def shards(
    dp, nt,
    residual, cotangent, sequence_ids,
    inner_proj, inner_mean, inner_square,
    shared_proj, shared_mean, shared_square,
    outer_proj, outer_mean, outer_square,
    conv_params, conv_mean, conv_square,
    norm_gains, gains_mean, gains_square,
    head_params, heads_mean, heads_square,
):
    t_rank = lax.axis_index("tensor").astype(jnp.int32)
    d_rank = lax.axis_index("dp").astype(jnp.int32)
    dp_me = d_rank[None]
    t_me = t_rank[None]
    rows_here = residual.shape[0]
    length = rows_here * nt
    width = inner_proj.shape[2]
    heads_here = head_params.shape[1]
    head_size = width // heads_here
    channels = width + 2 * N
    chunks = length // CHUNK
    wide = 2 * CHUNK
    band = min(2 * CHUNK, rows_here)
    per_piece = rows_here // band

    def pieces_of(value):
        return [value] + [swap(value, "tensor", nt, d) for d in range(1, nt)]

    def over_tensor(value, pieces=None):
        pieces = pieces_of(value) if pieces is None else pieces
        if nt == 2:
            first = jnp.concatenate(pieces, axis=0)
            second = jnp.concatenate(pieces[::-1], axis=0)
            return jnp.where(t_rank == 0, first, second)
        stacked = jnp.take(jnp.stack(pieces), jnp.arange(nt) ^ t_rank, axis=0)
        return stacked.reshape((nt * stacked.shape[1],) + stacked.shape[2:])

    kernel_rows, columns = conv_params.shape
    gain_count = norm_gains.shape[0]
    shared_size = shared_proj.size
    exact = jnp.concatenate([conv_params.reshape(-1), norm_gains])
    terms = []
    rest = exact
    for _ in range(3):
        term = lax.optimization_barrier(rest.astype(bf16))
        terms.append(term)
        rest = rest - term.astype(f32)
    common_width = 2 * N + LANES
    shared_rows = shared_proj.shape[0]
    packed = width == 1024 and shared_rows == 32
    if packed:
        wide_shared = jnp.pad(shared_proj.astype(bf16), ((0, 0), (0, common_width - 2 * N - H)))
        flat = jnp.concatenate(terms)
        flat = jnp.pad(flat, (0, 16 * 256 - flat.size)).reshape(16, 256)
        small = jnp.concatenate([wide_shared[:16], wide_shared[16:], flat], axis=1)
        small_rows = 16
    else:
        small = jnp.concatenate([shared_proj.astype(bf16).reshape(-1)] + terms)
        small_rows = -(-small.size // width)
        while small_rows * nt % 16:
            small_rows += 1
        small = jnp.pad(small, (0, small_rows * width - small.size)).reshape(small_rows, width)
    small_pair = over_tensor(small)
    token_pieces = pieces_of(residual)

    block_rows = D // dp
    value_shard = jnp.concatenate([inner_proj[1].astype(bf16), small_pair], axis=0)
    cut = -(-value_shard.shape[0] // 32) * 16
    first_line = gather_line(value_shard[:cut], dp)
    second_shard, first_line = tie(value_shard[cut:], first_line)
    second_line = gather_line(second_shard, dp)
    second_line, ids = tie(second_line, sequence_ids)
    first_near = jnp.concatenate([first_line] + plane_parts(first_line, dp), axis=0)
    other_shard = jnp.concatenate(
        [inner_proj[0].astype(bf16), outer_proj.T.astype(bf16)], axis=0
    )
    other_shard, second_line = tie(other_shard, second_line)
    other_line = gather_line(other_shard, dp)
    second_line, *parts = tie(second_line, *plane_parts(second_line, dp), *token_pieces)
    parts, token_pieces = parts[:-nt], parts[-nt:]
    second_near = jnp.concatenate([second_line] + parts, axis=0)
    cotangent_now, *token_pieces = tie(cotangent, *token_pieces)
    cot_pieces = pieces_of(cotangent_now)
    first_far, second_far = swap(first_near, "dp", dp, 1), swap(second_near, "dp", dp, 1)
    full = slice(None)
    moves = [(0, block_rows, full, 0, 1, 0, 0)]
    dims = [(dp, block_rows, width)]
    if packed:
        for t in range(nt):
            at = (block_rows + 16 * t, block_rows + 16 * t + 16)
            moves.append(at + (slice(0, common_width), 1, nt, t, 0))
            moves.append(at + (slice(common_width, 2 * common_width), 1, nt, t, 16))
            moves.append(at + (slice(2 * common_width, width), 2, nt, t, 0))
        dims += [(dp * nt, 32, common_width), (dp * nt, 16, 256)]
    else:
        moves.append((block_rows, block_rows + small_rows * nt, full, 1, 1, 0, 0))
        dims += [(dp, small_rows * nt, width)]
    value_w, *small_all = assemble(
        [first_near, second_near], [first_far, second_far], dp, dp_me, moves, dims
    )
    value_w = value_w.reshape(D, width)

    def halves(pieces):
        if nt == 2:
            return t_me, pieces[0], pieces[1]
        all_rows = over_tensor(None, pieces)
        return jnp.zeros((1,), jnp.int32), all_rows[: length // 2], all_rows[length // 2 :]

    if packed:
        shared_here = small_all[0].reshape(D, common_width)
        exact_all = small_all[1].reshape(dp * nt, -1)[:, : 3 * exact.size].astype(f32)
    else:
        small_all = small_all[0].reshape(dp * nt, small_rows * width)
        shared_here = small_all[:, :shared_size].reshape(D, -1)
        shared_here = jnp.pad(shared_here, ((0, 0), (0, common_width - 2 * N - H)))
        exact_all = small_all[:, shared_size : shared_size + 3 * exact.size].astype(f32)
    exact_all = exact_all.reshape(dp * nt, 3, exact.size)
    exact_all = (exact_all[:, 0] + exact_all[:, 1]) + exact_all[:, 2]
    conv_full = (
        exact_all[:, : kernel_rows * columns]
        .reshape(dp * nt, kernel_rows, columns)
        .transpose(1, 0, 2)
        .reshape(kernel_rows, -1)
    )
    gains_full = exact_all[:, kernel_rows * columns :].reshape(-1)

    pre_gain = gains_full[:D].reshape(1, D)
    post_gain = lax.dynamic_slice_in_dim(gains_full, D + t_rank * width, width).reshape(1, width)
    conv_here = jnp.concatenate(
        [lax.dynamic_slice_in_dim(conv_full, t_rank * width, width, 1), conv_full[:, DI:]], axis=1
    )
    conv_here = jnp.pad(conv_here, ((0, 8 - kernel_rows), (0, 0)))
    head_rows = jnp.stack([head_params[0], jnp.exp(head_params[1])])
    head_rows = jnp.pad(head_rows, ((0, 6), (0, LANES - heads_here)))
    skip = jnp.repeat(head_params[2], head_size).reshape(1, width)
    heads_of = (
        jnp.arange(width)[:, None] // head_size == jnp.arange(LANES)[None, :]
    ).astype(bf16)

    blocked = ids.reshape(chunks, CHUNK)
    ends, firsts = blocked[:, -1], blocked[:, 0]
    none = jnp.full((1,), -1, jnp.int32)
    before = jnp.concatenate([none, ends[:-1]])
    following = jnp.concatenate([firsts[1:], none])
    fills = [jnp.full((o,), -1, jnp.int32) for o in range(1, 4)]
    marks = [ids]
    marks += [jnp.concatenate([fills[o - 1], ids[:-o]]) == ids for o in range(1, 4)]
    marks += [jnp.concatenate([ids[o:], fills[o - 1]]) == ids for o in range(1, 4)]
    marks += [
        (blocked == before[:, None]).reshape(-1),
        (blocked == ends[:, None]).reshape(-1),
        jnp.broadcast_to((ends == before)[:, None], blocked.shape).reshape(-1),
        (blocked == following[:, None]).reshape(-1),
        ids < SEQ_SLOTS,
    ]
    aux = jnp.stack([m.astype(f32) for m in marks] + [jnp.zeros((length,), f32)] * 4, axis=1)
    segr = ids.astype(f32).reshape(1, length)
    aux_cols = aux.shape[1]

    steps = length // wide
    in_half = lambda i: i % (steps // 2)
    value_w, other_line, *cot_pieces = tie(value_w, other_line, *cot_pieces)
    plane = plane_parts(other_line, dp)
    tok_rank, tok0, tok1 = halves(token_pieces)
    normed, chans, pre, mixed, ssd, entering, step_in = call(
        functools.partial(scan_kernel, heads_here),
        (steps,),
        [
            rows(wide, D, in_half), rows(wide, D, in_half), whole((1, D)), whole((D, width)),
            whole((D, common_width)), whole((8, channels)), whole((1, width)), whole((8, LANES)),
            rows(wide, aux_cols), pl.BlockSpec((1, wide), lambda i, r: (0, i)),
        ],
        [
            rows(wide, D), rows(wide, channels), rows(wide, channels), rows(wide, channels),
            rows(wide, width), pl.BlockSpec((wide // CHUNK, N, width), lambda i, r: (i, 0, 0)),
            rows(wide, LANES),
        ],
        [
            shape(length, D, dtype=bf16), shape(length, channels), shape(length, channels),
            shape(length, channels, dtype=bf16), shape(length, width),
            shape(chunks, N, width), shape(length, LANES),
        ],
        [
            pltpu.VMEM((wide + 8, channels), f32), pltpu.VMEM((N, width), f32),
            pltpu.VMEM((CHUNK, width), f32), pltpu.VMEM((2, CHUNK, width), bf16),
        ],
        length * (2 * D * (width + common_width) + 12 * width * CHUNK),
        22,
        scalars=1,
    )(jnp.concatenate([tok_rank, t_me]), tok0, tok1, pre_gain, value_w, shared_here, conv_here, skip, head_rows, aux, segr)

    normed, *plane = tie(normed, *plane)
    plane = jnp.concatenate([other_line] + plane, axis=0)
    moves = [
        (0, block_rows, full, 0, 1, 0, 0), (block_rows, 2 * block_rows, full, 1, 1, 0, 0)
    ]
    gate_w, outer_t = assemble(
        [plane], [swap(plane, "dp", dp, 1)], dp, dp_me, moves, [(dp, block_rows, width)] * 2
    )
    gate_w, outer_t = gate_w.reshape(D, width), outer_t.reshape(D, width)
    cot_rank, cot0, cot1 = halves(cot_pieces)
    gate, scaled_grad, returned, sums = call(
        gate_kernel,
        (steps,),
        [
            rows(wide, D), rows(wide, D, in_half), rows(wide, D, in_half), rows(wide, aux_cols),
            rows(wide, width), whole((D, width)), whole((D, width)), whole((1, width)),
        ],
        [rows(wide, width), rows(wide, width), rows(wide, D), pl.BlockSpec((8, wide), lambda i, r: (0, i))],
        [
            shape(length, width), shape(length, width), shape(length, D, dtype=bf16),
            shape(8, length),
        ],
        [],
        4 * length * D * width,
        15,
        scalars=1,
    )(cot_rank, normed, cot0, cot1, aux, ssd, gate_w, outer_t, post_gain)
    distance = 1
    while distance < nt:
        sums = sums + swap(sums, "tensor", nt, distance)
        distance *= 2

    def relative(block, rank):
        return (rank ^ (block // per_piece)) * per_piece + block % per_piece

    def rel_rows(width_here, offset=0):
        return pl.BlockSpec((band, width_here), lambda i, r: (relative(i + offset, r[0]), 0))

    plain = lambda width_here: pl.BlockSpec((band, width_here), lambda i, r: (i, 0))
    branch, scaled, dssd, dgate, post_grad = call(
        norm_kernel,
        (length // band,),
        [
            rel_rows(width), rel_rows(width), rel_rows(width),
            pl.BlockSpec((8, band), lambda i, r: (0, relative(i, r[0]))),
            whole((D, width)), whole((1, width)),
        ],
        [plain(D), rel_rows(width), rel_rows(width), rel_rows(width), result((1, width))],
        [
            shape(length, D, dtype=bf16), shape(length, width, dtype=bf16),
            shape(length, width, dtype=bf16), shape(length, width, dtype=bf16), shape(1, width),
        ],
        [],
        2 * length * D * width,
        15,
        scalars=1,
    )(t_me, gate, scaled_grad, ssd, sums, outer_t, post_gain)
    outer_keep, outer_send = weight_grad(returned, scaled, dp, dp_me)
    dgate, outer_send = tie(dgate, outer_send)
    gate_keep, gate_send = weight_grad(normed, dgate, dp, dp_me)
    outer_line, outer_rest = start_sum(outer_keep, outer_send, dp)
    gate_line, gate_rest = start_sum(gate_keep, gate_send, dp)
    branch = branch.reshape(nt, rows_here, D)
    branch_received = [swap(branch[d], "tensor", nt, d) for d in range(1, nt)]
    dssd, *rests = tie(dssd, *outer_rest, *gate_rest)
    outer_rest, gate_rest = rests[: len(outer_rest)], rests[len(outer_rest) :]
    outer_received = middle_swaps(outer_rest, dp)
    gate_received = middle_swaps(gate_rest, dp)

    state = jnp.zeros((N, width), f32)
    win = jnp.zeros((8, channels), f32)
    carry = jnp.zeros((8, LANES), f32)
    back_parts = []
    filled = []
    top = chunks
    for part, count in enumerate((3, 3, chunks - 6)):
        back = lambda i, top=top: top - 1 - i
        top -= count
        *results, state, win, carry = call(
            functools.partial(scan_back_kernel, heads_here),
            (count,),
            [
                rows(CHUNK, width, back), rows(CHUNK, channels, back), rows(CHUNK, channels, back),
                rows(CHUNK, channels, back), rows(CHUNK, width, back),
                pl.BlockSpec((1, N, width), lambda i, r, back=back: (back(i), 0, 0)),
                rows(CHUNK, LANES, back), whole((8, channels)), whole((1, width)),
                whole((8, LANES)), rows(CHUNK, aux_cols, back),
                pl.BlockSpec((1, CHUNK), lambda i, r, back=back: (0, back(i))),
                whole((width, LANES)),
                whole((N, width)), whole((8, channels)), whole((8, LANES)),
            ]
            + [pl.BlockSpec(memory_space=pl.ANY)] * len(filled),
            [
                rows(CHUNK, width, back), rows(CHUNK, common_width, back), result((8, channels)),
                result((8, LANES)),
                result((N, width)), result((8, channels)), result((8, LANES)),
            ],
            [
                shape(length, width, dtype=bf16), shape(length, common_width),
                shape(8, channels), shape(8, LANES),
                shape(N, width), shape(8, channels), shape(8, LANES),
            ],
            [
                pltpu.VMEM((CHUNK, channels), f32), pltpu.VMEM((CHUNK + 8, channels), f32),
                pltpu.VMEM((2 * CHUNK, width), f32), pltpu.VMEM((CHUNK, width), f32),
                pltpu.VMEM((2, CHUNK, width), bf16), pltpu.VMEM((CHUNK, width), bf16),
                pltpu.VMEM((8, width), f32),
            ],
            count * CHUNK * 30 * width * CHUNK,
            14,
            scalars=1,
            aliases={17: 0, 18: 1} if filled else None,
        )(
            t_me, dssd, mixed, pre, chans, ssd, entering, step_in, conv_here, skip, head_rows, aux, segr,
            heads_of, state, win, carry, *filled,
        )
        filled = results[:2]
        back_parts.append(results[2:])
        if part == 0:
            state, outer_line, *outer_received = tie(state, outer_line, *outer_received)
            outer_block, outer_far = middle_sum(outer_line, outer_received)
            outer_far = high_swaps(outer_far, dp)
        if part == 1:
            state, gate_line, *rests = tie(
                state, gate_line, *branch_received, *gate_received, *outer_far
            )
            branch_received = rests[: nt - 1]
            gate_received, outer_far = rests[nt - 1 : -len(outer_far)], rests[-len(outer_far) :]
            gate_block, gate_far = middle_sum(gate_line, gate_received)
            gate_far = high_swaps(gate_far, dp)
    dval, dcommon = filled
    dval, *gate_far = tie(dval, *gate_far)

    branch_sum = branch[0].astype(f32)
    for piece in branch_received:
        branch_sum = branch_sum + piece.astype(f32)
    live_here = lax.dynamic_slice_in_dim(aux[:, LIVE], t_rank * rows_here, rows_here)
    tokens = residual.astype(f32)
    block_out = (tokens + branch_sum * live_here[:, None]).astype(bf16)

    def input_grad(count, offset, dtype, positions, dgate):
        return call(
            input_grad_kernel,
            (count * per_piece,),
            [
                rel_rows(width, offset), rel_rows(width, offset), rel_rows(common_width, offset),
                plain(D), whole((D, width)), whole((D, width)), whole((D, common_width)),
            ],
            [plain(D), result((1, D))],
            [shape(count * rows_here, D, dtype=dtype), shape(1, D)],
            [],
            4 * count * rows_here * D * (width + common_width),
            13,
            scalars=1,
        )(t_me, dgate, dval, dcommon, positions, gate_w, value_w, shared_here)

    keep, send = value_grad(normed, dval, dcommon, dp, dp_me)
    line, part = start_sum(keep, send, dp)
    two = width > 256
    lines, parts = [line], [part]
    if two:
        dval, *parts[0] = tie(dval, *parts[0])
        keep, send = weight_grad(normed, dval, dp, dp_me, skipped=1)
        line, part = start_sum(keep, send, dp)
        lines.append(line)
        parts.append(part)
    each = len(part)
    dgate, *flat = tie(dgate, *[item for part in parts for item in part])
    crossing = [middle_swaps(flat[at : at + each], dp) for at in range(0, len(flat), each)]
    others = token_pieces[1] if nt == 2 else jnp.concatenate(token_pieces[1:], axis=0)
    sent, pre_grad_sent = input_grad(nt - 1, per_piece, bf16, others, dgate)
    sent = sent.reshape(nt - 1, rows_here, D)
    received = [swap(sent[d - 1], "tensor", nt, d) for d in range(1, nt)]
    small_grads = [item for each_part in back_parts for item in each_part]
    dgate, pre_grad_sent, *rests = tie(dgate, pre_grad_sent, *crossing[0], *small_grads)
    crossing[0], small_grads = rests[:each], rests[each:]
    block, far = middle_sum(lines[0], crossing[0])
    blocks, fars = [block], [high_swaps(far, dp)]
    own, pre_grad_own = input_grad(1, 0, f32, residual, dgate)
    if two:
        pre_grad_own, *rests = tie(pre_grad_own, *crossing[1], *fars[0])
        crossing[1], fars[0] = rests[:each], rests[each:]
        block, far = middle_sum(lines[1], crossing[1])
        pre_grad_own, *far = tie(pre_grad_own, *far)
        blocks.append(block)
        fars.append(high_swaps(far, dp))
    dconv, dheads = [sum(small_grads[at::2]) for at in range(2)]
    conv_grad = lax.dynamic_update_slice(
        jnp.pad(dconv[:kernel_rows, width:], ((0, 0), (DI, 0))),
        dconv[:kernel_rows, :width],
        (0, t_rank * width),
    )
    post_all = lax.dynamic_update_slice(
        jnp.zeros((1, DI), f32), post_grad, (0, t_rank * width)
    )
    head_grad = dheads[:3, :heads_here]
    head_all = lax.dynamic_update_slice(
        jnp.zeros((3, H), f32), head_grad, (0, t_rank * heads_here)
    )
    vector = jnp.concatenate(
        [
            conv_grad.reshape(1, -1), pre_grad_sent + pre_grad_own, post_all, head_all.reshape(1, -1),
        ],
        axis=1,
    )
    for stage, (axis, size, distance) in enumerate(sum_stages(dp, nt)):
        vector = vector + swap(vector, axis, size, distance)
        if stage == 0:
            value_sums = [high_sum(blocks[0], fars[0])]
            vector, outer_block, gate_block = tie(vector, outer_block, gate_block)
            outer_part = high_sum(outer_block, outer_far)
            gate_part = high_sum(gate_block, gate_far)
        if stage == 1:
            vector, *received = tie(vector, *received)
        if stage == 1 and two:
            vector, *fars[1] = tie(vector, *fars[1])
            value_sums.append(high_sum(blocks[1], fars[1]))
    shared_sum = value_sums[0][:, 256:].reshape(nt, shared_rows, common_width)
    shared_mine = lax.dynamic_index_in_dim(shared_sum, t_rank, 0, False)
    for d in range(1, nt):
        piece = lax.dynamic_index_in_dim(shared_sum, t_rank ^ d, 0, False)
        shared_mine = shared_mine + swap(piece, "tensor", nt, d)
    shared_part = shared_mine[:, : 2 * N + H]
    value_part = jnp.concatenate([value_sums[0][:, :256]] + value_sums[1:], axis=1)
    conv_size = kernel_rows * (DI + 2 * N)
    place = d_rank * nt + t_rank
    conv_part = lax.dynamic_slice_in_dim(
        vector[0, :conv_size].reshape(kernel_rows, -1), place * columns, columns, 1
    )
    gains_part = lax.dynamic_slice_in_dim(vector[0], conv_size + place * gain_count, gain_count)
    heads_part = lax.dynamic_slice_in_dim(
        vector[0, conv_size + D + DI :].reshape(3, H), t_rank * heads_here, heads_here, 1
    )

    normed_grad = own
    for piece in received:
        normed_grad = normed_grad + piece.astype(f32)
    inverse = lax.rsqrt(jnp.mean(tokens * tokens, axis=1, keepdims=True) + norm_epsilon)
    normal_tokens = tokens * inverse
    normal_grad = normed_grad * pre_gain
    centered = normal_grad - normal_tokens * jnp.mean(
        normal_grad * normal_tokens, axis=1, keepdims=True
    )
    residual_grad = (cotangent.astype(f32) + inverse * centered).astype(bf16)

    inner_new = adam_step(
        inner_proj, inner_mean, inner_square, jnp.stack([gate_part, value_part]),
        rate_matrix, weight_decay,
    )
    shared_new = adam_step(
        shared_proj, shared_mean, shared_square, shared_part.reshape(shared_proj.shape),
        rate_matrix, weight_decay,
    )
    outer_new = adam_step(
        outer_proj, outer_mean, outer_square, outer_part.T, rate_matrix, weight_decay
    )
    conv_new = adam_step(conv_params, conv_mean, conv_square, conv_part, rate_vector, 0.0)
    gains_new = adam_step(norm_gains, gains_mean, gains_square, gains_part, rate_vector, 0.0)
    heads_new = adam_step(head_params, heads_mean, heads_square, heads_part, rate_heads, 0.0)
    return (
        (block_out, residual_grad)
        + inner_new + shared_new + outer_new + conv_new + gains_new + heads_new
    )


def solution(mesh):
    return jax.shard_map(
        functools.partial(shards, mesh.shape["dp"], mesh.shape["tensor"]),
        mesh=mesh,
        in_specs=(
            P(("dp", "tensor"), None),
            P(("dp", "tensor"), None),
            P("dp"),
            P(None, "dp", "tensor"),
            P(None, "dp", "tensor"),
            P(None, "dp", "tensor"),
            P(("dp", "tensor"), None),
            P(("dp", "tensor"), None),
            P(("dp", "tensor"), None),
            P("tensor", "dp"),
            P("tensor", "dp"),
            P("tensor", "dp"),
            P(None, ("dp", "tensor")),
            P(None, ("dp", "tensor")),
            P(None, ("dp", "tensor")),
            P(("dp", "tensor")),
            P(("dp", "tensor")),
            P(("dp", "tensor")),
            P(None, "tensor"),
            P(None, "tensor"),
            P(None, "tensor"),
        ),
        out_specs=(
            P(("dp", "tensor"), None),
            P(("dp", "tensor"), None),
            P(None, "dp", "tensor"),
            P(None, "dp", "tensor"),
            P(None, "dp", "tensor"),
            P(("dp", "tensor"), None),
            P(("dp", "tensor"), None),
            P(("dp", "tensor"), None),
            P("tensor", "dp"),
            P("tensor", "dp"),
            P("tensor", "dp"),
            P(None, ("dp", "tensor")),
            P(None, ("dp", "tensor")),
            P(None, ("dp", "tensor")),
            P(("dp", "tensor")),
            P(("dp", "tensor")),
            P(("dp", "tensor")),
            P(None, "tensor"),
            P(None, "tensor"),
            P(None, "tensor"),
        ),
        check_vma=False,
    )
```
